32 devices in a mesh: ctx: 16 (over z, y, x), head: 2 (over core).
Axes of the slice: x: 2, y: 2, z: 4, core: 2. Of those that a mesh axis runs over, the one named last changes fastest.
Arguments:
- queries: bfloat16 [4096, 32, 128], P('ctx', 'head'), may hold values from -300 to 300
- keys: bfloat16 [4096, 8, 128], P('ctx', 'head'), may hold values from -12 to 12
- values: bfloat16 [4096, 8, 128], P('ctx', 'head'), may hold values from -150 to 150
- tangent_queries: bfloat16 [4096, 32, 128], P('ctx', 'head'), may hold values from -6 to 6
- tangent_keys: bfloat16 [4096, 8, 128], P('ctx', 'head'), may hold values from -6 to 6
- tangent_values: bfloat16 [4096, 8, 128], P('ctx', 'head'), may hold values from -6 to 6
- doc_start: int32 [32], P('ctx'), may hold values from 0 to 31, as said below
- out_gain: float32 [4096], P('head'), may hold values from 0.1 to 1.9
Outputs:
- product_queries: float32 [4096, 32, 128], P('ctx', 'head')
- product_keys: float32 [4096, 8, 128], P('ctx', 'head')
- product_values: float32 [4096, 8, 128], P('ctx', 'head')
The draws below stay inside these ranges and needn't reach their ends.
Inputs may be any that keep to these rules, and one draw needn't show every extreme that they name: Documents are runs of whole mask blocks; doc_start[b] is the first block of b's document, so it never falls and doc_start[b] <= b. No document is longer than 16 blocks, and one is exactly 16 blocks long.
All inputs are finite; a program needn't handle non-finite values.
Results may differ from the reference program's by a relative error of at most 0.014.
Values may be sent and summed in bfloat16 or wider, within the bound.
No kernel may reach another device: no remote copies, remote signals or barrier semaphores. Data moves between devices by JAX's collectives and lax.ppermute only.
A program may use at most 192 MiB of HBM per device.

```python
import jax
import jax.numpy as jnp
from jax import lax

QH = 32
KVH = 8
HD = 128
TOK_DEV = 256
BLOCK = 128
DOC_DEVS = 8
TOKENS = 4096
DOC_BLOCKS = 16


def paired_rows(key):
    base = jax.random.fold_in(key, 11)
    key_rows = jnp.clip(jax.random.normal(jax.random.fold_in(base, 1), (TOKENS, KVH, HD), jnp.float32), -5.0, 5.0)
    query_rows = jnp.clip(jax.random.normal(jax.random.fold_in(base, 2), (TOKENS, QH, HD), jnp.float32), -5.0, 5.0)
    return (query_rows, key_rows)


def draw_queries(key, part):
    return paired_rows(key)[0].astype(jnp.bfloat16)


def draw_keys(key, part):
    return paired_rows(key)[1].astype(jnp.bfloat16)


def draw_values(key, part):
    base = jax.random.fold_in(key, 23)
    raw = jnp.clip(jax.random.normal(jax.random.fold_in(base, 1), (TOKENS, KVH, HD), jnp.float32), -5.0, 5.0)
    columns = jnp.exp(jax.random.uniform(jax.random.fold_in(base, 2), (1, KVH, HD), jnp.float32, 0.0, 2.302585))
    ladder = jnp.arange(KVH, dtype=jnp.float32) / (KVH - 1)
    rise = 3.0 ** (0.5 * ladder)
    return (raw * columns * rise[None, :, None]).astype(jnp.bfloat16)


def draw_doc_start(key, part):
    blocks = TOKENS // BLOCK
    longest = DOC_BLOCKS
    per_device = TOK_DEV // BLOCK
    lengths = jax.random.randint(jax.random.fold_in(key, 31), (blocks,), 1, longest + 1)
    starts = jnp.cumsum(lengths) - lengths
    marks = jnp.zeros((blocks + 1,), jnp.int32).at[jnp.minimum(starts, blocks)].set(1)[:blocks]
    slots = (blocks - longest - 1) // per_device + 1
    pick = jax.random.randint(jax.random.fold_in(key, 37), (), 0, slots) * per_device + 1
    places = jnp.arange(blocks)
    inside = (places > pick) & (places < pick + longest)
    marks = jnp.where(inside, 0, marks)
    marks = jnp.where((places == pick) | (places == pick + longest), 1, marks)
    return lax.cummax(jnp.where(marks == 1, places, 0), axis=0).astype(jnp.int32)


def levels(stream_key, shape, split, low, largest):
    loudness, own = 1.0, jax.random.fold_in(stream_key, 6)
    for dim, parts in split:
        steps = jnp.exp(jax.random.uniform(jax.random.fold_in(own, dim), (parts,), jnp.float32, low / len(split), largest / len(split)))
        loudness = loudness * jnp.repeat(steps, shape[dim] // parts).reshape([-1 if axis == dim else 1 for axis in range(len(shape))])
    return loudness


def bell_draw(stream_key, extent, deviation, bound, split=(), kind=jnp.bfloat16):
    values = jax.random.normal(stream_key, extent, jnp.float32) * deviation
    if len(split) > 0:
        values = levels(stream_key, extent, split, -0.22, 0.18) * values
    return jnp.clip(values, min=-bound, max=bound).astype(kind)


def setup_inputs(seed: int = 0) -> dict:
    arg_keys = jax.random.split(jax.random.key(seed), 9)
    return {
        "queries": draw_queries(jax.random.fold_in(arg_keys[8], 71), 0),
        "keys": draw_keys(jax.random.fold_in(arg_keys[8], 71), 0),
        "values": draw_values(jax.random.fold_in(arg_keys[8], 71), 0),
        "tangent_queries": bell_draw(arg_keys[3], (TOKENS, QH, HD), 1.0, 6.0, ((0, 16), (1, 2))),
        "tangent_keys": bell_draw(arg_keys[4], (TOKENS, KVH, HD), 1.0, 6.0, ((0, 16), (1, 2))),
        "tangent_values": bell_draw(arg_keys[5], (TOKENS, KVH, HD), 1.0, 6.0, ((0, 16), (1, 2))),
        "doc_start": draw_doc_start(jax.random.fold_in(arg_keys[8], 71), 0),
        "out_gain": jnp.clip(1.0 + 0.18 * jax.random.normal(arg_keys[7], (QH * HD,), jnp.float32), 0.1, 1.9),
    }


EPSILON = 1e-06

def rounded(entries):
    return lax.optimization_barrier(entries.astype(jnp.bfloat16)).astype(jnp.float32)

def reference(queries, keys, values, tangent_queries, tangent_keys, tangent_values, doc_start, out_gain):
    group = QH // KVH
    scale = HD ** (-0.5)
    rows = TOK_DEV
    span = rows + DOC_DEVS * TOK_DEV
    count = TOKENS // rows
    features = QH * HD
    starts = jnp.repeat(doc_start * BLOCK, BLOCK)
    query_float = queries.astype(jnp.float32).reshape(TOKENS, KVH, group, HD)
    slope_query = tangent_queries.astype(jnp.float32).reshape(TOKENS, KVH, group, HD)
    key_float = keys.astype(jnp.float32)
    value_float = values.astype(jnp.float32)
    slope_key = tangent_keys.astype(jnp.float32)
    slope_value = tangent_values.astype(jnp.float32)
    gain_heads = out_gain.reshape(KVH, group, 1, HD)

    def first_key(number):
        return jnp.clip(number * rows + rows - span, 0, TOKENS - span).astype(jnp.int32)

    def query_block(array, number):
        return lax.dynamic_slice_in_dim(array, (number * rows).astype(jnp.int32), rows, 0).transpose(1, 2, 0, 3)

    def key_block(array, first):
        return lax.dynamic_slice_in_dim(array, first, span, 0)

    def allowed_at(number, first):
        query_pos = number * rows + jnp.arange(rows, dtype=jnp.int32)
        key_pos = first + jnp.arange(span, dtype=jnp.int32)
        own_start = lax.dynamic_slice_in_dim(starts, (number * rows).astype(jnp.int32), rows, 0)
        return (key_pos[None, :] >= own_start[:, None]) & (key_pos[None, :] <= query_pos[:, None])

    def forward_block(number):
        first = first_key(number)
        allowed = allowed_at(number, first)
        query_here = query_block(query_float, number)
        slope_here = query_block(slope_query, number)
        key_here = key_block(key_float, first)
        value_here = key_block(value_float, first)
        key_slope = key_block(slope_key, first)
        value_slope = key_block(slope_value, first)
        scores = scale * jnp.einsum('kgtd,ukd->kgtu', query_here, key_here)
        slopes = scale * (jnp.einsum('kgtd,ukd->kgtu', slope_here, key_here) + jnp.einsum('kgtd,ukd->kgtu', query_here, key_slope))
        most = lax.optimization_barrier(jnp.max(jnp.where(allowed, scores, -jnp.inf), axis=-1))
        weights = jnp.where(allowed, jnp.exp(scores - most[..., None]), 0.0)
        total = lax.optimization_barrier(jnp.sum(weights, axis=-1))
        weighted = lax.optimization_barrier(jnp.sum(weights * slopes, axis=-1))
        weights_b = rounded(weights)
        mixed_b = rounded(weights * slopes)
        plain = jnp.einsum('kgtu,ukd->kgtd', weights_b, value_here)
        moving = jnp.einsum('kgtu,ukd->kgtd', mixed_b, value_here) + jnp.einsum('kgtu,ukd->kgtd', weights_b, value_slope)
        output = plain / total[..., None]
        moved = moving / total[..., None] - (weighted / total)[..., None] * output
        return (output, moved, most + jnp.log(total))
    numbers = jnp.arange(count, dtype=jnp.int32)
    output, moved, log_norm = lax.map(forward_block, numbers)

    def spread_rows(stat):
        return stat[:, None, None, :, None]
    square = lax.optimization_barrier(jnp.sum(output * output, axis=(1, 2, 4))) / features + EPSILON
    cross = lax.optimization_barrier(jnp.sum(output * moved, axis=(1, 2, 4)))
    root = jnp.sqrt(square)
    tangent_y = gain_heads * (moved - output * spread_rows(cross / (features * square))) / spread_rows(root)
    grad_out = gain_heads * tangent_y
    back = lax.optimization_barrier(jnp.sum(output * grad_out, axis=(1, 2, 4)))
    cotangent = rounded((grad_out - output * spread_rows(back / (features * square))) / spread_rows(root))
    row_dot = lax.optimization_barrier(jnp.sum(cotangent * output, axis=-1))

    def backward_block(carry, inputs):
        key_grad, value_grad = carry
        number, norm_here, cot_here, dot_here = inputs
        first = first_key(number)
        allowed = allowed_at(number, first)
        query_here = query_block(query_float, number)
        key_here = key_block(key_float, first)
        value_here = key_block(value_float, first)
        scores = scale * jnp.einsum('kgtd,ukd->kgtu', query_here, key_here)
        probs = jnp.where(allowed, jnp.exp(scores - norm_here[..., None]), 0.0)
        prob_dot = jnp.einsum('kgtd,ukd->kgtu', cot_here, value_here)
        score_grad = rounded(probs * (prob_dot - dot_here[..., None]) * scale)
        query_part = jnp.einsum('kgtu,ukd->kgtd', score_grad, key_here)
        key_part = jnp.einsum('kgtu,kgtd->ukd', score_grad, query_here)
        value_part = jnp.einsum('kgtu,kgtd->ukd', rounded(probs), cot_here)
        key_grad = lax.dynamic_update_slice_in_dim(key_grad, lax.dynamic_slice_in_dim(key_grad, first, span, 0) + key_part, first, 0)
        value_grad = lax.dynamic_update_slice_in_dim(value_grad, lax.dynamic_slice_in_dim(value_grad, first, span, 0) + value_part, first, 0)
        return ((key_grad, value_grad), query_part)
    empty = jnp.zeros((TOKENS, KVH, HD), jnp.float32)
    (product_keys, product_values), query_parts = lax.scan(backward_block, (empty, empty), (numbers, log_norm, cotangent, row_dot))
    product_queries = query_parts.transpose(0, 3, 1, 2, 4).reshape(TOKENS, QH, HD)
    return (product_queries, product_keys, product_values)
```

```python
import functools
import math

import jax
import jax.numpy as jnp
from jax import lax
from jax.experimental import pallas as pl
from jax.experimental.pallas import tpu as pltpu
from jax.sharding import Mesh, PartitionSpec as P

DOC_DEVS = 8
EPSILON = 1e-06
VMEM_BYTES = 40 * 1024 * 1024
LOG2E = math.log2(math.e)
MASKED = -1e30
F32 = jnp.float32
BF16 = jnp.bfloat16
ANY = pl.BlockSpec(memory_space=pl.ANY)
SMEM = pl.BlockSpec(memory_space=pltpu.SMEM)


def params():
    return pltpu.CompilerParams(vmem_limit_bytes=VMEM_BYTES)


def cost(flops, moved, powers=0):
    return pl.CostEstimate(flops=int(flops), bytes_accessed=int(moved), transcendentals=int(powers))


def nn(a, b):
    return lax.dot_general(a, b, (((1,), (0,)), ((), ())), preferred_element_type=F32)


def nt(a, b):
    return lax.dot_general(a, b, (((1,), (1,)), ((), ())), preferred_element_type=F32)


def split_heads(arrays, me, parts, per_part):
    count = len(arrays)
    total, width = arrays[0].shape
    heads = parts * per_part
    rows = total // heads

    def kernel(me_ref, *refs):
        ins, outs, wide = refs[:count], refs[count : count + parts], refs[-1]
        mine = me_ref[0]
        for a in range(count):
            wide[...] = ins[a][...].astype(F32)
            for m in range(parts):
                for r in range(per_part):
                    head = jnp.bitwise_xor(mine, m) * per_part + r
                    outs[m][a, r] = wide[pl.ds(head, rows, stride=heads), :].astype(BF16)

    return pl.pallas_call(
        kernel,
        in_specs=[SMEM] + [pl.BlockSpec(memory_space=pltpu.VMEM)] * count,
        out_specs=[pl.BlockSpec(memory_space=pltpu.VMEM)] * parts,
        out_shape=[jax.ShapeDtypeStruct((count, per_part, rows, width), BF16)] * parts,
        scratch_shapes=[pltpu.VMEM((total, width), F32)],
        compiler_params=params(),
        cost_estimate=cost(0, 4 * count * total * width),
        name="split_heads",
    )(me, *arrays)


def join_heads(pieces, me, count, per_part):
    parts = len(pieces)
    rows, width = pieces[0].shape[-2:]
    heads = parts * per_part

    def kernel(me_ref, *refs):
        ins, outs = refs[:parts], refs[parts:]
        mine = me_ref[0]
        for a in range(count):
            for m in range(parts):
                for r in range(per_part):
                    head = jnp.bitwise_xor(mine, m) * per_part + r
                    outs[a][pl.ds(head, rows, stride=heads), :] = ins[m][a, r].astype(F32)

    return pl.pallas_call(
        kernel,
        in_specs=[SMEM] + [pl.BlockSpec(memory_space=pltpu.VMEM)] * parts,
        out_specs=[pl.BlockSpec(memory_space=pltpu.VMEM)] * count,
        out_shape=[jax.ShapeDtypeStruct((rows * heads, width), F32)] * count,
        compiler_params=params(),
        cost_estimate=cost(0, 6 * count * rows * heads * width),
        name="join_heads",
    )(me, *pieces)


def copy_in(pairs, sems):
    copies = [pltpu.make_async_copy(src, dst, sems.at[i]) for i, (src, dst) in enumerate(pairs)]
    for c in copies:
        c.start()
    for c in copies:
        c.wait()


def slot_of(me_ref, m, rows):
    return pl.multiple_of(jnp.bitwise_xor(me_ref[0], m) * rows, rows)


class Shape:
    def __init__(self, parts, group, rows, width, block):
        self.parts, self.group, self.rows, self.width, self.block = parts, group, rows, width, block
        self.tokens = parts * rows
        self.blocks = self.tokens // block
        self.lanes = group * block
        self.scale = width**-0.5
        self.powers = self.scale * LOG2E


def diagonal(sh):
    shape = (sh.block, sh.lanes)
    key = lax.broadcasted_iota(jnp.int32, shape, 0)
    query = lax.broadcasted_iota(jnp.int32, shape, 1) % sh.block
    return key <= query


def query_rows(sh, q_s, which, qb):
    rows = pl.ds(pl.multiple_of(qb * sh.block, sh.block), sh.block)
    return q_s[which, :, rows, :].reshape(sh.lanes, sh.width)


def forward_tile(sh, kv_s, vt_s, acc, qq, start, size, state, masked):
    w = sh.width
    start = pl.multiple_of(start, sh.block)
    k = kv_s[0, pl.ds(start, size), :]
    tk = kv_s[2, pl.ds(start, size), :]
    left = jnp.concatenate([k, tk], axis=0)
    right = jnp.concatenate([jnp.zeros_like(k), k], axis=0)
    both = nt(jnp.concatenate([left, right], axis=1), qq)
    s = both[:size] * sh.powers
    d = both[size:] * sh.scale
    if masked:
        low = jnp.where(diagonal(sh), s[size - sh.block :], MASKED)
        s = low if size == sh.block else jnp.concatenate([s[: size - sh.block], low], axis=0)
    most = jnp.max(s, axis=0, keepdims=True)
    if state is not None:
        most = jnp.maximum(most, state[0])
        decay = jnp.exp2(state[0] - most)
    e = jnp.exp2(s - most)
    mix = e * d
    total = jnp.sum(e, axis=0, keepdims=True)
    cross = jnp.sum(mix, axis=0, keepdims=True)
    vt = vt_s[:, pl.ds(start, size)]
    plain = nn(vt, e.astype(BF16))
    moving = nn(vt[:w], mix.astype(BF16))
    if state is None:
        acc[:w, :] = plain[:w]
        acc[w:, :] = plain[w:] + moving
        return most, total, cross
    acc[:w, :] = acc[:w, :] * decay + plain[:w]
    acc[w:, :] = acc[w:, :] * decay + (plain[w:] + moving)
    return most, state[1] * decay + total, state[2] * decay + cross


def forward_loop(sh, kv_s, vt_s, acc, stat, qq, start, count):
    def step(i, state):
        at = (start + 2 * i) * sh.block
        return forward_tile(sh, kv_s, vt_s, acc, qq, at, 2 * sh.block, state, False)

    @pl.when(count > 0)
    def _():
        state = lax.fori_loop(0, count, step, tuple(stat[r : r + 1, :] for r in range(3)))
        for r in range(3):
            stat[r : r + 1, :] = state[r]


def load_keys(sh, me_ref, chunks, kv_s, q_parts, q_s, sems):
    pairs = []
    for m in range(sh.parts):
        slot = slot_of(me_ref, m, sh.rows)
        if q_parts is not None:
            pairs.append((q_parts[m].at[: q_s.shape[0]], q_s.at[:, :, pl.ds(slot, sh.rows), :]))
        for number, chunk in enumerate(chunks):
            rows = pl.ds(number * sh.tokens + slot, sh.rows)
            pairs.append((chunk[m].at[: kv_s.shape[0]], kv_s.at[:, rows, :]))
    copy_in(pairs, sems)


def transposed(x):
    return x.astype(F32).T.astype(BF16)


def forward_near(sh, me, starts, q_parts, chunks):
    parts, near = sh.parts, len(chunks)
    flat = [p for chunk in chunks for p in chunk]
    span = near * sh.tokens
    copies = parts * (1 + near)

    def kernel(me_ref, start_ref, *refs):
        q_in = refs[:parts]
        kv_in = [refs[parts * (1 + c) : parts * (2 + c)] for c in range(near)]
        acc, stat, q_s, kv_s, vt_s, sems = refs[copies:]
        qb = pl.program_id(0)

        @pl.when(qb == 0)
        def _():
            load_keys(sh, me_ref, kv_in, kv_s, q_in, q_s, sems)
            vt_s[: sh.width, :] = transposed(kv_s[1])
            vt_s[sh.width :, :] = transposed(kv_s[3])

        qq = jnp.concatenate([query_rows(sh, q_s, 0, qb), query_rows(sh, q_s, 1, qb)], axis=1)
        last = (near - 1) * sh.blocks + qb
        first = jnp.clip(start_ref[qb] + (near - 1) * sh.blocks, 0, last)
        count = last - first + 1
        odd = count % 2

        for size, hit in ((1, odd == 1), (2, odd == 0)):

            @pl.when(hit)
            def _(size=size):
                at = (last + 1 - size) * sh.block
                state = forward_tile(
                    sh, kv_s, vt_s, acc.at[0], qq, at, size * sh.block, None, True
                )
                for r in range(3):
                    stat[0, r : r + 1, :] = state[r]

        forward_loop(sh, kv_s, vt_s, acc.at[0], stat.at[0], qq, first, (count - 1) // 2)

    pair_work = 2 * sh.blocks * sh.block * sh.tokens * sh.group
    return pl.pallas_call(
        kernel,
        grid=(sh.blocks,),
        in_specs=[SMEM, SMEM] + [ANY] * copies,
        out_specs=[
            pl.BlockSpec((1, 2 * sh.width, sh.lanes), lambda i: (i, 0, 0)),
            pl.BlockSpec((1, 8, sh.lanes), lambda i: (i, 0, 0)),
        ],
        out_shape=[
            jax.ShapeDtypeStruct((sh.blocks, 2 * sh.width, sh.lanes), F32),
            jax.ShapeDtypeStruct((sh.blocks, 8, sh.lanes), F32),
        ],
        scratch_shapes=[
            pltpu.VMEM((2, sh.group, sh.tokens, sh.width), BF16),
            pltpu.VMEM((4, span, sh.width), BF16),
            pltpu.VMEM((2 * sh.width, span), BF16),
            pltpu.SemaphoreType.DMA((copies,)),
        ],
        compiler_params=params(),
        cost_estimate=cost(6 * pair_work * sh.width, 12 * sh.tokens * sh.lanes * 8, pair_work),
        name="forward_near",
    )(me, starts, *q_parts, *flat)


def forward_far(sh, me, starts, q_parts, chunk, distance, acc, stat, gain_square):
    parts = sh.parts
    copies = 2 * parts
    w = sh.width

    def kernel(me_ref, start_ref, *refs):
        q_in, kv_in = refs[:parts], refs[parts:copies]
        acc_in, stat_in, gain_ref, out, lse, sums = refs[copies : copies + 6]
        q_s, kv_s, vt_s, acc, stat, sems = refs[copies + 6 :]
        qb = pl.program_id(0)

        @pl.when(qb == 0)
        def _():
            load_keys(sh, me_ref, [kv_in], kv_s, q_in, q_s, sems)
            vt_s[:w, :] = transposed(kv_s[1])
            vt_s[w:, :] = transposed(kv_s[3])

        first = jnp.clip(start_ref[qb] + distance * sh.blocks, 0, sh.blocks)
        count = sh.blocks - first
        odd = count % 2
        stat[...] = stat_in[0]
        acc[...] = acc_in[0]

        @pl.when(count > 0)
        def _():
            qq = jnp.concatenate([query_rows(sh, q_s, 0, qb), query_rows(sh, q_s, 1, qb)], axis=1)

            @pl.when(odd == 1)
            def _():
                state = tuple(stat[r : r + 1, :] for r in range(3))
                state = forward_tile(
                    sh, kv_s, vt_s, acc, qq, first * sh.block, sh.block, state, False
                )
                for r in range(3):
                    stat[r : r + 1, :] = state[r]

            forward_loop(sh, kv_s, vt_s, acc, stat, qq, first + odd, count // 2)

        most, total, cross = (stat[r : r + 1, :] for r in range(3))
        inverse = 1.0 / total
        plain = acc[:w, :] * inverse
        moved = acc[w:, :] * inverse - (cross * inverse) * plain
        out[0, :w, :] = plain
        out[0, w:, :] = moved
        lse[0] = most + jnp.log2(total)
        square = plain * plain
        product = plain * moved
        gain = gain_ref[...]
        for r, value in enumerate((square, product, gain * square, gain * product)):
            line = jnp.sum(value, axis=0, keepdims=True)
            pieces = [line[:, g * sh.block : (g + 1) * sh.block] for g in range(sh.group)]
            sums[0, r : r + 1, :] = functools.reduce(jnp.add, pieces)

    wide = pl.BlockSpec((1, 2 * w, sh.lanes), lambda i: (i, 0, 0))
    return pl.pallas_call(
        kernel,
        grid=(sh.blocks,),
        in_specs=[SMEM, SMEM]
        + [ANY] * copies
        + [
            wide,
            pl.BlockSpec((1, 8, sh.lanes), lambda i: (i, 0, 0)),
            pl.BlockSpec((w, sh.lanes), lambda i: (0, 0)),
        ],
        out_specs=[
            wide,
            pl.BlockSpec((1, 1, sh.lanes), lambda i: (i, 0, 0)),
            pl.BlockSpec((1, 4, sh.block), lambda i: (i, 0, 0)),
        ],
        out_shape=[
            jax.ShapeDtypeStruct((sh.blocks, 2 * w, sh.lanes), F32),
            jax.ShapeDtypeStruct((sh.blocks, 1, sh.lanes), F32),
            jax.ShapeDtypeStruct((sh.blocks, 4, sh.block), F32),
        ],
        scratch_shapes=[
            pltpu.VMEM((2, sh.group, sh.tokens, w), BF16),
            pltpu.VMEM((4, sh.tokens, w), BF16),
            pltpu.VMEM((2 * w, sh.tokens), BF16),
            pltpu.VMEM((2 * w, sh.lanes), F32),
            pltpu.VMEM((8, sh.lanes), F32),
            pltpu.SemaphoreType.DMA((copies,)),
        ],
        compiler_params=params(),
        cost_estimate=cost(sh.tokens * sh.tokens * w, 24 * sh.tokens * sh.lanes * 2, sh.tokens),
        name="forward_far",
    )(me, starts, *q_parts, *chunk, acc, stat, gain_square)


def backward_tile(sh, kv_s, kt_s, dkv_s, dq_s, qg, q, g, lse, dot, start, size, masked):
    start = pl.multiple_of(start, sh.block)
    rows = pl.ds(start, size)
    k = kv_s[0, rows, :]
    v = kv_s[1, rows, :]
    empty = jnp.zeros_like(k)
    left = jnp.concatenate([k, empty], axis=0)
    right = jnp.concatenate([empty, v], axis=0)
    both = nt(jnp.concatenate([left, right], axis=1), qg)
    p = jnp.exp2(both[:size] * sh.powers - lse)
    if masked:
        low = jnp.where(diagonal(sh), p[size - sh.block :], 0.0)
        p = low if size == sh.block else jnp.concatenate([p[: size - sh.block], low], axis=0)
    ds = (p * (both[size:] - dot)).astype(BF16)
    dkv_s[0, rows, :] += nn(ds, q)
    dkv_s[1, rows, :] += nn(p.astype(BF16), g)
    dq_s[...] += nn(kt_s[:, rows], ds)


def backward_chunk(sh, me, starts, q_parts, chunk, distance, grads, lse, dots, dq, norm):
    parts = sh.parts
    copies = 2 * parts
    w = sh.width
    opening, closing = norm is not None, distance == 0

    def kernel(me_ref, start_ref, *refs):
        refs = list(refs)
        q_in, kv_in = refs[:parts], refs[parts:copies]
        del refs[:copies]
        lse_ref = refs.pop(0)
        if opening:
            out_ref, sums_ref, gain_ref = refs[:3]
            del refs[:3]
        else:
            grad_ref, dot_ref, dq_ref = refs[:3]
            del refs[:3]
        dkv_out, dq_out = refs[:2]
        del refs[:2]
        if opening:
            grad_ref, dot_ref = refs[:2]
            del refs[:2]
        q_s, kv_s, kt_s, dkv_s, dq_s, sems = refs
        qb = pl.program_id(0)

        @pl.when(qb == 0)
        def _():
            load_keys(sh, me_ref, [kv_in], kv_s, q_in, q_s, sems)
            kt_s[...] = transposed(kv_s[0])
            dkv_s[...] = jnp.zeros_like(dkv_s)

        if opening:
            features = norm[2]
            sums = jnp.concatenate([sums_ref[0]] * sh.group, axis=1)
            square = sums[0:1] / features + EPSILON
            inverse = lax.rsqrt(square)
            ratio = sums[1:2] / (features * square)
            back = (sums[3:4] - ratio * sums[2:3]) * inverse
            back = back / (features * square)
            plain = out_ref[0, :w, :]
            moved = out_ref[0, w:, :]
            first_grad = gain_ref[...] * (moved - plain * ratio) * inverse
            cot = ((first_grad - plain * back) * inverse).astype(BF16).astype(F32)
            dot_ref[0] = jnp.sum(cot * plain, axis=0, keepdims=True)
            grad_ref[0] = cot.T.astype(BF16)
            dq_s[...] = jnp.zeros_like(dq_s)
        else:
            dq_s[...] = dq_ref[0]

        top = sh.blocks if distance else qb + 1
        first = jnp.clip(start_ref[qb] + distance * sh.blocks, 0, top)
        count = top - first
        odd = count % 2

        @pl.when(count > 0)
        def _():
            q = query_rows(sh, q_s, 0, qb)
            g = grad_ref[0]
            qg = jnp.concatenate([q, g], axis=1)
            tile = functools.partial(
                backward_tile, sh, kv_s, kt_s, dkv_s, dq_s, qg, q, g, lse_ref[0], dot_ref[0]
            )
            block = sh.block
            if closing:

                @pl.when(odd == 1)
                def _():
                    tile(qb * block, block, True)

                @pl.when(odd == 0)
                def _():
                    tile((qb - 1) * block, 2 * block, True)

                low, pairs = first, (count - 1) // 2
            else:

                @pl.when(odd == 1)
                def _():
                    tile(first * block, block, False)

                low, pairs = first + odd, count // 2

            def step(i, carry):
                tile((low + 2 * i) * block, 2 * block, False)
                return carry

            lax.fori_loop(0, pairs, step, 0)

        if closing:
            dq_out[...] = (dq_s[...] * sh.scale).T.reshape(sh.group, sh.block, w).astype(BF16)
        else:
            dq_out[0] = dq_s[...]

        @pl.when(qb == sh.blocks - 1)
        def _():
            dkv_out[0] = (dkv_s[0] * sh.scale).astype(dkv_out.dtype)
            dkv_out[1] = dkv_s[1].astype(dkv_out.dtype)

    def by_block(*shape):
        return pl.BlockSpec((1,) + shape, lambda i: (i,) + (0,) * len(shape))

    in_specs = [SMEM, SMEM] + [ANY] * copies + [by_block(1, sh.lanes)]
    operands = [lse]
    grad_specs = [by_block(sh.lanes, w), by_block(1, sh.lanes)]
    dq_spec = by_block(w, sh.lanes)
    if opening:
        in_specs += [
            by_block(2 * w, sh.lanes),
            by_block(4, sh.block),
            pl.BlockSpec((w, sh.lanes), lambda i: (0, 0)),
        ]
        operands += [grads, norm[0], norm[1]]
    else:
        in_specs += grad_specs + [dq_spec]
        operands += [grads, dots, dq]
    dkv_type = F32 if not opening else BF16
    out_shape = [
        jax.ShapeDtypeStruct((2, sh.tokens, w), dkv_type),
        jax.ShapeDtypeStruct((sh.group, sh.tokens, w), BF16)
        if closing
        else jax.ShapeDtypeStruct((sh.blocks, w, sh.lanes), F32),
    ]
    out_specs = [
        pl.BlockSpec((2, sh.tokens, w), lambda i: (0, 0, 0)),
        pl.BlockSpec((sh.group, sh.block, w), lambda i: (0, i, 0)) if closing else dq_spec,
    ]
    if opening:
        out_shape += [
            jax.ShapeDtypeStruct((sh.blocks, sh.lanes, w), BF16),
            jax.ShapeDtypeStruct((sh.blocks, 1, sh.lanes), F32),
        ]
        out_specs += grad_specs
    work = sh.group * sh.tokens * sh.tokens
    return pl.pallas_call(
        kernel,
        grid=(sh.blocks,),
        in_specs=in_specs,
        out_specs=out_specs,
        out_shape=out_shape,
        scratch_shapes=[
            pltpu.VMEM((1, sh.group, sh.tokens, w), BF16),
            pltpu.VMEM((2, sh.tokens, w), BF16),
            pltpu.VMEM((w, sh.tokens), BF16),
            pltpu.VMEM((2, sh.tokens, w), F32),
            pltpu.VMEM((w, sh.lanes), F32),
            pltpu.SemaphoreType.DMA((copies,)),
        ],
        compiler_params=params(),
        cost_estimate=cost(10 * work * w, 12 * sh.tokens * sh.lanes * 4, work),
        name="backward_chunk",
    )(me, starts, *q_parts, *chunk, *operands)


def exchanged(pieces):
    parts = len(pieces)
    return [pieces[0]] + [
        lax.ppermute(pieces[m], "part", [(i, i ^ m) for i in range(parts)])
        for m in range(1, parts)
    ]


def moved_on(value, steps):
    count = lax.axis_size("span")
    pairs = [(i, i + steps) for i in range(count) if 0 <= i + steps < count]
    return lax.ppermute(value, "span", pairs)


def body(queries, keys, values, tangent_queries, tangent_keys, tangent_values, doc_start, out_gain):
    rows, query_heads, width = queries.shape
    key_heads = keys.shape[1]
    group = query_heads // key_heads
    parts = lax.axis_size("part")
    block = rows // doc_start.shape[0]
    features = query_heads * width * lax.axis_size("head")
    hops = -(-DOC_DEVS // parts)
    sh = Shape(parts, group, rows, width, block)
    place = lax.axis_index("part")
    me = place.astype(jnp.int32).reshape(1)

    def flat(array):
        return array.reshape(-1, width)

    kv = split_heads([flat(a) for a in (keys, values, tangent_keys, tangent_values)], me, parts, 1)
    chunks = [exchanged([piece.reshape(4, rows, width) for piece in kv])]
    q_parts = exchanged(split_heads([flat(queries), flat(tangent_queries)], me, parts, group))
    for _ in range(hops):
        chunks.append([moved_on(piece, 1) for piece in chunks[-1]])
    starts = lax.all_gather(doc_start, "part", tiled=True)
    starts = starts - lax.axis_index("span").astype(jnp.int32) * sh.blocks
    gain = lax.dynamic_index_in_dim(out_gain.reshape(key_heads, group, width), place, 0, False)
    gain_square = jnp.repeat((gain * gain).T, block, axis=1)

    near = [chunks[h] for h in range(hops - 1, -1, -1)]
    acc, stat = forward_near(sh, me, starts, q_parts, near)
    out, lse, sums = forward_far(
        sh, me, starts, q_parts, chunks[hops], hops, acc, stat, gain_square
    )
    sums = lax.psum(sums, ("part", "head"))

    carried, dq, grads, dots = backward_chunk(
        sh, me, starts, q_parts, chunks[hops], hops, out, lse, None, None,
        (sums, gain_square, features),
    )
    for distance in range(hops - 1, -1, -1):
        carried = moved_on(carried, -1)
        part, dq = backward_chunk(
            sh, me, starts, q_parts, chunks[distance], distance, grads, lse, dots, dq, None
        )
        carried = (carried.astype(F32) + part).astype(BF16)

    def slots(array):
        shape = array.shape[:1] + (parts, rows, width)
        cut = array.reshape(shape)
        return [
            lax.dynamic_index_in_dim(cut, jnp.bitwise_xor(place, m), 1, False)
            for m in range(parts)
        ]

    dq_pieces = exchanged([p.reshape(1, group, rows, width) for p in slots(dq)])
    dkv_pieces = exchanged([p.reshape(2, 1, rows, width) for p in slots(carried)])
    (product_queries,) = join_heads(dq_pieces, me, 1, group)
    product_keys, product_values = join_heads(dkv_pieces, me, 2, 1)
    return (
        product_queries.reshape(queries.shape),
        product_keys.reshape(keys.shape),
        product_values.reshape(keys.shape),
    )


def solution(mesh):
    def run(*arguments):
        count, heads = mesh.shape["ctx"], mesh.shape["head"]
        parts = arguments[1].shape[1] // heads
        split = Mesh(
            mesh.devices.reshape(count // parts, parts, heads), ("span", "part", "head")
        )
        ctx = ("span", "part")
        array = P(ctx, "head", None)
        return jax.shard_map(
            body,
            mesh=split,
            in_specs=(array,) * 6 + (P(ctx), P("head")),
            out_specs=(array,) * 3,
            check_vma=False,
        )(*arguments)

    return run
```

```python
import functools
import math

import jax
import jax.numpy as jnp
from jax import lax
from jax.experimental import pallas as pl
from jax.experimental.pallas import tpu as pltpu
from jax.sharding import Mesh, PartitionSpec as P

DOC_DEVS = 8
EPSILON = 1e-06
VMEM_BYTES = 60 * 1024 * 1024
NOTE_ROWS = 16
LOG2E = math.log2(math.e)
MASKED = -1e30
F32 = jnp.float32
BF16 = jnp.bfloat16
ANY = pl.BlockSpec(memory_space=pl.ANY)
SMEM = pl.BlockSpec(memory_space=pltpu.SMEM)


def params():
    return pltpu.CompilerParams(vmem_limit_bytes=VMEM_BYTES)


def cost(flops, moved, powers=0):
    return pl.CostEstimate(flops=int(flops), bytes_accessed=int(moved), transcendentals=int(powers))


def nn(a, b):
    return lax.dot_general(a, b, (((1,), (0,)), ((), ())), preferred_element_type=F32)


def nt(a, b):
    return lax.dot_general(a, b, (((1,), (1,)), ((), ())), preferred_element_type=F32)


def split_heads(arrays, me, parts, per_part, notes=None):
    count = len(arrays)
    total, width = arrays[0].shape
    heads = parts * per_part
    rows = total // heads
    length = count * per_part * rows
    extra = 0 if notes is None else NOTE_ROWS
    scalars = [me] if notes is None else [me, notes]

    def kernel(*refs):
        me_ref, *ins = refs[: len(scalars) + count]
        outs, wide = refs[len(scalars) + count : -1], refs[-1]
        mine = me_ref[0]
        if extra:
            note_ref = ins.pop(0)
            line = lax.broadcasted_iota(jnp.int32, (extra, width), 0)
            lines = jnp.zeros((extra, width), jnp.int32)
            for i in range(notes.shape[0]):
                lines = jnp.where(line == i, note_ref[i], lines)
            for out in outs:
                out[length:, :] = lines.astype(F32).astype(BF16)
        for a in range(count):
            wide[...] = ins[a][...].astype(F32)
            for m in range(parts):
                for r in range(per_part):
                    head = jnp.bitwise_xor(mine, m) * per_part + r
                    at = (a * per_part + r) * rows
                    outs[m][at : at + rows, :] = wide[pl.ds(head, rows, stride=heads), :].astype(BF16)

    return pl.pallas_call(
        kernel,
        in_specs=[SMEM] * len(scalars) + [pl.BlockSpec(memory_space=pltpu.VMEM)] * count,
        out_specs=[pl.BlockSpec(memory_space=pltpu.VMEM)] * parts,
        out_shape=[jax.ShapeDtypeStruct((length + extra, width), BF16)] * parts,
        scratch_shapes=[pltpu.VMEM((total, width), F32)],
        compiler_params=params(),
        cost_estimate=cost(0, 4 * count * total * width),
        name="split_heads",
    )(*scalars, *arrays)


def join_heads(pieces, me, count, per_part):
    parts = len(pieces)
    rows, width = pieces[0].shape[-2:]
    heads = parts * per_part

    def kernel(me_ref, *refs):
        ins, outs = refs[:parts], refs[parts:]
        mine = me_ref[0]
        for a in range(count):
            for m in range(parts):
                for r in range(per_part):
                    head = jnp.bitwise_xor(mine, m) * per_part + r
                    outs[a][pl.ds(head, rows, stride=heads), :] = ins[m][a, r].astype(F32)

    return pl.pallas_call(
        kernel,
        in_specs=[SMEM] + [pl.BlockSpec(memory_space=pltpu.VMEM)] * parts,
        out_specs=[pl.BlockSpec(memory_space=pltpu.VMEM)] * count,
        out_shape=[jax.ShapeDtypeStruct((rows * heads, width), F32)] * count,
        compiler_params=params(),
        cost_estimate=cost(0, 6 * count * rows * heads * width),
        name="join_heads",
    )(me, *pieces)


def copy_in(pairs, sems):
    copies = [pltpu.make_async_copy(src, dst, sems.at[i]) for i, (src, dst) in enumerate(pairs)]
    for c in copies:
        c.start()
    for c in copies:
        c.wait()


def slot_of(me_ref, m, rows):
    return pl.multiple_of(jnp.bitwise_xor(me_ref[0], m) * rows, rows)


class Shape:
    def __init__(self, parts, group, rows, width, block):
        self.parts, self.group, self.rows, self.width, self.block = parts, group, rows, width, block
        self.tokens = parts * rows
        self.blocks = self.tokens // block
        self.lanes = group * block
        self.scale = width**-0.5
        self.powers = self.scale * LOG2E


def diagonal(sh):
    shape = (sh.block, sh.lanes)
    key = lax.broadcasted_iota(jnp.int32, shape, 0)
    query = lax.broadcasted_iota(jnp.int32, shape, 1) % sh.block
    return key <= query


def query_rows(sh, q_s, which, qb):
    rows = pl.ds(pl.multiple_of(qb * sh.block, sh.block), sh.block)
    return q_s[which, :, rows, :].reshape(sh.lanes, sh.width)


def scores_tile(sh, kv_s, qq, start, size):
    k = kv_s[0, pl.ds(start, size), :]
    tk = kv_s[2, pl.ds(start, size), :]
    left = jnp.concatenate([k, tk], axis=0)
    right = jnp.concatenate([jnp.zeros_like(k), k], axis=0)
    both = nt(jnp.concatenate([left, right], axis=1), qq)
    return both[:size] * sh.powers, both[size:]


def mix_tile(sh, vt_s, acc, start, size, scores, state, masked):
    w = sh.width
    s, d = scores
    if masked:
        low = jnp.where(diagonal(sh), s[size - sh.block :], MASKED)
        s = low if size == sh.block else jnp.concatenate([s[: size - sh.block], low], axis=0)
    most = jnp.max(s, axis=0, keepdims=True)
    if state is not None:
        most = jnp.maximum(most, state[0])
        decay = jnp.exp2(state[0] - most)
    e = jnp.exp2(s - most)
    mix = e * d
    total = jnp.sum(e, axis=0, keepdims=True)
    cross = jnp.sum(mix, axis=0, keepdims=True)
    vt = vt_s[:, pl.ds(start, size)]
    plain = nn(vt, e.astype(BF16))
    moving = nn(vt[:w], mix.astype(BF16)) * sh.scale
    if state is None:
        acc[:w, :] = plain[:w]
        acc[w:, :] = plain[w:] + moving
        return most, total, cross
    acc[:w, :] = acc[:w, :] * decay + plain[:w]
    acc[w:, :] = acc[w:, :] * decay + (plain[w:] + moving)
    return most, state[1] * decay + total, state[2] * decay + cross


def block_rows(sh, block):
    return pl.multiple_of(block * sh.block, sh.block)


def load_state(stat):
    return tuple(stat[r : r + 1, :] for r in range(3))


def store_state(stat, state):
    for r in range(3):
        stat[r : r + 1, :] = state[r]


def forward_tiles(sh, kv_s, vt_s, acc, stat, qq, tiles, fresh=False, masked=False):
    places = [(block_rows(sh, block), blocks * sh.block) for block, blocks in tiles]
    scores = [scores_tile(sh, kv_s, qq, start, size) for start, size in places]
    state = None if fresh else load_state(stat)
    for (start, size), both in zip(places, scores):
        state = mix_tile(sh, vt_s, acc, start, size, both, state, masked)
    store_state(stat, state)


def paired_tiles(run, low, pairs):
    @pl.when(pairs % 2 == 1)
    def _():
        run([(low, 2)])

    def step(i, carry):
        at = low + 2 * (pairs % 2) + 4 * i
        run([(at, 2), (at + 2, 2)])
        return carry

    lax.fori_loop(0, pairs // 2, step, 0)


def load_chunk(sh, me_ref, sources, kv_s, q_parts, q_s, sems):
    pairs = []
    for m in range(sh.parts):
        slot = pl.ds(slot_of(me_ref, m, sh.rows), sh.rows)
        for i in range(q_s.shape[0]):
            for g in range(sh.group):
                at = (i * sh.group + g) * sh.rows
                pairs.append((q_parts[m].at[pl.ds(at, sh.rows), :], q_s.at[i, g, slot, :]))
        ref, base = sources[m]
        for i in range(kv_s.shape[0]):
            rows = pl.ds(base + i * sh.rows, sh.rows)
            pairs.append((ref.at[rows, :], kv_s.at[i, slot, :]))
    copy_in(pairs, sems)


def copies_of(sh, arrays, queries):
    return sh.parts * (arrays + queries * sh.group)


def transposed(x):
    return x.astype(F32).T.astype(BF16)


def located(chunk, refs):
    own, rest = chunk
    if isinstance(rest, list):
        return [(ref, 0) for ref in refs]
    pieces = 1 if rest is None else 1 + rest.shape[0] // own.shape[0]
    return [(refs[0], 0)] + [(refs[1], m * own.shape[0]) for m in range(pieces - 1)]


def chunk_arrays(chunk):
    own, rest = chunk
    if rest is None:
        return [own]
    return [own] + (rest if isinstance(rest, list) else [rest])


def back_of(sh, me_ref, back_ref, qb):
    per = sh.rows // sh.block
    return back_ref[jnp.bitwise_xor(me_ref[0], qb // per) * per + qb % per]


def forward_chunk(sh, me, back, q_parts, chunk, distance, state, gain_square=None):
    parts, w = sh.parts, sh.width
    kv = chunk_arrays(chunk)
    loads = parts + len(kv)
    opening, closing = state is None, gain_square is not None

    def kernel(me_ref, back_ref, *refs):
        refs = list(refs)
        q_in, kv_in = refs[:parts], refs[parts:loads]
        del refs[:loads]
        if not opening:
            acc_in, stat_in = refs[:2]
            del refs[:2]
        if closing:
            gain_ref, out, lse, sums, q_s, kv_s, vt_s, sems, acc, stat = refs
        else:
            acc_out, stat_out, q_s, kv_s, vt_s, sems = refs
            acc, stat = acc_out.at[0], stat_out.at[0]
        qb = pl.program_id(0)

        @pl.when(qb == 0)
        def _():
            load_chunk(sh, me_ref, located(chunk, kv_in), kv_s, q_in, q_s, sems)
            vt_s[:w, :] = transposed(kv_s[1])
            vt_s[w:, :] = transposed(kv_s[3])

        if not opening:
            acc[...] = acc_in[0]
            stat[...] = stat_in[0]
        top = sh.blocks if distance else qb + 1
        first = jnp.clip(qb - back_of(sh, me_ref, back_ref, qb) + distance * sh.blocks, 0, top)
        count = top - first

        @pl.when(count > 0)
        def _():
            qq = jnp.concatenate([query_rows(sh, q_s, 0, qb), query_rows(sh, q_s, 1, qb)], axis=1)
            run = functools.partial(forward_tiles, sh, kv_s, vt_s, acc, stat, qq)
            if opening:
                for size in (1, 2):

                    @pl.when(count % 2 == size % 2)
                    def _(size=size):
                        run([(top - size, size)], fresh=True, masked=True)

                paired_tiles(run, first, (count - 1) // 2)
            else:

                @pl.when(count % 2 == 1)
                def _():
                    run([(first, 1)])

                paired_tiles(run, first + count % 2, count // 2)

        if closing:
            most, total, cross = load_state(stat)
            inverse = 1.0 / total
            plain = acc[:w, :] * inverse
            moved = acc[w:, :] * inverse - (cross * inverse * sh.scale) * plain
            out[0, :w, :] = plain
            out[0, w:, :] = moved
            lse[0] = most + jnp.log2(total)
            square = plain * plain
            product = plain * moved
            gain = gain_ref[...]
            for r, value in enumerate((square, product, gain * square, gain * product)):
                line = jnp.sum(value, axis=0, keepdims=True)
                pieces = [line[:, g * sh.block : (g + 1) * sh.block] for g in range(sh.group)]
                sums[0, r : r + 1, :] = functools.reduce(jnp.add, pieces)

    def by_block(*shape):
        return pl.BlockSpec((1,) + shape, lambda i: (i,) + (0,) * len(shape))

    def array(*shape):
        return jax.ShapeDtypeStruct((sh.blocks,) + shape, F32)

    wide, stats = (2 * w, sh.lanes), (8, sh.lanes)
    in_specs = [SMEM, SMEM] + [ANY] * loads
    operands = [*q_parts, *kv]
    if not opening:
        in_specs += [by_block(*wide), by_block(*stats)]
        operands += state
    scratch = [
        pltpu.VMEM((2, sh.group, sh.tokens, w), BF16),
        pltpu.VMEM((4, sh.tokens, w), BF16),
        pltpu.VMEM((2 * w, sh.tokens), BF16),
        pltpu.SemaphoreType.DMA((copies_of(sh, 4, 2),)),
    ]
    if closing:
        in_specs.append(pl.BlockSpec((w, sh.lanes), lambda i: (0, 0)))
        operands.append(gain_square)
        shapes = [wide, (1, sh.lanes), (4, sh.block)]
        scratch += [pltpu.VMEM(wide, F32), pltpu.VMEM(stats, F32)]
    else:
        shapes = [wide, stats]
    work = sh.group * sh.tokens * sh.tokens // 2
    return pl.pallas_call(
        kernel,
        grid=(sh.blocks,),
        in_specs=in_specs,
        out_specs=[by_block(*shape) for shape in shapes],
        out_shape=[array(*shape) for shape in shapes],
        scratch_shapes=scratch,
        compiler_params=params(),
        cost_estimate=cost(24 * work * w, 24 * sh.tokens * sh.lanes * 2, work),
        name="forward_far" if closing else "forward_chunk",
    )(me, back, *operands)


def backward_scores(sh, kv_s, qg, start, size):
    k = kv_s[0, pl.ds(start, size), :]
    v = kv_s[1, pl.ds(start, size), :]
    empty = jnp.zeros_like(k)
    left = jnp.concatenate([k, empty], axis=0)
    right = jnp.concatenate([empty, v], axis=0)
    both = nt(jnp.concatenate([left, right], axis=1), qg)
    return both[:size], both[size:]


def backward_tiles(sh, kv_s, kt_s, dkv_s, dq_s, qg, lse, dot, tiles, masked=False):
    places = [(block_rows(sh, block), blocks * sh.block) for block, blocks in tiles]
    scores = [backward_scores(sh, kv_s, qg, start, size) for start, size in places]
    q, g = qg[:, : sh.width], qg[:, sh.width :]
    for (start, size), (s, dp) in zip(places, scores):
        rows = pl.ds(start, size)
        p = jnp.exp2(s * sh.powers - lse)
        if masked:
            low = jnp.where(diagonal(sh), p[size - sh.block :], 0.0)
            p = low if size == sh.block else jnp.concatenate([p[: size - sh.block], low], axis=0)
        ds = (p * (dp - dot)).astype(BF16)
        dkv_s[0, rows, :] += nn(ds, q)
        dkv_s[1, rows, :] += nn(p.astype(BF16), g)
        dq_s[...] += nn(kt_s[:, rows], ds)


def backward_chunk(sh, me, back, q_parts, chunk, distance, grads, lse, dots, dq, norm, order, held):
    parts, w = sh.parts, sh.width
    kv = chunk_arrays(chunk)
    loads = parts + len(kv)
    opening, closing = norm is not None, distance == 0
    per = sh.rows // sh.block
    steps = len(order) * per

    def query_block(i, me_ref):
        if order == list(range(parts)):
            return i
        partner = functools.reduce(
            lambda chosen, j: jnp.where(i // per == j, order[j], chosen), range(len(order)), order[0]
        )
        return jnp.bitwise_xor(me_ref[0], partner) * per + i % per

    def kernel(me_ref, back_ref, *refs):
        refs = list(refs)

        def take(count):
            taken = refs[:count]
            del refs[:count]
            return taken

        q_in, kv_in = take(parts), take(len(kv))
        (lse_ref,) = take(1)
        if opening:
            out_ref, gain_ref, *sum_refs = take(2 + len(norm[0]))
        else:
            grad_ref, dot_ref, dq_ref = take(3)
        (held_ref,) = take(1) if held is not None else (None,)
        (dkv_out,) = take(1)
        dq_out = take(len(order) if closing else 1)
        if opening:
            grad_ref, dot_ref = take(2)
        q_s, kv_s, kt_s, dkv_s, dq_s, sems = refs
        i = pl.program_id(0)
        qb = query_block(i, me_ref)

        @pl.when(i == 0)
        def _():
            load_chunk(sh, me_ref, located(chunk, kv_in), kv_s, q_in, q_s, sems)
            kt_s[...] = transposed(kv_s[0])
            dkv_s[...] = jnp.zeros_like(dkv_s) if held_ref is None else held_ref[...]

        if opening:
            features = norm[2]
            token = functools.reduce(jnp.add, [ref[0] for ref in sum_refs])
            sums = jnp.concatenate([token] * sh.group, axis=1)
            square = sums[0:1] / features + EPSILON
            inverse = lax.rsqrt(square)
            ratio = sums[1:2] / (features * square)
            again = (sums[3:4] - ratio * sums[2:3]) * inverse
            again = again / (features * square)
            plain = out_ref[0, :w, :]
            moved = out_ref[0, w:, :]
            first_grad = gain_ref[...] * (moved - plain * ratio) * inverse
            cot = ((first_grad - plain * again) * inverse).astype(BF16).astype(F32)
            dot_ref[0] = jnp.sum(cot * plain, axis=0, keepdims=True)
            grad_ref[0] = cot.T.astype(BF16)
            dq_s[...] = jnp.zeros_like(dq_s)
        else:
            dq_s[...] = dq_ref[0]

        top = sh.blocks if distance else qb + 1
        first = jnp.clip(qb - back_of(sh, me_ref, back_ref, qb) + distance * sh.blocks, 0, top)
        count = top - first

        @pl.when(count > 0)
        def _():
            qg = jnp.concatenate([query_rows(sh, q_s, 0, qb), grad_ref[0]], axis=1)
            run = functools.partial(
                backward_tiles, sh, kv_s, kt_s, dkv_s, dq_s, qg, lse_ref[0], dot_ref[0]
            )
            if closing:
                for size in (1, 2):

                    @pl.when(count % 2 == size % 2)
                    def _(size=size):
                        run([(top - size, size)], masked=True)

                paired_tiles(run, first, (count - 1) // 2)
            else:

                @pl.when(count % 2 == 1)
                def _():
                    run([(first, 1)])

                paired_tiles(run, first + count % 2, count // 2)

        if closing:
            done = (dq_s[...] * sh.scale).T.reshape(sh.group, sh.block, w).astype(BF16)
            for j, out in enumerate(dq_out):

                @pl.when(i // per == j)
                def _(out=out):
                    out[...] = done

        else:
            dq_out[0][0] = dq_s[...]

        @pl.when(i == steps - 1)
        def _():
            if dkv_out.dtype == BF16:
                dkv_out[0] = (dkv_s[0] * sh.scale).astype(BF16)
                dkv_out[1] = dkv_s[1].astype(BF16)
            else:
                dkv_out[...] = dkv_s[...]

    def by_block(*shape):
        return pl.BlockSpec(
            (1,) + shape, lambda i, me_ref, _: (query_block(i, me_ref),) + (0,) * len(shape)
        )

    grad_specs = [by_block(sh.lanes, w), by_block(1, sh.lanes)]
    whole = pl.BlockSpec((2, sh.tokens, w), lambda i, *_: (0, 0, 0))
    in_specs = [ANY] * loads + [by_block(1, sh.lanes)]
    operands = [*q_parts, *kv, lse]
    if opening:
        in_specs += [by_block(2 * w, sh.lanes), pl.BlockSpec((w, sh.lanes), lambda i, *_: (0, 0))]
        in_specs += [by_block(4, sh.block)] * len(norm[0])
        operands += [grads, norm[1], *norm[0]]
    else:
        in_specs += grad_specs + [by_block(w, sh.lanes)]
        operands += [grads, dots, dq]
    if held is not None:
        in_specs.append(whole)
        operands.append(held)
    out_shape = [jax.ShapeDtypeStruct((2, sh.tokens, w), BF16 if opening else F32)]
    out_specs = [whole]
    if closing:
        for j in range(len(order)):
            out_shape.append(jax.ShapeDtypeStruct((sh.group, sh.rows, w), BF16))
            out_specs.append(
                pl.BlockSpec(
                    (sh.group, sh.block, w),
                    lambda i, *_, j=j: (0, jnp.clip(i - j * per, 0, per - 1), 0),
                )
            )
    else:
        out_shape.append(jax.ShapeDtypeStruct((sh.blocks, w, sh.lanes), F32))
        out_specs.append(by_block(w, sh.lanes))
    if opening:
        out_shape += [
            jax.ShapeDtypeStruct((sh.blocks, sh.lanes, w), BF16),
            jax.ShapeDtypeStruct((sh.blocks, 1, sh.lanes), F32),
        ]
        out_specs += grad_specs
    work = sh.group * sh.tokens * sh.block * steps // 2
    return pl.pallas_call(
        kernel,
        grid_spec=pltpu.PrefetchScalarGridSpec(
            num_scalar_prefetch=2,
            grid=(steps,),
            in_specs=in_specs,
            out_specs=out_specs,
            scratch_shapes=[
                pltpu.VMEM((1, sh.group, sh.tokens, w), BF16),
                pltpu.VMEM((2, sh.tokens, w), BF16),
                pltpu.VMEM((w, sh.tokens), BF16),
                pltpu.VMEM((2, sh.tokens, w), F32),
                pltpu.VMEM((w, sh.lanes), F32),
                pltpu.SemaphoreType.DMA((copies_of(sh, 2, 1),)),
            ],
        ),
        out_shape=out_shape,
        compiler_params=params(),
        cost_estimate=cost(20 * work * w, 12 * sh.block * steps * sh.lanes * 4, work),
        name="backward_chunk",
    )(me, back, *operands)


def combine(sh, me, carried, held):
    def kernel(me_ref, carried_ref, held_ref, *outs):
        for m, out in enumerate(outs):
            slot = pl.ds(slot_of(me_ref, m, sh.rows), sh.rows)
            for a, factor in ((0, sh.scale), (1, 1.0)):
                part = held_ref[a, slot, :] * factor
                out[a] = (carried_ref[a, slot, :].astype(F32) + part).astype(BF16)

    vmem = pl.BlockSpec(memory_space=pltpu.VMEM)
    return pl.pallas_call(
        kernel,
        in_specs=[SMEM, vmem, vmem],
        out_specs=[vmem] * sh.parts,
        out_shape=[jax.ShapeDtypeStruct((2, sh.rows, sh.width), BF16)] * sh.parts,
        compiler_params=params(),
        cost_estimate=cost(0, 16 * sh.tokens * sh.width),
        name="combine",
    )(me, carried, held)


def exchanged(pieces):
    parts = len(pieces)
    return [pieces[0]] + [
        lax.ppermute(pieces[m], "part", [(i, i ^ m) for i in range(parts)])
        for m in range(1, parts)
    ]


def moved_on(value, steps):
    count = lax.axis_size("span")
    pairs = [(i, i + steps) for i in range(count) if 0 <= i + steps < count]
    return lax.ppermute(value, "span", pairs)


def summed_over_head(value):
    count = lax.axis_size("head")
    if count & (count - 1):
        return lax.psum(value, "head")
    step = 1
    while step < count:
        value = value + lax.ppermute(value, "head", [(i, i ^ step) for i in range(count)])
        step *= 2
    return value


def body(queries, keys, values, tangent_queries, tangent_keys, tangent_values, doc_start, out_gain):
    rows, query_heads, width = queries.shape
    key_heads = keys.shape[1]
    group = query_heads // key_heads
    parts = lax.axis_size("part")
    per = doc_start.shape[0]
    block = rows // per
    features = query_heads * width * lax.axis_size("head")
    hops = -(-DOC_DEVS // parts)
    sh = Shape(parts, group, rows, width, block)
    place = lax.axis_index("part")
    me = place.astype(jnp.int32).reshape(1)

    def flat(array):
        return array.reshape(-1, width)

    index = lax.axis_index("span") * parts + place
    notes = index.astype(jnp.int32) * per + jnp.arange(per, dtype=jnp.int32) - doc_start
    pieces = split_heads(
        [flat(a) for a in (keys, values, tangent_keys, tangent_values)], me, parts, 1, notes
    )
    q_rows, _ = lax.optimization_barrier(((flat(queries), flat(tangent_queries)), pieces[0]))
    q_pieces = split_heads(q_rows, me, parts, group)
    pieces = exchanged(pieces)
    chunks = [(pieces[0], pieces[1:])]
    rest = jnp.concatenate(pieces[1:], axis=0) if parts > 1 else None
    own = pieces[0]
    for _ in range(hops):
        own = moved_on(own, 1)
        rest = None if rest is None else moved_on(rest, 1)
        chunks.append((own, rest))
    q_parts = exchanged(q_pieces)
    back = jnp.concatenate([p[4 * rows : 4 * rows + per, 0] for p in pieces]).astype(jnp.int32)
    gain = lax.dynamic_index_in_dim(out_gain.reshape(key_heads, group, width), place, 0, False)
    gain_square = jnp.repeat((gain * gain).T, block, axis=1)

    state = None
    for distance in range(hops):
        state = forward_chunk(sh, me, back, q_parts, chunks[distance], distance, state)
    out, lse, sums = forward_chunk(
        sh, me, back, q_parts, chunks[hops], hops, state, gain_square
    )
    sums = summed_over_head(sums)
    norm = (exchanged([sums] * parts), gain_square, features)

    everyone = list(range(parts))
    carried, dq, grads, dots = backward_chunk(
        sh, me, back, q_parts, chunks[hops], hops, out, lse, None, None, norm, everyone, None
    )
    for distance in range(hops - 1, 0, -1):
        carried = moved_on(carried, -1)
        part, dq = backward_chunk(
            sh, me, back, q_parts, chunks[distance], distance, grads, lse, dots, dq, None,
            everyone, None,
        )
        factor = jnp.array([sh.scale, 1.0], F32)[:, None, None]
        carried = (carried.astype(F32) + part * factor).astype(BF16)
    carried = moved_on(carried, -1)
    half = parts // 2
    held, dq_pieces = None, [None] * parts
    for order in ([m for m in range(parts - 1, half - 1, -1)], [m for m in range(half)]):
        if order:
            held, *done = backward_chunk(
                sh, me, back, q_parts, chunks[0], 0, grads, lse, dots, dq, None, order, held
            )
            for m, piece in zip(order, done):
                dq_pieces[m] = piece.reshape(1, group, rows, width)
    dq_pieces = exchanged(dq_pieces)
    dkv_pieces = exchanged(combine(sh, me, carried, held))
    (product_queries,) = join_heads(dq_pieces, me, 1, group)
    dkv_pieces = [p.reshape(2, 1, rows, width) for p in dkv_pieces]
    product_keys, product_values = join_heads(dkv_pieces, me, 2, 1)
    return (
        product_queries.reshape(queries.shape),
        product_keys.reshape(keys.shape),
        product_values.reshape(keys.shape),
    )


def solution(mesh):
    def run(*arguments):
        count, heads = mesh.shape["ctx"], mesh.shape["head"]
        parts = arguments[1].shape[1] // heads
        split = Mesh(
            mesh.devices.reshape(count // parts, parts, heads), ("span", "part", "head")
        )
        ctx = ("span", "part")
        array = P(ctx, "head", None)
        return jax.shard_map(
            body,
            mesh=split,
            in_specs=(array,) * 6 + (P(ctx), P("head")),
            out_specs=(array,) * 3,
            check_vma=False,
        )(*arguments)

    return run
```

```python
import functools
import math

import jax
import jax.numpy as jnp
from jax import lax
from jax.experimental import pallas as pl
from jax.experimental.pallas import tpu as pltpu
from jax.sharding import Mesh, PartitionSpec as P

DOC_DEVS = 8
EPSILON = 1e-06
VMEM_BYTES = 18 * 1024 * 1024
NOTE_ROWS = 16
LOG2E = math.log2(math.e)
MASKED = -1e30
F32 = jnp.float32
BF16 = jnp.bfloat16
ANY = pl.BlockSpec(memory_space=pl.ANY)
SMEM = pl.BlockSpec(memory_space=pltpu.SMEM)


def params():
    return pltpu.CompilerParams(vmem_limit_bytes=VMEM_BYTES)


def cost(flops, moved, powers=0):
    return pl.CostEstimate(flops=int(flops), bytes_accessed=int(moved), transcendentals=int(powers))


def nn(a, b):
    return lax.dot_general(a, b, (((1,), (0,)), ((), ())), preferred_element_type=F32)


def nt(a, b):
    return lax.dot_general(a, b, (((1,), (1,)), ((), ())), preferred_element_type=F32)


def split_heads(arrays, parts, per_part, notes=None):
    count = len(arrays)
    total, width = arrays[0].shape
    heads = parts * per_part
    rows = total // heads
    length = count * per_part * rows
    extra = 0 if notes is None else NOTE_ROWS
    scalars = [] if notes is None else [notes]

    def kernel(*refs):
        ins = list(refs[: len(scalars) + count])
        outs, (held, wide, sems) = refs[len(scalars) + count : -3], refs[-3:]
        mine = lax.axis_index("part")
        if extra:
            note_ref = ins.pop(0)
        copies = [pltpu.make_async_copy(ins[a], held.at[a], sems.at[a]) for a in range(count)]
        for copy in copies:
            copy.start()
        if extra:
            first = (lax.axis_index("span") * parts + mine) * notes.shape[0]
            line = lax.broadcasted_iota(jnp.int32, (extra, width), 0)
            lines = jnp.zeros((extra, width), jnp.int32)
            for i in range(notes.shape[0]):
                lines = jnp.where(line == i, first + i - note_ref[i], lines)
            for out in outs:
                out[length:, :] = lines.astype(F32).astype(BF16)
        for a in range(count):
            copies[a].wait()
            wide[...] = held[a].astype(F32)
            for m in range(parts):
                for r in range(per_part):
                    head = jnp.bitwise_xor(mine, m) * per_part + r
                    at = (a * per_part + r) * rows
                    outs[m][at : at + rows, :] = wide[pl.ds(head, rows, stride=heads), :].astype(BF16)

    return pl.pallas_call(
        kernel,
        in_specs=[SMEM] * len(scalars) + [pl.BlockSpec(memory_space=pltpu.HBM)] * count,
        out_specs=[pl.BlockSpec(memory_space=pltpu.VMEM)] * parts,
        out_shape=[jax.ShapeDtypeStruct((length + extra, width), BF16)] * parts,
        scratch_shapes=[
            pltpu.VMEM((count, total, width), BF16),
            pltpu.VMEM((total, width), F32),
            pltpu.SemaphoreType.DMA((count,)),
        ],
        compiler_params=params(),
        cost_estimate=cost(0, 4 * count * total * width),
        name="split_heads",
    )(*scalars, *arrays)


def join_heads(pieces, count, per_part):
    parts = len(pieces)
    rows, width = pieces[0].shape[-2:]
    heads = parts * per_part

    steps = 4
    cut = rows // steps

    def kernel(*refs):
        ins, outs = refs[:parts], refs[parts:]
        mine = lax.axis_index("part")
        for a in range(count):
            for m in range(parts):
                for r in range(per_part):
                    head = jnp.bitwise_xor(mine, m) * per_part + r
                    outs[a][pl.ds(head, cut, stride=heads), :] = ins[m][a, r].astype(F32)

    return pl.pallas_call(
        kernel,
        grid=(steps,),
        in_specs=[pl.BlockSpec((count, per_part, cut, width), lambda i: (0, 0, i, 0))] * parts,
        out_specs=[pl.BlockSpec((cut * heads, width), lambda i: (i, 0))] * count,
        out_shape=[jax.ShapeDtypeStruct((rows * heads, width), F32)] * count,
        compiler_params=params(),
        cost_estimate=cost(0, 6 * count * rows * heads * width),
        name="join_heads",
    )(*pieces)


def copy_in(pairs, sems):
    copies = [pltpu.make_async_copy(src, dst, sems.at[i]) for i, (src, dst) in enumerate(pairs)]
    for c in copies:
        c.start()
    for c in copies:
        c.wait()


def slot_of(me_ref, m, rows):
    return pl.multiple_of(jnp.bitwise_xor(me_ref[0], m) * rows, rows)


class Shape:
    def __init__(self, parts, group, rows, width, block):
        self.parts, self.group, self.rows, self.width, self.block = parts, group, rows, width, block
        self.tokens = parts * rows
        self.blocks = self.tokens // block
        self.lanes = group * block
        self.scale = width**-0.5
        self.powers = self.scale * LOG2E


def diagonal(sh):
    shape = (sh.block, sh.block)
    key = lax.broadcasted_iota(jnp.int32, shape, 0)
    query = lax.broadcasted_iota(jnp.int32, shape, 1)
    return key <= query


def below_diagonal(sh, value, other):
    allowed = diagonal(sh)
    cut = [value[:, g * sh.block : (g + 1) * sh.block] for g in range(sh.group)]
    return jnp.concatenate([jnp.where(allowed, part, other) for part in cut], axis=1)


def query_rows(sh, q_s, which, qb):
    rows = pl.ds(pl.multiple_of(qb * sh.block, sh.block), sh.block)
    return q_s[which, :, rows, :].reshape(sh.lanes, sh.width)


def scores_tile(sh, kv_s, qq, start, size):
    k = kv_s[0, pl.ds(start, size), :]
    tk = kv_s[2, pl.ds(start, size), :]
    left = jnp.concatenate([k, tk], axis=0)
    right = jnp.concatenate([jnp.zeros_like(k), k], axis=0)
    both = nt(jnp.concatenate([left, right], axis=1), qq)
    return both[:size] * sh.powers, both[size:]


def mix_tile(sh, vt_s, acc, start, size, scores, state, masked):
    w = sh.width
    s, d = scores
    if masked:
        low = below_diagonal(sh, s[size - sh.block :], MASKED)
        s = low if size == sh.block else jnp.concatenate([s[: size - sh.block], low], axis=0)
    most = jnp.max(s, axis=0, keepdims=True)
    if state is not None:
        most = jnp.maximum(most, state[0])
        decay = jnp.exp2(state[0] - most)
    e = jnp.exp2(s - most)
    mix = e * d
    total = jnp.sum(e, axis=0, keepdims=True)
    cross = jnp.sum(mix, axis=0, keepdims=True)
    vt = vt_s[:, pl.ds(start, size)]
    plain = nn(vt, e.astype(BF16))
    moving = nn(vt[:w], mix.astype(BF16)) * sh.scale
    if state is None:
        acc[:w, :] = plain[:w]
        acc[w:, :] = plain[w:] + moving
        return most, total, cross
    acc[:w, :] = acc[:w, :] * decay + plain[:w]
    acc[w:, :] = acc[w:, :] * decay + (plain[w:] + moving)
    return most, state[1] * decay + total, state[2] * decay + cross


def block_rows(sh, block):
    return pl.multiple_of(block * sh.block, sh.block)


def load_state(stat):
    return tuple(stat[r : r + 1, :] for r in range(3))


def store_state(stat, state):
    for r in range(3):
        stat[r : r + 1, :] = state[r]


def forward_tiles(sh, kv_s, vt_s, acc, stat, qq, tiles, fresh=False, masked=False):
    places = [(block_rows(sh, block), blocks * sh.block) for block, blocks in tiles]
    scores = [scores_tile(sh, kv_s, qq, start, size) for start, size in places]
    state = None if fresh else load_state(stat)
    for (start, size), both in zip(places, scores):
        state = mix_tile(sh, vt_s, acc, start, size, both, state, masked)
    store_state(stat, state)


def paired_tiles(run, low, pairs):
    @pl.when(pairs % 2 == 1)
    def _():
        run([(low, 2)])

    def step(i, carry):
        at = low + 2 * (pairs % 2) + 4 * i
        run([(at, 2), (at + 2, 2)])
        return carry

    lax.fori_loop(0, pairs // 2, step, 0)


def load_chunk(sh, me_ref, sources, kv_s, q_parts, q_s, sems):
    pairs = []
    for m in range(sh.parts):
        slot = pl.ds(slot_of(me_ref, m, sh.rows), sh.rows)
        for i in range(q_s.shape[0]):
            for g in range(sh.group):
                at = (i * sh.group + g) * sh.rows
                pairs.append((q_parts[m].at[pl.ds(at, sh.rows), :], q_s.at[i, g, slot, :]))
        ref, base = sources[m]
        for i in range(kv_s.shape[0]):
            rows = pl.ds(base + i * sh.rows, sh.rows)
            pairs.append((ref.at[rows, :], kv_s.at[i, slot, :]))
    copy_in(pairs, sems)


def copies_of(sh, arrays, queries):
    return sh.parts * (arrays + queries * sh.group)


def transposed(x):
    return x.astype(F32).T.astype(BF16)


def located(chunk, refs):
    own, rest = chunk
    if isinstance(rest, list):
        return [(ref, 0) for ref in refs]
    pieces = 1 if rest is None else 1 + rest.shape[0] // own.shape[0]
    return [(refs[0], 0)] + [(refs[1], m * own.shape[0]) for m in range(pieces - 1)]


def chunk_arrays(chunk):
    own, rest = chunk
    if rest is None:
        return [own]
    return [own] + (rest if isinstance(rest, list) else [rest])


def back_of(sh, me_ref, back_ref, qb):
    per = sh.rows // sh.block
    return back_ref[jnp.bitwise_xor(me_ref[0], qb // per) * per + qb % per]


def forward_chunk(sh, me, back, q_parts, chunk, distance, state, gain_square=None):
    parts, w = sh.parts, sh.width
    kv = chunk_arrays(chunk)
    loads = parts + len(kv)
    opening, closing = state is None, gain_square is not None

    def kernel(me_ref, back_ref, *refs):
        refs = list(refs)
        q_in, kv_in = refs[:parts], refs[parts:loads]
        del refs[:loads]
        if not opening:
            acc_in, stat_in = refs[:2]
            del refs[:2]
        if closing:
            gain_ref, out, lse, sums, q_s, kv_s, vt_s, sems, acc, stat = refs
        else:
            acc_out, stat_out, q_s, kv_s, vt_s, sems = refs
            acc, stat = acc_out.at[0], stat_out.at[0]
        qb = pl.program_id(0)

        @pl.when(qb == 0)
        def _():
            load_chunk(sh, me_ref, located(chunk, kv_in), kv_s, q_in, q_s, sems)
            vt_s[:w, :] = transposed(kv_s[1])
            vt_s[w:, :] = transposed(kv_s[3])

        if not opening:
            acc[...] = acc_in[0]
            stat[...] = stat_in[0]
        top = sh.blocks if distance else qb + 1
        first = jnp.clip(qb - back_of(sh, me_ref, back_ref, qb) + distance * sh.blocks, 0, top)
        count = top - first

        @pl.when(count > 0)
        def _():
            qq = jnp.concatenate([query_rows(sh, q_s, 0, qb), query_rows(sh, q_s, 1, qb)], axis=1)
            run = functools.partial(forward_tiles, sh, kv_s, vt_s, acc, stat, qq)
            if opening:
                for size in (1, 2):

                    @pl.when(count % 2 == size % 2)
                    def _(size=size):
                        run([(top - size, size)], fresh=True, masked=True)

                paired_tiles(run, first, (count - 1) // 2)
            else:

                @pl.when(count % 2 == 1)
                def _():
                    run([(first, 1)])

                paired_tiles(run, first + count % 2, count // 2)

        if closing:
            most, total, cross = load_state(stat)
            inverse = 1.0 / total
            plain = acc[:w, :] * inverse
            moved = acc[w:, :] * inverse - (cross * inverse * sh.scale) * plain
            out[0, :w, :] = plain
            out[0, w:, :] = moved
            lse[0] = most + jnp.log2(total)
            square = plain * plain
            product = plain * moved
            gain = gain_ref[...]
            for r, value in enumerate((square, product, gain * square, gain * product)):
                line = jnp.sum(value, axis=0, keepdims=True)
                pieces = [line[:, g * sh.block : (g + 1) * sh.block] for g in range(sh.group)]
                sums[0, r : r + 1, :] = functools.reduce(jnp.add, pieces)

    def by_block(*shape):
        return pl.BlockSpec((1,) + shape, lambda i: (i,) + (0,) * len(shape))

    def array(*shape):
        return jax.ShapeDtypeStruct((sh.blocks,) + shape, F32)

    wide, stats = (2 * w, sh.lanes), (8, sh.lanes)
    in_specs = [SMEM, SMEM] + [ANY] * loads
    operands = [*q_parts, *kv]
    if not opening:
        in_specs += [by_block(*wide), by_block(*stats)]
        operands += state
    scratch = [
        pltpu.VMEM((2, sh.group, sh.tokens, w), BF16),
        pltpu.VMEM((4, sh.tokens, w), BF16),
        pltpu.VMEM((2 * w, sh.tokens), BF16),
        pltpu.SemaphoreType.DMA((copies_of(sh, 4, 2),)),
    ]
    if closing:
        in_specs.append(pl.BlockSpec((w, sh.lanes), lambda i: (0, 0)))
        operands.append(gain_square)
        shapes = [wide, (1, sh.lanes), (4, sh.block)]
        scratch += [pltpu.VMEM(wide, F32), pltpu.VMEM(stats, F32)]
    else:
        shapes = [wide, stats]
    work = sh.group * sh.tokens * sh.tokens // 2
    return pl.pallas_call(
        kernel,
        grid=(sh.blocks,),
        in_specs=in_specs,
        out_specs=[by_block(*shape) for shape in shapes],
        out_shape=[array(*shape) for shape in shapes],
        scratch_shapes=scratch,
        compiler_params=params(),
        cost_estimate=cost((24 if closing else 96) * work * w, 24 * sh.tokens * sh.lanes * 2, work),
        name="forward_far" if closing else "forward_chunk",
    )(me, back, *operands)


def backward_scores(sh, kv_s, qg, start, size):
    k = kv_s[0, pl.ds(start, size), :]
    v = kv_s[1, pl.ds(start, size), :]
    empty = jnp.zeros_like(k)
    left = jnp.concatenate([k, empty], axis=0)
    right = jnp.concatenate([empty, v], axis=0)
    both = nt(jnp.concatenate([left, right], axis=1), qg)
    return both[:size], both[size:]


def backward_tiles(sh, kv_s, kt_s, dkv_s, dq_s, qg, lse, dot, tiles, masked=False):
    places = [(block_rows(sh, block), blocks * sh.block) for block, blocks in tiles]
    scores = [backward_scores(sh, kv_s, qg, start, size) for start, size in places]
    q, g = qg[:, : sh.width], qg[:, sh.width :]
    for (start, size), (s, dp) in zip(places, scores):
        rows = pl.ds(start, size)
        p = jnp.exp2(s * sh.powers - lse)
        if masked:
            low = below_diagonal(sh, p[size - sh.block :], 0.0)
            p = low if size == sh.block else jnp.concatenate([p[: size - sh.block], low], axis=0)
        ds = (p * (dp - dot)).astype(BF16)
        dkv_s[0, rows, :] += nn(ds, q)
        dkv_s[1, rows, :] += nn(p.astype(BF16), g)
        dq_s[...] += nn(kt_s[:, rows], ds)


def backward_chunk(sh, me, back, q_parts, chunk, distance, grads, lse, dots, dq, norm, order, held):
    parts, w = sh.parts, sh.width
    kv = chunk_arrays(chunk)
    loads = parts + len(kv)
    opening, closing = norm is not None, distance == 0
    per = sh.rows // sh.block
    steps = len(order) * per

    def query_block(i, me_ref):
        if order == list(range(parts)):
            return i
        partner = functools.reduce(
            lambda chosen, j: jnp.where(i // per == j, order[j], chosen), range(len(order)), order[0]
        )
        return jnp.bitwise_xor(me_ref[0], partner) * per + i % per

    def kernel(me_ref, back_ref, *refs):
        refs = list(refs)

        def take(count):
            taken = refs[:count]
            del refs[:count]
            return taken

        q_in, kv_in = take(parts), take(len(kv))
        (lse_ref,) = take(1)
        if opening:
            out_ref, gain_ref, *sum_refs = take(2 + len(norm[0]))
        else:
            grad_ref, dot_ref, dq_ref = take(3)
        (held_ref,) = take(1) if held is not None else (None,)
        (dkv_out,) = take(1)
        dq_out = take(len(order) if closing else 1)
        if opening:
            grad_ref, dot_ref = take(2)
        q_s, kv_s, kt_s, dkv_s, dq_s, sems = refs
        i = pl.program_id(0)
        qb = query_block(i, me_ref)

        @pl.when(i == 0)
        def _():
            load_chunk(sh, me_ref, located(chunk, kv_in), kv_s, q_in, q_s, sems)
            kt_s[...] = transposed(kv_s[0])
            dkv_s[...] = jnp.zeros_like(dkv_s) if held_ref is None else held_ref[...]

        if opening:
            features = norm[2]
            token = functools.reduce(jnp.add, [ref[0] for ref in sum_refs])
            sums = jnp.concatenate([token] * sh.group, axis=1)
            square = sums[0:1] / features + EPSILON
            inverse = lax.rsqrt(square)
            ratio = sums[1:2] / (features * square)
            again = (sums[3:4] - ratio * sums[2:3]) * inverse
            again = again / (features * square)
            plain = out_ref[0, :w, :]
            moved = out_ref[0, w:, :]
            first_grad = gain_ref[...] * (moved - plain * ratio) * inverse
            cot = ((first_grad - plain * again) * inverse).astype(BF16).astype(F32)
            dot_ref[0] = jnp.sum(cot * plain, axis=0, keepdims=True)
            grad_ref[0] = cot.T.astype(BF16)
            dq_s[...] = jnp.zeros_like(dq_s)
        else:
            dq_s[...] = dq_ref[0]

        top = sh.blocks if distance else qb + 1
        first = jnp.clip(qb - back_of(sh, me_ref, back_ref, qb) + distance * sh.blocks, 0, top)
        count = top - first

        @pl.when(count > 0)
        def _():
            qg = jnp.concatenate([query_rows(sh, q_s, 0, qb), grad_ref[0]], axis=1)
            run = functools.partial(
                backward_tiles, sh, kv_s, kt_s, dkv_s, dq_s, qg, lse_ref[0], dot_ref[0]
            )
            if closing:
                for size in (1, 2):

                    @pl.when(count % 2 == size % 2)
                    def _(size=size):
                        run([(top - size, size)], masked=True)

                paired_tiles(run, first, (count - 1) // 2)
            else:

                @pl.when(count % 2 == 1)
                def _():
                    run([(first, 1)])

                paired_tiles(run, first + count % 2, count // 2)

        if closing:
            done = (dq_s[...] * sh.scale).T.reshape(sh.group, sh.block, w).astype(BF16)
            for j, out in enumerate(dq_out):

                @pl.when(i // per == j)
                def _(out=out):
                    out[...] = done

        else:
            dq_out[0][0] = dq_s[...]

        @pl.when(i == steps - 1)
        def _():
            factor = 1.0 if closing else sh.scale
            dkv_out[0] = (dkv_s[0] * factor).astype(dkv_out.dtype)
            dkv_out[1] = dkv_s[1].astype(dkv_out.dtype)

    def by_block(*shape):
        return pl.BlockSpec(
            (1,) + shape, lambda i, me_ref, _: (query_block(i, me_ref),) + (0,) * len(shape)
        )

    grad_specs = [by_block(sh.lanes, w), by_block(1, sh.lanes)]
    whole = pl.BlockSpec((2, sh.tokens, w), lambda i, *_: (0, 0, 0))
    in_specs = [ANY] * loads + [by_block(1, sh.lanes)]
    operands = [*q_parts, *kv, lse]
    if opening:
        in_specs += [by_block(2 * w, sh.lanes), pl.BlockSpec((w, sh.lanes), lambda i, *_: (0, 0))]
        in_specs += [by_block(4, sh.block)] * len(norm[0])
        operands += [grads, norm[1], *norm[0]]
    else:
        in_specs += grad_specs + [by_block(w, sh.lanes)]
        operands += [grads, dots, dq]
    if held is not None:
        in_specs.append(whole)
        operands.append(held)
    out_shape = [jax.ShapeDtypeStruct((2, sh.tokens, w), BF16 if opening else F32)]
    out_specs = [whole]
    if closing:
        for j in range(len(order)):
            out_shape.append(jax.ShapeDtypeStruct((sh.group, sh.rows, w), BF16))
            out_specs.append(
                pl.BlockSpec(
                    (sh.group, sh.block, w),
                    lambda i, *_, j=j: (0, jnp.clip(i - j * per, 0, per - 1), 0),
                )
            )
    else:
        out_shape.append(jax.ShapeDtypeStruct((sh.blocks, w, sh.lanes), F32))
        out_specs.append(by_block(w, sh.lanes))
    if opening:
        out_shape += [
            jax.ShapeDtypeStruct((sh.blocks, sh.lanes, w), BF16),
            jax.ShapeDtypeStruct((sh.blocks, 1, sh.lanes), F32),
        ]
        out_specs += grad_specs
    work = sh.group * sh.tokens * sh.block * steps // 2
    return pl.pallas_call(
        kernel,
        grid_spec=pltpu.PrefetchScalarGridSpec(
            num_scalar_prefetch=2,
            grid=(steps,),
            in_specs=in_specs,
            out_specs=out_specs,
            scratch_shapes=[
                pltpu.VMEM((1, sh.group, sh.tokens, w), BF16),
                pltpu.VMEM((2, sh.tokens, w), BF16),
                pltpu.VMEM((w, sh.tokens), BF16),
                pltpu.VMEM((2, sh.tokens, w), F32),
                pltpu.VMEM((w, sh.lanes), F32),
                pltpu.SemaphoreType.DMA((copies_of(sh, 2, 1),)),
            ],
        ),
        out_shape=out_shape,
        compiler_params=params(),
        cost_estimate=cost(20 * work * w, 12 * sh.block * steps * sh.lanes * 4, work),
        name="backward_chunk",
    )(me, back, *operands)


def combine(sh, me, carried, held):
    def kernel(me_ref, carried_ref, held_ref, *outs):
        for m, out in enumerate(outs):
            slot = pl.ds(slot_of(me_ref, m, sh.rows), sh.rows)
            for a, factor in ((0, sh.scale), (1, 1.0)):
                part = held_ref[a, slot, :] * factor
                out[a] = (carried_ref[a, slot, :].astype(F32) + part).astype(BF16)

    vmem = pl.BlockSpec(memory_space=pltpu.VMEM)
    return pl.pallas_call(
        kernel,
        in_specs=[SMEM, vmem, vmem],
        out_specs=[vmem] * sh.parts,
        out_shape=[jax.ShapeDtypeStruct((2, sh.rows, sh.width), BF16)] * sh.parts,
        compiler_params=params(),
        cost_estimate=cost(0, 1),
        name="combine",
    )(me, carried, held)


def exchanged(pieces):
    parts = len(pieces)
    return [pieces[0]] + [
        lax.ppermute(pieces[m], "part", [(i, i ^ m) for i in range(parts)])
        for m in range(1, parts)
    ]


def moved_on(value, steps):
    count = lax.axis_size("span")
    pairs = [(i, i + steps) for i in range(count) if 0 <= i + steps < count]
    return lax.ppermute(value, "span", pairs)


def summed_over_head(value):
    count = lax.axis_size("head")
    if count & (count - 1):
        return lax.psum(value, "head")
    step = 1
    while step < count:
        value = value + lax.ppermute(value, "head", [(i, i ^ step) for i in range(count)])
        step *= 2
    return value


def body(queries, keys, values, tangent_queries, tangent_keys, tangent_values, doc_start, out_gain):
    rows, query_heads, width = queries.shape
    key_heads = keys.shape[1]
    group = query_heads // key_heads
    parts = lax.axis_size("part")
    per = doc_start.shape[0]
    block = rows // per
    features = query_heads * width * lax.axis_size("head")
    hops = -(-DOC_DEVS // parts)
    sh = Shape(parts, group, rows, width, block)
    place = lax.axis_index("part")
    me = place.astype(jnp.int32).reshape(1)

    def flat(array):
        return array.reshape(-1, width)

    pieces = split_heads(
        [flat(a) for a in (keys, values, tangent_keys, tangent_values)], parts, 1, doc_start
    )
    q_rows, _ = lax.optimization_barrier(((flat(queries), flat(tangent_queries)), pieces[0]))
    q_pieces = split_heads(q_rows, parts, group)
    owns = [pieces[0]]
    for _ in range(hops):
        owns.append(moved_on(owns[-1], 1))
    pieces = exchanged(pieces)
    rests = [pieces[1:]]
    if parts > 1:
        late, _, q_pieces = lax.optimization_barrier((pieces[1:], owns[1:], q_pieces))
        rest = jnp.concatenate(late, axis=0)
        for _ in range(hops):
            rest = moved_on(rest, 1)
            rests.append(rest)
    chunks = list(zip(owns, rests if parts > 1 else [None] * (hops + 1)))
    q_parts = exchanged(q_pieces)
    back = jnp.concatenate([p[4 * rows : 4 * rows + per, 0] for p in pieces]).astype(jnp.int32)
    gain = lax.dynamic_index_in_dim(out_gain.reshape(key_heads, group, width), place, 0, False)
    gain_square = jnp.repeat((gain * gain).T, block, axis=1)

    state = None
    for distance in range(hops):
        state = forward_chunk(sh, me, back, q_parts, chunks[distance], distance, state)
    out, lse, sums = forward_chunk(
        sh, me, back, q_parts, chunks[hops], hops, state, gain_square
    )
    sums = summed_over_head(sums)
    norm = (exchanged([sums] * parts), gain_square, features)

    everyone = list(range(parts))
    carried, dq, grads, dots = backward_chunk(
        sh, me, back, q_parts, chunks[hops], hops, out, lse, None, None, norm, everyone, None
    )
    for distance in range(hops - 1, 0, -1):
        carried = moved_on(carried, -1)
        part, dq = backward_chunk(
            sh, me, back, q_parts, chunks[distance], distance, grads, lse, dots, dq, None,
            everyone, None,
        )
        carried = (carried.astype(F32) + part).astype(BF16)
    carried = moved_on(carried, -1)
    half = parts // 2
    held, dq_pieces = None, [None] * parts
    for order in ([m for m in range(parts - 1, half - 1, -1)], [m for m in range(half)]):
        if order:
            held, *done = backward_chunk(
                sh, me, back, q_parts, chunks[0], 0, grads, lse, dots, dq, None, order, held
            )
            for m, piece in zip(order, done):
                dq_pieces[m] = piece.reshape(1, group, rows, width)
    dq_pieces = exchanged(dq_pieces)
    dq_pieces[half:], held = lax.optimization_barrier((dq_pieces[half:], held))
    dkv_pieces = exchanged(combine(sh, me, carried, held))
    (product_queries,) = join_heads(dq_pieces, 1, group)
    dkv_pieces = [p.reshape(2, 1, rows, width) for p in dkv_pieces]
    product_keys, product_values = join_heads(dkv_pieces, 2, 1)
    return (
        product_queries.reshape(queries.shape),
        product_keys.reshape(keys.shape),
        product_values.reshape(keys.shape),
    )


def solution(mesh):
    def run(*arguments):
        count, heads = mesh.shape["ctx"], mesh.shape["head"]
        parts = arguments[1].shape[1] // heads
        split = Mesh(
            mesh.devices.reshape(count // parts, parts, heads), ("span", "part", "head")
        )
        ctx = ("span", "part")
        array = P(ctx, "head", None)
        return jax.shard_map(
            body,
            mesh=split,
            in_specs=(array,) * 6 + (P(ctx), P("head")),
            out_specs=(array,) * 3,
            check_vma=False,
        )(*arguments)

    return run
```

```python
import functools
import math

import jax
import jax.numpy as jnp
from jax import lax
from jax.experimental import pallas as pl
from jax.experimental.pallas import tpu as pltpu
from jax.sharding import Mesh, PartitionSpec as P

DOC_DEVS = 8
EPSILON = 1e-06
VMEM_BYTES = 18 * 1024 * 1024
NOTE_ROWS = 16
WIDE_VMEM_BYTES = 60 * 1024 * 1024
LOG2E = math.log2(math.e)
MASKED = -1e30
F32 = jnp.float32
BF16 = jnp.bfloat16
SMEM = pl.BlockSpec(memory_space=pltpu.SMEM)
VMEM = pl.BlockSpec(memory_space=pltpu.VMEM)


def params(size=VMEM_BYTES):
    return pltpu.CompilerParams(vmem_limit_bytes=size)


def cost(flops, moved, powers=0):
    return pl.CostEstimate(flops=int(flops), bytes_accessed=int(moved), transcendentals=int(powers))


def nn(a, b):
    return lax.dot_general(a, b, (((1,), (0,)), ((), ())), preferred_element_type=F32)


def nt(a, b):
    return lax.dot_general(a, b, (((1,), (1,)), ((), ())), preferred_element_type=F32)


def split_heads(arrays, parts, per_part, notes=None):
    count = len(arrays)
    total, width = arrays[0].shape
    heads = parts * per_part
    rows = total // heads
    length = count * per_part * rows
    extra = 0 if notes is None else NOTE_ROWS
    scalars = [] if notes is None else [notes]

    def kernel(*refs):
        ins = list(refs[: len(scalars) + count])
        outs, (held, wide, sems) = refs[len(scalars) + count : -3], refs[-3:]
        mine = lax.axis_index("part")
        if extra:
            note_ref = ins.pop(0)
        copies = [pltpu.make_async_copy(ins[a], held.at[a], sems.at[a]) for a in range(count)]
        for copy in copies:
            copy.start()
        if extra:
            first = (lax.axis_index("span") * parts + mine) * notes.shape[0]
            line = lax.broadcasted_iota(jnp.int32, (extra, width), 0)
            lines = jnp.zeros((extra, width), jnp.int32)
            for i in range(notes.shape[0]):
                lines = jnp.where(line == i, first + i - note_ref[i], lines)
            for out in outs:
                out[length:, :] = lines.astype(F32).astype(BF16)
        for a in range(count):
            copies[a].wait()
            wide[...] = held[a].astype(F32)
            for m in range(parts):
                for r in range(per_part):
                    head = jnp.bitwise_xor(mine, m) * per_part + r
                    at = (a * per_part + r) * rows
                    outs[m][at : at + rows, :] = wide[pl.ds(head, rows, stride=heads), :].astype(BF16)

    return pl.pallas_call(
        kernel,
        in_specs=[SMEM] * len(scalars) + [pl.BlockSpec(memory_space=pltpu.HBM)] * count,
        out_specs=[pl.BlockSpec(memory_space=pltpu.VMEM)] * parts,
        out_shape=[jax.ShapeDtypeStruct((length + extra, width), BF16)] * parts,
        scratch_shapes=[
            pltpu.VMEM((count, total, width), BF16),
            pltpu.VMEM((total, width), F32),
            pltpu.SemaphoreType.DMA((count,)),
        ],
        compiler_params=params(VMEM_BYTES if notes is None else WIDE_VMEM_BYTES),
        cost_estimate=cost(0, 4 * count * total * width),
        name="split_heads",
    )(*scalars, *arrays)


def join_heads(pieces, count, per_part):
    parts = len(pieces)
    rows, width = pieces[0].shape[-2:]
    heads = parts * per_part

    steps = 4
    cut = rows // steps

    def kernel(*refs):
        ins, outs = refs[:parts], refs[parts:]
        mine = lax.axis_index("part")
        for a in range(count):
            for m in range(parts):
                for r in range(per_part):
                    head = jnp.bitwise_xor(mine, m) * per_part + r
                    outs[a][pl.ds(head, cut, stride=heads), :] = ins[m][a, r].astype(F32)

    return pl.pallas_call(
        kernel,
        grid=(steps,),
        in_specs=[pl.BlockSpec((count, per_part, cut, width), lambda i: (0, 0, i, 0))] * parts,
        out_specs=[pl.BlockSpec((cut * heads, width), lambda i: (i, 0))] * count,
        out_shape=[jax.ShapeDtypeStruct((rows * heads, width), F32)] * count,
        compiler_params=params(),
        cost_estimate=cost(0, 6 * count * rows * heads * width),
        name="join_heads",
    )(*pieces)


def slot_of(me_ref, m, rows):
    return pl.multiple_of(jnp.bitwise_xor(me_ref[0], m) * rows, rows)


class Shape:
    def __init__(self, parts, group, rows, width, block):
        self.parts, self.group, self.rows, self.width, self.block = parts, group, rows, width, block
        self.tokens = parts * rows
        self.blocks = self.tokens // block
        self.lanes = group * block
        self.scale = width**-0.5
        self.powers = self.scale * LOG2E


def diagonal(sh):
    shape = (sh.block, sh.block)
    key = lax.broadcasted_iota(jnp.int32, shape, 0)
    query = lax.broadcasted_iota(jnp.int32, shape, 1)
    return key <= query


def below_diagonal(sh, value, other):
    allowed = diagonal(sh)
    cut = [value[:, g * sh.block : (g + 1) * sh.block] for g in range(sh.group)]
    return jnp.concatenate([jnp.where(allowed, part, other) for part in cut], axis=1)


def scores_tile(keys, qq, start, size):
    k_s, tk_s = keys
    k = k_s[pl.ds(start, size), :]
    tk = tk_s[pl.ds(start, size), :]
    left = jnp.concatenate([k, tk], axis=0)
    right = jnp.concatenate([jnp.zeros_like(k), k], axis=0)
    both = nt(jnp.concatenate([left, right], axis=1), qq)
    return both[:size], both[size:]


def mix_tile(sh, vt_s, acc, start, size, scores, state, masked):
    w = sh.width
    s, d = scores[0] * sh.powers, scores[1]
    if masked:
        low = below_diagonal(sh, s[size - sh.block :], MASKED)
        s = low if size == sh.block else jnp.concatenate([s[: size - sh.block], low], axis=0)
    most = jnp.max(s, axis=0, keepdims=True)
    if state is not None:
        most = jnp.maximum(most, state[0])
        decay = jnp.exp2(state[0] - most)
    e = jnp.exp2(s - most)
    mix = e * d
    total = jnp.sum(e, axis=0, keepdims=True)
    cross = jnp.sum(mix, axis=0, keepdims=True)
    vt = vt_s[:, pl.ds(start, size)]
    plain = nn(vt, e.astype(BF16))
    moving = nn(vt[:w], mix.astype(BF16)) * sh.scale
    if state is None:
        acc[:w, :] = plain[:w]
        acc[w:, :] = plain[w:] + moving
        return most, total, cross
    acc[:w, :] = acc[:w, :] * decay + plain[:w]
    acc[w:, :] = acc[w:, :] * decay + (plain[w:] + moving)
    return most, state[1] * decay + total, state[2] * decay + cross


def block_rows(sh, block):
    return pl.multiple_of(block * sh.block, sh.block)


def load_state(stat):
    return tuple(stat[r : r + 1, :] for r in range(3))


def store_state(stat, state):
    for r in range(3):
        stat[r : r + 1, :] = state[r]


def forward_tiles(sh, keys, vt_s, acc, stat, qq, tiles, fresh=False, masked=False):
    places = [(block_rows(sh, block), blocks * sh.block) for block, blocks in tiles]
    scores = [scores_tile(keys, qq, start, size) for start, size in places]
    state = None if fresh else load_state(stat)
    for (start, size), both in zip(places, scores):
        state = mix_tile(sh, vt_s, acc, start, size, both, state, masked)
    store_state(stat, state)


def paired_tiles(run, low, pairs):
    @pl.when(pairs % 2 == 1)
    def _():
        run([(low, 2)])

    def step(i, carry):
        at = low + 2 * (pairs % 2) + 4 * i
        run([(at, 2), (at + 2, 2)])
        return carry

    lax.fori_loop(0, pairs // 2, step, 0)


def lay_chunk(sh, me_ref, sources, targets):
    for m, (ref, base) in enumerate(sources):
        slot = pl.ds(slot_of(me_ref, m, sh.rows), sh.rows)
        for i, target in enumerate(targets):
            at = base + i * sh.rows
            target[slot, :] = ref[at : at + sh.rows, :]


def lay_queries(sh, me_ref, pieces, qq):
    per = sh.rows // sh.block
    for m, ref in enumerate(pieces):
        for i in range(2):
            for g in range(sh.group):
                for r in range(per):
                    block = jnp.bitwise_xor(me_ref[0], m) * per + r
                    at = (i * sh.group + g) * sh.rows + r * sh.block
                    qq[
                        block,
                        g * sh.block : (g + 1) * sh.block,
                        i * sh.width : (i + 1) * sh.width,
                    ] = ref[at : at + sh.block, :]


def transposed(x):
    return x.astype(F32).T.astype(BF16)


def located(chunk, refs):
    own, rest = chunk
    if isinstance(rest, list):
        return [(ref, 0) for ref in refs]
    pieces = 1 if rest is None else 1 + rest.shape[0] // own.shape[0]
    return [(refs[0], 0)] + [(refs[1], m * own.shape[0]) for m in range(pieces - 1)]


def chunk_arrays(chunk):
    own, rest = chunk
    if rest is None:
        return [own]
    return [own] + (rest if isinstance(rest, list) else [rest])


def back_of(sh, me_ref, back_ref, qb):
    per = sh.rows // sh.block
    return back_ref[jnp.bitwise_xor(me_ref[0], qb // per) * per + qb % per]


def each_block(count, run):
    def step(i, carry):
        run(i)
        return carry

    lax.fori_loop(0, count, step, 0)


def forward_chunk(sh, me, back, queries, chunk, distance, state, gain_square=None):
    w = sh.width
    kv = chunk_arrays(chunk)
    opening, closing = state is None, gain_square is not None

    def kernel(me_ref, back_ref, *refs):
        refs = list(refs)

        def take(count):
            taken = refs[:count]
            del refs[:count]
            return taken

        q_in = take(len(queries))
        kv_in = take(len(kv))
        if not opening:
            take(2)
        if closing:
            (gain_ref,) = take(1)
        k_s, v_s, kt_s, accs, stats = take(5)
        if opening:
            (qq_s,) = take(1)
            lay_queries(sh, me_ref, q_in, qq_s)
        else:
            (qq_s,) = q_in
        if closing:
            lse, sums = take(2)
        tk_s, tv_s, vt_s = refs
        lay_chunk(sh, me_ref, located(chunk, kv_in), (k_s, v_s, tk_s, tv_s))
        kt_s[...] = transposed(k_s[...])
        vt_s[:w, :] = transposed(v_s[...])
        vt_s[w:, :] = transposed(tv_s[...])

        def query_block(qb):
            acc, stat = accs.at[qb], stats.at[qb]
            top = sh.blocks if distance else qb + 1
            first = jnp.clip(qb - back_of(sh, me_ref, back_ref, qb) + distance * sh.blocks, 0, top)
            count = top - first

            @pl.when(count > 0)
            def _():
                run = functools.partial(
                    forward_tiles, sh, (k_s, tk_s), vt_s, acc, stat, qq_s[qb]
                )
                if opening:
                    for size in (1, 2):

                        @pl.when(count % 2 == size % 2)
                        def _(size=size):
                            run([(top - size, size)], fresh=True, masked=True)

                    paired_tiles(run, first, (count - 1) // 2)
                else:

                    @pl.when(count % 2 == 1)
                    def _():
                        run([(first, 1)])

                    paired_tiles(run, first + count % 2, count // 2)

            if closing:
                most, total, cross = load_state(stat)
                inverse = 1.0 / total
                plain = acc[:w, :] * inverse
                moved = acc[w:, :] * inverse - (cross * inverse * sh.scale) * plain
                acc[:w, :] = plain
                acc[w:, :] = moved
                lse[qb] = most + jnp.log2(total)
                square = plain * plain
                product = plain * moved
                gain = gain_ref[...]
                for r, value in enumerate((square, product, gain * square, gain * product)):
                    line = jnp.sum(value, axis=0, keepdims=True)
                    pieces = [line[:, g * sh.block : (g + 1) * sh.block] for g in range(sh.group)]
                    sums[qb, r : r + 1, :] = functools.reduce(jnp.add, pieces)

        each_block(sh.blocks, query_block)

    def array(*shape, dtype=F32):
        return jax.ShapeDtypeStruct(shape, dtype)

    out_shape = [
        array(sh.tokens, w, dtype=BF16),
        array(sh.tokens, w, dtype=BF16),
        array(w, sh.tokens, dtype=BF16),
        array(sh.blocks, 2 * w, sh.lanes),
        array(sh.blocks, 8, sh.lanes),
    ]
    if opening:
        out_shape.append(array(sh.blocks, sh.lanes, 2 * w, dtype=BF16))
    if closing:
        out_shape += [array(sh.blocks, 1, sh.lanes), array(sh.blocks, 4, sh.block)]
    operands = [*queries, *kv]
    aliases = {}
    if not opening:
        aliases = {2 + len(operands): 3, 3 + len(operands): 4}
        operands += state
    if closing:
        operands.append(gain_square)
    work = sh.group * sh.tokens * sh.tokens // 2
    return pl.pallas_call(
        kernel,
        in_specs=[SMEM, SMEM] + [VMEM] * len(operands),
        out_specs=[VMEM] * len(out_shape),
        out_shape=out_shape,
        input_output_aliases=aliases,
        scratch_shapes=[
            pltpu.VMEM((sh.tokens, w), BF16),
            pltpu.VMEM((sh.tokens, w), BF16),
            pltpu.VMEM((2 * w, sh.tokens), BF16),
        ],
        compiler_params=params(),
        cost_estimate=cost(24 * work * w, 12 * sh.tokens * sh.lanes * 2, work),
        name="forward_far" if closing else "forward_chunk",
    )(me, back, *operands)


def backward_scores(keys, qg, start, size):
    k_s, v_s = keys
    k = k_s[pl.ds(start, size), :]
    v = v_s[pl.ds(start, size), :]
    empty = jnp.zeros_like(k)
    left = jnp.concatenate([k, empty], axis=0)
    right = jnp.concatenate([empty, v], axis=0)
    both = nt(jnp.concatenate([left, right], axis=1), qg)
    return both[:size], both[size:]


def backward_tiles(sh, keys, kt_s, dkv_s, dq_s, qg, lse, dot, tiles, masked=False):
    places = [(block_rows(sh, block), blocks * sh.block) for block, blocks in tiles]
    scores = [backward_scores(keys, qg, start, size) for start, size in places]
    q, g = qg[:, : sh.width], qg[:, sh.width :]
    for (start, size), (s, dp) in zip(places, scores):
        rows = pl.ds(start, size)
        p = jnp.exp2(s * sh.powers - lse)
        if masked:
            low = below_diagonal(sh, p[size - sh.block :], 0.0)
            p = low if size == sh.block else jnp.concatenate([p[: size - sh.block], low], axis=0)
        ds = (p * (dp - dot)).astype(BF16)
        dkv_s[0, rows, :] += nn(ds, q)
        dkv_s[1, rows, :] += nn(p.astype(BF16), g)
        dq_s[...] += nn(kt_s[:, rows], ds)


def backward_chunk(sh, me, back, qq, keys, distance, grads, lse, dots, dq, norm, order, held):
    w = sh.width
    opening, closing = norm is not None, distance == 0
    per = sh.rows // sh.block
    everyone = order == list(range(sh.parts))

    def kernel(me_ref, back_ref, *refs):
        refs = list(refs)

        def take(count):
            taken = refs[:count]
            del refs[:count]
            return taken

        qq_s, k_s, v_s, kt_s, lse_s = take(5)
        if opening:
            out_s, gain_ref, *sum_refs = take(2 + len(norm[0]))
        else:
            grad_s, dot_s, dq_in = take(3)
        (held_ref,) = take(1) if held is not None else (None,)
        (dkv_out,) = take(1)
        dq_out = take(len(order) if closing else 1)
        if opening:
            grad_s, dot_s = take(2)
        dkv_s, dq_own = refs
        dkv_s[...] = jnp.zeros_like(dkv_s) if held_ref is None else held_ref[...]

        def query_block(i):
            qb = i
            if not everyone:
                partner = functools.reduce(
                    lambda chosen, j: jnp.where(i // per == j, order[j], chosen),
                    range(len(order)),
                    order[0],
                )
                qb = jnp.bitwise_xor(me_ref[0], partner) * per + i % per
            dq_s = dq_own if closing else dq_out[0].at[qb]
            if opening:
                features = norm[2]
                token = functools.reduce(jnp.add, [ref[qb] for ref in sum_refs])
                sums = jnp.concatenate([token] * sh.group, axis=1)
                square = sums[0:1] / features + EPSILON
                inverse = lax.rsqrt(square)
                ratio = sums[1:2] / (features * square)
                again = (sums[3:4] - ratio * sums[2:3]) * inverse
                again = again / (features * square)
                plain = out_s[qb, :w, :]
                moved = out_s[qb, w:, :]
                first_grad = gain_ref[...] * (moved - plain * ratio) * inverse
                cot = ((first_grad - plain * again) * inverse).astype(BF16).astype(F32)
                dot_s[qb] = jnp.sum(cot * plain, axis=0, keepdims=True)
                grad_s[qb] = cot.T.astype(BF16)
                dq_s[...] = jnp.zeros((w, sh.lanes), F32)
            elif closing:
                dq_s[...] = dq_in[qb]

            top = sh.blocks if distance else qb + 1
            first = jnp.clip(qb - back_of(sh, me_ref, back_ref, qb) + distance * sh.blocks, 0, top)
            count = top - first

            @pl.when(count > 0)
            def _():
                qg = jnp.concatenate([qq_s[qb, :, :w], grad_s[qb]], axis=1)
                run = functools.partial(
                    backward_tiles, sh, (k_s, v_s), kt_s, dkv_s, dq_s, qg, lse_s[qb], dot_s[qb]
                )
                if closing:
                    for size in (1, 2):

                        @pl.when(count % 2 == size % 2)
                        def _(size=size):
                            run([(top - size, size)], masked=True)

                    paired_tiles(run, first, (count - 1) // 2)
                else:

                    @pl.when(count % 2 == 1)
                    def _():
                        run([(first, 1)])

                    paired_tiles(run, first + count % 2, count // 2)

            if closing:
                done = (dq_s[...] * sh.scale).T.reshape(sh.group, sh.block, w).astype(BF16)
                at = pl.ds(pl.multiple_of(i % per * sh.block, sh.block), sh.block)
                for j, out in enumerate(dq_out):

                    @pl.when(i // per == j)
                    def _(out=out):
                        out[:, at, :] = done

        each_block(len(order) * per, query_block)
        factor = 1.0 if closing else sh.scale
        dkv_out[0] = (dkv_s[0] * factor).astype(dkv_out.dtype)
        dkv_out[1] = dkv_s[1].astype(dkv_out.dtype)

    def array(*shape, dtype=F32):
        return jax.ShapeDtypeStruct(shape, dtype)

    operands = [qq, *keys, lse]
    if opening:
        operands += [grads, norm[1], *norm[0]]
    else:
        operands += [grads, dots, dq]
    aliases = {}
    if not opening and not closing:
        aliases = {1 + len(operands): 1}
    if held is not None:
        operands.append(held)
    out_shape = [array(2, sh.tokens, w, dtype=BF16 if opening else F32)]
    if closing:
        out_shape += [array(sh.group, sh.rows, w, dtype=BF16)] * len(order)
    else:
        out_shape.append(array(sh.blocks, w, sh.lanes))
    if opening:
        out_shape += [
            array(sh.blocks, sh.lanes, w, dtype=BF16),
            array(sh.blocks, 1, sh.lanes),
        ]
    work = sh.group * sh.tokens * len(order) * sh.rows // 2
    return pl.pallas_call(
        kernel,
        in_specs=[SMEM, SMEM] + [VMEM] * len(operands),
        out_specs=[VMEM] * len(out_shape),
        out_shape=out_shape,
        input_output_aliases=aliases,
        scratch_shapes=[
            pltpu.VMEM((2, sh.tokens, w), F32),
            pltpu.VMEM((w, sh.lanes), F32),
        ],
        compiler_params=params(),
        cost_estimate=cost(20 * work * w, 12 * len(order) * sh.rows * sh.lanes * 4, work),
        name="backward_chunk",
    )(me, back, *operands)


def combine(sh, me, carried, held):
    def kernel(me_ref, carried_ref, held_ref, *outs):
        for m, out in enumerate(outs):
            slot = pl.ds(slot_of(me_ref, m, sh.rows), sh.rows)
            for a, factor in ((0, sh.scale), (1, 1.0)):
                part = held_ref[a, slot, :] * factor
                out[a] = (carried_ref[a, slot, :].astype(F32) + part).astype(BF16)

    return pl.pallas_call(
        kernel,
        in_specs=[SMEM, VMEM, VMEM],
        out_specs=[VMEM] * sh.parts,
        out_shape=[jax.ShapeDtypeStruct((2, sh.rows, sh.width), BF16)] * sh.parts,
        compiler_params=params(),
        cost_estimate=cost(0, 1),
        name="combine",
    )(me, carried, held)


def exchanged(pieces):
    parts = len(pieces)
    return [pieces[0]] + [
        lax.ppermute(pieces[m], "part", [(i, i ^ m) for i in range(parts)])
        for m in range(1, parts)
    ]


def moved_on(value, steps):
    count = lax.axis_size("span")
    pairs = [(i, i + steps) for i in range(count) if 0 <= i + steps < count]
    return lax.ppermute(value, "span", pairs)


def summed_over_head(value):
    count = lax.axis_size("head")
    if count & (count - 1):
        return lax.psum(value, "head")
    step = 1
    while step < count:
        value = value + lax.ppermute(value, "head", [(i, i ^ step) for i in range(count)])
        step *= 2
    return value


def body(queries, keys, values, tangent_queries, tangent_keys, tangent_values, doc_start, out_gain):
    rows, query_heads, width = queries.shape
    key_heads = keys.shape[1]
    group = query_heads // key_heads
    parts = lax.axis_size("part")
    per = doc_start.shape[0]
    block = rows // per
    features = query_heads * width * lax.axis_size("head")
    hops = -(-DOC_DEVS // parts)
    sh = Shape(parts, group, rows, width, block)
    place = lax.axis_index("part")
    me = place.astype(jnp.int32).reshape(1)

    def flat(array):
        return array.reshape(-1, width)

    pieces = split_heads(
        [flat(a) for a in (keys, values, tangent_keys, tangent_values)], parts, 1, doc_start
    )
    q_rows, _ = lax.optimization_barrier(((flat(queries), flat(tangent_queries)), pieces[0]))
    q_pieces = split_heads(q_rows, parts, group)
    owns = [pieces[0]]
    for _ in range(hops):
        owns.append(moved_on(owns[-1], 1))
    pieces = exchanged(pieces)
    rests = [pieces[1:]]
    if parts > 1:
        late, _, q_pieces = lax.optimization_barrier((pieces[1:], owns[1:], q_pieces))
        rest = jnp.concatenate(late, axis=0)
        for _ in range(hops):
            rest = moved_on(rest, 1)
            rests.append(rest)
    chunks = list(zip(owns, rests if parts > 1 else [None] * (hops + 1)))
    q_parts = exchanged(q_pieces)
    back = jnp.concatenate([p[4 * rows : 4 * rows + per, 0] for p in pieces]).astype(jnp.int32)
    gain = lax.dynamic_index_in_dim(out_gain.reshape(key_heads, group, width), place, 0, False)
    gain_square = jnp.repeat((gain * gain).T, block, axis=1)

    state, spans = None, []
    for distance in range(hops):
        k, v, kt, acc, stat, *laid = forward_chunk(
            sh, me, back, [qq] if distance else q_parts, chunks[distance], distance, state
        )
        qq = laid[0] if laid else qq
        state = [acc, stat]
        spans.append((k, v, kt))
    k, v, kt, out, _, lse, sums = forward_chunk(
        sh, me, back, [qq], chunks[hops], hops, state, gain_square
    )
    spans.append((k, v, kt))
    sums = summed_over_head(sums)
    norm = (exchanged([sums] * parts), gain_square, features)

    everyone = list(range(parts))
    carried, dq, grads, dots = backward_chunk(
        sh, me, back, qq, spans[hops], hops, out, lse, None, None, norm, everyone, None
    )
    for distance in range(hops - 1, 0, -1):
        carried = moved_on(carried, -1)
        part, dq = backward_chunk(
            sh, me, back, qq, spans[distance], distance, grads, lse, dots, dq, None,
            everyone, None,
        )
        carried = (carried.astype(F32) + part).astype(BF16)
    carried = moved_on(carried, -1)
    half = parts // 2
    held, dq_pieces = None, [None] * parts
    for order in ([m for m in range(parts - 1, half - 1, -1)], [m for m in range(half)]):
        if order:
            held, *done = backward_chunk(
                sh, me, back, qq, spans[0], 0, grads, lse, dots, dq, None, order, held
            )
            for m, piece in zip(order, done):
                dq_pieces[m] = piece.reshape(1, group, rows, width)
    dq_pieces = exchanged(dq_pieces)
    dq_pieces[half:], held = lax.optimization_barrier((dq_pieces[half:], held))
    dkv_pieces = exchanged(combine(sh, me, carried, held))
    (product_queries,) = join_heads(dq_pieces, 1, group)
    dkv_pieces = [p.reshape(2, 1, rows, width) for p in dkv_pieces]
    product_keys, product_values = join_heads(dkv_pieces, 2, 1)
    return (
        product_queries.reshape(queries.shape),
        product_keys.reshape(keys.shape),
        product_values.reshape(keys.shape),
    )


def solution(mesh):
    def run(*arguments):
        count, heads = mesh.shape["ctx"], mesh.shape["head"]
        parts = arguments[1].shape[1] // heads
        split = Mesh(
            mesh.devices.reshape(count // parts, parts, heads), ("span", "part", "head")
        )
        ctx = ("span", "part")
        array = P(ctx, "head", None)
        return jax.shard_map(
            body,
            mesh=split,
            in_specs=(array,) * 6 + (P(ctx), P("head")),
            out_specs=(array,) * 3,
            check_vma=False,
        )(*arguments)

    return run
```

```python
import functools
import math

import jax
import jax.numpy as jnp
from jax import lax
from jax.experimental import pallas as pl
from jax.experimental.pallas import tpu as pltpu
from jax.sharding import Mesh, PartitionSpec as P

DOC_DEVS = 8
EPSILON = 1e-06
VMEM_BYTES = 18 * 1024 * 1024
NOTE_ROWS = 16
WIDE_VMEM_BYTES = 60 * 1024 * 1024
LOG2E = math.log2(math.e)
MASKED = -1e30
F32 = jnp.float32
BF16 = jnp.bfloat16
SMEM = pl.BlockSpec(memory_space=pltpu.SMEM)
VMEM = pl.BlockSpec(memory_space=pltpu.VMEM)


def params(size=VMEM_BYTES):
    return pltpu.CompilerParams(vmem_limit_bytes=size)


def cost(flops, moved, powers=0):
    return pl.CostEstimate(flops=int(flops), bytes_accessed=int(moved), transcendentals=int(powers))


def nn(a, b):
    return lax.dot_general(a, b, (((1,), (0,)), ((), ())), preferred_element_type=F32)


def nt(a, b):
    return lax.dot_general(a, b, (((1,), (1,)), ((), ())), preferred_element_type=F32)


def split_heads(arrays, parts, per_part, notes=None):
    count = len(arrays)
    total, width = arrays[0].shape
    heads = parts * per_part
    rows = total // heads
    length = count * per_part * rows
    extra = 0 if notes is None else NOTE_ROWS
    scalars = [] if notes is None else [notes]

    def kernel(*refs):
        ins = list(refs[: len(scalars) + count])
        outs, (held, wide, sems) = refs[len(scalars) + count : -3], refs[-3:]
        mine = lax.axis_index("part")
        if extra:
            note_ref = ins.pop(0)
        copies = [pltpu.make_async_copy(ins[a], held.at[a], sems.at[a]) for a in range(count)]
        for copy in copies:
            copy.start()
        if extra:
            first = (lax.axis_index("span") * parts + mine) * notes.shape[0]
            line = lax.broadcasted_iota(jnp.int32, (extra, width), 0)
            lines = jnp.zeros((extra, width), jnp.int32)
            for i in range(notes.shape[0]):
                lines = jnp.where(line == i, first + i - note_ref[i], lines)
            for out in outs:
                out[length:, :] = lines.astype(F32).astype(BF16)
        for a in range(count):
            copies[a].wait()
            wide[...] = held[a].astype(F32)
            for m in range(parts):
                for r in range(per_part):
                    head = jnp.bitwise_xor(mine, m) * per_part + r
                    at = (a * per_part + r) * rows
                    outs[m][at : at + rows, :] = wide[pl.ds(head, rows, stride=heads), :].astype(BF16)

    return pl.pallas_call(
        kernel,
        in_specs=[SMEM] * len(scalars) + [pl.BlockSpec(memory_space=pltpu.HBM)] * count,
        out_specs=[pl.BlockSpec(memory_space=pltpu.VMEM)] * parts,
        out_shape=[jax.ShapeDtypeStruct((length + extra, width), BF16)] * parts,
        scratch_shapes=[
            pltpu.VMEM((count, total, width), BF16),
            pltpu.VMEM((total, width), F32),
            pltpu.SemaphoreType.DMA((count,)),
        ],
        compiler_params=params(VMEM_BYTES if notes is None else WIDE_VMEM_BYTES),
        cost_estimate=cost(0, 4 * count * total * width),
        name="split_heads",
    )(*scalars, *arrays)


def join_heads(pieces, count, per_part):
    parts = len(pieces)
    rows, width = pieces[0].shape[-2:]
    heads = parts * per_part

    steps = 4
    cut = rows // steps

    def kernel(*refs):
        ins, outs = refs[:parts], refs[parts:]
        mine = lax.axis_index("part")
        for a in range(count):
            for m in range(parts):
                for r in range(per_part):
                    head = jnp.bitwise_xor(mine, m) * per_part + r
                    outs[a][pl.ds(head, cut, stride=heads), :] = ins[m][a, r].astype(F32)

    return pl.pallas_call(
        kernel,
        grid=(steps,),
        in_specs=[pl.BlockSpec((count, per_part, cut, width), lambda i: (0, 0, i, 0))] * parts,
        out_specs=[pl.BlockSpec((cut * heads, width), lambda i: (i, 0))] * count,
        out_shape=[jax.ShapeDtypeStruct((rows * heads, width), F32)] * count,
        compiler_params=params(),
        cost_estimate=cost(0, 6 * count * rows * heads * width),
        name="join_heads",
    )(*pieces)


def slot_of(me_ref, m, rows):
    return pl.multiple_of(jnp.bitwise_xor(me_ref[0], m) * rows, rows)


class Shape:
    def __init__(self, parts, group, rows, width, block):
        self.parts, self.group, self.rows, self.width, self.block = parts, group, rows, width, block
        self.tokens = parts * rows
        self.blocks = self.tokens // block
        self.lanes = group * block
        self.scale = width**-0.5
        self.powers = self.scale * LOG2E


def diagonal(sh):
    shape = (sh.block, sh.block)
    key = lax.broadcasted_iota(jnp.int32, shape, 0)
    query = lax.broadcasted_iota(jnp.int32, shape, 1)
    return key <= query


def below_diagonal(sh, value, other):
    allowed = diagonal(sh)
    cut = [value[:, g * sh.block : (g + 1) * sh.block] for g in range(sh.group)]
    return jnp.concatenate([jnp.where(allowed, part, other) for part in cut], axis=1)


def scores_tile(keys, qq, start, size):
    k_s, tk_s = keys
    k = k_s[pl.ds(start, size), :]
    tk = tk_s[pl.ds(start, size), :]
    left = jnp.concatenate([k, tk], axis=0)
    right = jnp.concatenate([jnp.zeros_like(k), k], axis=0)
    both = nt(jnp.concatenate([left, right], axis=1), qq)
    return both[:size], both[size:]


def mix_tile(sh, vt_s, acc, start, size, scores, state, masked):
    w = sh.width
    s, d = scores[0] * sh.powers, scores[1]
    if masked:
        low = below_diagonal(sh, s[size - sh.block :], MASKED)
        s = low if size == sh.block else jnp.concatenate([s[: size - sh.block], low], axis=0)
    most = jnp.max(s, axis=0, keepdims=True)
    if state is not None:
        most = jnp.maximum(most, state[0])
        decay = jnp.exp2(state[0] - most)
    e = jnp.exp2(s - most)
    mix = e * d
    total = jnp.sum(e, axis=0, keepdims=True)
    cross = jnp.sum(mix, axis=0, keepdims=True)
    vt = vt_s[:, pl.ds(start, size)]
    plain = nn(vt, e.astype(BF16))
    moving = nn(vt[:w], mix.astype(BF16)) * sh.scale
    if state is None:
        acc[:w, :] = plain[:w]
        acc[w:, :] = plain[w:] + moving
        return most, total, cross
    acc[:w, :] = acc[:w, :] * decay + plain[:w]
    acc[w:, :] = acc[w:, :] * decay + (plain[w:] + moving)
    return most, state[1] * decay + total, state[2] * decay + cross


def block_rows(sh, block):
    return pl.multiple_of(block * sh.block, sh.block)


def load_state(stat):
    return tuple(stat[r : r + 1, :] for r in range(3))


def store_state(stat, state):
    for r in range(3):
        stat[r : r + 1, :] = state[r]


def forward_tiles(sh, keys, vt_s, acc, stat, qq, tiles, masked):
    places = [(block_rows(sh, block), blocks * sh.block) for block, blocks in tiles]
    scores = [scores_tile(keys, qq, start, size) for start, size in places]
    state = None if masked else load_state(stat)
    for i, ((start, size), both) in enumerate(zip(places, scores)):
        state = mix_tile(sh, vt_s, acc, start, size, both, state, masked and i == 0)
    store_state(stat, state)


def tiles_up(low, blocks):
    odd = blocks % 2
    return [(low, 1)] * odd + [(low + odd + 2 * i, 2) for i in range(blocks // 2)]


def tiles_down(top, blocks):
    first = 2 - blocks % 2
    return [(top - first, first)] + [
        (top - first - 2 * i, 2) for i in range(1, (blocks - first) // 2 + 1)
    ]


def by_count(sh, low, count, run, masked):
    head = jnp.where(count <= 6, count, 3 + lax.rem(jnp.maximum(count - 7, 0), 4))
    fours = (count - head) // 4
    for blocks in range(1, min(6, sh.blocks) + 1):

        @pl.when(head == blocks)
        def _(blocks=blocks):
            if masked:
                run(tiles_down(low + count, blocks), True)
            else:
                run(tiles_up(low, blocks), False)

    def step(i, carry):
        run(tiles_up(low + (0 if masked else head) + 4 * i, 4), None)
        return carry

    if sh.blocks > 6:
        lax.fori_loop(0, fours, step, 0)


def lay_chunk(sh, me_ref, sources, targets):
    for m, (ref, base) in enumerate(sources):
        slot = pl.ds(slot_of(me_ref, m, sh.rows), sh.rows)
        for i, target in enumerate(targets):
            at = base + i * sh.rows
            target[slot, :] = ref[at : at + sh.rows, :]


def lay_queries(sh, me_ref, pieces, qq):
    per = sh.rows // sh.block
    for m, ref in enumerate(pieces):
        for i in range(2):
            for g in range(sh.group):
                for r in range(per):
                    block = jnp.bitwise_xor(me_ref[0], m) * per + r
                    at = (i * sh.group + g) * sh.rows + r * sh.block
                    qq[
                        block,
                        g * sh.block : (g + 1) * sh.block,
                        i * sh.width : (i + 1) * sh.width,
                    ] = ref[at : at + sh.block, :]


def transposed(x):
    return x.astype(F32).T.astype(BF16)


def located(sh, refs):
    if len(refs) == sh.parts:
        return [(ref, 0) for ref in refs]
    length = refs[0].shape[0] // sh.parts
    return [(refs[0], m * length) for m in range(sh.parts)]


def back_of(sh, me_ref, back_ref, qb):
    per = sh.rows // sh.block
    return back_ref[jnp.bitwise_xor(me_ref[0], qb // per) * per + qb % per]


def each_block(count, run):
    def step(i, carry):
        run(i)
        return carry

    lax.fori_loop(0, count, step, 0)


def forward_chunk(sh, me, back, queries, chunk, distance, state, gain_square=None):
    w = sh.width
    kv = chunk
    opening, closing = state is None, gain_square is not None

    def kernel(me_ref, back_ref, *refs):
        refs = list(refs)

        def take(count):
            taken = refs[:count]
            del refs[:count]
            return taken

        q_in = take(len(queries))
        kv_in = take(len(kv))
        if not opening:
            take(2)
        if closing:
            (gain_ref,) = take(1)
        k_s, v_s, kt_s, accs, stats = take(5)
        if opening:
            (qq_s,) = take(1)
            lay_queries(sh, me_ref, q_in, qq_s)
        else:
            (qq_s,) = q_in
        if closing:
            lse, sums = take(2)
        tk_s, tv_s, vt_s = refs
        lay_chunk(sh, me_ref, located(sh, kv_in), (k_s, v_s, tk_s, tv_s))
        kt_s[...] = transposed(k_s[...])
        vt_s[:w, :] = transposed(v_s[...])
        vt_s[w:, :] = transposed(tv_s[...])

        def query_block(qb):
            acc, stat = accs.at[qb], stats.at[qb]
            top = sh.blocks if distance else qb + 1
            first = jnp.clip(qb - back_of(sh, me_ref, back_ref, qb) + distance * sh.blocks, 0, top)
            count = top - first

            @pl.when(count > 0)
            def _():
                run = functools.partial(
                    forward_tiles, sh, (k_s, tk_s), vt_s, acc, stat, qq_s[qb]
                )
                by_count(sh, first, count, run, opening)

            if closing:
                most, total, cross = load_state(stat)
                inverse = 1.0 / total
                plain = acc[:w, :] * inverse
                moved = acc[w:, :] * inverse - (cross * inverse * sh.scale) * plain
                acc[:w, :] = plain
                acc[w:, :] = moved
                lse[qb] = most + jnp.log2(total)
                square = plain * plain
                product = plain * moved
                gain = gain_ref[...]
                for r, value in enumerate((square, product, gain * square, gain * product)):
                    line = jnp.sum(value, axis=0, keepdims=True)
                    pieces = [line[:, g * sh.block : (g + 1) * sh.block] for g in range(sh.group)]
                    sums[qb, r : r + 1, :] = functools.reduce(jnp.add, pieces)

        each_block(sh.blocks, query_block)

    def array(*shape, dtype=F32):
        return jax.ShapeDtypeStruct(shape, dtype)

    out_shape = [
        array(sh.tokens, w, dtype=BF16),
        array(sh.tokens, w, dtype=BF16),
        array(w, sh.tokens, dtype=BF16),
        array(sh.blocks, 2 * w, sh.lanes),
        array(sh.blocks, 8, sh.lanes),
    ]
    if opening:
        out_shape.append(array(sh.blocks, sh.lanes, 2 * w, dtype=BF16))
    if closing:
        out_shape += [array(sh.blocks, 1, sh.lanes), array(sh.blocks, 4, sh.block)]
    operands = [*queries, *kv]
    aliases = {}
    if not opening:
        aliases = {2 + len(operands): 3, 3 + len(operands): 4}
        operands += state
    if closing:
        operands.append(gain_square)
    work = sh.group * sh.tokens * sh.tokens // 2
    return pl.pallas_call(
        kernel,
        in_specs=[SMEM, SMEM] + [VMEM] * len(operands),
        out_specs=[VMEM] * len(out_shape),
        out_shape=out_shape,
        input_output_aliases=aliases,
        scratch_shapes=[
            pltpu.VMEM((sh.tokens, w), BF16),
            pltpu.VMEM((sh.tokens, w), BF16),
            pltpu.VMEM((2 * w, sh.tokens), BF16),
        ],
        compiler_params=params(),
        cost_estimate=cost(24 * work * w, 12 * sh.tokens * sh.lanes * 2, work),
        name="forward_far" if closing else "forward_chunk",
    )(me, back, *operands)


def backward_scores(keys, qg, start, size):
    k_s, v_s = keys
    k = k_s[pl.ds(start, size), :]
    v = v_s[pl.ds(start, size), :]
    empty = jnp.zeros_like(k)
    left = jnp.concatenate([k, empty], axis=0)
    right = jnp.concatenate([empty, v], axis=0)
    both = nt(jnp.concatenate([left, right], axis=1), qg)
    return both[:size], both[size:]


def backward_tiles(sh, keys, kt_s, dkv_s, dq_s, qg, lse, dot, tiles, masked):
    places = [(block_rows(sh, block), blocks * sh.block) for block, blocks in tiles]
    scores = [backward_scores(keys, qg, start, size) for start, size in places]
    q, g = qg[:, : sh.width], qg[:, sh.width :]
    for i, ((start, size), (s, dp)) in enumerate(zip(places, scores)):
        rows = pl.ds(start, size)
        p = jnp.exp2(s * sh.powers - lse)
        if masked and i == 0:
            low = below_diagonal(sh, p[size - sh.block :], 0.0)
            p = low if size == sh.block else jnp.concatenate([p[: size - sh.block], low], axis=0)
        ds = (p * (dp - dot)).astype(BF16)
        dkv_s[0, rows, :] += nn(ds, q)
        dkv_s[1, rows, :] += nn(p.astype(BF16), g)
        dq_s[...] += nn(kt_s[:, rows], ds)


def backward_chunk(sh, me, back, qq, keys, distance, grads, lse, dots, dq, norm, order, held):
    w = sh.width
    opening, closing = norm is not None, distance == 0
    per = sh.rows // sh.block
    everyone = order == list(range(sh.parts))

    def kernel(me_ref, back_ref, *refs):
        refs = list(refs)

        def take(count):
            taken = refs[:count]
            del refs[:count]
            return taken

        qq_s, k_s, v_s, kt_s, lse_s = take(5)
        if opening:
            out_s, gain_ref, *sum_refs = take(2 + len(norm[0]))
        else:
            grad_s, dot_s, dq_in = take(3)
        (held_ref,) = take(1) if held is not None else (None,)
        (dkv_out,) = take(1)
        dq_out = take(len(order) if closing else 1)
        if opening:
            grad_s, dot_s = take(2)
        dkv_s, dq_own = refs
        dkv_s[...] = jnp.zeros_like(dkv_s) if held_ref is None else held_ref[...]

        def query_block(i):
            qb = i
            if not everyone:
                partner = functools.reduce(
                    lambda chosen, j: jnp.where(i // per == j, order[j], chosen),
                    range(len(order)),
                    order[0],
                )
                qb = jnp.bitwise_xor(me_ref[0], partner) * per + i % per
            dq_s = dq_own if closing else dq_out[0].at[qb]
            if opening:
                features = norm[2]
                token = functools.reduce(jnp.add, [ref[qb] for ref in sum_refs])
                sums = jnp.concatenate([token] * sh.group, axis=1)
                square = sums[0:1] / features + EPSILON
                inverse = lax.rsqrt(square)
                ratio = sums[1:2] / (features * square)
                again = (sums[3:4] - ratio * sums[2:3]) * inverse
                again = again / (features * square)
                plain = out_s[qb, :w, :]
                moved = out_s[qb, w:, :]
                first_grad = gain_ref[...] * (moved - plain * ratio) * inverse
                cot = ((first_grad - plain * again) * inverse).astype(BF16).astype(F32)
                dot_s[qb] = jnp.sum(cot * plain, axis=0, keepdims=True)
                grad_s[qb] = cot.T.astype(BF16)
                dq_s[...] = jnp.zeros((w, sh.lanes), F32)
            elif closing:
                dq_s[...] = dq_in[qb]

            top = sh.blocks if distance else qb + 1
            first = jnp.clip(qb - back_of(sh, me_ref, back_ref, qb) + distance * sh.blocks, 0, top)
            count = top - first

            @pl.when(count > 0)
            def _():
                qg = jnp.concatenate([qq_s[qb, :, :w], grad_s[qb]], axis=1)
                run = functools.partial(
                    backward_tiles, sh, (k_s, v_s), kt_s, dkv_s, dq_s, qg, lse_s[qb], dot_s[qb]
                )
                by_count(sh, first, count, run, closing)

            if closing:
                done = (dq_s[...] * sh.scale).T.reshape(sh.group, sh.block, w).astype(BF16)
                at = pl.ds(pl.multiple_of(i % per * sh.block, sh.block), sh.block)
                for j, out in enumerate(dq_out):

                    @pl.when(i // per == j)
                    def _(out=out):
                        out[:, at, :] = done

        each_block(len(order) * per, query_block)
        factor = 1.0 if closing else sh.scale
        dkv_out[0] = (dkv_s[0] * factor).astype(dkv_out.dtype)
        dkv_out[1] = dkv_s[1].astype(dkv_out.dtype)

    def array(*shape, dtype=F32):
        return jax.ShapeDtypeStruct(shape, dtype)

    operands = [qq, *keys, lse]
    if opening:
        operands += [grads, norm[1], *norm[0]]
    else:
        operands += [grads, dots, dq]
    aliases = {}
    if not opening and not closing:
        aliases = {1 + len(operands): 1}
    if held is not None:
        operands.append(held)
    out_shape = [array(2, sh.tokens, w, dtype=BF16 if opening else F32)]
    if closing:
        out_shape += [array(sh.group, sh.rows, w, dtype=BF16)] * len(order)
    else:
        out_shape.append(array(sh.blocks, w, sh.lanes))
    if opening:
        out_shape += [
            array(sh.blocks, sh.lanes, w, dtype=BF16),
            array(sh.blocks, 1, sh.lanes),
        ]
    work = sh.group * sh.tokens * len(order) * sh.rows // 2
    return pl.pallas_call(
        kernel,
        in_specs=[SMEM, SMEM] + [VMEM] * len(operands),
        out_specs=[VMEM] * len(out_shape),
        out_shape=out_shape,
        input_output_aliases=aliases,
        scratch_shapes=[
            pltpu.VMEM((2, sh.tokens, w), F32),
            pltpu.VMEM((w, sh.lanes), F32),
        ],
        compiler_params=params(),
        cost_estimate=cost(20 * work * w, 12 * len(order) * sh.rows * sh.lanes * 4, work),
        name="backward_chunk",
    )(me, back, *operands)


def combine(sh, me, carried, held):
    def kernel(me_ref, carried_ref, held_ref, *outs):
        for m, out in enumerate(outs):
            slot = pl.ds(slot_of(me_ref, m, sh.rows), sh.rows)
            for a, factor in ((0, sh.scale), (1, 1.0)):
                part = held_ref[a, slot, :] * factor
                out[a] = (carried_ref[a, slot, :].astype(F32) + part).astype(BF16)

    return pl.pallas_call(
        kernel,
        in_specs=[SMEM, VMEM, VMEM],
        out_specs=[VMEM] * sh.parts,
        out_shape=[jax.ShapeDtypeStruct((2, sh.rows, sh.width), BF16)] * sh.parts,
        compiler_params=params(),
        cost_estimate=cost(0, 1),
        name="combine",
    )(me, carried, held)


def exchanged(pieces):
    parts = len(pieces)
    return [pieces[0]] + [
        lax.ppermute(pieces[m], "part", [(i, i ^ m) for i in range(parts)])
        for m in range(1, parts)
    ]


def moved_on(value, steps):
    count = lax.axis_size("span")
    pairs = [(i, i + steps) for i in range(count) if 0 <= i + steps < count]
    return lax.ppermute(value, "span", pairs)


def summed_over_head(value):
    count = lax.axis_size("head")
    if count & (count - 1):
        return lax.psum(value, "head")
    step = 1
    while step < count:
        value = value + lax.ppermute(value, "head", [(i, i ^ step) for i in range(count)])
        step *= 2
    return value


def body(queries, keys, values, tangent_queries, tangent_keys, tangent_values, doc_start, out_gain):
    rows, query_heads, width = queries.shape
    key_heads = keys.shape[1]
    group = query_heads // key_heads
    parts = lax.axis_size("part")
    per = doc_start.shape[0]
    block = rows // per
    features = query_heads * width * lax.axis_size("head")
    hops = -(-DOC_DEVS // parts)
    sh = Shape(parts, group, rows, width, block)
    place = lax.axis_index("part")
    me = place.astype(jnp.int32).reshape(1)

    def flat(array):
        return array.reshape(-1, width)

    pieces = split_heads(
        [flat(a) for a in (keys, values, tangent_keys, tangent_values)], parts, 1, doc_start
    )
    q_rows, _ = lax.optimization_barrier(((flat(queries), flat(tangent_queries)), pieces[0]))
    q_pieces = split_heads(q_rows, parts, group)
    pieces = exchanged(pieces)
    late, q_pieces = lax.optimization_barrier((pieces, q_pieces))
    chunks = [pieces, [jnp.concatenate(late, axis=0) if parts > 1 else late[0]]]
    chunks[1] = [moved_on(chunks[1][0], 1)]
    for _ in range(hops - 1):
        chunks.append([moved_on(chunks[-1][0], 1)])
    q_parts = exchanged(q_pieces)
    back = jnp.concatenate([p[4 * rows : 4 * rows + per, 0] for p in pieces]).astype(jnp.int32)
    gain = lax.dynamic_index_in_dim(out_gain.reshape(key_heads, group, width), place, 0, False)
    gain_square = jnp.repeat((gain * gain).T, block, axis=1)

    state, spans = None, []
    for distance in range(hops):
        k, v, kt, acc, stat, *laid = forward_chunk(
            sh, me, back, [qq] if distance else q_parts, chunks[distance], distance, state
        )
        qq = laid[0] if laid else qq
        state = [acc, stat]
        spans.append((k, v, kt))
    k, v, kt, out, _, lse, sums = forward_chunk(
        sh, me, back, [qq], chunks[hops], hops, state, gain_square
    )
    spans.append((k, v, kt))
    sums = summed_over_head(sums)
    norm = (exchanged([sums] * parts), gain_square, features)

    everyone = list(range(parts))
    carried, dq, grads, dots = backward_chunk(
        sh, me, back, qq, spans[hops], hops, out, lse, None, None, norm, everyone, None
    )
    for distance in range(hops - 1, 0, -1):
        carried = moved_on(carried, -1)
        part, dq = backward_chunk(
            sh, me, back, qq, spans[distance], distance, grads, lse, dots, dq, None,
            everyone, None,
        )
        carried = (carried.astype(F32) + part).astype(BF16)
    carried = moved_on(carried, -1)
    held, dq_pieces = None, [None] * parts
    for order in ([parts - 1], list(range(parts - 2, -1, -1))):
        if order:
            held, *done = backward_chunk(
                sh, me, back, qq, spans[0], 0, grads, lse, dots, dq, None, order, held
            )
            for m, piece in zip(order, done):
                dq_pieces[m] = piece.reshape(1, group, rows, width)
    dq_pieces = exchanged(dq_pieces)
    dq_pieces[-1], held = lax.optimization_barrier((dq_pieces[-1], held))
    dkv_pieces = exchanged(combine(sh, me, carried, held))
    (product_queries,) = join_heads(dq_pieces, 1, group)
    dkv_pieces = [p.reshape(2, 1, rows, width) for p in dkv_pieces]
    product_keys, product_values = join_heads(dkv_pieces, 2, 1)
    return (
        product_queries.reshape(queries.shape),
        product_keys.reshape(keys.shape),
        product_values.reshape(keys.shape),
    )


def solution(mesh):
    def run(*arguments):
        count, heads = mesh.shape["ctx"], mesh.shape["head"]
        parts = arguments[1].shape[1] // heads
        split = Mesh(
            mesh.devices.reshape(count // parts, parts, heads), ("span", "part", "head")
        )
        ctx = ("span", "part")
        array = P(ctx, "head", None)
        return jax.shard_map(
            body,
            mesh=split,
            in_specs=(array,) * 6 + (P(ctx), P("head")),
            out_specs=(array,) * 3,
            check_vma=False,
        )(*arguments)

    return run
```

```python
import functools
import math

import jax
import jax.numpy as jnp
from jax import lax
from jax.experimental import pallas as pl
from jax.experimental.pallas import tpu as pltpu
from jax.sharding import Mesh, PartitionSpec as P

DOC_DEVS = 8
EPSILON = 1e-06
VMEM_BYTES = 18 * 1024 * 1024
NOTE_ROWS = 16
WIDE_VMEM_BYTES = 60 * 1024 * 1024
LOG2E = math.log2(math.e)
MASKED = -1e30
F32 = jnp.float32
BF16 = jnp.bfloat16
SMEM = pl.BlockSpec(memory_space=pltpu.SMEM)
VMEM = pl.BlockSpec(memory_space=pltpu.VMEM)


def params(size=VMEM_BYTES):
    return pltpu.CompilerParams(vmem_limit_bytes=size)


def cost(flops, moved, powers=0):
    return pl.CostEstimate(flops=int(flops), bytes_accessed=int(moved), transcendentals=int(powers))


def nn(a, b):
    return lax.dot_general(a, b, (((1,), (0,)), ((), ())), preferred_element_type=F32)


def nt(a, b):
    return lax.dot_general(a, b, (((1,), (1,)), ((), ())), preferred_element_type=F32)


def split_heads(arrays, parts, per_part, notes=None):
    count = len(arrays)
    total, width = arrays[0].shape
    heads = parts * per_part
    rows = total // heads
    length = count * per_part * rows
    extra = 0 if notes is None else NOTE_ROWS
    scalars = [] if notes is None else [notes]

    def kernel(*refs):
        ins = list(refs[: len(scalars) + count])
        outs, (held, wide, sems) = refs[len(scalars) + count : -3], refs[-3:]
        mine = lax.axis_index("part")
        if extra:
            note_ref = ins.pop(0)
        copies = [pltpu.make_async_copy(ins[a], held.at[a], sems.at[a]) for a in range(count)]
        for copy in copies:
            copy.start()
        if extra:
            first = (lax.axis_index("span") * parts + mine) * notes.shape[0]
            line = lax.broadcasted_iota(jnp.int32, (extra, width), 0)
            lines = jnp.zeros((extra, width), jnp.int32)
            for i in range(notes.shape[0]):
                lines = jnp.where(line == i, first + i - note_ref[i], lines)
            for out in outs:
                out[length:, :] = lines.astype(F32).astype(BF16)
        for a in range(count):
            copies[a].wait()
            wide[...] = held[a].astype(F32)
            for m in range(parts):
                for r in range(per_part):
                    head = jnp.bitwise_xor(mine, m) * per_part + r
                    at = (a * per_part + r) * rows
                    outs[m][at : at + rows, :] = wide[pl.ds(head, rows, stride=heads), :].astype(BF16)

    return pl.pallas_call(
        kernel,
        in_specs=[SMEM] * len(scalars) + [pl.BlockSpec(memory_space=pltpu.HBM)] * count,
        out_specs=[pl.BlockSpec(memory_space=pltpu.VMEM)] * parts,
        out_shape=[jax.ShapeDtypeStruct((length + extra, width), BF16)] * parts,
        scratch_shapes=[
            pltpu.VMEM((count, total, width), BF16),
            pltpu.VMEM((total, width), F32),
            pltpu.SemaphoreType.DMA((count,)),
        ],
        compiler_params=params(VMEM_BYTES if notes is None else WIDE_VMEM_BYTES),
        cost_estimate=cost(0, 4 * count * total * width),
        name="split_heads",
    )(*scalars, *arrays)


def join_heads(pieces, count, per_part):
    parts = len(pieces)
    rows, width = pieces[0].shape[-2:]
    heads = parts * per_part

    steps = 4
    cut = rows // steps

    def kernel(*refs):
        ins, outs = refs[:parts], refs[parts:]
        mine = lax.axis_index("part")
        for a in range(count):
            for m in range(parts):
                for r in range(per_part):
                    head = jnp.bitwise_xor(mine, m) * per_part + r
                    outs[a][pl.ds(head, cut, stride=heads), :] = ins[m][a, r].astype(F32)

    return pl.pallas_call(
        kernel,
        grid=(steps,),
        in_specs=[pl.BlockSpec((count, per_part, cut, width), lambda i: (0, 0, i, 0))] * parts,
        out_specs=[pl.BlockSpec((cut * heads, width), lambda i: (i, 0))] * count,
        out_shape=[jax.ShapeDtypeStruct((rows * heads, width), F32)] * count,
        compiler_params=params(),
        cost_estimate=cost(0, 6 * count * rows * heads * width),
        name="join_heads",
    )(*pieces)


def slot_of(me_ref, m, rows):
    return pl.multiple_of(jnp.bitwise_xor(me_ref[0], m) * rows, rows)


class Shape:
    def __init__(self, parts, group, rows, width, block):
        self.parts, self.group, self.rows, self.width, self.block = parts, group, rows, width, block
        self.tokens = parts * rows
        self.blocks = self.tokens // block
        self.lanes = group * block
        self.scale = width**-0.5
        self.powers = self.scale * LOG2E


def diagonal(sh):
    shape = (sh.block, sh.block)
    key = lax.broadcasted_iota(jnp.int32, shape, 0)
    query = lax.broadcasted_iota(jnp.int32, shape, 1)
    return key <= query


def below_diagonal(sh, value, other):
    allowed = diagonal(sh)
    cut = [value[:, g * sh.block : (g + 1) * sh.block] for g in range(sh.group)]
    return jnp.concatenate([jnp.where(allowed, part, other) for part in cut], axis=1)


def scores_tile(keys, qq, start, size):
    k_s, tk_s = keys
    k = k_s[pl.ds(start, size), :]
    tk = tk_s[pl.ds(start, size), :]
    left = jnp.concatenate([k, tk], axis=0)
    right = jnp.concatenate([jnp.zeros_like(k), k], axis=0)
    both = nt(jnp.concatenate([left, right], axis=1), qq)
    return both[:size], both[size:]


def mix_tile(sh, vt_s, acc, start, size, scores, state, masked):
    w = sh.width
    s, d = scores[0] * sh.powers, scores[1]
    if masked:
        low = below_diagonal(sh, s[size - sh.block :], MASKED)
        s = low if size == sh.block else jnp.concatenate([s[: size - sh.block], low], axis=0)
    most = jnp.max(s, axis=0, keepdims=True)
    if state is not None:
        most = jnp.maximum(most, state[0])
        decay = jnp.exp2(state[0] - most)
    e = jnp.exp2(s - most)
    mix = e * d
    total = jnp.sum(e, axis=0, keepdims=True)
    cross = jnp.sum(mix, axis=0, keepdims=True)
    vt = vt_s[:, pl.ds(start, size)]
    plain = nn(vt, e.astype(BF16))
    moving = nn(vt[:w], mix.astype(BF16)) * sh.scale
    if state is None:
        acc[:w, :] = plain[:w]
        acc[w:, :] = plain[w:] + moving
        return most, total, cross
    acc[:w, :] = acc[:w, :] * decay + plain[:w]
    acc[w:, :] = acc[w:, :] * decay + (plain[w:] + moving)
    return most, state[1] * decay + total, state[2] * decay + cross


def block_rows(sh, block):
    return pl.multiple_of(block * sh.block, sh.block)


def load_state(stat):
    return tuple(stat[r : r + 1, :] for r in range(3))


def store_state(stat, state):
    for r in range(3):
        stat[r : r + 1, :] = state[r]


def forward_tiles(sh, keys, vt_s, acc, stat, qq, tiles, masked):
    places = [(block_rows(sh, block), blocks * sh.block) for block, blocks in tiles]
    scores = [scores_tile(keys, qq, start, size) for start, size in places]
    state = None if masked else load_state(stat)
    for i, ((start, size), both) in enumerate(zip(places, scores)):
        state = mix_tile(sh, vt_s, acc, start, size, both, state, masked and i == 0)
    store_state(stat, state)


def tiles_up(low, blocks):
    odd = blocks % 2
    return [(low, 1)] * odd + [(low + odd + 2 * i, 2) for i in range(blocks // 2)]


def tiles_down(top, blocks):
    first = 2 - blocks % 2
    return [(top - first, first)] + [
        (top - first - 2 * i, 2) for i in range(1, (blocks - first) // 2 + 1)
    ]


def by_count(sh, low, count, run, masked):
    head = jnp.where(count <= 6, count, 3 + lax.rem(jnp.maximum(count - 7, 0), 4))
    fours = (count - head) // 4
    for blocks in range(1, min(6, sh.blocks) + 1):

        @pl.when(head == blocks)
        def _(blocks=blocks):
            if masked:
                run(tiles_down(low + count, blocks), True)
            else:
                run(tiles_up(low, blocks), False)

    def step(i, carry):
        run(tiles_up(low + (0 if masked else head) + 4 * i, 4), None)
        return carry

    if sh.blocks > 6:
        lax.fori_loop(0, fours, step, 0)


def lay_chunk(sh, me_ref, sources, targets):
    for m, (ref, base) in enumerate(sources):
        slot = pl.ds(slot_of(me_ref, m, sh.rows), sh.rows)
        for i, target in enumerate(targets):
            at = base + i * sh.rows
            target[slot, :] = ref[at : at + sh.rows, :]


def lay_queries(sh, me_ref, pieces, qq):
    per = sh.rows // sh.block
    for m, ref in enumerate(pieces):
        for i in range(2):
            for g in range(sh.group):
                for r in range(per):
                    block = jnp.bitwise_xor(me_ref[0], m) * per + r
                    at = (i * sh.group + g) * sh.rows + r * sh.block
                    qq[
                        block,
                        g * sh.block : (g + 1) * sh.block,
                        i * sh.width : (i + 1) * sh.width,
                    ] = ref[at : at + sh.block, :]


def transposed(x):
    return x.astype(F32).T.astype(BF16)


def located(sh, refs):
    length = refs[0].shape[0]
    return [(ref, at) for ref in refs for at in range(0, ref.shape[0], length)]


def back_of(sh, me_ref, back_ref, qb):
    per = sh.rows // sh.block
    return back_ref[jnp.bitwise_xor(me_ref[0], qb // per) * per + qb % per]


def each_block(count, run):
    def step(i, carry):
        run(i)
        return carry

    lax.fori_loop(0, count, step, 0)


def forward_chunk(sh, me, back, queries, chunk, distance, state, gain_square=None):
    w = sh.width
    kv = chunk
    opening, closing = state is None, gain_square is not None

    def kernel(me_ref, back_ref, *refs):
        refs = list(refs)

        def take(count):
            taken = refs[:count]
            del refs[:count]
            return taken

        q_in = take(len(queries))
        kv_in = take(len(kv))
        if not opening:
            take(2)
        if closing:
            (gain_ref,) = take(1)
        k_s, v_s, kt_s, accs, stats = take(5)
        if opening:
            (qq_s,) = take(1)
            lay_queries(sh, me_ref, q_in, qq_s)
        else:
            (qq_s,) = q_in
        if closing:
            lse, sums = take(2)
        tk_s, tv_s, vt_s = refs
        lay_chunk(sh, me_ref, located(sh, kv_in), (k_s, v_s, tk_s, tv_s))
        kt_s[...] = transposed(k_s[...])
        vt_s[:w, :] = transposed(v_s[...])
        vt_s[w:, :] = transposed(tv_s[...])

        def query_block(qb):
            acc, stat = accs.at[qb], stats.at[qb]
            top = sh.blocks if distance else qb + 1
            first = jnp.clip(qb - back_of(sh, me_ref, back_ref, qb) + distance * sh.blocks, 0, top)
            count = top - first

            @pl.when(count > 0)
            def _():
                run = functools.partial(
                    forward_tiles, sh, (k_s, tk_s), vt_s, acc, stat, qq_s[qb]
                )
                by_count(sh, first, count, run, opening)

            if closing:
                most, total, cross = load_state(stat)
                inverse = 1.0 / total
                plain = acc[:w, :] * inverse
                moved = acc[w:, :] * inverse - (cross * inverse * sh.scale) * plain
                acc[:w, :] = plain
                acc[w:, :] = moved
                lse[qb] = most + jnp.log2(total)
                square = plain * plain
                product = plain * moved
                gain = gain_ref[...]
                for r, value in enumerate((square, product, gain * square, gain * product)):
                    line = jnp.sum(value, axis=0, keepdims=True)
                    pieces = [line[:, g * sh.block : (g + 1) * sh.block] for g in range(sh.group)]
                    sums[qb, r : r + 1, :] = functools.reduce(jnp.add, pieces)

        each_block(sh.blocks, query_block)

    def array(*shape, dtype=F32):
        return jax.ShapeDtypeStruct(shape, dtype)

    out_shape = [
        array(sh.tokens, w, dtype=BF16),
        array(sh.tokens, w, dtype=BF16),
        array(w, sh.tokens, dtype=BF16),
        array(sh.blocks, 2 * w, sh.lanes),
        array(sh.blocks, 8, sh.lanes),
    ]
    if opening:
        out_shape.append(array(sh.blocks, sh.lanes, 2 * w, dtype=BF16))
    if closing:
        out_shape += [array(sh.blocks, 1, sh.lanes), array(sh.blocks, 4, sh.block)]
    operands = [*queries, *kv]
    aliases = {}
    if not opening:
        aliases = {2 + len(operands): 3, 3 + len(operands): 4}
        operands += state
    if closing:
        operands.append(gain_square)
    work = sh.group * sh.tokens * sh.tokens // 2
    return pl.pallas_call(
        kernel,
        in_specs=[SMEM, SMEM] + [VMEM] * len(operands),
        out_specs=[VMEM] * len(out_shape),
        out_shape=out_shape,
        input_output_aliases=aliases,
        scratch_shapes=[
            pltpu.VMEM((sh.tokens, w), BF16),
            pltpu.VMEM((sh.tokens, w), BF16),
            pltpu.VMEM((2 * w, sh.tokens), BF16),
        ],
        compiler_params=params(),
        cost_estimate=cost(24 * work * w, 12 * sh.tokens * sh.lanes * 2, work),
        name="forward_far" if closing else "forward_chunk",
    )(me, back, *operands)


def backward_scores(keys, qg, start, size):
    k_s, v_s = keys
    k = k_s[pl.ds(start, size), :]
    v = v_s[pl.ds(start, size), :]
    empty = jnp.zeros_like(k)
    left = jnp.concatenate([k, empty], axis=0)
    right = jnp.concatenate([empty, v], axis=0)
    both = nt(jnp.concatenate([left, right], axis=1), qg)
    return both[:size], both[size:]


def backward_tiles(sh, keys, kt_s, dkv_s, dq_s, qg, lse, dot, tiles, masked):
    places = [(block_rows(sh, block), blocks * sh.block) for block, blocks in tiles]
    scores = [backward_scores(keys, qg, start, size) for start, size in places]
    q, g = qg[:, : sh.width], qg[:, sh.width :]
    for i, ((start, size), (s, dp)) in enumerate(zip(places, scores)):
        rows = pl.ds(start, size)
        p = jnp.exp2(s * sh.powers - lse)
        if masked and i == 0:
            low = below_diagonal(sh, p[size - sh.block :], 0.0)
            p = low if size == sh.block else jnp.concatenate([p[: size - sh.block], low], axis=0)
        ds = (p * (dp - dot)).astype(BF16)
        dkv_s[0, rows, :] += nn(ds, q)
        dkv_s[1, rows, :] += nn(p.astype(BF16), g)
        dq_s[...] += nn(kt_s[:, rows], ds)


def backward_chunk(sh, me, back, qq, keys, distance, grads, lse, dots, dq, norm, order, held):
    w = sh.width
    opening, closing = norm is not None, distance == 0
    per = sh.rows // sh.block
    everyone = order == list(range(sh.parts))

    def kernel(me_ref, back_ref, *refs):
        refs = list(refs)

        def take(count):
            taken = refs[:count]
            del refs[:count]
            return taken

        qq_s, k_s, v_s, kt_s, lse_s = take(5)
        if opening:
            out_s, gain_ref, *sum_refs = take(2 + len(norm[0]))
        else:
            grad_s, dot_s, dq_in = take(3)
        (held_ref,) = take(1) if held is not None else (None,)
        (dkv_out,) = take(1)
        dq_out = take(len(order) if closing else 1)
        if opening:
            grad_s, dot_s = take(2)
        dkv_s, dq_own = refs
        dkv_s[...] = jnp.zeros_like(dkv_s) if held_ref is None else held_ref[...]

        def query_block(i):
            qb = i
            if not everyone:
                partner = functools.reduce(
                    lambda chosen, j: jnp.where(i // per == j, order[j], chosen),
                    range(len(order)),
                    order[0],
                )
                qb = jnp.bitwise_xor(me_ref[0], partner) * per + i % per
            dq_s = dq_own if closing else dq_out[0].at[qb]
            if opening:
                features = norm[2]
                token = functools.reduce(jnp.add, [ref[qb] for ref in sum_refs])
                sums = jnp.concatenate([token] * sh.group, axis=1)
                square = sums[0:1] / features + EPSILON
                inverse = lax.rsqrt(square)
                ratio = sums[1:2] / (features * square)
                again = (sums[3:4] - ratio * sums[2:3]) * inverse
                again = again / (features * square)
                plain = out_s[qb, :w, :]
                moved = out_s[qb, w:, :]
                first_grad = gain_ref[...] * (moved - plain * ratio) * inverse
                cot = ((first_grad - plain * again) * inverse).astype(BF16).astype(F32)
                dot_s[qb] = jnp.sum(cot * plain, axis=0, keepdims=True)
                grad_s[qb] = cot.T.astype(BF16)
                dq_s[...] = jnp.zeros((w, sh.lanes), F32)
            elif closing:
                dq_s[...] = dq_in[qb]

            top = sh.blocks if distance else qb + 1
            first = jnp.clip(qb - back_of(sh, me_ref, back_ref, qb) + distance * sh.blocks, 0, top)
            count = top - first

            @pl.when(count > 0)
            def _():
                qg = jnp.concatenate([qq_s[qb, :, :w], grad_s[qb]], axis=1)
                run = functools.partial(
                    backward_tiles, sh, (k_s, v_s), kt_s, dkv_s, dq_s, qg, lse_s[qb], dot_s[qb]
                )
                by_count(sh, first, count, run, closing)

            if closing:
                done = (dq_s[...] * sh.scale).T.reshape(sh.group, sh.block, w).astype(BF16)
                at = pl.ds(pl.multiple_of(i % per * sh.block, sh.block), sh.block)
                for j, out in enumerate(dq_out):

                    @pl.when(i // per == j)
                    def _(out=out):
                        out[:, at, :] = done

        each_block(len(order) * per, query_block)
        factor = 1.0 if closing else sh.scale
        dkv_out[0] = (dkv_s[0] * factor).astype(dkv_out.dtype)
        dkv_out[1] = dkv_s[1].astype(dkv_out.dtype)

    def array(*shape, dtype=F32):
        return jax.ShapeDtypeStruct(shape, dtype)

    operands = [qq, *keys, lse]
    if opening:
        operands += [grads, norm[1], *norm[0]]
    else:
        operands += [grads, dots, dq]
    aliases = {}
    if not opening and not closing:
        aliases = {1 + len(operands): 1}
    if held is not None:
        operands.append(held)
    out_shape = [array(2, sh.tokens, w, dtype=BF16 if opening else F32)]
    if closing:
        out_shape += [array(sh.group, sh.rows, w, dtype=BF16)] * len(order)
    else:
        out_shape.append(array(sh.blocks, w, sh.lanes))
    if opening:
        out_shape += [
            array(sh.blocks, sh.lanes, w, dtype=BF16),
            array(sh.blocks, 1, sh.lanes),
        ]
    work = sh.group * sh.tokens * len(order) * sh.rows // 2
    return pl.pallas_call(
        kernel,
        in_specs=[SMEM, SMEM] + [VMEM] * len(operands),
        out_specs=[VMEM] * len(out_shape),
        out_shape=out_shape,
        input_output_aliases=aliases,
        scratch_shapes=[
            pltpu.VMEM((2, sh.tokens, w), F32),
            pltpu.VMEM((w, sh.lanes), F32),
        ],
        compiler_params=params(),
        cost_estimate=cost(20 * work * w, 12 * len(order) * sh.rows * sh.lanes * 4, work),
        name="backward_chunk",
    )(me, back, *operands)


def combine(sh, me, carried, held):
    def kernel(me_ref, carried_ref, held_ref, *outs):
        for m, out in enumerate(outs):
            slot = pl.ds(slot_of(me_ref, m, sh.rows), sh.rows)
            for a, factor in ((0, sh.scale), (1, 1.0)):
                part = held_ref[a, slot, :] * factor
                out[a] = (carried_ref[a, slot, :].astype(F32) + part).astype(BF16)

    return pl.pallas_call(
        kernel,
        in_specs=[SMEM, VMEM, VMEM],
        out_specs=[VMEM] * sh.parts,
        out_shape=[jax.ShapeDtypeStruct((2, sh.rows, sh.width), BF16)] * sh.parts,
        compiler_params=params(),
        cost_estimate=cost(0, 1),
        name="combine",
    )(me, carried, held)


def exchanged(pieces):
    parts = len(pieces)
    return [pieces[0]] + [
        lax.ppermute(pieces[m], "part", [(i, i ^ m) for i in range(parts)])
        for m in range(1, parts)
    ]


def moved_on(value, steps):
    count = lax.axis_size("span")
    pairs = [(i, i + steps) for i in range(count) if 0 <= i + steps < count]
    return lax.ppermute(value, "span", pairs)


def summed_over_head(value):
    count = lax.axis_size("head")
    if count & (count - 1):
        return lax.psum(value, "head")
    step = 1
    while step < count:
        value = value + lax.ppermute(value, "head", [(i, i ^ step) for i in range(count)])
        step *= 2
    return value


def body(queries, keys, values, tangent_queries, tangent_keys, tangent_values, doc_start, out_gain):
    rows, query_heads, width = queries.shape
    key_heads = keys.shape[1]
    group = query_heads // key_heads
    parts = lax.axis_size("part")
    per = doc_start.shape[0]
    block = rows // per
    features = query_heads * width * lax.axis_size("head")
    hops = -(-DOC_DEVS // parts)
    sh = Shape(parts, group, rows, width, block)
    place = lax.axis_index("part")
    me = place.astype(jnp.int32).reshape(1)

    def flat(array):
        return array.reshape(-1, width)

    pieces = split_heads(
        [flat(a) for a in (keys, values, tangent_keys, tangent_values)], parts, 1, doc_start
    )
    q_rows, _ = lax.optimization_barrier(((flat(queries), flat(tangent_queries)), pieces[0]))
    q_pieces = split_heads(q_rows, parts, group)
    own = moved_on(pieces[0], 1)
    pieces = exchanged(pieces)
    chunks = [pieces]
    if parts > 1:
        own, q_pieces = lax.optimization_barrier((own, q_pieces))
        owns = [own]
        for _ in range(hops - 1):
            owns.append(moved_on(owns[-1], 1))
        late, owns = lax.optimization_barrier((pieces[1:], owns))
        rest = jnp.concatenate(late, axis=0)
        for own in owns:
            rest = moved_on(rest, 1)
            chunks.append([own, rest])
    else:
        for _ in range(hops):
            chunks.append([own])
            own = moved_on(own, 1)
    q_parts = exchanged(q_pieces)
    back = jnp.concatenate([p[4 * rows : 4 * rows + per, 0] for p in pieces]).astype(jnp.int32)
    gain = lax.dynamic_index_in_dim(out_gain.reshape(key_heads, group, width), place, 0, False)
    gain_square = jnp.repeat((gain * gain).T, block, axis=1)

    state, spans = None, []
    for distance in range(hops):
        k, v, kt, acc, stat, *laid = forward_chunk(
            sh, me, back, [qq] if distance else q_parts, chunks[distance], distance, state
        )
        qq = laid[0] if laid else qq
        state = [acc, stat]
        spans.append((k, v, kt))
    k, v, kt, out, _, lse, sums = forward_chunk(
        sh, me, back, [qq], chunks[hops], hops, state, gain_square
    )
    spans.append((k, v, kt))
    sums = summed_over_head(sums)
    norm = (exchanged([sums] * parts), gain_square, features)

    everyone = list(range(parts))
    half = parts // 2

    def closing(dq, order, held):
        return backward_chunk(
            sh, me, back, qq, spans[0], 0, grads, lse, dots, dq, None, order, held
        )

    carried, dq, grads, dots = backward_chunk(
        sh, me, back, qq, spans[hops], hops, out, lse, None, None, norm, everyone, None
    )
    for distance in range(hops - 1, 0, -1):
        arriving = moved_on(carried, -1)
        part, dq = backward_chunk(
            sh, me, back, qq, spans[distance], distance, grads, lse, dots, dq, None,
            everyone, None,
        )
        if distance == 1:
            held, *done = closing(dq, everyone[half:][::-1], None)
            arriving, held = lax.optimization_barrier((arriving, held))
        carried = (arriving.astype(F32) + part).astype(BF16)
    carried = moved_on(carried, -1)
    dq_pieces = done[::-1]
    if half:
        held, *done = closing(dq, everyone[:half][::-1], held)
        dq_pieces = done[::-1] + dq_pieces
    dq_pieces = [piece.reshape(1, group, rows, width) for piece in dq_pieces]
    dq_pieces = exchanged(dq_pieces)
    dq_pieces[half:], held = lax.optimization_barrier((dq_pieces[half:], held))
    dkv_pieces = exchanged(combine(sh, me, carried, held))
    (product_queries,) = join_heads(dq_pieces, 1, group)
    dkv_pieces = [p.reshape(2, 1, rows, width) for p in dkv_pieces]
    product_keys, product_values = join_heads(dkv_pieces, 2, 1)
    return (
        product_queries.reshape(queries.shape),
        product_keys.reshape(keys.shape),
        product_values.reshape(keys.shape),
    )


def solution(mesh):
    def run(*arguments):
        count, heads = mesh.shape["ctx"], mesh.shape["head"]
        parts = arguments[1].shape[1] // heads
        split = Mesh(
            mesh.devices.reshape(count // parts, parts, heads), ("span", "part", "head")
        )
        ctx = ("span", "part")
        array = P(ctx, "head", None)
        return jax.shard_map(
            body,
            mesh=split,
            in_specs=(array,) * 6 + (P(ctx), P("head")),
            out_specs=(array,) * 3,
            check_vma=False,
        )(*arguments)

    return run
```

```python
import functools
import math

import jax
import jax.numpy as jnp
from jax import lax
from jax.experimental import pallas as pl
from jax.experimental.pallas import tpu as pltpu
from jax.sharding import Mesh, PartitionSpec as P

DOC_DEVS = 8
EPSILON = 1e-06
VMEM_BYTES = 18 * 1024 * 1024
NOTE_ROWS = 16
WIDE_VMEM_BYTES = 60 * 1024 * 1024
LOG2E = math.log2(math.e)
MASKED = -1e30
F32 = jnp.float32
BF16 = jnp.bfloat16
SMEM = pl.BlockSpec(memory_space=pltpu.SMEM)
VMEM = pl.BlockSpec(memory_space=pltpu.VMEM)


def params(size=VMEM_BYTES):
    return pltpu.CompilerParams(vmem_limit_bytes=size)


def cost(flops, moved, powers=0):
    return pl.CostEstimate(flops=int(flops), bytes_accessed=int(moved), transcendentals=int(powers))


def nn(a, b):
    return lax.dot_general(a, b, (((1,), (0,)), ((), ())), preferred_element_type=F32)


def nt(a, b):
    return lax.dot_general(a, b, (((1,), (1,)), ((), ())), preferred_element_type=F32)


def split_heads(arrays, parts, per_part, notes=None):
    count = len(arrays)
    total, width = arrays[0].shape
    heads = parts * per_part
    rows = total // heads
    length = count * per_part * rows
    extra = 0 if notes is None else NOTE_ROWS
    scalars = [] if notes is None else [notes]

    def kernel(*refs):
        ins = list(refs[: len(scalars) + count])
        outs, (held, wide, sems) = refs[len(scalars) + count : -3], refs[-3:]
        mine = lax.axis_index("part")
        if extra:
            note_ref = ins.pop(0)
        copies = [pltpu.make_async_copy(ins[a], held.at[a], sems.at[a]) for a in range(count)]
        for copy in copies:
            copy.start()
        if extra:
            first = (lax.axis_index("span") * parts + mine) * notes.shape[0]
            line = lax.broadcasted_iota(jnp.int32, (extra, width), 0)
            lines = jnp.zeros((extra, width), jnp.int32)
            for i in range(notes.shape[0]):
                lines = jnp.where(line == i, first + i - note_ref[i], lines)
            for out in outs:
                out[length:, :] = lines.astype(F32).astype(BF16)
        for a in range(count):
            copies[a].wait()
            wide[...] = held[a].astype(F32)
            for m in range(parts):
                for r in range(per_part):
                    head = jnp.bitwise_xor(mine, m) * per_part + r
                    at = (a * per_part + r) * rows
                    outs[m][at : at + rows, :] = wide[pl.ds(head, rows, stride=heads), :].astype(BF16)

    return pl.pallas_call(
        kernel,
        in_specs=[SMEM] * len(scalars) + [pl.BlockSpec(memory_space=pltpu.HBM)] * count,
        out_specs=[pl.BlockSpec(memory_space=pltpu.VMEM)] * parts,
        out_shape=[jax.ShapeDtypeStruct((length + extra, width), BF16)] * parts,
        scratch_shapes=[
            pltpu.VMEM((count, total, width), BF16),
            pltpu.VMEM((total, width), F32),
            pltpu.SemaphoreType.DMA((count,)),
        ],
        compiler_params=params(VMEM_BYTES if notes is None else WIDE_VMEM_BYTES),
        cost_estimate=cost(0, 4 * count * total * width),
        name="split_heads",
    )(*scalars, *arrays)


def join_heads(pieces, count, per_part):
    parts = len(pieces)
    rows, width = pieces[0].shape[-2:]
    heads = parts * per_part

    steps = 4
    cut = rows // steps

    def kernel(*refs):
        ins, outs = refs[:parts], refs[parts:]
        mine = lax.axis_index("part")
        for a in range(count):
            for m in range(parts):
                for r in range(per_part):
                    head = jnp.bitwise_xor(mine, m) * per_part + r
                    outs[a][pl.ds(head, cut, stride=heads), :] = ins[m][a, r].astype(F32)

    return pl.pallas_call(
        kernel,
        grid=(steps,),
        in_specs=[pl.BlockSpec((count, per_part, cut, width), lambda i: (0, 0, i, 0))] * parts,
        out_specs=[pl.BlockSpec((cut * heads, width), lambda i: (i, 0))] * count,
        out_shape=[jax.ShapeDtypeStruct((rows * heads, width), F32)] * count,
        compiler_params=params(),
        cost_estimate=cost(0, 6 * count * rows * heads * width),
        name="join_heads",
    )(*pieces)


def slot_of(me_ref, m, rows):
    return pl.multiple_of(jnp.bitwise_xor(me_ref[0], m) * rows, rows)


class Shape:
    def __init__(self, parts, group, rows, width, block):
        self.parts, self.group, self.rows, self.width, self.block = parts, group, rows, width, block
        self.tokens = parts * rows
        self.blocks = self.tokens // block
        self.lanes = group * block
        self.scale = width**-0.5
        self.powers = self.scale * LOG2E


def diagonal(sh):
    shape = (sh.block, sh.block)
    key = lax.broadcasted_iota(jnp.int32, shape, 0)
    query = lax.broadcasted_iota(jnp.int32, shape, 1)
    return key <= query


def below_diagonal(sh, value, other):
    allowed = diagonal(sh)
    cut = [value[:, g * sh.block : (g + 1) * sh.block] for g in range(sh.group)]
    return jnp.concatenate([jnp.where(allowed, part, other) for part in cut], axis=1)


def scores_tile(keys, qq, start, size):
    k_s, tk_s = keys
    k = k_s[pl.ds(start, size), :]
    tk = tk_s[pl.ds(start, size), :]
    left = jnp.concatenate([k, tk], axis=0)
    right = jnp.concatenate([jnp.zeros_like(k), k], axis=0)
    both = nt(jnp.concatenate([left, right], axis=1), qq)
    return both[:size], both[size:]


def mix_tile(sh, vt_s, acc, start, size, scores, state, masked):
    w = sh.width
    s, d = scores[0] * sh.powers, scores[1]
    if masked:
        low = below_diagonal(sh, s[size - sh.block :], MASKED)
        s = low if size == sh.block else jnp.concatenate([s[: size - sh.block], low], axis=0)
    most = jnp.max(s, axis=0, keepdims=True)
    if state is not None:
        most = jnp.maximum(most, state[0])
        decay = jnp.exp2(state[0] - most)
    e = jnp.exp2(s - most)
    mix = e * d
    total = jnp.sum(e, axis=0, keepdims=True)
    cross = jnp.sum(mix, axis=0, keepdims=True)
    vt = vt_s[:, pl.ds(start, size)]
    plain = nn(vt, e.astype(BF16))
    moving = nn(vt[:w], mix.astype(BF16)) * sh.scale
    if state is None:
        acc[:w, :] = plain[:w]
        acc[w:, :] = plain[w:] + moving
        return most, total, cross
    acc[:w, :] = acc[:w, :] * decay + plain[:w]
    acc[w:, :] = acc[w:, :] * decay + (plain[w:] + moving)
    return most, state[1] * decay + total, state[2] * decay + cross


def block_rows(sh, block):
    return pl.multiple_of(block * sh.block, sh.block)


def load_state(stat):
    return tuple(stat[r : r + 1, :] for r in range(3))


def store_state(stat, state):
    for r in range(3):
        stat[r : r + 1, :] = state[r]


def forward_tiles(sh, keys, vt_s, acc, stat, qq, tiles, masked):
    places = [(block_rows(sh, block), blocks * sh.block) for block, blocks in tiles]
    scores = [scores_tile(keys, qq, start, size) for start, size in places]
    state = None if masked else load_state(stat)
    for i, ((start, size), both) in enumerate(zip(places, scores)):
        state = mix_tile(sh, vt_s, acc, start, size, both, state, masked and i == 0)
    store_state(stat, state)


def tiles_up(low, blocks):
    odd = blocks % 2
    return [(low, 1)] * odd + [(low + odd + 2 * i, 2) for i in range(blocks // 2)]


def tiles_down(top, blocks):
    first = 2 - blocks % 2
    return [(top - first, first)] + [
        (top - first - 2 * i, 2) for i in range(1, (blocks - first) // 2 + 1)
    ]


def by_count(sh, low, count, run, masked):
    head = jnp.where(count <= 6, count, 3 + lax.rem(jnp.maximum(count - 7, 0), 4))
    fours = (count - head) // 4
    for blocks in range(1, min(6, sh.blocks) + 1):

        @pl.when(head == blocks)
        def _(blocks=blocks):
            if masked:
                run(tiles_down(low + count, blocks), True)
            else:
                run(tiles_up(low, blocks), False)

    def step(i, carry):
        run(tiles_up(low + (0 if masked else head) + 4 * i, 4), None)
        return carry

    if sh.blocks > 6:
        lax.fori_loop(0, fours, step, 0)


def lay_chunk(sh, me_ref, sources, targets):
    for m, (ref, base) in enumerate(sources):
        slot = pl.ds(slot_of(me_ref, m, sh.rows), sh.rows)
        for i, target in enumerate(targets):
            at = base + i * sh.rows
            target[slot, :] = ref[at : at + sh.rows, :]


def lay_queries(sh, me_ref, pieces, qq):
    per = sh.rows // sh.block
    for m, ref in enumerate(pieces):
        for i in range(2):
            for g in range(sh.group):
                for r in range(per):
                    block = jnp.bitwise_xor(me_ref[0], m) * per + r
                    at = (i * sh.group + g) * sh.rows + r * sh.block
                    qq[
                        block,
                        g * sh.block : (g + 1) * sh.block,
                        i * sh.width : (i + 1) * sh.width,
                    ] = ref[at : at + sh.block, :]


def transposed(x):
    return x.astype(F32).T.astype(BF16)


def located(sh, refs):
    length = refs[0].shape[0]
    return [(ref, at) for ref in refs for at in range(0, ref.shape[0], length)]


def back_of(sh, me_ref, back_ref, qb):
    per = sh.rows // sh.block
    return back_ref[jnp.bitwise_xor(me_ref[0], qb // per) * per + qb % per]


def each_block(count, run):
    def step(i, carry):
        run(i)
        return carry

    lax.fori_loop(0, count, step, 0)


def forward_chunk(sh, me, back, queries, chunk, distance, state, gain_square=None):
    w = sh.width
    kv = chunk
    opening, closing = state is None, gain_square is not None

    def kernel(me_ref, back_ref, *refs):
        refs = list(refs)

        def take(count):
            taken = refs[:count]
            del refs[:count]
            return taken

        q_in = take(len(queries))
        kv_in = take(len(kv))
        if not opening:
            take(2)
        if closing:
            (gain_ref,) = take(1)
        k_s, v_s, kt_s, accs, stats = take(5)
        if opening:
            (qq_s,) = take(1)
            lay_queries(sh, me_ref, q_in, qq_s)
        else:
            (qq_s,) = q_in
        if closing:
            lse, sums = take(2)
        tk_s, tv_s, vt_s = refs
        lay_chunk(sh, me_ref, located(sh, kv_in), (k_s, v_s, tk_s, tv_s))
        kt_s[...] = transposed(k_s[...])
        vt_s[:w, :] = transposed(v_s[...])
        vt_s[w:, :] = transposed(tv_s[...])

        def query_block(qb):
            acc, stat = accs.at[qb], stats.at[qb]
            top = sh.blocks if distance else qb + 1
            first = jnp.clip(qb - back_of(sh, me_ref, back_ref, qb) + distance * sh.blocks, 0, top)
            count = top - first

            @pl.when(count > 0)
            def _():
                run = functools.partial(
                    forward_tiles, sh, (k_s, tk_s), vt_s, acc, stat, qq_s[qb]
                )
                by_count(sh, first, count, run, opening)

            if closing:
                most, total, cross = load_state(stat)
                inverse = 1.0 / total
                plain = acc[:w, :] * inverse
                moved = acc[w:, :] * inverse - (cross * inverse * sh.scale) * plain
                acc[:w, :] = plain
                acc[w:, :] = moved
                lse[qb] = most + jnp.log2(total)
                square = plain * plain
                product = plain * moved
                gain = gain_ref[...]
                for r, value in enumerate((square, product, gain * square, gain * product)):
                    line = jnp.sum(value, axis=0, keepdims=True)
                    pieces = [line[:, g * sh.block : (g + 1) * sh.block] for g in range(sh.group)]
                    sums[qb, r : r + 1, :] = functools.reduce(jnp.add, pieces)

        each_block(sh.blocks, query_block)

    def array(*shape, dtype=F32):
        return jax.ShapeDtypeStruct(shape, dtype)

    out_shape = [
        array(sh.tokens, w, dtype=BF16),
        array(sh.tokens, w, dtype=BF16),
        array(w, sh.tokens, dtype=BF16),
        array(sh.blocks, 2 * w, sh.lanes),
        array(sh.blocks, 8, sh.lanes),
    ]
    if opening:
        out_shape.append(array(sh.blocks, sh.lanes, 2 * w, dtype=BF16))
    if closing:
        out_shape += [array(sh.blocks, 1, sh.lanes), array(sh.blocks, 4, sh.block)]
    operands = [*queries, *kv]
    aliases = {}
    if not opening:
        aliases = {2 + len(operands): 3, 3 + len(operands): 4}
        operands += state
    if closing:
        operands.append(gain_square)
    work = sh.group * sh.tokens * sh.tokens // 2
    return pl.pallas_call(
        kernel,
        in_specs=[SMEM, SMEM] + [VMEM] * len(operands),
        out_specs=[VMEM] * len(out_shape),
        out_shape=out_shape,
        input_output_aliases=aliases,
        scratch_shapes=[
            pltpu.VMEM((sh.tokens, w), BF16),
            pltpu.VMEM((sh.tokens, w), BF16),
            pltpu.VMEM((2 * w, sh.tokens), BF16),
        ],
        compiler_params=params(),
        cost_estimate=cost(24 * work * w, 12 * sh.tokens * sh.lanes * 2, work),
        name="forward_far" if closing else "forward_chunk",
    )(me, back, *operands)


def backward_scores(keys, qg, start, size):
    k_s, v_s = keys
    k = k_s[pl.ds(start, size), :]
    v = v_s[pl.ds(start, size), :]
    empty = jnp.zeros_like(k)
    left = jnp.concatenate([k, empty], axis=0)
    right = jnp.concatenate([empty, v], axis=0)
    both = nt(jnp.concatenate([left, right], axis=1), qg)
    return both[:size], both[size:]


def backward_tiles(sh, keys, kt_s, dkv_s, dq_s, qg, lse, dot, tiles, masked):
    places = [(block_rows(sh, block), blocks * sh.block) for block, blocks in tiles]
    scores = [backward_scores(keys, qg, start, size) for start, size in places]
    q, g = qg[:, : sh.width], qg[:, sh.width :]
    for i, ((start, size), (s, dp)) in enumerate(zip(places, scores)):
        rows = pl.ds(start, size)
        p = jnp.exp2(s * sh.powers - lse)
        if masked and i == 0:
            low = below_diagonal(sh, p[size - sh.block :], 0.0)
            p = low if size == sh.block else jnp.concatenate([p[: size - sh.block], low], axis=0)
        ds = (p * (dp - dot)).astype(BF16)
        dkv_s[0, rows, :] += nn(ds, q)
        dkv_s[1, rows, :] += nn(p.astype(BF16), g)
        dq_s[...] += nn(kt_s[:, rows], ds)


def backward_chunk(sh, me, back, qq, keys, distance, grads, lse, dots, dq, norm, order, held):
    w = sh.width
    opening, closing = norm is not None, distance == 0
    per = sh.rows // sh.block
    everyone = order == list(range(sh.parts))

    def kernel(me_ref, back_ref, *refs):
        refs = list(refs)

        def take(count):
            taken = refs[:count]
            del refs[:count]
            return taken

        qq_s, k_s, v_s, kt_s, lse_s = take(5)
        if opening:
            out_s, gain_ref, *sum_refs = take(2 + len(norm[0]))
        else:
            grad_s, dot_s, dq_in = take(3)
        (held_ref,) = take(1) if held is not None else (None,)
        (dkv_out,) = take(1)
        dq_out = take(len(order) if closing else 1)
        if opening:
            grad_s, dot_s = take(2)
        dkv_s, dq_own = refs
        dkv_s[...] = jnp.zeros_like(dkv_s) if held_ref is None else held_ref[...]

        def query_block(i):
            qb = i
            if not everyone:
                partner = functools.reduce(
                    lambda chosen, j: jnp.where(i // per == j, order[j], chosen),
                    range(len(order)),
                    order[0],
                )
                qb = jnp.bitwise_xor(me_ref[0], partner) * per + i % per
            dq_s = dq_own if closing else dq_out[0].at[qb]
            if opening:
                features = norm[2]
                token = functools.reduce(jnp.add, [ref[qb] for ref in sum_refs])
                sums = jnp.concatenate([token] * sh.group, axis=1)
                square = sums[0:1] / features + EPSILON
                inverse = lax.rsqrt(square)
                ratio = sums[1:2] / (features * square)
                again = (sums[3:4] - ratio * sums[2:3]) * inverse
                again = again / (features * square)
                plain = out_s[qb, :w, :]
                moved = out_s[qb, w:, :]
                first_grad = gain_ref[...] * (moved - plain * ratio) * inverse
                cot = ((first_grad - plain * again) * inverse).astype(BF16).astype(F32)
                dot_s[qb] = jnp.sum(cot * plain, axis=0, keepdims=True)
                grad_s[qb] = cot.T.astype(BF16)
                dq_s[...] = jnp.zeros((w, sh.lanes), F32)
            elif closing:
                dq_s[...] = dq_in[qb]

            top = sh.blocks if distance else qb + 1
            first = jnp.clip(qb - back_of(sh, me_ref, back_ref, qb) + distance * sh.blocks, 0, top)
            count = top - first

            @pl.when(count > 0)
            def _():
                qg = jnp.concatenate([qq_s[qb, :, :w], grad_s[qb]], axis=1)
                run = functools.partial(
                    backward_tiles, sh, (k_s, v_s), kt_s, dkv_s, dq_s, qg, lse_s[qb], dot_s[qb]
                )
                by_count(sh, first, count, run, closing)

            if closing:
                done = (dq_s[...] * sh.scale).T.reshape(sh.group, sh.block, w).astype(BF16)
                at = pl.ds(pl.multiple_of(i % per * sh.block, sh.block), sh.block)
                for j, out in enumerate(dq_out):

                    @pl.when(i // per == j)
                    def _(out=out):
                        out[:, at, :] = done

        each_block(len(order) * per, query_block)
        factor = 1.0 if closing else sh.scale
        dkv_out[0] = (dkv_s[0] * factor).astype(dkv_out.dtype)
        dkv_out[1] = dkv_s[1].astype(dkv_out.dtype)

    def array(*shape, dtype=F32):
        return jax.ShapeDtypeStruct(shape, dtype)

    operands = [qq, *keys, lse]
    if opening:
        operands += [grads, norm[1], *norm[0]]
    else:
        operands += [grads, dots, dq]
    aliases = {}
    if not opening and not closing:
        aliases = {1 + len(operands): 1}
    if held is not None:
        operands.append(held)
    out_shape = [array(2, sh.tokens, w, dtype=BF16 if opening else F32)]
    if closing:
        out_shape += [array(sh.group, sh.rows, w, dtype=BF16)] * len(order)
    else:
        out_shape.append(array(sh.blocks, w, sh.lanes))
    if opening:
        out_shape += [
            array(sh.blocks, sh.lanes, w, dtype=BF16),
            array(sh.blocks, 1, sh.lanes),
        ]
    work = sh.group * sh.tokens * len(order) * sh.rows // 2
    return pl.pallas_call(
        kernel,
        in_specs=[SMEM, SMEM] + [VMEM] * len(operands),
        out_specs=[VMEM] * len(out_shape),
        out_shape=out_shape,
        input_output_aliases=aliases,
        scratch_shapes=[
            pltpu.VMEM((2, sh.tokens, w), F32),
            pltpu.VMEM((w, sh.lanes), F32),
        ],
        compiler_params=params(),
        cost_estimate=cost(20 * work * w, 12 * len(order) * sh.rows * sh.lanes * 4, work),
        name="backward_chunk",
    )(me, back, *operands)


def combine(sh, me, carried, held):
    def kernel(me_ref, carried_ref, held_ref, *outs):
        for m, out in enumerate(outs):
            slot = pl.ds(slot_of(me_ref, m, sh.rows), sh.rows)
            for a, factor in ((0, sh.scale), (1, 1.0)):
                part = held_ref[a, slot, :] * factor
                out[a] = (carried_ref[a, slot, :].astype(F32) + part).astype(BF16)

    return pl.pallas_call(
        kernel,
        in_specs=[SMEM, VMEM, VMEM],
        out_specs=[VMEM] * sh.parts,
        out_shape=[jax.ShapeDtypeStruct((2, sh.rows, sh.width), BF16)] * sh.parts,
        compiler_params=params(),
        cost_estimate=cost(0, 1),
        name="combine",
    )(me, carried, held)


def exchanged(pieces):
    parts = len(pieces)
    return [pieces[0]] + [
        lax.ppermute(pieces[m], "part", [(i, i ^ m) for i in range(parts)])
        for m in range(1, parts)
    ]


def moved_on(value, steps):
    count = lax.axis_size("span")
    pairs = [(i, i + steps) for i in range(count) if 0 <= i + steps < count]
    return lax.ppermute(value, "span", pairs)


def summed_over_head(value):
    count = lax.axis_size("head")
    if count & (count - 1):
        return lax.psum(value, "head")
    step = 1
    while step < count:
        value = value + lax.ppermute(value, "head", [(i, i ^ step) for i in range(count)])
        step *= 2
    return value


def body(queries, keys, values, tangent_queries, tangent_keys, tangent_values, doc_start, out_gain):
    rows, query_heads, width = queries.shape
    key_heads = keys.shape[1]
    group = query_heads // key_heads
    parts = lax.axis_size("part")
    per = doc_start.shape[0]
    block = rows // per
    features = query_heads * width * lax.axis_size("head")
    hops = -(-DOC_DEVS // parts)
    sh = Shape(parts, group, rows, width, block)
    place = lax.axis_index("part")
    me = place.astype(jnp.int32).reshape(1)

    def flat(array):
        return array.reshape(-1, width)

    pieces = split_heads(
        [flat(a) for a in (keys, values, tangent_keys, tangent_values)], parts, 1, doc_start
    )
    q_rows, _ = lax.optimization_barrier(((flat(queries), flat(tangent_queries)), pieces[0]))
    q_pieces = split_heads(q_rows, parts, group)
    own = moved_on(pieces[0], 1)
    pieces = exchanged(pieces)
    chunks = [pieces]
    if parts > 1:
        own, q_pieces = lax.optimization_barrier((own, q_pieces))
        owns = [own]
        for _ in range(hops - 1):
            owns.append(moved_on(owns[-1], 1))
        late, owns = lax.optimization_barrier((pieces[1:], owns))
        rest = jnp.concatenate([moved_on(piece, 1) for piece in late], axis=0)
        chunks.append([owns[0], rest])
        for own in owns[1:]:
            rest = moved_on(rest, 1)
            chunks.append([own, rest])
    else:
        for _ in range(hops):
            chunks.append([own])
            own = moved_on(own, 1)
    q_parts = exchanged(q_pieces)
    back = jnp.concatenate([p[4 * rows : 4 * rows + per, 0] for p in pieces]).astype(jnp.int32)
    gain = lax.dynamic_index_in_dim(out_gain.reshape(key_heads, group, width), place, 0, False)
    gain_square = jnp.repeat((gain * gain).T, block, axis=1)

    state, spans = None, []
    for distance in range(hops):
        k, v, kt, acc, stat, *laid = forward_chunk(
            sh, me, back, [qq] if distance else q_parts, chunks[distance], distance, state
        )
        qq = laid[0] if laid else qq
        state = [acc, stat]
        spans.append((k, v, kt))
    k, v, kt, out, _, lse, sums = forward_chunk(
        sh, me, back, [qq], chunks[hops], hops, state, gain_square
    )
    spans.append((k, v, kt))
    sums = summed_over_head(sums)
    norm = (exchanged([sums] * parts), gain_square, features)

    everyone = list(range(parts))
    half = parts // 2

    def closing(dq, order, held):
        return backward_chunk(
            sh, me, back, qq, spans[0], 0, grads, lse, dots, dq, None, order, held
        )

    carried, dq, grads, dots = backward_chunk(
        sh, me, back, qq, spans[hops], hops, out, lse, None, None, norm, everyone, None
    )
    for distance in range(hops - 1, 0, -1):
        arriving = moved_on(carried, -1)
        part, dq = backward_chunk(
            sh, me, back, qq, spans[distance], distance, grads, lse, dots, dq, None,
            everyone, None,
        )
        if distance == 1:
            held, *done = closing(dq, everyone[half:][::-1], None)
            arriving, held = lax.optimization_barrier((arriving, held))
        carried = (arriving.astype(F32) + part).astype(BF16)
    carried = moved_on(carried, -1)
    dq_pieces = done[::-1]
    if half:
        held, *done = closing(dq, everyone[:half][::-1], held)
        dq_pieces = done[::-1] + dq_pieces
    dq_pieces = [piece.reshape(1, group, rows, width) for piece in dq_pieces]
    dq_pieces = exchanged(dq_pieces)
    dq_pieces[half:], held = lax.optimization_barrier((dq_pieces[half:], held))
    dkv_pieces = exchanged(combine(sh, me, carried, held))
    (product_queries,) = join_heads(dq_pieces, 1, group)
    dkv_pieces = [p.reshape(2, 1, rows, width) for p in dkv_pieces]
    product_keys, product_values = join_heads(dkv_pieces, 2, 1)
    return (
        product_queries.reshape(queries.shape),
        product_keys.reshape(keys.shape),
        product_values.reshape(keys.shape),
    )


def solution(mesh):
    def run(*arguments):
        count, heads = mesh.shape["ctx"], mesh.shape["head"]
        parts = arguments[1].shape[1] // heads
        split = Mesh(
            mesh.devices.reshape(count // parts, parts, heads), ("span", "part", "head")
        )
        ctx = ("span", "part")
        array = P(ctx, "head", None)
        return jax.shard_map(
            body,
            mesh=split,
            in_specs=(array,) * 6 + (P(ctx), P("head")),
            out_specs=(array,) * 3,
            check_vma=False,
        )(*arguments)

    return run
```

```python
import functools
import math

import jax
import jax.numpy as jnp
from jax import lax
from jax.experimental import pallas as pl
from jax.experimental.pallas import tpu as pltpu
from jax.sharding import Mesh, PartitionSpec as P

DOC_DEVS = 8
EPSILON = 1e-06
VMEM_BYTES = 18 * 1024 * 1024
NOTE_ROWS = 16
ONES_ROWS = 16
WIDE_VMEM_BYTES = 60 * 1024 * 1024
LOG2E = math.log2(math.e)
MASKED = -1e30
F32 = jnp.float32
BF16 = jnp.bfloat16
SMEM = pl.BlockSpec(memory_space=pltpu.SMEM)
VMEM = pl.BlockSpec(memory_space=pltpu.VMEM)


def params(size=VMEM_BYTES):
    return pltpu.CompilerParams(vmem_limit_bytes=size)


def cost(flops, moved, powers=0):
    return pl.CostEstimate(flops=int(flops), bytes_accessed=int(moved), transcendentals=int(powers))


def nn(a, b):
    return lax.dot_general(a, b, (((1,), (0,)), ((), ())), preferred_element_type=F32)


def nt(a, b):
    return lax.dot_general(a, b, (((1,), (1,)), ((), ())), preferred_element_type=F32)


def split_heads(arrays, parts, per_part, notes=None):
    count = len(arrays)
    total, width = arrays[0].shape
    heads = parts * per_part
    rows = total // heads
    length = count * per_part * rows
    extra = 0 if notes is None else NOTE_ROWS
    scalars = [] if notes is None else [notes]

    def kernel(*refs):
        ins = list(refs[: len(scalars) + count])
        outs, (held, wide, sems) = refs[len(scalars) + count : -3], refs[-3:]
        mine = lax.axis_index("part")
        if extra:
            note_ref = ins.pop(0)
        copies = [pltpu.make_async_copy(ins[a], held.at[a], sems.at[a]) for a in range(count)]
        for copy in copies:
            copy.start()
        if extra:
            first = (lax.axis_index("span") * parts + mine) * notes.shape[0]
            line = lax.broadcasted_iota(jnp.int32, (extra, width), 0)
            lines = jnp.zeros((extra, width), jnp.int32)
            for i in range(notes.shape[0]):
                lines = jnp.where(line == i, first + i - note_ref[i], lines)
            for out in outs:
                out[length:, :] = lines.astype(F32).astype(BF16)
        for a in range(count):
            copies[a].wait()
            wide[...] = held[a].astype(F32)
            for m in range(parts):
                for r in range(per_part):
                    head = jnp.bitwise_xor(mine, m) * per_part + r
                    at = (a * per_part + r) * rows
                    outs[m][at : at + rows, :] = wide[pl.ds(head, rows, stride=heads), :].astype(BF16)

    return pl.pallas_call(
        kernel,
        in_specs=[SMEM] * len(scalars) + [pl.BlockSpec(memory_space=pltpu.HBM)] * count,
        out_specs=[pl.BlockSpec(memory_space=pltpu.VMEM)] * parts,
        out_shape=[jax.ShapeDtypeStruct((length + extra, width), BF16)] * parts,
        scratch_shapes=[
            pltpu.VMEM((count, total, width), BF16),
            pltpu.VMEM((total, width), F32),
            pltpu.SemaphoreType.DMA((count,)),
        ],
        compiler_params=params(VMEM_BYTES if notes is None else WIDE_VMEM_BYTES),
        cost_estimate=cost(0, 4 * count * total * width),
        name="split_heads",
    )(*scalars, *arrays)


def join_heads(pieces, count, per_part):
    parts = len(pieces)
    rows, width = pieces[0].shape[-2:]
    heads = parts * per_part

    steps = 4
    cut = rows // steps

    def kernel(*refs):
        ins, outs = refs[:parts], refs[parts:]
        mine = lax.axis_index("part")
        for a in range(count):
            for m in range(parts):
                for r in range(per_part):
                    head = jnp.bitwise_xor(mine, m) * per_part + r
                    outs[a][pl.ds(head, cut, stride=heads), :] = ins[m][a, r].astype(F32)

    return pl.pallas_call(
        kernel,
        grid=(steps,),
        in_specs=[pl.BlockSpec((count, per_part, cut, width), lambda i: (0, 0, i, 0))] * parts,
        out_specs=[pl.BlockSpec((cut * heads, width), lambda i: (i, 0))] * count,
        out_shape=[jax.ShapeDtypeStruct((rows * heads, width), F32)] * count,
        compiler_params=params(),
        cost_estimate=cost(0, 6 * count * rows * heads * width),
        name="join_heads",
    )(*pieces)


def slot_of(me_ref, m, rows):
    return pl.multiple_of(jnp.bitwise_xor(me_ref[0], m) * rows, rows)


class Shape:
    def __init__(self, parts, group, rows, width, block):
        self.parts, self.group, self.rows, self.width, self.block = parts, group, rows, width, block
        self.tokens = parts * rows
        self.blocks = self.tokens // block
        self.lanes = group * block
        self.scale = width**-0.5
        self.powers = self.scale * LOG2E


def diagonal(sh):
    shape = (sh.block, sh.block)
    key = lax.broadcasted_iota(jnp.int32, shape, 0)
    query = lax.broadcasted_iota(jnp.int32, shape, 1)
    return key <= query


def below_diagonal(sh, value, other):
    allowed = diagonal(sh)
    cut = [value[:, g * sh.block : (g + 1) * sh.block] for g in range(sh.group)]
    return jnp.concatenate([jnp.where(allowed, part, other) for part in cut], axis=1)


def scores_tile(keys, qq, start, size):
    k_s, tk_s = keys
    k = k_s[pl.ds(start, size), :]
    tk = tk_s[pl.ds(start, size), :]
    left = jnp.concatenate([k, tk], axis=0)
    right = jnp.concatenate([jnp.zeros_like(k), k], axis=0)
    both = nt(jnp.concatenate([left, right], axis=1), qq)
    return both[:size], both[size:]


def mix_tile(sh, vt_s, acc, start, size, scores, state, masked):
    w = sh.width
    s, d = scores
    if masked:
        low = below_diagonal(sh, s[size - sh.block :], MASKED)
        s = low if size == sh.block else jnp.concatenate([s[: size - sh.block], low], axis=0)
    most = jnp.max(s, axis=0, keepdims=True) * sh.powers
    if state is not None:
        most = jnp.maximum(most, state[0])
        decay = jnp.exp2(state[0] - most)
    e = jnp.exp2(s * sh.powers - most)
    mix = e * d
    at = pl.ds(start, size)
    plain = nn(vt_s[:, at], e.astype(BF16))
    moving = nn(vt_s[w:, at], mix.astype(BF16))
    total, cross = plain[2 * w : 2 * w + 1], moving[w : w + 1]
    tangent = plain[:w] + moving[:w] * sh.scale
    if state is None:
        acc[:w, :] = plain[w : 2 * w]
        acc[w:, :] = tangent
        return most, total, cross
    acc[:w, :] = acc[:w, :] * decay + plain[w : 2 * w]
    acc[w:, :] = acc[w:, :] * decay + tangent
    return most, state[1] * decay + total, state[2] * decay + cross


def block_rows(sh, block):
    return pl.multiple_of(block * sh.block, sh.block)


def load_state(stat):
    return tuple(stat[r : r + 1, :] for r in range(3))


def store_state(stat, state):
    for r in range(3):
        stat[r : r + 1, :] = state[r]


def forward_tiles(sh, keys, vt_s, acc, stat, qq, tiles, masked):
    places = [(block_rows(sh, block), blocks * sh.block) for block, blocks in tiles]
    scores = [scores_tile(keys, qq, start, size) for start, size in places]
    state = None if masked else load_state(stat)
    for i, ((start, size), both) in enumerate(zip(places, scores)):
        state = mix_tile(sh, vt_s, acc, start, size, both, state, masked and i == 0)
    store_state(stat, state)


def by_count(sh, low, count, run, masked):
    head = jnp.where(count <= 6, count, 3 + lax.rem(jnp.maximum(count - 7, 0), 4))
    fours = (count - head) // 4
    for blocks in range(1, min(6, sh.blocks) + 1):

        @pl.when(head == blocks)
        def _(blocks=blocks):
            if masked:
                run([(low + count - blocks, blocks)], True)
            else:
                run([(low, blocks)], False)

    def step(i, carry):
        run([(low + (0 if masked else head) + 4 * i, 4)], False)
        return carry

    if sh.blocks > 6:
        lax.fori_loop(0, fours, step, 0)


def lay_chunk(sh, me_ref, sources, targets):
    for m, (ref, base) in enumerate(sources):
        slot = pl.ds(slot_of(me_ref, m, sh.rows), sh.rows)
        for i, target in enumerate(targets):
            at = base + i * sh.rows
            target[slot, :] = ref[at : at + sh.rows, :]


def lay_queries(sh, me_ref, pieces, qq):
    per = sh.rows // sh.block
    for m, ref in enumerate(pieces):
        for i in range(2):
            for g in range(sh.group):
                for r in range(per):
                    block = jnp.bitwise_xor(me_ref[0], m) * per + r
                    at = (i * sh.group + g) * sh.rows + r * sh.block
                    qq[
                        block,
                        g * sh.block : (g + 1) * sh.block,
                        i * sh.width : (i + 1) * sh.width,
                    ] = ref[at : at + sh.block, :]


def transposed(x):
    return x.astype(F32).T.astype(BF16)


def located(sh, refs):
    length = refs[0].shape[0]
    return [(ref, at) for ref in refs for at in range(0, ref.shape[0], length)]


def back_of(sh, me_ref, back_ref, qb):
    per = sh.rows // sh.block
    return back_ref[jnp.bitwise_xor(me_ref[0], qb // per) * per + qb % per]


def each_block(count, run):
    def step(i, carry):
        run(i)
        return carry

    lax.fori_loop(0, count, step, 0)


def forward_chunk(sh, me, back, queries, chunk, distance, state, gain_square=None):
    w = sh.width
    kv = chunk
    opening, closing = state is None, gain_square is not None

    def kernel(me_ref, back_ref, *refs):
        refs = list(refs)

        def take(count):
            taken = refs[:count]
            del refs[:count]
            return taken

        q_in = take(len(queries))
        kv_in = take(len(kv))
        if not opening:
            take(2)
        if closing:
            (gain_ref,) = take(1)
        k_s, v_s, kt_s, accs, stats = take(5)
        if opening:
            (qq_s,) = take(1)
            lay_queries(sh, me_ref, q_in, qq_s)
        else:
            (qq_s,) = q_in
        if closing:
            lse, sums = take(2)
        tk_s, tv_s, vt_s = refs
        lay_chunk(sh, me_ref, located(sh, kv_in), (k_s, v_s, tk_s, tv_s))
        kt_s[...] = transposed(k_s[...])
        vt_s[:w, :] = transposed(tv_s[...])
        vt_s[w : 2 * w, :] = transposed(v_s[...])
        vt_s[2 * w :, :] = jnp.ones((ONES_ROWS, sh.tokens), BF16)

        def query_block(qb):
            acc, stat = accs.at[qb], stats.at[qb]
            top = sh.blocks if distance else qb + 1
            first = jnp.clip(qb - back_of(sh, me_ref, back_ref, qb) + distance * sh.blocks, 0, top)
            count = top - first

            @pl.when(count > 0)
            def _():
                run = functools.partial(
                    forward_tiles, sh, (k_s, tk_s), vt_s, acc, stat, qq_s[qb]
                )
                by_count(sh, first, count, run, opening)

            if closing:
                most, total, cross = load_state(stat)
                inverse = 1.0 / total
                plain = acc[:w, :] * inverse
                moved = acc[w:, :] * inverse - (cross * inverse * sh.scale) * plain
                acc[:w, :] = plain
                acc[w:, :] = moved
                lse[qb] = most + jnp.log2(total)
                square = plain * plain
                product = plain * moved
                gain = gain_ref[...]
                for r, value in enumerate((square, product, gain * square, gain * product)):
                    line = jnp.sum(value, axis=0, keepdims=True)
                    pieces = [line[:, g * sh.block : (g + 1) * sh.block] for g in range(sh.group)]
                    sums[qb, r : r + 1, :] = functools.reduce(jnp.add, pieces)

        each_block(sh.blocks, query_block)

    def array(*shape, dtype=F32):
        return jax.ShapeDtypeStruct(shape, dtype)

    out_shape = [
        array(sh.tokens, w, dtype=BF16),
        array(sh.tokens, w, dtype=BF16),
        array(w, sh.tokens, dtype=BF16),
        array(sh.blocks, 2 * w, sh.lanes),
        array(sh.blocks, 8, sh.lanes),
    ]
    if opening:
        out_shape.append(array(sh.blocks, sh.lanes, 2 * w, dtype=BF16))
    if closing:
        out_shape += [array(sh.blocks, 1, sh.lanes), array(sh.blocks, 4, sh.block)]
    operands = [*queries, *kv]
    aliases = {}
    if not opening:
        aliases = {2 + len(operands): 3, 3 + len(operands): 4}
        operands += state
    if closing:
        operands.append(gain_square)
    work = sh.group * sh.tokens * sh.tokens // 2
    return pl.pallas_call(
        kernel,
        in_specs=[SMEM, SMEM] + [VMEM] * len(operands),
        out_specs=[VMEM] * len(out_shape),
        out_shape=out_shape,
        input_output_aliases=aliases,
        scratch_shapes=[
            pltpu.VMEM((sh.tokens, w), BF16),
            pltpu.VMEM((sh.tokens, w), BF16),
            pltpu.VMEM((2 * w + ONES_ROWS, sh.tokens), BF16),
        ],
        compiler_params=params(),
        cost_estimate=cost(24 * work * w, 12 * sh.tokens * sh.lanes * 2, work),
        name="forward_far" if closing else "forward_chunk",
    )(me, back, *operands)


def backward_scores(keys, qg, start, size):
    k_s, v_s = keys
    k = k_s[pl.ds(start, size), :]
    v = v_s[pl.ds(start, size), :]
    empty = jnp.zeros_like(k)
    left = jnp.concatenate([k, empty], axis=0)
    right = jnp.concatenate([empty, v], axis=0)
    both = nt(jnp.concatenate([left, right], axis=1), qg)
    return both[:size], both[size:]


def backward_tiles(sh, keys, kt_s, dkv_s, dq_s, qg, lse, dot, tiles, masked):
    places = [(block_rows(sh, block), blocks * sh.block) for block, blocks in tiles]
    scores = [backward_scores(keys, qg, start, size) for start, size in places]
    q, g = qg[:, : sh.width], qg[:, sh.width :]
    for i, ((start, size), (s, dp)) in enumerate(zip(places, scores)):
        rows = pl.ds(start, size)
        p = jnp.exp2(s * sh.powers - lse)
        if masked and i == 0:
            low = below_diagonal(sh, p[size - sh.block :], 0.0)
            p = low if size == sh.block else jnp.concatenate([p[: size - sh.block], low], axis=0)
        ds = (p * (dp - dot)).astype(BF16)
        dkv_s[0, rows, :] += nn(ds, q)
        dkv_s[1, rows, :] += nn(p.astype(BF16), g)
        dq_s[...] += nn(kt_s[:, rows], ds)


def backward_chunk(sh, me, back, qq, keys, distance, grads, lse, dots, dq, norm, order, held):
    w = sh.width
    opening, closing = norm is not None, distance == 0
    per = sh.rows // sh.block
    everyone = order == list(range(sh.parts))

    def kernel(me_ref, back_ref, *refs):
        refs = list(refs)

        def take(count):
            taken = refs[:count]
            del refs[:count]
            return taken

        qq_s, k_s, v_s, kt_s, lse_s = take(5)
        if opening:
            out_s, gain_ref, *sum_refs = take(2 + len(norm[0]))
        else:
            grad_s, dot_s, dq_in = take(3)
        (held_ref,) = take(1) if held is not None else (None,)
        (dkv_out,) = take(1)
        dq_out = take(len(order) if closing else 1)
        if opening:
            grad_s, dot_s = take(2)
        dkv_s, dq_own = refs
        dkv_s[...] = jnp.zeros_like(dkv_s) if held_ref is None else held_ref[...]

        def query_block(i):
            qb = i
            if not everyone:
                partner = functools.reduce(
                    lambda chosen, j: jnp.where(i // per == j, order[j], chosen),
                    range(len(order)),
                    order[0],
                )
                qb = jnp.bitwise_xor(me_ref[0], partner) * per + i % per
            dq_s = dq_own if closing else dq_out[0].at[qb]
            if opening:
                features = norm[2]
                token = functools.reduce(jnp.add, [ref[qb] for ref in sum_refs])
                sums = jnp.concatenate([token] * sh.group, axis=1)
                square = sums[0:1] / features + EPSILON
                inverse = lax.rsqrt(square)
                ratio = sums[1:2] / (features * square)
                again = (sums[3:4] - ratio * sums[2:3]) * inverse
                again = again / (features * square)
                plain = out_s[qb, :w, :]
                moved = out_s[qb, w:, :]
                first_grad = gain_ref[...] * (moved - plain * ratio) * inverse
                cot = ((first_grad - plain * again) * inverse).astype(BF16).astype(F32)
                dot_s[qb] = jnp.sum(cot * plain, axis=0, keepdims=True)
                grad_s[qb] = cot.T.astype(BF16)
                dq_s[...] = jnp.zeros((w, sh.lanes), F32)
            elif closing:
                dq_s[...] = dq_in[qb]

            top = sh.blocks if distance else qb + 1
            first = jnp.clip(qb - back_of(sh, me_ref, back_ref, qb) + distance * sh.blocks, 0, top)
            count = top - first

            @pl.when(count > 0)
            def _():
                qg = jnp.concatenate([qq_s[qb, :, :w], grad_s[qb]], axis=1)
                run = functools.partial(
                    backward_tiles, sh, (k_s, v_s), kt_s, dkv_s, dq_s, qg, lse_s[qb], dot_s[qb]
                )
                by_count(sh, first, count, run, closing)

            if closing:
                done = (dq_s[...] * sh.scale).T.reshape(sh.group, sh.block, w).astype(BF16)
                at = pl.ds(pl.multiple_of(i % per * sh.block, sh.block), sh.block)
                for j, out in enumerate(dq_out):

                    @pl.when(i // per == j)
                    def _(out=out):
                        out[:, at, :] = done

        each_block(len(order) * per, query_block)
        factor = 1.0 if closing else sh.scale
        dkv_out[0] = (dkv_s[0] * factor).astype(dkv_out.dtype)
        dkv_out[1] = dkv_s[1].astype(dkv_out.dtype)

    def array(*shape, dtype=F32):
        return jax.ShapeDtypeStruct(shape, dtype)

    operands = [qq, *keys, lse]
    if opening:
        operands += [grads, norm[1], *norm[0]]
    else:
        operands += [grads, dots, dq]
    aliases = {}
    if not opening and not closing:
        aliases = {1 + len(operands): 1}
    if held is not None:
        operands.append(held)
    out_shape = [array(2, sh.tokens, w, dtype=BF16 if opening else F32)]
    if closing:
        out_shape += [array(sh.group, sh.rows, w, dtype=BF16)] * len(order)
    else:
        out_shape.append(array(sh.blocks, w, sh.lanes))
    if opening:
        out_shape += [
            array(sh.blocks, sh.lanes, w, dtype=BF16),
            array(sh.blocks, 1, sh.lanes),
        ]
    work = sh.group * sh.tokens * len(order) * sh.rows // 2
    return pl.pallas_call(
        kernel,
        in_specs=[SMEM, SMEM] + [VMEM] * len(operands),
        out_specs=[VMEM] * len(out_shape),
        out_shape=out_shape,
        input_output_aliases=aliases,
        scratch_shapes=[
            pltpu.VMEM((2, sh.tokens, w), F32),
            pltpu.VMEM((w, sh.lanes), F32),
        ],
        compiler_params=params(),
        cost_estimate=cost(20 * work * w, 12 * len(order) * sh.rows * sh.lanes * 4, work),
        name="backward_chunk",
    )(me, back, *operands)


def combine(sh, me, carried, held):
    def kernel(me_ref, carried_ref, held_ref, *outs):
        for m, out in enumerate(outs):
            slot = pl.ds(slot_of(me_ref, m, sh.rows), sh.rows)
            for a, factor in ((0, sh.scale), (1, 1.0)):
                part = held_ref[a, slot, :] * factor
                out[a] = (carried_ref[a, slot, :].astype(F32) + part).astype(BF16)

    return pl.pallas_call(
        kernel,
        in_specs=[SMEM, VMEM, VMEM],
        out_specs=[VMEM] * sh.parts,
        out_shape=[jax.ShapeDtypeStruct((2, sh.rows, sh.width), BF16)] * sh.parts,
        compiler_params=params(),
        cost_estimate=cost(0, 1),
        name="combine",
    )(me, carried, held)


def exchanged(pieces):
    parts = len(pieces)
    return [pieces[0]] + [
        lax.ppermute(pieces[m], "part", [(i, i ^ m) for i in range(parts)])
        for m in range(1, parts)
    ]


def moved_on(value, steps):
    count = lax.axis_size("span")
    pairs = [(i, i + steps) for i in range(count) if 0 <= i + steps < count]
    return lax.ppermute(value, "span", pairs)


def summed_over_head(value):
    count = lax.axis_size("head")
    if count & (count - 1):
        return lax.psum(value, "head")
    step = 1
    while step < count:
        value = value + lax.ppermute(value, "head", [(i, i ^ step) for i in range(count)])
        step *= 2
    return value


def body(queries, keys, values, tangent_queries, tangent_keys, tangent_values, doc_start, out_gain):
    rows, query_heads, width = queries.shape
    key_heads = keys.shape[1]
    group = query_heads // key_heads
    parts = lax.axis_size("part")
    per = doc_start.shape[0]
    block = rows // per
    features = query_heads * width * lax.axis_size("head")
    hops = -(-DOC_DEVS // parts)
    sh = Shape(parts, group, rows, width, block)
    place = lax.axis_index("part")
    me = place.astype(jnp.int32).reshape(1)

    def flat(array):
        return array.reshape(-1, width)

    pieces = split_heads(
        [flat(a) for a in (keys, values, tangent_keys, tangent_values)], parts, 1, doc_start
    )
    q_rows, _ = lax.optimization_barrier(((flat(queries), flat(tangent_queries)), pieces[0]))
    q_pieces = split_heads(q_rows, parts, group)
    own = moved_on(pieces[0], 1)
    pieces = exchanged(pieces)
    chunks = [pieces]
    if parts > 1:
        own, q_pieces = lax.optimization_barrier((own, q_pieces))
        owns = [own]
        for _ in range(hops - 1):
            owns.append(moved_on(owns[-1], 1))
        late, owns = lax.optimization_barrier((pieces[1:], owns))
        rest = jnp.concatenate([moved_on(piece, 1) for piece in late], axis=0)
        chunks.append([owns[0], rest])
        for own in owns[1:]:
            rest = moved_on(rest, 1)
            chunks.append([own, rest])
    else:
        for _ in range(hops):
            chunks.append([own])
            own = moved_on(own, 1)
    q_parts = exchanged(q_pieces)
    back = jnp.concatenate([p[4 * rows : 4 * rows + per, 0] for p in pieces]).astype(jnp.int32)
    gain = lax.dynamic_index_in_dim(out_gain.reshape(key_heads, group, width), place, 0, False)
    gain_square = jnp.repeat((gain * gain).T, block, axis=1)

    state, spans = None, []
    for distance in range(hops):
        k, v, kt, acc, stat, *laid = forward_chunk(
            sh, me, back, [qq] if distance else q_parts, chunks[distance], distance, state
        )
        qq = laid[0] if laid else qq
        state = [acc, stat]
        spans.append((k, v, kt))
    k, v, kt, out, _, lse, sums = forward_chunk(
        sh, me, back, [qq], chunks[hops], hops, state, gain_square
    )
    spans.append((k, v, kt))
    sums = summed_over_head(sums)
    norm = (exchanged([sums] * parts), gain_square, features)

    everyone = list(range(parts))
    half = parts // 2

    def closing(dq, order, held):
        return backward_chunk(
            sh, me, back, qq, spans[0], 0, grads, lse, dots, dq, None, order, held
        )

    carried, dq, grads, dots = backward_chunk(
        sh, me, back, qq, spans[hops], hops, out, lse, None, None, norm, everyone, None
    )
    for distance in range(hops - 1, 0, -1):
        arriving = moved_on(carried, -1)
        part, dq = backward_chunk(
            sh, me, back, qq, spans[distance], distance, grads, lse, dots, dq, None,
            everyone, None,
        )
        if distance == 1:
            held, *done = closing(dq, everyone[half:][::-1], None)
            arriving, held = lax.optimization_barrier((arriving, held))
        carried = (arriving.astype(F32) + part).astype(BF16)
    carried = moved_on(carried, -1)
    dq_pieces = done[::-1]
    if half:
        held, *done = closing(dq, everyone[:half][::-1], held)
        dq_pieces = done[::-1] + dq_pieces
    dq_pieces = [piece.reshape(1, group, rows, width) for piece in dq_pieces]
    dq_pieces = exchanged(dq_pieces)
    dq_pieces[half:], held = lax.optimization_barrier((dq_pieces[half:], held))
    dkv_pieces = exchanged(combine(sh, me, carried, held))
    (product_queries,) = join_heads(dq_pieces, 1, group)
    dkv_pieces = [p.reshape(2, 1, rows, width) for p in dkv_pieces]
    product_keys, product_values = join_heads(dkv_pieces, 2, 1)
    return (
        product_queries.reshape(queries.shape),
        product_keys.reshape(keys.shape),
        product_values.reshape(keys.shape),
    )


def solution(mesh):
    def run(*arguments):
        count, heads = mesh.shape["ctx"], mesh.shape["head"]
        parts = arguments[1].shape[1] // heads
        split = Mesh(
            mesh.devices.reshape(count // parts, parts, heads), ("span", "part", "head")
        )
        ctx = ("span", "part")
        array = P(ctx, "head", None)
        return jax.shard_map(
            body,
            mesh=split,
            in_specs=(array,) * 6 + (P(ctx), P("head")),
            out_specs=(array,) * 3,
            check_vma=False,
        )(*arguments)

    return run
```

```python
import functools
import math

import jax
import jax.numpy as jnp
from jax import lax
from jax.experimental import pallas as pl
from jax.experimental.pallas import tpu as pltpu
from jax.sharding import Mesh, PartitionSpec as P

DOC_DEVS = 8
EPSILON = 1e-06
VMEM_BYTES = 18 * 1024 * 1024
NOTE_ROWS = 16
ONES_ROWS = 16
WIDE_VMEM_BYTES = 60 * 1024 * 1024
LOG2E = math.log2(math.e)
MASKED = -1e30
F32 = jnp.float32
BF16 = jnp.bfloat16
SMEM = pl.BlockSpec(memory_space=pltpu.SMEM)
VMEM = pl.BlockSpec(memory_space=pltpu.VMEM)


def params(size=VMEM_BYTES):
    return pltpu.CompilerParams(vmem_limit_bytes=size)


def cost(flops, moved, powers=0):
    return pl.CostEstimate(flops=int(flops), bytes_accessed=int(moved), transcendentals=int(powers))


def nn(a, b):
    return lax.dot_general(a, b, (((1,), (0,)), ((), ())), preferred_element_type=F32)


def nt(a, b):
    return lax.dot_general(a, b, (((1,), (1,)), ((), ())), preferred_element_type=F32)


def split_heads(arrays, parts, per_part, notes=None):
    count = len(arrays)
    total, width = arrays[0].shape
    heads = parts * per_part
    rows = total // heads
    length = count * per_part * rows
    extra = 0 if notes is None else NOTE_ROWS
    scalars = [] if notes is None else [notes]

    def kernel(*refs):
        ins = list(refs[: len(scalars) + count])
        outs, (held, wide, sems) = refs[len(scalars) + count : -3], refs[-3:]
        mine = lax.axis_index("part")
        if extra:
            note_ref = ins.pop(0)
        copies = [pltpu.make_async_copy(ins[a], held.at[a], sems.at[a]) for a in range(count)]
        for copy in copies:
            copy.start()
        if extra:
            first = (lax.axis_index("span") * parts + mine) * notes.shape[0]
            line = lax.broadcasted_iota(jnp.int32, (extra, width), 0)
            lines = jnp.zeros((extra, width), jnp.int32)
            for i in range(notes.shape[0]):
                lines = jnp.where(line == i, first + i - note_ref[i], lines)
            for out in outs:
                out[length:, :] = lines.astype(F32).astype(BF16)
        for a in range(count):
            copies[a].wait()
            wide[...] = held[a].astype(F32)
            for m in range(parts):
                for r in range(per_part):
                    head = jnp.bitwise_xor(mine, m) * per_part + r
                    at = (a * per_part + r) * rows
                    outs[m][at : at + rows, :] = wide[pl.ds(head, rows, stride=heads), :].astype(BF16)

    return pl.pallas_call(
        kernel,
        in_specs=[SMEM] * len(scalars) + [pl.BlockSpec(memory_space=pltpu.HBM)] * count,
        out_specs=[pl.BlockSpec(memory_space=pltpu.VMEM)] * parts,
        out_shape=[jax.ShapeDtypeStruct((length + extra, width), BF16)] * parts,
        scratch_shapes=[
            pltpu.VMEM((count, total, width), BF16),
            pltpu.VMEM((total, width), F32),
            pltpu.SemaphoreType.DMA((count,)),
        ],
        compiler_params=params(VMEM_BYTES if notes is None else WIDE_VMEM_BYTES),
        cost_estimate=cost(0, 4 * count * total * width),
        name="split_heads",
    )(*scalars, *arrays)


def join_heads(pieces, count, per_part):
    parts = len(pieces)
    rows, width = pieces[0].shape[-2:]
    heads = parts * per_part

    steps = 4
    cut = rows // steps

    def kernel(*refs):
        ins, outs = refs[:parts], refs[parts:]
        mine = lax.axis_index("part")
        for a in range(count):
            for m in range(parts):
                for r in range(per_part):
                    head = jnp.bitwise_xor(mine, m) * per_part + r
                    outs[a][pl.ds(head, cut, stride=heads), :] = ins[m][a, r].astype(F32)

    return pl.pallas_call(
        kernel,
        grid=(steps,),
        in_specs=[pl.BlockSpec((count, per_part, cut, width), lambda i: (0, 0, i, 0))] * parts,
        out_specs=[pl.BlockSpec((cut * heads, width), lambda i: (i, 0))] * count,
        out_shape=[jax.ShapeDtypeStruct((rows * heads, width), F32)] * count,
        compiler_params=params(),
        cost_estimate=cost(0, 6 * count * rows * heads * width),
        name="join_heads",
    )(*pieces)


def slot_of(me_ref, m, rows):
    return pl.multiple_of(jnp.bitwise_xor(me_ref[0], m) * rows, rows)


class Shape:
    def __init__(self, parts, group, rows, width, block):
        self.parts, self.group, self.rows, self.width, self.block = parts, group, rows, width, block
        self.tokens = parts * rows
        self.blocks = self.tokens // block
        self.lanes = group * block
        self.scale = width**-0.5
        self.powers = self.scale * LOG2E


def diagonal(sh):
    shape = (sh.block, sh.block)
    key = lax.broadcasted_iota(jnp.int32, shape, 0)
    query = lax.broadcasted_iota(jnp.int32, shape, 1)
    return key <= query


def below_diagonal(sh, value, other):
    allowed = diagonal(sh)
    cut = [value[:, g * sh.block : (g + 1) * sh.block] for g in range(sh.group)]
    return jnp.concatenate([jnp.where(allowed, part, other) for part in cut], axis=1)


def scores_tile(keys, qq, start, size):
    k_s, tk_s = keys
    k = k_s[pl.ds(start, size), :]
    tk = tk_s[pl.ds(start, size), :]
    left = jnp.concatenate([k, tk], axis=0)
    right = jnp.concatenate([jnp.zeros_like(k), k], axis=0)
    both = nt(jnp.concatenate([left, right], axis=1), qq)
    return both[:size], both[size:]


def mix_tile(sh, vt_s, acc, start, size, scores, state, masked):
    w = sh.width
    s, d = scores
    if masked:
        low = below_diagonal(sh, s[size - sh.block :], MASKED)
        s = low if size == sh.block else jnp.concatenate([s[: size - sh.block], low], axis=0)
    most = jnp.max(s, axis=0, keepdims=True) * sh.powers
    if state is not None:
        most = jnp.maximum(most, state[0])
        decay = jnp.exp2(state[0] - most)
    e = jnp.exp2(s * sh.powers - most)
    mix = e * d
    at = pl.ds(start, size)
    plain = nn(vt_s[:, at], e.astype(BF16))
    moving = nn(vt_s[w:, at], mix.astype(BF16))
    total, cross = plain[2 * w : 2 * w + 1], moving[w : w + 1]
    tangent = plain[:w] + moving[:w] * sh.scale
    if state is None:
        acc[:w, :] = plain[w : 2 * w]
        acc[w:, :] = tangent
        return most, total, cross
    acc[:w, :] = acc[:w, :] * decay + plain[w : 2 * w]
    acc[w:, :] = acc[w:, :] * decay + tangent
    return most, state[1] * decay + total, state[2] * decay + cross


def block_rows(sh, block):
    return pl.multiple_of(block * sh.block, sh.block)


def load_state(stat):
    return tuple(stat[r : r + 1, :] for r in range(3))


def store_state(stat, state):
    for r in range(3):
        stat[r : r + 1, :] = state[r]


def forward_tiles(sh, keys, vt_s, acc, stat, qq, tiles, masked):
    places = [(block_rows(sh, block), blocks * sh.block) for block, blocks in tiles]
    scores = [scores_tile(keys, qq, start, size) for start, size in places]
    state = None if masked else load_state(stat)
    for i, ((start, size), both) in enumerate(zip(places, scores)):
        state = mix_tile(sh, vt_s, acc, start, size, both, state, masked and i == 0)
    store_state(stat, state)


def by_count(sh, low, count, run, masked):
    head = jnp.where(count <= 6, count, 3 + lax.rem(jnp.maximum(count - 7, 0), 4))
    fours = (count - head) // 4
    for blocks in range(1, min(6, sh.blocks) + 1):

        @pl.when(head == blocks)
        def _(blocks=blocks):
            if masked:
                run([(low + count - blocks, blocks)], True)
            else:
                run([(low, blocks)], False)

    def step(i, carry):
        run([(low + (0 if masked else head) + 4 * i, 4)], False)
        return carry

    if sh.blocks > 6:
        lax.fori_loop(0, fours, step, 0)


def lay_chunk(sh, me_ref, sources, targets):
    for m, (ref, base) in enumerate(sources):
        slot = pl.ds(slot_of(me_ref, m, sh.rows), sh.rows)
        for i, target in enumerate(targets):
            at = base + i * sh.rows
            target[slot, :] = ref[at : at + sh.rows, :]


def lay_queries(sh, me_ref, pieces, qq):
    per = sh.rows // sh.block
    for m, ref in enumerate(pieces):
        for i in range(2):
            for g in range(sh.group):
                for r in range(per):
                    block = jnp.bitwise_xor(me_ref[0], m) * per + r
                    at = (i * sh.group + g) * sh.rows + r * sh.block
                    qq[
                        block,
                        g * sh.block : (g + 1) * sh.block,
                        i * sh.width : (i + 1) * sh.width,
                    ] = ref[at : at + sh.block, :]


def transposed(x):
    return x.astype(F32).T.astype(BF16)


def located(sh, refs):
    length = refs[0].shape[0]
    return [(ref, at) for ref in refs for at in range(0, ref.shape[0], length)]


def back_of(sh, me_ref, back_ref, qb):
    per = sh.rows // sh.block
    return back_ref[jnp.bitwise_xor(me_ref[0], qb // per) * per + qb % per]


def each_block(count, run):
    def step(i, carry):
        run(i)
        return carry

    lax.fori_loop(0, count, step, 0)


def forward_chunk(sh, me, back, queries, chunk, distance, state, gain_square=None):
    w = sh.width
    kv = chunk
    opening, closing = state is None, gain_square is not None

    def kernel(me_ref, back_ref, *refs):
        refs = list(refs)

        def take(count):
            taken = refs[:count]
            del refs[:count]
            return taken

        q_in = take(len(queries))
        kv_in = take(len(kv))
        if not opening:
            take(2)
        if closing:
            (gain_ref,) = take(1)
        k_s, v_s, kt_s, accs, stats = take(5)
        if opening:
            (qq_s,) = take(1)
            lay_queries(sh, me_ref, q_in, qq_s)
        else:
            (qq_s,) = q_in
        if closing:
            lse, sums = take(2)
        tk_s, tv_s, vt_s = refs
        lay_chunk(sh, me_ref, located(sh, kv_in), (k_s, v_s, tk_s, tv_s))
        kt_s[...] = transposed(k_s[...])
        vt_s[:w, :] = transposed(tv_s[...])
        vt_s[w : 2 * w, :] = transposed(v_s[...])
        vt_s[2 * w :, :] = jnp.ones((ONES_ROWS, sh.tokens), BF16)

        def query_block(qb):
            acc, stat = accs.at[qb], stats.at[qb]
            top = sh.blocks if distance else qb + 1
            first = jnp.clip(qb - back_of(sh, me_ref, back_ref, qb) + distance * sh.blocks, 0, top)
            count = top - first

            @pl.when(count > 0)
            def _():
                run = functools.partial(
                    forward_tiles, sh, (k_s, tk_s), vt_s, acc, stat, qq_s[qb]
                )
                by_count(sh, first, count, run, opening)

            if closing:
                most, total, cross = load_state(stat)
                inverse = 1.0 / total
                plain = acc[:w, :] * inverse
                moved = acc[w:, :] * inverse - (cross * inverse * sh.scale) * plain
                acc[:w, :] = plain
                acc[w:, :] = moved
                lse[qb] = most + jnp.log2(total)
                square = plain * plain
                product = plain * moved
                gain = gain_ref[...]
                for r, value in enumerate((square, product, gain * square, gain * product)):
                    line = jnp.sum(value, axis=0, keepdims=True)
                    pieces = [line[:, g * sh.block : (g + 1) * sh.block] for g in range(sh.group)]
                    sums[qb, r : r + 1, :] = functools.reduce(jnp.add, pieces)

        each_block(sh.blocks, query_block)

    def array(*shape, dtype=F32):
        return jax.ShapeDtypeStruct(shape, dtype)

    out_shape = [
        array(sh.tokens, w, dtype=BF16),
        array(sh.tokens, w, dtype=BF16),
        array(w, sh.tokens, dtype=BF16),
        array(sh.blocks, 2 * w, sh.lanes),
        array(sh.blocks, 8, sh.lanes),
    ]
    if opening:
        out_shape.append(array(sh.blocks, sh.lanes, 2 * w, dtype=BF16))
    if closing:
        out_shape += [array(sh.blocks, 1, sh.lanes), array(sh.blocks, 4, sh.block)]
    operands = [*queries, *kv]
    aliases = {}
    if not opening:
        aliases = {2 + len(operands): 3, 3 + len(operands): 4}
        operands += state
    if closing:
        operands.append(gain_square)
    work = sh.group * sh.tokens * sh.tokens // 2
    return pl.pallas_call(
        kernel,
        in_specs=[SMEM, SMEM] + [VMEM] * len(operands),
        out_specs=[VMEM] * len(out_shape),
        out_shape=out_shape,
        input_output_aliases=aliases,
        scratch_shapes=[
            pltpu.VMEM((sh.tokens, w), BF16),
            pltpu.VMEM((sh.tokens, w), BF16),
            pltpu.VMEM((2 * w + ONES_ROWS, sh.tokens), BF16),
        ],
        compiler_params=params(),
        cost_estimate=cost(24 * work * w, 12 * sh.tokens * sh.lanes * 2, work),
        name="forward_far" if closing else "forward_chunk",
    )(me, back, *operands)


def backward_scores(keys, qg, start, size):
    k_s, v_s = keys
    k = k_s[pl.ds(start, size), :]
    v = v_s[pl.ds(start, size), :]
    empty = jnp.zeros_like(k)
    left = jnp.concatenate([k, empty], axis=0)
    right = jnp.concatenate([empty, v], axis=0)
    both = nt(jnp.concatenate([left, right], axis=1), qg)
    return both[:size], both[size:]


def backward_tiles(sh, keys, kt_s, dkv_s, dq_s, qg, lse, dot, tiles, masked):
    places = [(block_rows(sh, block), blocks * sh.block) for block, blocks in tiles]
    scores = [backward_scores(keys, qg, start, size) for start, size in places]
    q, g = qg[:, : sh.width], qg[:, sh.width :]
    for i, ((start, size), (s, dp)) in enumerate(zip(places, scores)):
        rows = pl.ds(start, size)
        p = jnp.exp2(s * sh.powers - lse)
        if masked and i == 0:
            low = below_diagonal(sh, p[size - sh.block :], 0.0)
            p = low if size == sh.block else jnp.concatenate([p[: size - sh.block], low], axis=0)
        ds = (p * (dp - dot)).astype(BF16)
        dkv_s[0, rows, :] += nn(ds, q)
        dkv_s[1, rows, :] += nn(p.astype(BF16), g)
        dq_s[...] += nn(kt_s[:, rows], ds)


def backward_chunk(sh, me, back, qq, keys, distance, grads, lse, dots, dq, norm, order, held):
    w = sh.width
    opening, closing = norm is not None, distance == 0
    per = sh.rows // sh.block
    everyone = order == list(range(sh.parts))

    def kernel(me_ref, back_ref, *refs):
        refs = list(refs)

        def take(count):
            taken = refs[:count]
            del refs[:count]
            return taken

        qq_s, k_s, v_s, kt_s, lse_s = take(5)
        if opening:
            out_s, gain_ref, *sum_refs = take(2 + len(norm[0]))
        else:
            grad_s, dot_s, dq_in = take(3)
        (held_ref,) = take(1) if held is not None else (None,)
        (dkv_out,) = take(1)
        dq_out = take(len(order) if closing else 1)
        if opening:
            grad_s, dot_s = take(2)
        dkv_s, dq_own = (dkv_out, *refs) if closing else refs
        if held_ref is None:
            dkv_s[...] = jnp.zeros_like(dkv_s)

        def query_block(i):
            qb = i
            if not everyone:
                partner = functools.reduce(
                    lambda chosen, j: jnp.where(i // per == j, order[j], chosen),
                    range(len(order)),
                    order[0],
                )
                qb = jnp.bitwise_xor(me_ref[0], partner) * per + i % per
            dq_s = dq_own if closing else dq_out[0].at[qb]
            if opening:
                features = norm[2]
                token = functools.reduce(jnp.add, [ref[qb] for ref in sum_refs])
                sums = jnp.concatenate([token] * sh.group, axis=1)
                square = sums[0:1] / features + EPSILON
                inverse = lax.rsqrt(square)
                ratio = sums[1:2] / (features * square)
                again = (sums[3:4] - ratio * sums[2:3]) * inverse
                again = again / (features * square)
                plain = out_s[qb, :w, :]
                moved = out_s[qb, w:, :]
                first_grad = gain_ref[...] * (moved - plain * ratio) * inverse
                cot = ((first_grad - plain * again) * inverse).astype(BF16).astype(F32)
                dot_s[qb] = jnp.sum(cot * plain, axis=0, keepdims=True)
                grad_s[qb] = cot.T.astype(BF16)
                dq_s[...] = jnp.zeros((w, sh.lanes), F32)
            elif closing:
                dq_s[...] = dq_in[qb]

            top = sh.blocks if distance else qb + 1
            first = jnp.clip(qb - back_of(sh, me_ref, back_ref, qb) + distance * sh.blocks, 0, top)
            count = top - first

            @pl.when(count > 0)
            def _():
                qg = jnp.concatenate([qq_s[qb, :, :w], grad_s[qb]], axis=1)
                run = functools.partial(
                    backward_tiles, sh, (k_s, v_s), kt_s, dkv_s, dq_s, qg, lse_s[qb], dot_s[qb]
                )
                by_count(sh, first, count, run, closing)

            if closing:
                done = (dq_s[...] * sh.scale).T.reshape(sh.group, sh.block, w).astype(BF16)
                at = pl.ds(pl.multiple_of(i % per * sh.block, sh.block), sh.block)
                for j, out in enumerate(dq_out):

                    @pl.when(i // per == j)
                    def _(out=out):
                        out[:, at, :] = done

        each_block(len(order) * per, query_block)
        if not closing:
            dkv_out[0] = (dkv_s[0] * sh.scale).astype(BF16)
            dkv_out[1] = dkv_s[1].astype(BF16)

    def array(*shape, dtype=F32):
        return jax.ShapeDtypeStruct(shape, dtype)

    operands = [qq, *keys, lse]
    if opening:
        operands += [grads, norm[1], *norm[0]]
    else:
        operands += [grads, dots, dq]
    aliases = {}
    if not opening and not closing:
        aliases = {1 + len(operands): 1}
    if held is not None:
        aliases = {2 + len(operands): 0}
        operands.append(held)
    out_shape = [array(2, sh.tokens, w, dtype=F32 if closing else BF16)]
    if closing:
        out_shape += [array(sh.group, sh.rows, w, dtype=BF16)] * len(order)
    else:
        out_shape.append(array(sh.blocks, w, sh.lanes))
    if opening:
        out_shape += [
            array(sh.blocks, sh.lanes, w, dtype=BF16),
            array(sh.blocks, 1, sh.lanes),
        ]
    work = sh.group * sh.tokens * len(order) * sh.rows // 2
    return pl.pallas_call(
        kernel,
        in_specs=[SMEM, SMEM] + [VMEM] * len(operands),
        out_specs=[VMEM] * len(out_shape),
        out_shape=out_shape,
        input_output_aliases=aliases,
        scratch_shapes=[pltpu.VMEM((2, sh.tokens, w), F32)] * (not closing)
        + [pltpu.VMEM((w, sh.lanes), F32)],
        compiler_params=params(),
        cost_estimate=cost(20 * work * w, 12 * len(order) * sh.rows * sh.lanes * 4, work),
        name="backward_chunk",
    )(me, back, *operands)


def combine(sh, me, arrived, held):
    count = len(arrived)

    def kernel(me_ref, held_ref, *refs):
        for m, out in enumerate(refs[count:]):
            slot = pl.ds(slot_of(me_ref, m, sh.rows), sh.rows)
            for a, factor in ((0, sh.scale), (1, 1.0)):
                part = held_ref[a, slot, :] * factor
                for ref in refs[:count]:
                    part += ref[a, slot, :].astype(F32)
                out[a] = part.astype(BF16)

    return pl.pallas_call(
        kernel,
        in_specs=[SMEM] + [VMEM] * (1 + count),
        out_specs=[VMEM] * sh.parts,
        out_shape=[jax.ShapeDtypeStruct((2, sh.rows, sh.width), BF16)] * sh.parts,
        compiler_params=params(),
        cost_estimate=cost(0, 1),
        name="combine",
    )(me, held, *arrived)


def exchanged(pieces):
    parts = len(pieces)
    return [pieces[0]] + [
        lax.ppermute(pieces[m], "part", [(i, i ^ m) for i in range(parts)])
        for m in range(1, parts)
    ]


def moved_on(value, steps):
    count = lax.axis_size("span")
    pairs = [(i, i + steps) for i in range(count) if 0 <= i + steps < count]
    return lax.ppermute(value, "span", pairs)


def summed_over_head(value):
    count = lax.axis_size("head")
    if count & (count - 1):
        return lax.psum(value, "head")
    step = 1
    while step < count:
        value = value + lax.ppermute(value, "head", [(i, i ^ step) for i in range(count)])
        step *= 2
    return value


def body(queries, keys, values, tangent_queries, tangent_keys, tangent_values, doc_start, out_gain):
    rows, query_heads, width = queries.shape
    key_heads = keys.shape[1]
    group = query_heads // key_heads
    parts = lax.axis_size("part")
    per = doc_start.shape[0]
    block = rows // per
    features = query_heads * width * lax.axis_size("head")
    hops = -(-DOC_DEVS // parts)
    sh = Shape(parts, group, rows, width, block)
    place = lax.axis_index("part")
    me = place.astype(jnp.int32).reshape(1)

    def flat(array):
        return array.reshape(-1, width)

    pieces = split_heads(
        [flat(a) for a in (keys, values, tangent_keys, tangent_values)], parts, 1, doc_start
    )
    q_rows, _ = lax.optimization_barrier(((flat(queries), flat(tangent_queries)), pieces[0]))
    q_pieces = split_heads(q_rows, parts, group)
    own = moved_on(pieces[0], 1)
    pieces = exchanged(pieces)
    chunks = [pieces]
    if parts > 1:
        own, q_pieces = lax.optimization_barrier((own, q_pieces))
        owns = [own]
        for _ in range(hops - 1):
            owns.append(moved_on(owns[-1], 1))
        late, owns = lax.optimization_barrier((pieces[1:], owns))
        rest = jnp.concatenate([moved_on(piece, 1) for piece in late], axis=0)
        chunks.append([owns[0], rest])
        for own in owns[1:]:
            rest = moved_on(rest, 1)
            chunks.append([own, rest])
    else:
        for _ in range(hops):
            chunks.append([own])
            own = moved_on(own, 1)
    q_parts = exchanged(q_pieces)
    back = jnp.concatenate([p[4 * rows : 4 * rows + per, 0] for p in pieces]).astype(jnp.int32)
    gain = lax.dynamic_index_in_dim(out_gain.reshape(key_heads, group, width), place, 0, False)
    gain_square = jnp.repeat((gain * gain).T, block, axis=1)

    state, spans = None, []
    for distance in range(hops):
        k, v, kt, acc, stat, *laid = forward_chunk(
            sh, me, back, [qq] if distance else q_parts, chunks[distance], distance, state
        )
        qq = laid[0] if laid else qq
        state = [acc, stat]
        spans.append((k, v, kt))
    k, v, kt, out, _, lse, sums = forward_chunk(
        sh, me, back, [qq], chunks[hops], hops, state, gain_square
    )
    spans.append((k, v, kt))
    sums = summed_over_head(sums)
    norm = (exchanged([sums] * parts), gain_square, features)

    everyone = list(range(parts))
    part, dq, grads, dots = backward_chunk(
        sh, me, back, qq, spans[hops], hops, out, lse, None, None, norm, everyone, None
    )
    arrived = [moved_on(part, -hops)]
    for distance in range(hops - 1, 0, -1):
        part, dq = backward_chunk(
            sh, me, back, qq, spans[distance], distance, grads, lse, dots, dq, None,
            everyone, None,
        )
        arrived.append(moved_on(part, -distance))
    turns = [turn[::-1] for turn in (everyone[2:], everyone[:2]) if turn]
    held, dq_pieces = None, [None] * parts
    for order in turns:
        held, *done = backward_chunk(
            sh, me, back, qq, spans[0], 0, grads, lse, dots, dq, None, order, held
        )
        for m, piece in zip(order, done):
            dq_pieces[m] = piece.reshape(1, group, rows, width)
    dq_pieces = exchanged(dq_pieces)
    dq_pieces[2:], held = lax.optimization_barrier((dq_pieces[2:], held))
    dkv_pieces = exchanged(combine(sh, me, arrived, held))
    (product_queries,) = join_heads(dq_pieces, 1, group)
    dkv_pieces = [p.reshape(2, 1, rows, width) for p in dkv_pieces]
    product_keys, product_values = join_heads(dkv_pieces, 2, 1)
    return (
        product_queries.reshape(queries.shape),
        product_keys.reshape(keys.shape),
        product_values.reshape(keys.shape),
    )


def solution(mesh):
    def run(*arguments):
        count, heads = mesh.shape["ctx"], mesh.shape["head"]
        parts = arguments[1].shape[1] // heads
        split = Mesh(
            mesh.devices.reshape(count // parts, parts, heads), ("span", "part", "head")
        )
        ctx = ("span", "part")
        array = P(ctx, "head", None)
        return jax.shard_map(
            body,
            mesh=split,
            in_specs=(array,) * 6 + (P(ctx), P("head")),
            out_specs=(array,) * 3,
            check_vma=False,
        )(*arguments)

    return run
```

```python
import functools
import math

import jax
import jax.numpy as jnp
from jax import lax
from jax.experimental import pallas as pl
from jax.experimental.pallas import tpu as pltpu
from jax.sharding import Mesh, PartitionSpec as P

DOC_DEVS = 8
EPSILON = 1e-06
VMEM_BYTES = 18 * 1024 * 1024
NOTE_ROWS = 16
ONES_ROWS = 16
WIDE_VMEM_BYTES = 60 * 1024 * 1024
LOG2E = math.log2(math.e)
MASKED = -1e30
F32 = jnp.float32
BF16 = jnp.bfloat16
SMEM = pl.BlockSpec(memory_space=pltpu.SMEM)
VMEM = pl.BlockSpec(memory_space=pltpu.VMEM)


def params(size=VMEM_BYTES):
    return pltpu.CompilerParams(vmem_limit_bytes=size)


def cost(flops, moved, powers=0):
    return pl.CostEstimate(flops=int(flops), bytes_accessed=int(moved), transcendentals=int(powers))


def nn(a, b):
    return lax.dot_general(a, b, (((1,), (0,)), ((), ())), preferred_element_type=F32)


def nt(a, b):
    return lax.dot_general(a, b, (((1,), (1,)), ((), ())), preferred_element_type=F32)


def split_heads(arrays, parts, per_part, notes=None):
    count = len(arrays)
    total, width = arrays[0].shape
    heads = parts * per_part
    rows = total // heads
    length = count * per_part * rows
    extra = 0 if notes is None else NOTE_ROWS
    scalars = [] if notes is None else [notes]

    def kernel(*refs):
        ins = list(refs[: len(scalars) + count])
        outs, (held, wide, sems) = refs[len(scalars) + count : -3], refs[-3:]
        mine = lax.axis_index("part")
        if extra:
            note_ref = ins.pop(0)
        copies = [pltpu.make_async_copy(ins[a], held.at[a], sems.at[a]) for a in range(count)]
        for copy in copies:
            copy.start()
        if extra:
            first = (lax.axis_index("span") * parts + mine) * notes.shape[0]
            line = lax.broadcasted_iota(jnp.int32, (extra, width), 0)
            lines = jnp.zeros((extra, width), jnp.int32)
            for i in range(notes.shape[0]):
                lines = jnp.where(line == i, first + i - note_ref[i], lines)
            for out in outs:
                out[length:, :] = lines.astype(F32).astype(BF16)
        for a in range(count):
            copies[a].wait()
            wide[...] = held[a].astype(F32)
            for m in range(parts):
                for r in range(per_part):
                    head = jnp.bitwise_xor(mine, m) * per_part + r
                    at = (a * per_part + r) * rows
                    outs[m][at : at + rows, :] = wide[pl.ds(head, rows, stride=heads), :].astype(BF16)

    return pl.pallas_call(
        kernel,
        in_specs=[SMEM] * len(scalars) + [pl.BlockSpec(memory_space=pltpu.HBM)] * count,
        out_specs=[pl.BlockSpec(memory_space=pltpu.VMEM)] * parts,
        out_shape=[jax.ShapeDtypeStruct((length + extra, width), BF16)] * parts,
        scratch_shapes=[
            pltpu.VMEM((count, total, width), BF16),
            pltpu.VMEM((total, width), F32),
            pltpu.SemaphoreType.DMA((count,)),
        ],
        compiler_params=params(VMEM_BYTES if notes is None else WIDE_VMEM_BYTES),
        cost_estimate=cost(0, 4 * count * total * width),
        name="split_heads",
    )(*scalars, *arrays)


def join_heads(pieces, count, per_part):
    parts = len(pieces)
    rows, width = pieces[0].shape[-2:]
    heads = parts * per_part

    steps = 4
    cut = rows // steps

    def kernel(*refs):
        ins, outs = refs[:parts], refs[parts:]
        mine = lax.axis_index("part")
        for a in range(count):
            for m in range(parts):
                for r in range(per_part):
                    head = jnp.bitwise_xor(mine, m) * per_part + r
                    outs[a][pl.ds(head, cut, stride=heads), :] = ins[m][a, r].astype(F32)

    return pl.pallas_call(
        kernel,
        grid=(steps,),
        in_specs=[pl.BlockSpec((count, per_part, cut, width), lambda i: (0, 0, i, 0))] * parts,
        out_specs=[pl.BlockSpec((cut * heads, width), lambda i: (i, 0))] * count,
        out_shape=[jax.ShapeDtypeStruct((rows * heads, width), F32)] * count,
        compiler_params=params(),
        cost_estimate=cost(0, 6 * count * rows * heads * width),
        name="join_heads",
    )(*pieces)


def slot_of(me_ref, m, rows):
    return pl.multiple_of(jnp.bitwise_xor(me_ref[0], m) * rows, rows)


class Shape:
    def __init__(self, parts, group, rows, width, block):
        self.parts, self.group, self.rows, self.width, self.block = parts, group, rows, width, block
        self.tokens = parts * rows
        self.blocks = self.tokens // block
        self.lanes = group * block
        self.scale = width**-0.5
        self.powers = self.scale * LOG2E


def diagonal(sh):
    shape = (sh.block, sh.block)
    key = lax.broadcasted_iota(jnp.int32, shape, 0)
    query = lax.broadcasted_iota(jnp.int32, shape, 1)
    return key <= query


def below_diagonal(sh, value, other):
    allowed = diagonal(sh)
    cut = [value[:, at : at + sh.block] for at in range(0, value.shape[1], sh.block)]
    return jnp.concatenate([jnp.where(allowed, part, other) for part in cut], axis=1)


def halves(sh):
    if sh.group % 2:
        return [slice(0, sh.lanes)]
    return [slice(0, sh.lanes // 2), slice(sh.lanes // 2, sh.lanes)]


def stacked_keys(keys, start, size):
    k_s, tk_s = keys
    k = k_s[pl.ds(start, size), :]
    tk = tk_s[pl.ds(start, size), :]
    left = jnp.concatenate([k, tk], axis=0)
    right = jnp.concatenate([jnp.zeros_like(k), k], axis=0)
    return jnp.concatenate([left, right], axis=1)


def mix_tile(sh, vt_s, acc, lanes, start, size, both, state, masked):
    w = sh.width
    s, d = both[:size], both[size:]
    if masked:
        low = below_diagonal(sh, s[size - sh.block :], MASKED)
        s = low if size == sh.block else jnp.concatenate([s[: size - sh.block], low], axis=0)
    most = jnp.max(s, axis=0, keepdims=True) * sh.powers
    if state is not None:
        most = jnp.maximum(most, state[0])
        decay = jnp.exp2(state[0] - most)
    e = jnp.exp2(s * sh.powers - most)
    mix = e * d
    at = pl.ds(start, size)
    plain = nn(vt_s[:, at], e.astype(BF16))
    moving = nn(vt_s[w:, at], mix.astype(BF16))
    total, cross = plain[2 * w : 2 * w + 1], moving[w : w + 1]
    tangent = plain[:w] + moving[:w] * sh.scale
    if state is None:
        acc[:w, lanes] = plain[w : 2 * w]
        acc[w:, lanes] = tangent
        return most, total, cross
    acc[:w, lanes] = acc[:w, lanes] * decay + plain[w : 2 * w]
    acc[w:, lanes] = acc[w:, lanes] * decay + tangent
    return most, state[1] * decay + total, state[2] * decay + cross


def block_rows(sh, block):
    return pl.multiple_of(block * sh.block, sh.block)


def load_state(stat, lanes):
    return tuple(stat[r : r + 1, lanes] for r in range(3))


def forward_tile(sh, keys, vt_s, acc, stat, qq, block, blocks, masked):
    start, size = block_rows(sh, block), blocks * sh.block
    stacked = stacked_keys(keys, start, size)
    scores = [nt(stacked, qq[lanes, :]) for lanes in halves(sh)]
    for lanes, both in zip(halves(sh), scores):
        state = None if masked else load_state(stat, lanes)
        state = mix_tile(sh, vt_s, acc, lanes, start, size, both, state, masked)
        for r in range(3):
            stat[r : r + 1, lanes] = state[r]


def by_count(sh, low, count, run, masked):
    head = jnp.where(count <= 6, count, 3 + lax.rem(jnp.maximum(count - 7, 0), 4))
    fours = (count - head) // 4
    for blocks in range(1, min(6, sh.blocks) + 1):

        @pl.when(head == blocks)
        def _(blocks=blocks):
            if masked:
                run(low + count - blocks, blocks, True)
            else:
                run(low, blocks, False)

    def step(i, carry):
        run(low + (0 if masked else head) + 4 * i, 4, False)
        return carry

    if sh.blocks > 6:
        lax.fori_loop(0, fours, step, 0)


def lay_chunk(sh, me_ref, sources, targets):
    for m, (ref, base) in enumerate(sources):
        slot = pl.ds(slot_of(me_ref, m, sh.rows), sh.rows)
        for i, target in enumerate(targets):
            at = base + i * sh.rows
            target[slot, :] = ref[at : at + sh.rows, :]


def lay_queries(sh, me_ref, pieces, qq):
    per = sh.rows // sh.block
    for m, ref in enumerate(pieces):
        for i in range(2):
            for g in range(sh.group):
                for r in range(per):
                    block = jnp.bitwise_xor(me_ref[0], m) * per + r
                    at = (i * sh.group + g) * sh.rows + r * sh.block
                    qq[
                        block,
                        g * sh.block : (g + 1) * sh.block,
                        i * sh.width : (i + 1) * sh.width,
                    ] = ref[at : at + sh.block, :]


def transposed(x):
    return x.astype(F32).T.astype(BF16)


def located(sh, refs):
    length = refs[0].shape[0]
    return [(ref, at) for ref in refs for at in range(0, ref.shape[0], length)]


def back_of(sh, me_ref, back_ref, qb):
    per = sh.rows // sh.block
    return back_ref[jnp.bitwise_xor(me_ref[0], qb // per) * per + qb % per]


def each_block(count, run):
    def step(i, carry):
        run(i)
        return carry

    lax.fori_loop(0, count, step, 0)


def forward_chunk(sh, me, back, queries, chunk, distance, state, gain_square=None):
    w = sh.width
    kv = chunk
    opening, closing = state is None, gain_square is not None

    def kernel(me_ref, back_ref, *refs):
        refs = list(refs)

        def take(count):
            taken = refs[:count]
            del refs[:count]
            return taken

        q_in = take(len(queries))
        kv_in = take(len(kv))
        if not opening:
            take(2)
        if closing:
            (gain_ref,) = take(1)
        k_s, v_s, kt_s, accs, stats = take(5)
        if opening:
            (qq_s,) = take(1)
            lay_queries(sh, me_ref, q_in, qq_s)
        else:
            (qq_s,) = q_in
        if closing:
            lse, sums = take(2)
        tk_s, tv_s, vt_s = refs
        lay_chunk(sh, me_ref, located(sh, kv_in), (k_s, v_s, tk_s, tv_s))
        kt_s[...] = transposed(k_s[...])
        vt_s[:w, :] = transposed(tv_s[...])
        vt_s[w : 2 * w, :] = transposed(v_s[...])
        vt_s[2 * w :, :] = jnp.ones((ONES_ROWS, sh.tokens), BF16)

        def query_block(qb):
            acc, stat = accs.at[qb], stats.at[qb]
            top = sh.blocks if distance else qb + 1
            first = jnp.clip(qb - back_of(sh, me_ref, back_ref, qb) + distance * sh.blocks, 0, top)
            count = top - first

            @pl.when(count > 0)
            def _():
                run = functools.partial(
                    forward_tile, sh, (k_s, tk_s), vt_s, acc, stat, qq_s[qb]
                )
                by_count(sh, first, count, run, opening)

            if closing:
                most, total, cross = load_state(stat, slice(None))
                inverse = 1.0 / total
                plain = acc[:w, :] * inverse
                moved = acc[w:, :] * inverse - (cross * inverse * sh.scale) * plain
                acc[:w, :] = plain
                acc[w:, :] = moved
                lse[qb] = most + jnp.log2(total)
                square = plain * plain
                product = plain * moved
                gain = gain_ref[...]
                for r, value in enumerate((square, product, gain * square, gain * product)):
                    line = jnp.sum(value, axis=0, keepdims=True)
                    pieces = [line[:, g * sh.block : (g + 1) * sh.block] for g in range(sh.group)]
                    sums[qb, r : r + 1, :] = functools.reduce(jnp.add, pieces)

        each_block(sh.blocks, query_block)

    def array(*shape, dtype=F32):
        return jax.ShapeDtypeStruct(shape, dtype)

    out_shape = [
        array(sh.tokens, w, dtype=BF16),
        array(sh.tokens, w, dtype=BF16),
        array(w, sh.tokens, dtype=BF16),
        array(sh.blocks, 2 * w, sh.lanes),
        array(sh.blocks, 8, sh.lanes),
    ]
    if opening:
        out_shape.append(array(sh.blocks, sh.lanes, 2 * w, dtype=BF16))
    if closing:
        out_shape += [array(sh.blocks, 1, sh.lanes), array(sh.blocks, 4, sh.block)]
    operands = [*queries, *kv]
    aliases = {}
    if not opening:
        aliases = {2 + len(operands): 3, 3 + len(operands): 4}
        operands += state
    if closing:
        operands.append(gain_square)
    work = sh.group * sh.tokens * sh.tokens // 2
    return pl.pallas_call(
        kernel,
        in_specs=[SMEM, SMEM] + [VMEM] * len(operands),
        out_specs=[VMEM] * len(out_shape),
        out_shape=out_shape,
        input_output_aliases=aliases,
        scratch_shapes=[
            pltpu.VMEM((sh.tokens, w), BF16),
            pltpu.VMEM((sh.tokens, w), BF16),
            pltpu.VMEM((2 * w + ONES_ROWS, sh.tokens), BF16),
        ],
        compiler_params=params(),
        cost_estimate=cost(24 * work * w, 12 * sh.tokens * sh.lanes * 2, work),
        name="forward_far" if closing else "forward_chunk",
    )(me, back, *operands)


def backward_tile(sh, keys, kt_s, dkv_s, dq_s, qg, lse, dot, block, blocks, masked):
    start, size = block_rows(sh, block), blocks * sh.block
    rows = pl.ds(start, size)
    k_s, v_s = keys
    k, v = k_s[rows, :], v_s[rows, :]
    empty = jnp.zeros_like(k)
    left = jnp.concatenate([k, empty], axis=0)
    right = jnp.concatenate([empty, v], axis=0)
    stacked = jnp.concatenate([left, right], axis=1)
    scores = [nt(stacked, qg[lanes, :]) for lanes in halves(sh)]
    for lanes, both in zip(halves(sh), scores):
        p = jnp.exp2(both[:size] * sh.powers - lse[:, lanes])
        if masked:
            low = below_diagonal(sh, p[size - sh.block :], 0.0)
            p = low if size == sh.block else jnp.concatenate([p[: size - sh.block], low], axis=0)
        ds = (p * (both[size:] - dot[:, lanes])).astype(BF16)
        dkv_s[0, rows, :] += nn(ds, qg[lanes, : sh.width])
        dkv_s[1, rows, :] += nn(p.astype(BF16), qg[lanes, sh.width :])
        dq_s[:, lanes] += nn(kt_s[:, rows], ds)


def backward_chunk(sh, me, back, qq, keys, distance, grads, lse, dots, dq, norm, order, held):
    w = sh.width
    opening, closing = norm is not None, distance == 0
    per = sh.rows // sh.block
    everyone = order == list(range(sh.parts))

    def kernel(me_ref, back_ref, *refs):
        refs = list(refs)

        def take(count):
            taken = refs[:count]
            del refs[:count]
            return taken

        qq_s, k_s, v_s, kt_s, lse_s = take(5)
        if opening:
            out_s, gain_ref, *sum_refs = take(2 + len(norm[0]))
        else:
            grad_s, dot_s, dq_in = take(3)
        (held_ref,) = take(1) if held is not None else (None,)
        (dkv_out,) = take(1)
        dq_out = take(len(order) if closing else 1)
        if opening:
            grad_s, dot_s = take(2)
        dkv_s, dq_own = (dkv_out, *refs) if closing else refs
        if held_ref is None:
            dkv_s[...] = jnp.zeros_like(dkv_s)

        def query_block(i):
            qb = i
            if not everyone:
                partner = functools.reduce(
                    lambda chosen, j: jnp.where(i // per == j, order[j], chosen),
                    range(len(order)),
                    order[0],
                )
                qb = jnp.bitwise_xor(me_ref[0], partner) * per + i % per
            dq_s = dq_own if closing else dq_out[0].at[qb]
            if opening:
                features = norm[2]
                token = functools.reduce(jnp.add, [ref[qb] for ref in sum_refs])
                sums = jnp.concatenate([token] * sh.group, axis=1)
                square = sums[0:1] / features + EPSILON
                inverse = lax.rsqrt(square)
                ratio = sums[1:2] / (features * square)
                again = (sums[3:4] - ratio * sums[2:3]) * inverse
                again = again / (features * square)
                plain = out_s[qb, :w, :]
                moved = out_s[qb, w:, :]
                first_grad = gain_ref[...] * (moved - plain * ratio) * inverse
                cot = ((first_grad - plain * again) * inverse).astype(BF16).astype(F32)
                dot_s[qb] = jnp.sum(cot * plain, axis=0, keepdims=True)
                grad_s[qb] = cot.T.astype(BF16)
                dq_s[...] = jnp.zeros((w, sh.lanes), F32)
            elif closing:
                dq_s[...] = dq_in[qb]

            top = sh.blocks if distance else qb + 1
            first = jnp.clip(qb - back_of(sh, me_ref, back_ref, qb) + distance * sh.blocks, 0, top)
            count = top - first

            @pl.when(count > 0)
            def _():
                qg = jnp.concatenate([qq_s[qb, :, :w], grad_s[qb]], axis=1)
                run = functools.partial(
                    backward_tile, sh, (k_s, v_s), kt_s, dkv_s, dq_s, qg, lse_s[qb], dot_s[qb]
                )
                by_count(sh, first, count, run, closing)

            if closing:
                done = (dq_s[...] * sh.scale).T.reshape(sh.group, sh.block, w).astype(BF16)
                at = pl.ds(pl.multiple_of(i % per * sh.block, sh.block), sh.block)
                for j, out in enumerate(dq_out):

                    @pl.when(i // per == j)
                    def _(out=out):
                        out[:, at, :] = done

        each_block(len(order) * per, query_block)
        if not closing:
            dkv_out[0] = (dkv_s[0] * sh.scale).astype(BF16)
            dkv_out[1] = dkv_s[1].astype(BF16)

    def array(*shape, dtype=F32):
        return jax.ShapeDtypeStruct(shape, dtype)

    operands = [qq, *keys, lse]
    if opening:
        operands += [grads, norm[1], *norm[0]]
    else:
        operands += [grads, dots, dq]
    aliases = {}
    if not opening and not closing:
        aliases = {1 + len(operands): 1}
    if held is not None:
        aliases = {2 + len(operands): 0}
        operands.append(held)
    out_shape = [array(2, sh.tokens, w, dtype=F32 if closing else BF16)]
    if closing:
        out_shape += [array(sh.group, sh.rows, w, dtype=BF16)] * len(order)
    else:
        out_shape.append(array(sh.blocks, w, sh.lanes))
    if opening:
        out_shape += [
            array(sh.blocks, sh.lanes, w, dtype=BF16),
            array(sh.blocks, 1, sh.lanes),
        ]
    work = sh.group * sh.tokens * len(order) * sh.rows // 2
    return pl.pallas_call(
        kernel,
        in_specs=[SMEM, SMEM] + [VMEM] * len(operands),
        out_specs=[VMEM] * len(out_shape),
        out_shape=out_shape,
        input_output_aliases=aliases,
        scratch_shapes=[pltpu.VMEM((2, sh.tokens, w), F32)] * (not closing)
        + [pltpu.VMEM((w, sh.lanes), F32)],
        compiler_params=params(),
        cost_estimate=cost(20 * work * w, 12 * len(order) * sh.rows * sh.lanes * 4, work),
        name="backward_chunk",
    )(me, back, *operands)


def combine(sh, me, arrived, held):
    count = len(arrived)

    def kernel(me_ref, held_ref, *refs):
        for m, out in enumerate(refs[count:]):
            slot = pl.ds(slot_of(me_ref, m, sh.rows), sh.rows)
            for a, factor in ((0, sh.scale), (1, 1.0)):
                part = held_ref[a, slot, :] * factor
                for ref in refs[:count]:
                    part += ref[a, slot, :].astype(F32)
                out[a] = part.astype(BF16)

    return pl.pallas_call(
        kernel,
        in_specs=[SMEM] + [VMEM] * (1 + count),
        out_specs=[VMEM] * sh.parts,
        out_shape=[jax.ShapeDtypeStruct((2, sh.rows, sh.width), BF16)] * sh.parts,
        compiler_params=params(),
        cost_estimate=cost(0, 1),
        name="combine",
    )(me, held, *arrived)


def exchanged(pieces):
    parts = len(pieces)
    return [pieces[0]] + [
        lax.ppermute(pieces[m], "part", [(i, i ^ m) for i in range(parts)])
        for m in range(1, parts)
    ]


def moved_on(value, steps):
    count = lax.axis_size("span")
    pairs = [(i, i + steps) for i in range(count) if 0 <= i + steps < count]
    return lax.ppermute(value, "span", pairs)


def shares(value):
    parts, heads = lax.axis_size("part"), lax.axis_size("head")
    count = parts * heads
    if count & (count - 1):
        return [lax.psum(value, ("part", "head"))]
    return [value] + [
        lax.ppermute(value, ("part", "head"), [(i, i ^ m) for i in range(count)])
        for m in range(count - 1, 0, -1)
    ]


def body(queries, keys, values, tangent_queries, tangent_keys, tangent_values, doc_start, out_gain):
    rows, query_heads, width = queries.shape
    key_heads = keys.shape[1]
    group = query_heads // key_heads
    parts = lax.axis_size("part")
    per = doc_start.shape[0]
    block = rows // per
    features = query_heads * width * lax.axis_size("head")
    hops = -(-DOC_DEVS // parts)
    sh = Shape(parts, group, rows, width, block)
    place = lax.axis_index("part")
    me = place.astype(jnp.int32).reshape(1)

    def flat(array):
        return array.reshape(-1, width)

    pieces = split_heads(
        [flat(a) for a in (keys, values, tangent_keys, tangent_values)], parts, 1, doc_start
    )
    q_rows, _ = lax.optimization_barrier(((flat(queries), flat(tangent_queries)), pieces[0]))
    q_pieces = split_heads(q_rows, parts, group)
    own = moved_on(pieces[0], 1)
    pieces = exchanged(pieces)
    chunks = [pieces]
    if parts > 1:
        own, q_pieces = lax.optimization_barrier((own, q_pieces))
        owns = [own]
        for _ in range(hops - 1):
            owns.append(moved_on(owns[-1], 1))
        late, owns = lax.optimization_barrier((pieces[1:], owns))
        rest = jnp.concatenate([moved_on(piece, 1) for piece in late], axis=0)
        chunks.append([owns[0], rest])
        for own in owns[1:]:
            rest = moved_on(rest, 1)
            chunks.append([own, rest])
    else:
        for _ in range(hops):
            chunks.append([own])
            own = moved_on(own, 1)
    q_parts = exchanged(q_pieces)
    back = jnp.concatenate([p[4 * rows : 4 * rows + per, 0] for p in pieces]).astype(jnp.int32)
    gain = lax.dynamic_index_in_dim(out_gain.reshape(key_heads, group, width), place, 0, False)
    gain_square = jnp.repeat((gain * gain).T, block, axis=1)

    state, spans = None, []
    for distance in range(hops):
        k, v, kt, acc, stat, *laid = forward_chunk(
            sh, me, back, [qq] if distance else q_parts, chunks[distance], distance, state
        )
        qq = laid[0] if laid else qq
        state = [acc, stat]
        spans.append((k, v, kt))
    k, v, kt, out, _, lse, sums = forward_chunk(
        sh, me, back, [qq], chunks[hops], hops, state, gain_square
    )
    spans.append((k, v, kt))
    norm = (shares(sums), gain_square, features)

    everyone = list(range(parts))
    part, dq, grads, dots = backward_chunk(
        sh, me, back, qq, spans[hops], hops, out, lse, None, None, norm, everyone, None
    )
    arrived = [moved_on(part, -hops)]
    for distance in range(hops - 1, 0, -1):
        part, dq = backward_chunk(
            sh, me, back, qq, spans[distance], distance, grads, lse, dots, dq, None,
            everyone, None,
        )
        arrived.append(moved_on(part, -distance))
    turns = [turn[::-1] for turn in (everyone[-1:], everyone[:-1]) if turn]
    held, dq_pieces = None, [None] * parts
    for order in turns:
        held, *done = backward_chunk(
            sh, me, back, qq, spans[0], 0, grads, lse, dots, dq, None, order, held
        )
        for m, piece in zip(order, done):
            dq_pieces[m] = piece.reshape(1, group, rows, width)
    dq_pieces = exchanged(dq_pieces)
    dq_pieces[-1], held = lax.optimization_barrier((dq_pieces[-1], held))
    dkv_pieces = exchanged(combine(sh, me, arrived, held))
    (product_queries,) = join_heads(dq_pieces, 1, group)
    dkv_pieces = [p.reshape(2, 1, rows, width) for p in dkv_pieces]
    product_keys, product_values = join_heads(dkv_pieces, 2, 1)
    return (
        product_queries.reshape(queries.shape),
        product_keys.reshape(keys.shape),
        product_values.reshape(keys.shape),
    )


def solution(mesh):
    def run(*arguments):
        count, heads = mesh.shape["ctx"], mesh.shape["head"]
        parts = arguments[1].shape[1] // heads
        split = Mesh(
            mesh.devices.reshape(count // parts, parts, heads), ("span", "part", "head")
        )
        ctx = ("span", "part")
        array = P(ctx, "head", None)
        return jax.shard_map(
            body,
            mesh=split,
            in_specs=(array,) * 6 + (P(ctx), P("head")),
            out_specs=(array,) * 3,
            check_vma=False,
        )(*arguments)

    return run
```

```python
import functools

import jax
import jax.numpy as jnp
from jax import lax
from jax.experimental import pallas as pl
from jax.experimental.pallas import tpu as pltpu
from jax.sharding import Mesh, PartitionSpec as P

DOC_DEVS = 8
EPSILON = 1e-06
VMEM_BYTES = 18 * 1024 * 1024
NOTE_ROWS = 16
ONES_ROWS = 16
WIDE_VMEM_BYTES = 60 * 1024 * 1024
MASKED = -1e30
F32 = jnp.float32
BF16 = jnp.bfloat16
SMEM = pl.BlockSpec(memory_space=pltpu.SMEM)
VMEM = pl.BlockSpec(memory_space=pltpu.VMEM)


def params(size=VMEM_BYTES):
    return pltpu.CompilerParams(vmem_limit_bytes=size)


def cost(flops, moved, powers=0):
    return pl.CostEstimate(flops=int(flops), bytes_accessed=int(moved), transcendentals=int(powers))


def nn(a, b):
    return lax.dot_general(a, b, (((1,), (0,)), ((), ())), preferred_element_type=F32)


def nt(a, b):
    return lax.dot_general(a, b, (((1,), (1,)), ((), ())), preferred_element_type=F32)


def split_heads(arrays, parts, per_part, notes=None):
    count = len(arrays)
    total, width = arrays[0].shape
    heads = parts * per_part
    rows = total // heads
    length = count * per_part * rows
    extra = 0 if notes is None else NOTE_ROWS
    scalars = [] if notes is None else [notes]

    def kernel(*refs):
        ins = list(refs[: len(scalars) + count])
        outs, (held, wide, sems) = refs[len(scalars) + count : -3], refs[-3:]
        mine = lax.axis_index("part")
        if extra:
            note_ref = ins.pop(0)
        copies = [pltpu.make_async_copy(ins[a], held.at[a], sems.at[a]) for a in range(count)]
        for copy in copies:
            copy.start()
        if extra:
            first = (lax.axis_index("span") * parts + mine) * notes.shape[0]
            line = lax.broadcasted_iota(jnp.int32, (extra, width), 0)
            lines = jnp.zeros((extra, width), jnp.int32)
            for i in range(notes.shape[0]):
                lines = jnp.where(line == i, first + i - note_ref[i], lines)
            for out in outs:
                out[length:, :] = lines.astype(F32).astype(BF16)
        for a in range(count):
            copies[a].wait()
            wide[...] = held[a].astype(F32)
            for m in range(parts):
                for r in range(per_part):
                    head = jnp.bitwise_xor(mine, m) * per_part + r
                    at = (a * per_part + r) * rows
                    outs[m][at : at + rows, :] = wide[pl.ds(head, rows, stride=heads), :].astype(BF16)

    return pl.pallas_call(
        kernel,
        in_specs=[SMEM] * len(scalars) + [pl.BlockSpec(memory_space=pltpu.HBM)] * count,
        out_specs=[pl.BlockSpec(memory_space=pltpu.VMEM)] * parts,
        out_shape=[jax.ShapeDtypeStruct((length + extra, width), BF16)] * parts,
        scratch_shapes=[
            pltpu.VMEM((count, total, width), BF16),
            pltpu.VMEM((total, width), F32),
            pltpu.SemaphoreType.DMA((count,)),
        ],
        compiler_params=params(VMEM_BYTES if notes is None else WIDE_VMEM_BYTES),
        cost_estimate=cost(0, 4 * count * total * width),
        name="split_heads",
    )(*scalars, *arrays)


def join_heads(pieces, count, per_part):
    parts = len(pieces)
    rows, width = pieces[0].shape[-2:]
    heads = parts * per_part

    steps = 4
    cut = rows // steps

    def kernel(*refs):
        ins, outs = refs[:parts], refs[parts:]
        mine = lax.axis_index("part")
        for a in range(count):
            for m in range(parts):
                for r in range(per_part):
                    head = jnp.bitwise_xor(mine, m) * per_part + r
                    outs[a][pl.ds(head, cut, stride=heads), :] = ins[m][a, r].astype(F32)

    return pl.pallas_call(
        kernel,
        grid=(steps,),
        in_specs=[pl.BlockSpec((count, per_part, cut, width), lambda i: (0, 0, i, 0))] * parts,
        out_specs=[pl.BlockSpec((cut * heads, width), lambda i: (i, 0))] * count,
        out_shape=[jax.ShapeDtypeStruct((rows * heads, width), F32)] * count,
        compiler_params=params(),
        cost_estimate=cost(0, 6 * count * rows * heads * width),
        name="join_heads",
    )(*pieces)


def slot_of(me_ref, m, rows):
    return pl.multiple_of(jnp.bitwise_xor(me_ref[0], m) * rows, rows)


class Shape:
    def __init__(self, parts, group, rows, width, block):
        self.parts, self.group, self.rows, self.width, self.block = parts, group, rows, width, block
        self.tokens = parts * rows
        self.blocks = self.tokens // block
        self.lanes = group * block
        self.scale = width**-0.5


def diagonal(sh):
    shape = (sh.block, sh.block)
    key = lax.broadcasted_iota(jnp.int32, shape, 0)
    query = lax.broadcasted_iota(jnp.int32, shape, 1)
    return key <= query


def below_diagonal(sh, value, other):
    allowed = diagonal(sh)
    cut = [value[:, at : at + sh.block] for at in range(0, value.shape[1], sh.block)]
    return jnp.concatenate([jnp.where(allowed, part, other) for part in cut], axis=1)


def halves(sh):
    if sh.group % 2:
        return [slice(0, sh.lanes)]
    return [slice(0, sh.lanes // 2), slice(sh.lanes // 2, sh.lanes)]


def stacked_keys(keys, start, size):
    k_s, tk_s = keys
    k = k_s[pl.ds(start, size), :]
    tk = tk_s[pl.ds(start, size), :]
    left = jnp.concatenate([k, tk], axis=0)
    right = jnp.concatenate([jnp.zeros_like(k), k], axis=0)
    return jnp.concatenate([left, right], axis=1)


def pieces_of(sh, start, blocks):
    sizes = [2] * (blocks // 2) + [1] * (blocks % 2)
    firsts = [sum(sizes[:i]) for i in range(len(sizes))]
    return [
        (pl.multiple_of(start + first * sh.block, sh.block), size * sh.block, i == len(sizes) - 1)
        for i, (first, size) in enumerate(zip(firsts, sizes))
    ]


def cut_diagonal(sh, value, other):
    low = below_diagonal(sh, value[value.shape[0] - sh.block :], other)
    if value.shape[0] == sh.block:
        return low
    return jnp.concatenate([value[: value.shape[0] - sh.block], low], axis=0)


def block_rows(sh, block):
    return pl.multiple_of(block * sh.block, sh.block)


def load_state(stat, lanes):
    return tuple(stat[r : r + 1, lanes] for r in range(3))


def forward_tile(sh, keys, vt_s, acc, stat, qq, block, blocks, masked):
    w = sh.width
    start = block_rows(sh, block)
    pieces = pieces_of(sh, start, blocks)
    stacked = [stacked_keys(keys, at, size) for at, size, _ in pieces]
    at = pl.ds(start, blocks * sh.block)
    lanes = halves(sh)
    scores = [[] for _ in lanes]
    mixed = [[] for _ in lanes]
    most = [None for _ in lanes]
    state = [None if masked else load_state(stat, part) for part in lanes]

    def score(h, c):
        both = nt(stacked[c], qq[lanes[h], :])
        s, d = both[: pieces[c][1]], both[pieces[c][1] :]
        if masked and pieces[c][2]:
            s = cut_diagonal(sh, s, MASKED)
        scores[h].append((s, d))

    def top(h):
        peaks = [jnp.max(s, axis=0, keepdims=True) for s, _ in scores[h]]
        most[h] = functools.reduce(jnp.maximum, peaks) * sh.scale
        if not masked:
            most[h] = jnp.maximum(most[h], state[h][0])

    def soften(h, c):
        s, d = scores[h][c]
        e = jnp.exp(s * sh.scale - most[h])
        mixed[h].append((e.astype(BF16), (e * d).astype(BF16)))

    def gather(h, i):
        return jnp.concatenate([pair[i] for pair in mixed[h]], axis=0)

    def finish(h, plain, moving):
        total, cross = plain[2 * w : 2 * w + 1], moving[w : w + 1]
        tangent = plain[:w] + moving[:w] * sh.scale
        plain = plain[w : 2 * w]
        if not masked:
            decay = jnp.exp(state[h][0] - most[h])
            plain = acc[:w, lanes[h]] * decay + plain
            tangent = acc[w:, lanes[h]] * decay + tangent
            total, cross = state[h][1] * decay + total, state[h][2] * decay + cross
        acc[:w, lanes[h]] = plain
        acc[w:, lanes[h]] = tangent
        for r, value in enumerate((most[h], total, cross)):
            stat[r : r + 1, lanes[h]] = value

    for h in range(len(lanes) + 1):
        if h > 0:
            top(h - 1)
        for c in range(len(pieces)):
            if h < len(lanes):
                score(h, c)
            if h > 0:
                soften(h - 1, c)
        if h > 0:
            plain = nn(vt_s[:, at], gather(h - 1, 0))
            moving = nn(vt_s[w:, at], gather(h - 1, 1))
            finish(h - 1, plain, moving)


def by_count(sh, low, count, run, masked):
    head = jnp.where(count <= 6, count, 3 + lax.rem(jnp.maximum(count - 7, 0), 4))
    fours = (count - head) // 4
    for blocks in range(1, min(6, sh.blocks) + 1):

        @pl.when(head == blocks)
        def _(blocks=blocks):
            if masked:
                run(low + count - blocks, blocks, True)
            else:
                run(low, blocks, False)

    def step(i, carry):
        run(low + (0 if masked else head) + 4 * i, 4, False)
        return carry

    if sh.blocks > 6:
        lax.fori_loop(0, fours, step, 0)


def lay_chunk(sh, me_ref, sources, targets):
    for m, (ref, base) in enumerate(sources):
        slot = pl.ds(slot_of(me_ref, m, sh.rows), sh.rows)
        for i, target in enumerate(targets):
            at = base + i * sh.rows
            target[slot, :] = ref[at : at + sh.rows, :]


def lay_queries(sh, me_ref, pieces, qq):
    per = sh.rows // sh.block
    for m, ref in enumerate(pieces):
        for i in range(2):
            for g in range(sh.group):
                for r in range(per):
                    block = jnp.bitwise_xor(me_ref[0], m) * per + r
                    at = (i * sh.group + g) * sh.rows + r * sh.block
                    qq[
                        block,
                        g * sh.block : (g + 1) * sh.block,
                        i * sh.width : (i + 1) * sh.width,
                    ] = ref[at : at + sh.block, :]


def transposed(x):
    return x.astype(F32).T.astype(BF16)


def located(sh, refs):
    length = refs[0].shape[0]
    return [(ref, at) for ref in refs for at in range(0, ref.shape[0], length)]


def back_of(sh, me_ref, back_ref, qb):
    per = sh.rows // sh.block
    return back_ref[jnp.bitwise_xor(me_ref[0], qb // per) * per + qb % per]


def each_block(count, run):
    def step(i, carry):
        run(i)
        return carry

    lax.fori_loop(0, count, step, 0)


def forward_chunk(sh, me, back, queries, chunk, distance, state, gain_square=None):
    w = sh.width
    kv = chunk
    opening, closing = state is None, gain_square is not None

    def kernel(me_ref, back_ref, *refs):
        refs = list(refs)

        def take(count):
            taken = refs[:count]
            del refs[:count]
            return taken

        q_in = take(len(queries))
        kv_in = take(len(kv))
        if not opening:
            take(2)
        if closing:
            (gain_ref,) = take(1)
        k_s, v_s, kt_s, accs, stats = take(5)
        if opening:
            (qq_s,) = take(1)
            lay_queries(sh, me_ref, q_in, qq_s)
        else:
            (qq_s,) = q_in
        if closing:
            lse, sums = take(2)
        tk_s, tv_s, vt_s = refs
        lay_chunk(sh, me_ref, located(sh, kv_in), (k_s, v_s, tk_s, tv_s))
        kt_s[...] = transposed(k_s[...])
        vt_s[:w, :] = transposed(tv_s[...])
        vt_s[w : 2 * w, :] = transposed(v_s[...])
        vt_s[2 * w :, :] = jnp.ones((ONES_ROWS, sh.tokens), BF16)

        def query_block(qb):
            acc, stat = accs.at[qb], stats.at[qb]
            top = sh.blocks if distance else qb + 1
            first = jnp.clip(qb - back_of(sh, me_ref, back_ref, qb) + distance * sh.blocks, 0, top)
            count = top - first

            @pl.when(count > 0)
            def _():
                run = functools.partial(
                    forward_tile, sh, (k_s, tk_s), vt_s, acc, stat, qq_s[qb]
                )
                by_count(sh, first, count, run, opening)

            if closing:
                most, total, cross = load_state(stat, slice(None))
                inverse = 1.0 / total
                plain = acc[:w, :] * inverse
                moved = acc[w:, :] * inverse - (cross * inverse * sh.scale) * plain
                acc[:w, :] = plain
                acc[w:, :] = moved
                lse[qb] = most + jnp.log(total)
                square = plain * plain
                product = plain * moved
                gain = gain_ref[...]
                for r, value in enumerate((square, product, gain * square, gain * product)):
                    line = jnp.sum(value, axis=0, keepdims=True)
                    pieces = [line[:, g * sh.block : (g + 1) * sh.block] for g in range(sh.group)]
                    sums[qb, r : r + 1, :] = functools.reduce(jnp.add, pieces)

        each_block(sh.blocks, query_block)

    def array(*shape, dtype=F32):
        return jax.ShapeDtypeStruct(shape, dtype)

    out_shape = [
        array(sh.tokens, w, dtype=BF16),
        array(sh.tokens, w, dtype=BF16),
        array(w, sh.tokens, dtype=BF16),
        array(sh.blocks, 2 * w, sh.lanes),
        array(sh.blocks, 8, sh.lanes),
    ]
    if opening:
        out_shape.append(array(sh.blocks, sh.lanes, 2 * w, dtype=BF16))
    if closing:
        out_shape += [array(sh.blocks, 1, sh.lanes), array(sh.blocks, 4, sh.block)]
    operands = [*queries, *kv]
    aliases = {}
    if not opening:
        aliases = {2 + len(operands): 3, 3 + len(operands): 4}
        operands += state
    if closing:
        operands.append(gain_square)
    work = sh.group * sh.tokens * sh.tokens // 2
    return pl.pallas_call(
        kernel,
        in_specs=[SMEM, SMEM] + [VMEM] * len(operands),
        out_specs=[VMEM] * len(out_shape),
        out_shape=out_shape,
        input_output_aliases=aliases,
        scratch_shapes=[
            pltpu.VMEM((sh.tokens, w), BF16),
            pltpu.VMEM((sh.tokens, w), BF16),
            pltpu.VMEM((2 * w + ONES_ROWS, sh.tokens), BF16),
        ],
        compiler_params=params(),
        cost_estimate=cost(24 * work * w, 12 * sh.tokens * sh.lanes * 2, work),
        name="forward_far" if closing else "forward_chunk",
    )(me, back, *operands)


def backward_tile(sh, keys, kt_s, dkv_s, dq_s, qg, lse, dot, block, blocks, masked):
    w = sh.width
    pieces = pieces_of(sh, block_rows(sh, block), blocks)
    items = [(lanes, piece) for lanes in halves(sh) for piece in pieces]
    k_s, v_s = keys
    scores, grads = {}, {}

    def score(i):
        lanes, (at, size, _) = items[i]
        k, v = k_s[pl.ds(at, size), :], v_s[pl.ds(at, size), :]
        empty = jnp.zeros_like(k)
        left = jnp.concatenate([k, empty], axis=0)
        right = jnp.concatenate([empty, v], axis=0)
        scores[i] = nt(jnp.concatenate([left, right], axis=1), qg[lanes, :])

    def soften(i):
        lanes, (_, size, ends) = items[i]
        p = jnp.exp(scores[i][:size] * sh.scale - lse[:, lanes])
        if masked and ends:
            p = cut_diagonal(sh, p, 0.0)
        ds = p * (scores[i][size:] - dot[:, lanes])
        grads[i] = (p.astype(BF16), ds.astype(BF16))

    def spread(i):
        lanes, (at, size, _) = items[i]
        p, ds = grads[i]
        rows = pl.ds(at, size)
        dkv_s[0, rows, :] += nn(ds, qg[lanes, :w])
        dkv_s[1, rows, :] += nn(p, qg[lanes, w:])
        dq_s[:, lanes] += nn(kt_s[:, rows], ds)

    for i in range(len(items) + 2):
        if i < len(items):
            score(i)
        if 0 < i <= len(items):
            soften(i - 1)
        if i > 1:
            spread(i - 2)


def backward_chunk(sh, me, back, qq, keys, distance, grads, lse, dots, dq, norm, order, held):
    w = sh.width
    opening, closing = norm is not None, distance == 0
    per = sh.rows // sh.block
    everyone = order == list(range(sh.parts))

    def kernel(me_ref, back_ref, *refs):
        refs = list(refs)

        def take(count):
            taken = refs[:count]
            del refs[:count]
            return taken

        qq_s, k_s, v_s, kt_s, lse_s = take(5)
        if opening:
            out_s, gain_ref, *sum_refs = take(2 + len(norm[0]))
        else:
            grad_s, dot_s, dq_in = take(3)
        (held_ref,) = take(1) if held is not None else (None,)
        (dkv_out,) = take(1)
        dq_out = take(len(order) if closing else 1)
        if opening:
            grad_s, dot_s = take(2)
        dkv_s, dq_own = (dkv_out, *refs) if closing else refs
        if held_ref is None:
            dkv_s[...] = jnp.zeros_like(dkv_s)

        def query_block(i):
            qb = i
            if not everyone:
                partner = functools.reduce(
                    lambda chosen, j: jnp.where(i // per == j, order[j], chosen),
                    range(len(order)),
                    order[0],
                )
                qb = jnp.bitwise_xor(me_ref[0], partner) * per + i % per
            dq_s = dq_own if closing else dq_out[0].at[qb]
            if opening:
                features = norm[2]
                token = functools.reduce(jnp.add, [ref[qb] for ref in sum_refs])
                sums = jnp.concatenate([token] * sh.group, axis=1)
                square = sums[0:1] / features + EPSILON
                inverse = lax.rsqrt(square)
                ratio = sums[1:2] / (features * square)
                again = (sums[3:4] - ratio * sums[2:3]) * inverse
                again = again / (features * square)
                plain = out_s[qb, :w, :]
                moved = out_s[qb, w:, :]
                first_grad = gain_ref[...] * (moved - plain * ratio) * inverse
                cot = ((first_grad - plain * again) * inverse).astype(BF16).astype(F32)
                dot_s[qb] = jnp.sum(cot * plain, axis=0, keepdims=True)
                grad_s[qb] = cot.T.astype(BF16)
                dq_s[...] = jnp.zeros((w, sh.lanes), F32)
            elif closing:
                dq_s[...] = dq_in[qb]

            top = sh.blocks if distance else qb + 1
            first = jnp.clip(qb - back_of(sh, me_ref, back_ref, qb) + distance * sh.blocks, 0, top)
            count = top - first

            @pl.when(count > 0)
            def _():
                qg = jnp.concatenate([qq_s[qb, :, :w], grad_s[qb]], axis=1)
                run = functools.partial(
                    backward_tile, sh, (k_s, v_s), kt_s, dkv_s, dq_s, qg, lse_s[qb], dot_s[qb]
                )
                by_count(sh, first, count, run, closing)

            if closing:
                done = (dq_s[...] * sh.scale).T.reshape(sh.group, sh.block, w).astype(BF16)
                at = pl.ds(pl.multiple_of(i % per * sh.block, sh.block), sh.block)
                for j, out in enumerate(dq_out):

                    @pl.when(i // per == j)
                    def _(out=out):
                        out[:, at, :] = done

        each_block(len(order) * per, query_block)
        if not closing:
            dkv_out[0] = (dkv_s[0] * sh.scale).astype(BF16)
            dkv_out[1] = dkv_s[1].astype(BF16)

    def array(*shape, dtype=F32):
        return jax.ShapeDtypeStruct(shape, dtype)

    operands = [qq, *keys, lse]
    if opening:
        operands += [grads, norm[1], *norm[0]]
    else:
        operands += [grads, dots, dq]
    aliases = {}
    if not opening and not closing:
        aliases = {1 + len(operands): 1}
    if held is not None:
        aliases = {2 + len(operands): 0}
        operands.append(held)
    out_shape = [array(2, sh.tokens, w, dtype=F32 if closing else BF16)]
    if closing:
        out_shape += [array(sh.group, sh.rows, w, dtype=BF16)] * len(order)
    else:
        out_shape.append(array(sh.blocks, w, sh.lanes))
    if opening:
        out_shape += [
            array(sh.blocks, sh.lanes, w, dtype=BF16),
            array(sh.blocks, 1, sh.lanes),
        ]
    work = sh.group * sh.tokens * len(order) * sh.rows // 2
    return pl.pallas_call(
        kernel,
        in_specs=[SMEM, SMEM] + [VMEM] * len(operands),
        out_specs=[VMEM] * len(out_shape),
        out_shape=out_shape,
        input_output_aliases=aliases,
        scratch_shapes=[pltpu.VMEM((2, sh.tokens, w), F32)] * (not closing)
        + [pltpu.VMEM((w, sh.lanes), F32)],
        compiler_params=params(),
        cost_estimate=cost(20 * work * w, 12 * len(order) * sh.rows * sh.lanes * 4, work),
        name="backward_chunk",
    )(me, back, *operands)


def combine(sh, me, arrived, held):
    count = len(arrived)

    def kernel(me_ref, held_ref, *refs):
        for m, out in enumerate(refs[count:]):
            slot = pl.ds(slot_of(me_ref, m, sh.rows), sh.rows)
            for a, factor in ((0, sh.scale), (1, 1.0)):
                part = held_ref[a, slot, :] * factor
                for ref in refs[:count]:
                    part += ref[a, slot, :].astype(F32)
                out[a] = part.astype(BF16)

    return pl.pallas_call(
        kernel,
        in_specs=[SMEM] + [VMEM] * (1 + count),
        out_specs=[VMEM] * sh.parts,
        out_shape=[jax.ShapeDtypeStruct((2, sh.rows, sh.width), BF16)] * sh.parts,
        compiler_params=params(),
        cost_estimate=cost(0, 1),
        name="combine",
    )(me, held, *arrived)


def exchanged(pieces):
    parts = len(pieces)
    return [pieces[0]] + [
        lax.ppermute(pieces[m], "part", [(i, i ^ m) for i in range(parts)])
        for m in range(1, parts)
    ]


def moved_on(value, steps):
    count = lax.axis_size("span")
    pairs = [(i, i + steps) for i in range(count) if 0 <= i + steps < count]
    return lax.ppermute(value, "span", pairs)


def summed_over_head(value):
    count = lax.axis_size("head")
    if count & (count - 1):
        return lax.psum(value, "head")
    step = 1
    while step < count:
        value = value + lax.ppermute(value, "head", [(i, i ^ step) for i in range(count)])
        step *= 2
    return value


def body(queries, keys, values, tangent_queries, tangent_keys, tangent_values, doc_start, out_gain):
    rows, query_heads, width = queries.shape
    key_heads = keys.shape[1]
    group = query_heads // key_heads
    parts = lax.axis_size("part")
    per = doc_start.shape[0]
    block = rows // per
    features = query_heads * width * lax.axis_size("head")
    hops = -(-DOC_DEVS // parts)
    sh = Shape(parts, group, rows, width, block)
    place = lax.axis_index("part")
    me = place.astype(jnp.int32).reshape(1)

    def flat(array):
        return array.reshape(-1, width)

    pieces = split_heads(
        [flat(a) for a in (keys, values, tangent_keys, tangent_values)], parts, 1, doc_start
    )
    q_rows, _ = lax.optimization_barrier(((flat(queries), flat(tangent_queries)), pieces[0]))
    q_pieces = split_heads(q_rows, parts, group)
    own = moved_on(pieces[0], 1)
    pieces = exchanged(pieces)
    chunks = [pieces]
    if parts > 1:
        own, q_pieces = lax.optimization_barrier((own, q_pieces))
        owns = [own]
        for _ in range(hops - 1):
            owns.append(moved_on(owns[-1], 1))
        late, owns = lax.optimization_barrier((pieces[1:], owns))
        rest = jnp.concatenate([moved_on(piece, 1) for piece in late], axis=0)
        chunks.append([owns[0], rest])
        for own in owns[1:]:
            rest = moved_on(rest, 1)
            chunks.append([own, rest])
    else:
        for _ in range(hops):
            chunks.append([own])
            own = moved_on(own, 1)
    q_parts = exchanged(q_pieces)
    back = jnp.concatenate([p[4 * rows : 4 * rows + per, 0] for p in pieces]).astype(jnp.int32)
    gain = lax.dynamic_index_in_dim(out_gain.reshape(key_heads, group, width), place, 0, False)
    gain_square = jnp.repeat((gain * gain).T, block, axis=1)

    state, spans = None, []
    for distance in range(hops):
        k, v, kt, acc, stat, *laid = forward_chunk(
            sh, me, back, [qq] if distance else q_parts, chunks[distance], distance, state
        )
        qq = laid[0] if laid else qq
        state = [acc, stat]
        spans.append((k, v, kt))
    k, v, kt, out, _, lse, sums = forward_chunk(
        sh, me, back, [qq], chunks[hops], hops, state, gain_square
    )
    spans.append((k, v, kt))
    norm = (exchanged([summed_over_head(sums)] * parts), gain_square, features)

    everyone = list(range(parts))
    part, dq, grads, dots = backward_chunk(
        sh, me, back, qq, spans[hops], hops, out, lse, None, None, norm, everyone, None
    )
    arrived = [moved_on(part, -hops)]
    for distance in range(hops - 1, 0, -1):
        part, dq = backward_chunk(
            sh, me, back, qq, spans[distance], distance, grads, lse, dots, dq, None,
            everyone, None,
        )
        arrived.append(moved_on(part, -distance))
    turns = [turn[::-1] for turn in (everyone[-1:], everyone[:-1]) if turn]
    held, dq_pieces = None, [None] * parts
    for order in turns:
        held, *done = backward_chunk(
            sh, me, back, qq, spans[0], 0, grads, lse, dots, dq, None, order, held
        )
        for m, piece in zip(order, done):
            dq_pieces[m] = piece.reshape(1, group, rows, width)
    dq_pieces = exchanged(dq_pieces)
    dq_pieces[-1], held = lax.optimization_barrier((dq_pieces[-1], held))
    dkv_pieces = exchanged(combine(sh, me, arrived, held))
    (product_queries,) = join_heads(dq_pieces, 1, group)
    dkv_pieces = [p.reshape(2, 1, rows, width) for p in dkv_pieces]
    product_keys, product_values = join_heads(dkv_pieces, 2, 1)
    return (
        product_queries.reshape(queries.shape),
        product_keys.reshape(keys.shape),
        product_values.reshape(keys.shape),
    )


def solution(mesh):
    def run(*arguments):
        count, heads = mesh.shape["ctx"], mesh.shape["head"]
        parts = arguments[1].shape[1] // heads
        split = Mesh(
            mesh.devices.reshape(count // parts, parts, heads), ("span", "part", "head")
        )
        ctx = ("span", "part")
        array = P(ctx, "head", None)
        return jax.shard_map(
            body,
            mesh=split,
            in_specs=(array,) * 6 + (P(ctx), P("head")),
            out_specs=(array,) * 3,
            check_vma=False,
        )(*arguments)

    return run
```

```python
import functools

import jax
import jax.numpy as jnp
from jax import lax
from jax.experimental import pallas as pl
from jax.experimental.pallas import tpu as pltpu
from jax.sharding import Mesh, PartitionSpec as P

DOC_DEVS = 8
EPSILON = 1e-06
VMEM_BYTES = 18 * 1024 * 1024
NOTE_ROWS = 16
ONES_ROWS = 16
WIDE_VMEM_BYTES = 60 * 1024 * 1024
MASKED = -1e30
F32 = jnp.float32
BF16 = jnp.bfloat16
SMEM = pl.BlockSpec(memory_space=pltpu.SMEM)
VMEM = pl.BlockSpec(memory_space=pltpu.VMEM)


def params(size=VMEM_BYTES):
    return pltpu.CompilerParams(vmem_limit_bytes=size)


def cost(flops, moved, powers=0):
    return pl.CostEstimate(flops=int(flops), bytes_accessed=int(moved), transcendentals=int(powers))


def nn(a, b):
    return lax.dot_general(a, b, (((1,), (0,)), ((), ())), preferred_element_type=F32)


def nt(a, b):
    return lax.dot_general(a, b, (((1,), (1,)), ((), ())), preferred_element_type=F32)


def split_heads(arrays, parts, per_part, notes=None):
    count = len(arrays)
    total, width = arrays[0].shape
    heads = parts * per_part
    rows = total // heads
    length = count * per_part * rows
    extra = 0 if notes is None else NOTE_ROWS
    scalars = [] if notes is None else [notes]

    def kernel(*refs):
        ins = list(refs[: len(scalars) + count])
        outs, (held, wide, sems) = refs[len(scalars) + count : -3], refs[-3:]
        mine = lax.axis_index("part")
        if extra:
            note_ref = ins.pop(0)
        copies = [pltpu.make_async_copy(ins[a], held.at[a], sems.at[a]) for a in range(count)]
        for copy in copies:
            copy.start()
        if extra:
            first = (lax.axis_index("span") * parts + mine) * notes.shape[0]
            line = lax.broadcasted_iota(jnp.int32, (extra, width), 0)
            lines = jnp.zeros((extra, width), jnp.int32)
            for i in range(notes.shape[0]):
                lines = jnp.where(line == i, first + i - note_ref[i], lines)
            for out in outs:
                out[length:, :] = lines.astype(F32).astype(BF16)
        for a in range(count):
            copies[a].wait()
            wide[...] = held[a].astype(F32)
            for m in range(parts):
                for r in range(per_part):
                    head = jnp.bitwise_xor(mine, m) * per_part + r
                    at = (a * per_part + r) * rows
                    outs[m][at : at + rows, :] = wide[pl.ds(head, rows, stride=heads), :].astype(BF16)

    return pl.pallas_call(
        kernel,
        in_specs=[SMEM] * len(scalars) + [pl.BlockSpec(memory_space=pltpu.HBM)] * count,
        out_specs=[pl.BlockSpec(memory_space=pltpu.VMEM)] * parts,
        out_shape=[jax.ShapeDtypeStruct((length + extra, width), BF16)] * parts,
        scratch_shapes=[
            pltpu.VMEM((count, total, width), BF16),
            pltpu.VMEM((total, width), F32),
            pltpu.SemaphoreType.DMA((count,)),
        ],
        compiler_params=params(VMEM_BYTES if notes is None else WIDE_VMEM_BYTES),
        cost_estimate=cost(0, 4 * count * total * width),
        name="split_heads",
    )(*scalars, *arrays)


def join_heads(pieces, count, per_part):
    parts = len(pieces)
    rows, width = pieces[0].shape[-2:]
    heads = parts * per_part

    steps = 4
    cut = rows // steps

    def kernel(*refs):
        ins, outs = refs[:parts], refs[parts:]
        mine = lax.axis_index("part")
        for a in range(count):
            for m in range(parts):
                for r in range(per_part):
                    head = jnp.bitwise_xor(mine, m) * per_part + r
                    outs[a][pl.ds(head, cut, stride=heads), :] = ins[m][a, r].astype(F32)

    return pl.pallas_call(
        kernel,
        grid=(steps,),
        in_specs=[pl.BlockSpec((count, per_part, cut, width), lambda i: (0, 0, i, 0))] * parts,
        out_specs=[pl.BlockSpec((cut * heads, width), lambda i: (i, 0))] * count,
        out_shape=[jax.ShapeDtypeStruct((rows * heads, width), F32)] * count,
        compiler_params=params(),
        cost_estimate=cost(0, 6 * count * rows * heads * width),
        name="join_heads",
    )(*pieces)


def slot_of(me_ref, m, rows):
    return pl.multiple_of(jnp.bitwise_xor(me_ref[0], m) * rows, rows)


class Shape:
    def __init__(self, parts, group, rows, width, block):
        self.parts, self.group, self.rows, self.width, self.block = parts, group, rows, width, block
        self.tokens = parts * rows
        self.blocks = self.tokens // block
        self.lanes = group * block
        self.scale = width**-0.5


def diagonal(sh):
    shape = (sh.block, sh.block)
    key = lax.broadcasted_iota(jnp.int32, shape, 0)
    query = lax.broadcasted_iota(jnp.int32, shape, 1)
    return key <= query


def below_diagonal(sh, value, other):
    allowed = diagonal(sh)
    cut = [value[:, at : at + sh.block] for at in range(0, value.shape[1], sh.block)]
    return jnp.concatenate([jnp.where(allowed, part, other) for part in cut], axis=1)


def halves(sh):
    if sh.group % 2:
        return [slice(0, sh.lanes)]
    return [slice(0, sh.lanes // 2), slice(sh.lanes // 2, sh.lanes)]


def stacked_keys(keys, start, size):
    k_s, tk_s = keys
    k = k_s[pl.ds(start, size), :]
    tk = tk_s[pl.ds(start, size), :]
    left = jnp.concatenate([k, tk], axis=0)
    right = jnp.concatenate([jnp.zeros_like(k), k], axis=0)
    return jnp.concatenate([left, right], axis=1)


def pieces_of(sh, start, blocks):
    sizes = [2] * (blocks // 2) + [1] * (blocks % 2)
    firsts = [sum(sizes[:i]) for i in range(len(sizes))]
    return [
        (pl.multiple_of(start + first * sh.block, sh.block), size * sh.block, i == len(sizes) - 1)
        for i, (first, size) in enumerate(zip(firsts, sizes))
    ]


def cut_diagonal(sh, value, other):
    low = below_diagonal(sh, value[value.shape[0] - sh.block :], other)
    if value.shape[0] == sh.block:
        return low
    return jnp.concatenate([value[: value.shape[0] - sh.block], low], axis=0)


def block_rows(sh, block):
    return pl.multiple_of(block * sh.block, sh.block)


def load_state(stat, lanes):
    return tuple(stat[r : r + 1, lanes] for r in range(3))


def forward_tile(sh, keys, vt_s, acc, stat, qq, block, blocks, masked):
    w = sh.width
    start = block_rows(sh, block)
    pieces = pieces_of(sh, start, blocks)
    stacked = [stacked_keys(keys, at, size) for at, size, _ in pieces]
    at = pl.ds(start, blocks * sh.block)
    lanes = halves(sh)
    scores = [[] for _ in lanes]
    mixed = [[] for _ in lanes]
    most = [None for _ in lanes]
    state = [None if masked else load_state(stat, part) for part in lanes]

    def score(h, c):
        both = nt(stacked[c], qq[lanes[h], :])
        s, d = both[: pieces[c][1]], both[pieces[c][1] :]
        if masked and pieces[c][2]:
            s = cut_diagonal(sh, s, MASKED)
        scores[h].append((s, d))

    def top(h):
        peaks = [jnp.max(s, axis=0, keepdims=True) for s, _ in scores[h]]
        most[h] = functools.reduce(jnp.maximum, peaks) * sh.scale
        if not masked:
            most[h] = jnp.maximum(most[h], state[h][0])

    def soften(h, c):
        s, d = scores[h][c]
        e = jnp.exp(s * sh.scale - most[h])
        mixed[h].append((e.astype(BF16), (e * d).astype(BF16)))

    def gather(h, i):
        return jnp.concatenate([pair[i] for pair in mixed[h]], axis=0)

    def finish(h, plain, moving):
        total, cross = plain[2 * w : 2 * w + 1], moving[w : w + 1]
        tangent = plain[:w] + moving[:w] * sh.scale
        plain = plain[w : 2 * w]
        if not masked:
            decay = jnp.exp(state[h][0] - most[h])
            plain = acc[:w, lanes[h]] * decay + plain
            tangent = acc[w:, lanes[h]] * decay + tangent
            total, cross = state[h][1] * decay + total, state[h][2] * decay + cross
        acc[:w, lanes[h]] = plain
        acc[w:, lanes[h]] = tangent
        for r, value in enumerate((most[h], total, cross)):
            stat[r : r + 1, lanes[h]] = value

    for h in range(len(lanes) + 1):
        if h > 0:
            top(h - 1)
        for c in range(len(pieces)):
            if h < len(lanes):
                score(h, c)
            if h > 0:
                soften(h - 1, c)
        if h > 0:
            plain = nn(vt_s[:, at], gather(h - 1, 0))
            moving = nn(vt_s[w:, at], gather(h - 1, 1))
            finish(h - 1, plain, moving)


def by_count(sh, low, count, run, masked):
    head = jnp.where(count <= 6, count, 3 + lax.rem(jnp.maximum(count - 7, 0), 4))
    fours = (count - head) // 4
    for blocks in range(1, min(6, sh.blocks) + 1):

        @pl.when(head == blocks)
        def _(blocks=blocks):
            if masked:
                run(low + count - blocks, blocks, True)
            else:
                run(low, blocks, False)

    def step(i, carry):
        run(low + (0 if masked else head) + 4 * i, 4, False)
        return carry

    if sh.blocks > 6:
        lax.fori_loop(0, fours, step, 0)


def lay_chunk(sh, me_ref, sources, targets):
    for m, (ref, base) in enumerate(sources):
        slot = pl.ds(slot_of(me_ref, m, sh.rows), sh.rows)
        for i, target in enumerate(targets):
            at = base + i * sh.rows
            target[slot, :] = ref[at : at + sh.rows, :]


def lay_queries(sh, me_ref, order, pieces, qq):
    per = sh.rows // sh.block
    for m, ref in zip(order, pieces):
        for i in range(2):
            for g in range(sh.group):
                for r in range(per):
                    block = jnp.bitwise_xor(me_ref[0], m) * per + r
                    at = (i * sh.group + g) * sh.rows + r * sh.block
                    qq[
                        block,
                        g * sh.block : (g + 1) * sh.block,
                        i * sh.width : (i + 1) * sh.width,
                    ] = ref[at : at + sh.block, :]


def lay_span(sh, me_ref, sources, laid):
    w = sh.width
    k_s, v_s, kt_s, tk_s, vt_s, tv_s = laid
    lay_chunk(sh, me_ref, sources, (k_s, v_s, tk_s, tv_s))
    kt_s[...] = transposed(k_s[...])
    vt_s[:w, :] = transposed(tv_s[...])
    vt_s[w : 2 * w, :] = transposed(v_s[...])
    vt_s[2 * w :, :] = jnp.ones((ONES_ROWS, sh.tokens), BF16)


def transposed(x):
    return x.astype(F32).T.astype(BF16)


def located(sh, refs):
    length = refs[0].shape[0]
    return [(ref, at) for ref in refs for at in range(0, ref.shape[0], length)]


def back_of(sh, me_ref, back_ref, qb):
    per = sh.rows // sh.block
    return back_ref[jnp.bitwise_xor(me_ref[0], qb // per) * per + qb % per]


def each_block(count, run):
    def step(i, carry):
        run(i)
        return carry

    lax.fori_loop(0, count, step, 0)


def block_in_turn(sh, me_ref, order, i):
    per = sh.rows // sh.block
    if order == list(range(sh.parts)):
        return i
    partner = order[0]
    for j in range(1, len(order)):
        partner = jnp.where(i // per == j, order[j], partner)
    return jnp.bitwise_xor(me_ref[0], partner) * per + i % per


def forward_own(sh, me, back, order, queries, chunk, before):
    w = sh.width
    first = before is None
    turns = len(order) * (sh.rows // sh.block)

    def kernel(me_ref, back_ref, *refs):
        refs = list(refs)

        def take(count):
            taken = refs[:count]
            del refs[:count]
            return taken

        q_in = take(len(order))
        if first:
            kv_in = take(len(chunk))
            accs, stats, qq_s = take(3)
            laid = refs
            lay_span(sh, me_ref, located(sh, kv_in), laid)
        else:
            laid = take(len(chunk))
            take(3)
            accs, stats, qq_s = refs
        k_s, _, _, tk_s, vt_s = laid[:5]
        lay_queries(sh, me_ref, order, q_in, qq_s)

        def query_block(i):
            qb = block_in_turn(sh, me_ref, order, i)
            low = jnp.clip(qb - back_of(sh, me_ref, back_ref, qb), 0, qb)
            run = functools.partial(
                forward_tile, sh, (k_s, tk_s), vt_s, accs.at[qb], stats.at[qb], qq_s[qb]
            )
            by_count(sh, low, qb + 1 - low, run, True)

        each_block(turns, query_block)

    def array(*shape, dtype=F32):
        return jax.ShapeDtypeStruct(shape, dtype)

    span = array(sh.tokens, w, dtype=BF16)
    out_shape = [
        array(sh.blocks, 2 * w, sh.lanes),
        array(sh.blocks, 8, sh.lanes),
        array(sh.blocks, sh.lanes, 2 * w, dtype=BF16),
    ]
    operands = [*queries, *chunk]
    aliases = {}
    if first:
        out_shape += [span, span, array(w, sh.tokens, dtype=BF16), span]
        out_shape.append(array(2 * w + ONES_ROWS, sh.tokens, dtype=BF16))
    else:
        aliases = {2 + len(operands) + i: i for i in range(3)}
        operands += before
    work = sh.group * sh.tokens * sh.block * turns // 2
    return pl.pallas_call(
        kernel,
        in_specs=[SMEM, SMEM] + [VMEM] * len(operands),
        out_specs=[VMEM] * len(out_shape),
        out_shape=out_shape,
        input_output_aliases=aliases,
        scratch_shapes=[pltpu.VMEM((sh.tokens, w), BF16)] * first,
        compiler_params=params(),
        cost_estimate=cost(12 * work * w, 4 * sh.tokens * sh.lanes, work),
        name="forward_own",
    )(me, back, *operands)


def forward_chunk(sh, me, back, qq, chunk, distance, state, gain_square=None):
    w = sh.width
    closing = gain_square is not None

    def kernel(me_ref, back_ref, qq_s, *refs):
        refs = list(refs)

        def take(count):
            taken = refs[:count]
            del refs[:count]
            return taken

        kv_in = take(len(chunk))
        take(2)
        if closing:
            (gain_ref,) = take(1)
        k_s, v_s, kt_s, accs, stats = take(5)
        if closing:
            lse, sums = take(2)
        tk_s, tv_s, vt_s = refs
        lay_span(sh, me_ref, located(sh, kv_in), (k_s, v_s, kt_s, tk_s, vt_s, tv_s))

        def query_block(qb):
            acc, stat = accs.at[qb], stats.at[qb]
            first = qb - back_of(sh, me_ref, back_ref, qb) + distance * sh.blocks
            first = jnp.clip(first, 0, sh.blocks)
            count = sh.blocks - first

            @pl.when(count > 0)
            def _():
                run = functools.partial(
                    forward_tile, sh, (k_s, tk_s), vt_s, acc, stat, qq_s[qb]
                )
                by_count(sh, first, count, run, False)

            if closing:
                most, total, cross = load_state(stat, slice(None))
                inverse = 1.0 / total
                plain = acc[:w, :] * inverse
                moved = acc[w:, :] * inverse - (cross * inverse * sh.scale) * plain
                acc[:w, :] = plain
                acc[w:, :] = moved
                lse[qb] = most + jnp.log(total)
                square = plain * plain
                product = plain * moved
                gain = gain_ref[...]
                for r, value in enumerate((square, product, gain * square, gain * product)):
                    line = jnp.sum(value, axis=0, keepdims=True)
                    pieces = [line[:, g * sh.block : (g + 1) * sh.block] for g in range(sh.group)]
                    sums[qb, r : r + 1, :] = functools.reduce(jnp.add, pieces)

        each_block(sh.blocks, query_block)

    def array(*shape, dtype=F32):
        return jax.ShapeDtypeStruct(shape, dtype)

    out_shape = [
        array(sh.tokens, w, dtype=BF16),
        array(sh.tokens, w, dtype=BF16),
        array(w, sh.tokens, dtype=BF16),
        array(sh.blocks, 2 * w, sh.lanes),
        array(sh.blocks, 8, sh.lanes),
    ]
    if closing:
        out_shape += [array(sh.blocks, 1, sh.lanes), array(sh.blocks, 4, sh.block)]
    operands = [qq, *chunk]
    aliases = {2 + len(operands): 3, 3 + len(operands): 4}
    operands += state
    if closing:
        operands.append(gain_square)
    work = sh.group * sh.tokens * sh.tokens // 2
    return pl.pallas_call(
        kernel,
        in_specs=[SMEM, SMEM] + [VMEM] * len(operands),
        out_specs=[VMEM] * len(out_shape),
        out_shape=out_shape,
        input_output_aliases=aliases,
        scratch_shapes=[
            pltpu.VMEM((sh.tokens, w), BF16),
            pltpu.VMEM((sh.tokens, w), BF16),
            pltpu.VMEM((2 * w + ONES_ROWS, sh.tokens), BF16),
        ],
        compiler_params=params(),
        cost_estimate=cost(24 * work * w, 12 * sh.tokens * sh.lanes * 2, work),
        name="forward_far" if closing else "forward_chunk",
    )(me, back, *operands)


def backward_tile(sh, keys, kt_s, dkv_s, dq_s, qg, lse, dot, block, blocks, masked):
    start, size = block_rows(sh, block), blocks * sh.block
    rows = pl.ds(start, size)
    k_s, v_s = keys
    k, v = k_s[rows, :], v_s[rows, :]
    empty = jnp.zeros_like(k)
    left = jnp.concatenate([k, empty], axis=0)
    right = jnp.concatenate([empty, v], axis=0)
    stacked = jnp.concatenate([left, right], axis=1)
    scores = [nt(stacked, qg[lanes, :]) for lanes in halves(sh)]
    for lanes, both in zip(halves(sh), scores):
        p = jnp.exp(both[:size] * sh.scale - lse[:, lanes])
        if masked:
            p = cut_diagonal(sh, p, 0.0)
        ds = (p * (both[size:] - dot[:, lanes])).astype(BF16)
        dkv_s[0, rows, :] += nn(ds, qg[lanes, : sh.width])
        dkv_s[1, rows, :] += nn(p.astype(BF16), qg[lanes, sh.width :])
        dq_s[:, lanes] += nn(kt_s[:, rows], ds)


def backward_chunk(sh, me, back, qq, keys, distance, grads, lse, dots, dq, norm, order, held):
    w = sh.width
    opening, closing = norm is not None, distance == 0
    per = sh.rows // sh.block

    def kernel(me_ref, back_ref, *refs):
        refs = list(refs)

        def take(count):
            taken = refs[:count]
            del refs[:count]
            return taken

        qq_s, k_s, v_s, kt_s, lse_s = take(5)
        if opening:
            out_s, gain_ref, *sum_refs = take(2 + len(norm[0]))
        else:
            grad_s, dot_s, dq_in = take(3)
        (held_ref,) = take(1) if held is not None else (None,)
        (dkv_out,) = take(1)
        dq_out = take(len(order) if closing else 1)
        if opening:
            grad_s, dot_s = take(2)
        dkv_s, dq_own = (dkv_out, *refs) if closing else refs
        if held_ref is None:
            dkv_s[...] = jnp.zeros_like(dkv_s)

        def query_block(i):
            qb = block_in_turn(sh, me_ref, order, i)
            dq_s = dq_own if closing else dq_out[0].at[qb]
            if opening:
                features = norm[2]
                token = functools.reduce(jnp.add, [ref[qb] for ref in sum_refs])
                sums = jnp.concatenate([token] * sh.group, axis=1)
                square = sums[0:1] / features + EPSILON
                inverse = lax.rsqrt(square)
                ratio = sums[1:2] / (features * square)
                again = (sums[3:4] - ratio * sums[2:3]) * inverse
                again = again / (features * square)
                plain = out_s[qb, :w, :]
                moved = out_s[qb, w:, :]
                first_grad = gain_ref[...] * (moved - plain * ratio) * inverse
                cot = ((first_grad - plain * again) * inverse).astype(BF16).astype(F32)
                dot_s[qb] = jnp.sum(cot * plain, axis=0, keepdims=True)
                grad_s[qb] = cot.T.astype(BF16)
                dq_s[...] = jnp.zeros((w, sh.lanes), F32)
            elif closing:
                dq_s[...] = dq_in[qb]

            top = sh.blocks if distance else qb + 1
            first = jnp.clip(qb - back_of(sh, me_ref, back_ref, qb) + distance * sh.blocks, 0, top)
            count = top - first

            @pl.when(count > 0)
            def _():
                qg = jnp.concatenate([qq_s[qb, :, :w], grad_s[qb]], axis=1)
                run = functools.partial(
                    backward_tile, sh, (k_s, v_s), kt_s, dkv_s, dq_s, qg, lse_s[qb], dot_s[qb]
                )
                by_count(sh, first, count, run, closing)

            if closing:
                done = (dq_s[...] * sh.scale).T.reshape(sh.group, sh.block, w).astype(BF16)
                at = pl.ds(pl.multiple_of(i % per * sh.block, sh.block), sh.block)
                for j, out in enumerate(dq_out):

                    @pl.when(i // per == j)
                    def _(out=out):
                        out[:, at, :] = done

        each_block(len(order) * per, query_block)
        if not closing:
            dkv_out[0] = (dkv_s[0] * sh.scale).astype(BF16)
            dkv_out[1] = dkv_s[1].astype(BF16)

    def array(*shape, dtype=F32):
        return jax.ShapeDtypeStruct(shape, dtype)

    operands = [qq, *keys, lse]
    if opening:
        operands += [grads, norm[1], *norm[0]]
    else:
        operands += [grads, dots, dq]
    aliases = {}
    if not opening and not closing:
        aliases = {1 + len(operands): 1}
    if held is not None:
        aliases = {2 + len(operands): 0}
        operands.append(held)
    out_shape = [array(2, sh.tokens, w, dtype=F32 if closing else BF16)]
    if closing:
        out_shape += [array(sh.group, sh.rows, w, dtype=BF16)] * len(order)
    else:
        out_shape.append(array(sh.blocks, w, sh.lanes))
    if opening:
        out_shape += [
            array(sh.blocks, sh.lanes, w, dtype=BF16),
            array(sh.blocks, 1, sh.lanes),
        ]
    work = sh.group * sh.tokens * len(order) * sh.rows // 2
    return pl.pallas_call(
        kernel,
        in_specs=[SMEM, SMEM] + [VMEM] * len(operands),
        out_specs=[VMEM] * len(out_shape),
        out_shape=out_shape,
        input_output_aliases=aliases,
        scratch_shapes=[pltpu.VMEM((2, sh.tokens, w), F32)] * (not closing)
        + [pltpu.VMEM((w, sh.lanes), F32)],
        compiler_params=params(),
        cost_estimate=cost(20 * work * w, 12 * len(order) * sh.rows * sh.lanes * 4, work),
        name="backward_chunk",
    )(me, back, *operands)


def combine(sh, me, arrived, held):
    count = len(arrived)

    def kernel(me_ref, held_ref, *refs):
        for m, out in enumerate(refs[count:]):
            slot = pl.ds(slot_of(me_ref, m, sh.rows), sh.rows)
            for a, factor in ((0, sh.scale), (1, 1.0)):
                part = held_ref[a, slot, :] * factor
                for ref in refs[:count]:
                    part += ref[a, slot, :].astype(F32)
                out[a] = part.astype(BF16)

    return pl.pallas_call(
        kernel,
        in_specs=[SMEM] + [VMEM] * (1 + count),
        out_specs=[VMEM] * sh.parts,
        out_shape=[jax.ShapeDtypeStruct((2, sh.rows, sh.width), BF16)] * sh.parts,
        compiler_params=params(),
        cost_estimate=cost(0, 1),
        name="combine",
    )(me, held, *arrived)


def exchanged_with(piece, parts, m):
    return lax.ppermute(piece, "part", [(i, i ^ m) for i in range(parts)]) if m else piece


def exchanged(pieces, parts):
    return [exchanged_with(piece, parts, m) for m, piece in enumerate(pieces)]


def moved_on(value, steps):
    count = lax.axis_size("span")
    pairs = [(i, i + steps) for i in range(count) if 0 <= i + steps < count]
    return lax.ppermute(value, "span", pairs)


def summed_over_head(value):
    count = lax.axis_size("head")
    if count & (count - 1):
        return lax.psum(value, "head")
    step = 1
    while step < count:
        value = value + lax.ppermute(value, "head", [(i, i ^ step) for i in range(count)])
        step *= 2
    return value


def body(queries, keys, values, tangent_queries, tangent_keys, tangent_values, doc_start, out_gain):
    rows, query_heads, width = queries.shape
    key_heads = keys.shape[1]
    group = query_heads // key_heads
    parts = lax.axis_size("part")
    per = doc_start.shape[0]
    block = rows // per
    features = query_heads * width * lax.axis_size("head")
    hops = -(-DOC_DEVS // parts)
    sh = Shape(parts, group, rows, width, block)
    place = lax.axis_index("part")
    me = place.astype(jnp.int32).reshape(1)

    def flat(array):
        return array.reshape(-1, width)

    pieces = split_heads(
        [flat(a) for a in (keys, values, tangent_keys, tangent_values)], parts, 1, doc_start
    )
    q_rows, _ = lax.optimization_barrier(((flat(queries), flat(tangent_queries)), pieces[0]))
    q_pieces = split_heads(q_rows, parts, group)
    own = moved_on(pieces[0], 1)
    pieces = exchanged(pieces, parts)
    chunks = [pieces]
    if parts > 1:
        own, q_pieces = lax.optimization_barrier((own, q_pieces))
        owns = [own]
        for _ in range(hops - 1):
            owns.append(moved_on(owns[-1], 1))
        late, owns = lax.optimization_barrier((pieces[1:], owns))
        rest = jnp.concatenate([moved_on(piece, 1) for piece in late], axis=0)
        chunks.append([owns[0], rest])
        for own in owns[1:]:
            rest = moved_on(rest, 1)
            chunks.append([own, rest])
    else:
        for _ in range(hops):
            chunks.append([own])
            own = moved_on(own, 1)
    q_parts = exchanged(q_pieces[:-1], parts)
    if parts > 1:
        last, _ = lax.optimization_barrier((q_pieces[-1], q_parts[min(1, parts - 2)]))
        q_parts.append(exchanged_with(last, parts, parts - 1))
    else:
        q_parts = q_pieces
    back = jnp.concatenate([p[4 * rows : 4 * rows + per, 0] for p in pieces]).astype(jnp.int32)
    gain = lax.dynamic_index_in_dim(out_gain.reshape(key_heads, group, width), place, 0, False)
    gain_square = jnp.repeat((gain * gain).T, block, axis=1)

    everyone = list(range(parts))
    before, laid = None, chunks[0]
    for order in [everyone[:1], everyone[1:-1], everyone[-1:]] if parts > 1 else [everyone]:
        if order:
            turn = forward_own(sh, me, back, order, [q_parts[m] for m in order], laid, before)
            laid = turn[3:] or laid
            before = list(turn[:3])
    *state, qq = before
    spans = [tuple(laid[:3])]
    for distance in range(1, hops):
        k, v, kt, *state = forward_chunk(sh, me, back, qq, chunks[distance], distance, state)
        spans.append((k, v, kt))
    k, v, kt, out, _, lse, sums = forward_chunk(
        sh, me, back, qq, chunks[hops], hops, state, gain_square
    )
    spans.append((k, v, kt))
    norm = (exchanged([summed_over_head(sums)] * parts, parts), gain_square, features)

    part, dq, grads, dots = backward_chunk(
        sh, me, back, qq, spans[hops], hops, out, lse, None, None, norm, everyone, None
    )
    arrived = [moved_on(part, -hops)]
    for distance in range(hops - 1, 0, -1):
        part, dq = backward_chunk(
            sh, me, back, qq, spans[distance], distance, grads, lse, dots, dq, None,
            everyone, None,
        )
        arrived.append(moved_on(part, -distance))
    turns = [turn[::-1] for turn in (everyone[-1:], everyone[:-1]) if turn]
    held, dq_pieces = None, [None] * parts
    for order in turns:
        held, *done = backward_chunk(
            sh, me, back, qq, spans[0], 0, grads, lse, dots, dq, None, order, held
        )
        for m, piece in zip(order, done):
            dq_pieces[m] = piece.reshape(1, group, rows, width)
    dq_pieces = exchanged(dq_pieces, parts)
    dq_pieces[-1], held = lax.optimization_barrier((dq_pieces[-1], held))
    dkv_pieces = exchanged(combine(sh, me, arrived, held), parts)
    (product_queries,) = join_heads(dq_pieces, 1, group)
    dkv_pieces = [p.reshape(2, 1, rows, width) for p in dkv_pieces]
    product_keys, product_values = join_heads(dkv_pieces, 2, 1)
    return (
        product_queries.reshape(queries.shape),
        product_keys.reshape(keys.shape),
        product_values.reshape(keys.shape),
    )


def solution(mesh):
    def run(*arguments):
        count, heads = mesh.shape["ctx"], mesh.shape["head"]
        parts = arguments[1].shape[1] // heads
        split = Mesh(
            mesh.devices.reshape(count // parts, parts, heads), ("span", "part", "head")
        )
        ctx = ("span", "part")
        array = P(ctx, "head", None)
        return jax.shard_map(
            body,
            mesh=split,
            in_specs=(array,) * 6 + (P(ctx), P("head")),
            out_specs=(array,) * 3,
            check_vma=False,
        )(*arguments)

    return run
```

```python
import functools

import jax
import jax.numpy as jnp
from jax import lax
from jax.experimental import pallas as pl
from jax.experimental.pallas import tpu as pltpu
from jax.sharding import Mesh, PartitionSpec as P

DOC_DEVS = 8
EPSILON = 1e-06
VMEM_BYTES = 18 * 1024 * 1024
NOTE_ROWS = 16
ONES_ROWS = 16
WIDE_VMEM_BYTES = 60 * 1024 * 1024
MASKED = -1e30
F32 = jnp.float32
BF16 = jnp.bfloat16
SMEM = pl.BlockSpec(memory_space=pltpu.SMEM)
VMEM = pl.BlockSpec(memory_space=pltpu.VMEM)


def params(size=VMEM_BYTES):
    return pltpu.CompilerParams(vmem_limit_bytes=size)


def cost(flops, moved, powers=0):
    return pl.CostEstimate(flops=int(flops), bytes_accessed=int(moved), transcendentals=int(powers))


def nn(a, b):
    return lax.dot_general(a, b, (((1,), (0,)), ((), ())), preferred_element_type=F32)


def nt(a, b):
    return lax.dot_general(a, b, (((1,), (1,)), ((), ())), preferred_element_type=F32)


def split_heads(arrays, parts, per_part, notes=None):
    count = len(arrays)
    total, width = arrays[0].shape
    heads = parts * per_part
    rows = total // heads
    length = count * per_part * rows
    extra = 0 if notes is None else NOTE_ROWS
    scalars = [] if notes is None else [notes]

    def kernel(*refs):
        ins = list(refs[: len(scalars) + count])
        outs, (held, wide, sems) = refs[len(scalars) + count : -3], refs[-3:]
        mine = lax.axis_index("part")
        if extra:
            note_ref = ins.pop(0)
        copies = [pltpu.make_async_copy(ins[a], held.at[a], sems.at[a]) for a in range(count)]
        for copy in copies:
            copy.start()
        if extra:
            first = (lax.axis_index("span") * parts + mine) * notes.shape[0]
            line = lax.broadcasted_iota(jnp.int32, (extra, width), 0)
            lines = jnp.zeros((extra, width), jnp.int32)
            for i in range(notes.shape[0]):
                lines = jnp.where(line == i, first + i - note_ref[i], lines)
            for out in outs:
                out[length:, :] = lines.astype(F32).astype(BF16)
        for a in range(count):
            copies[a].wait()
            wide[...] = held[a].astype(F32)
            for m in range(parts):
                for r in range(per_part):
                    head = jnp.bitwise_xor(mine, m) * per_part + r
                    at = (a * per_part + r) * rows
                    outs[m][at : at + rows, :] = wide[pl.ds(head, rows, stride=heads), :].astype(BF16)

    return pl.pallas_call(
        kernel,
        in_specs=[SMEM] * len(scalars) + [pl.BlockSpec(memory_space=pltpu.HBM)] * count,
        out_specs=[pl.BlockSpec(memory_space=pltpu.VMEM)] * parts,
        out_shape=[jax.ShapeDtypeStruct((length + extra, width), BF16)] * parts,
        scratch_shapes=[
            pltpu.VMEM((count, total, width), BF16),
            pltpu.VMEM((total, width), F32),
            pltpu.SemaphoreType.DMA((count,)),
        ],
        compiler_params=params(VMEM_BYTES if notes is None else WIDE_VMEM_BYTES),
        cost_estimate=cost(0, 4 * count * total * width),
        name="split_heads",
    )(*scalars, *arrays)


def join_heads(pieces, count, per_part):
    parts = len(pieces)
    rows, width = pieces[0].shape[-2:]
    heads = parts * per_part

    steps = 4
    cut = rows // steps

    def kernel(*refs):
        ins, outs = refs[:parts], refs[parts:]
        mine = lax.axis_index("part")
        for a in range(count):
            for m in range(parts):
                for r in range(per_part):
                    head = jnp.bitwise_xor(mine, m) * per_part + r
                    outs[a][pl.ds(head, cut, stride=heads), :] = ins[m][a, r].astype(F32)

    return pl.pallas_call(
        kernel,
        grid=(steps,),
        in_specs=[pl.BlockSpec((count, per_part, cut, width), lambda i: (0, 0, i, 0))] * parts,
        out_specs=[pl.BlockSpec((cut * heads, width), lambda i: (i, 0))] * count,
        out_shape=[jax.ShapeDtypeStruct((rows * heads, width), F32)] * count,
        compiler_params=params(),
        cost_estimate=cost(0, 6 * count * rows * heads * width),
        name="join_heads",
    )(*pieces)


def slot_of(me_ref, m, rows):
    return pl.multiple_of(jnp.bitwise_xor(me_ref[0], m) * rows, rows)


class Shape:
    def __init__(self, parts, group, rows, width, block):
        self.parts, self.group, self.rows, self.width, self.block = parts, group, rows, width, block
        self.tokens = parts * rows
        self.blocks = self.tokens // block
        self.lanes = group * block
        self.scale = width**-0.5


def diagonal(sh):
    shape = (sh.block, sh.block)
    key = lax.broadcasted_iota(jnp.int32, shape, 0)
    query = lax.broadcasted_iota(jnp.int32, shape, 1)
    return key <= query


def below_diagonal(sh, value, other):
    allowed = diagonal(sh)
    cut = [value[:, at : at + sh.block] for at in range(0, value.shape[1], sh.block)]
    return jnp.concatenate([jnp.where(allowed, part, other) for part in cut], axis=1)


def halves(sh):
    if sh.group % 2:
        return [slice(0, sh.lanes)]
    return [slice(0, sh.lanes // 2), slice(sh.lanes // 2, sh.lanes)]


def stacked_keys(keys, start, size):
    k_s, tk_s = keys
    k = k_s[pl.ds(start, size), :]
    tk = tk_s[pl.ds(start, size), :]
    left = jnp.concatenate([k, tk], axis=0)
    right = jnp.concatenate([jnp.zeros_like(k), k], axis=0)
    return jnp.concatenate([left, right], axis=1)


def pieces_of(sh, start, blocks):
    sizes = [2] * (blocks // 2) + [1] * (blocks % 2)
    firsts = [sum(sizes[:i]) for i in range(len(sizes))]
    return [
        (pl.multiple_of(start + first * sh.block, sh.block), size * sh.block, i == len(sizes) - 1)
        for i, (first, size) in enumerate(zip(firsts, sizes))
    ]


def cut_diagonal(sh, value, other):
    low = below_diagonal(sh, value[value.shape[0] - sh.block :], other)
    if value.shape[0] == sh.block:
        return low
    return jnp.concatenate([value[: value.shape[0] - sh.block], low], axis=0)


def block_rows(sh, block):
    return pl.multiple_of(block * sh.block, sh.block)


def load_state(stat, lanes):
    return tuple(stat[r : r + 1, lanes] for r in range(3))


def forward_tile(sh, keys, vt_s, acc, stat, kept, qq, block, blocks, masked):
    w = sh.width
    start = block_rows(sh, block)
    pieces = pieces_of(sh, start, blocks)
    stacked = [stacked_keys(keys, at, size) for at, size, _ in pieces]
    at = pl.ds(start, blocks * sh.block)
    lanes = halves(sh)
    scores = [[] for _ in lanes]
    mixed = [[] for _ in lanes]
    most = [None for _ in lanes]
    state = [None if masked else load_state(stat, part) for part in lanes]

    def score(h, c):
        both = nt(stacked[c], qq[lanes[h], :])
        s, d = both[: pieces[c][1]], both[pieces[c][1] :]
        if masked and pieces[c][2]:
            s = cut_diagonal(sh, s, MASKED)
        scores[h].append((s, d))

    def top(h):
        peaks = [jnp.max(s, axis=0, keepdims=True) for s, _ in scores[h]]
        most[h] = functools.reduce(jnp.maximum, peaks) * sh.scale
        if not masked:
            most[h] = jnp.maximum(most[h], state[h][0])
        if kept is not None:
            for j in range(blocks):
                kept[1][block + j, :, lanes[h]] = most[h]

    def soften(h, c):
        s, d = scores[h][c]
        e = jnp.exp(s * sh.scale - most[h])
        mixed[h].append((e.astype(BF16), (e * d).astype(BF16)))
        if kept is not None:
            kept[0][pl.ds(pieces[c][0], pieces[c][1]), lanes[h]] = mixed[h][-1][0]

    def gather(h, i):
        return jnp.concatenate([pair[i] for pair in mixed[h]], axis=0)

    def finish(h, plain, moving):
        total, cross = plain[2 * w : 2 * w + 1], moving[w : w + 1]
        tangent = plain[:w] + moving[:w] * sh.scale
        plain = plain[w : 2 * w]
        if not masked:
            decay = jnp.exp(state[h][0] - most[h])
            plain = acc[:w, lanes[h]] * decay + plain
            tangent = acc[w:, lanes[h]] * decay + tangent
            total, cross = state[h][1] * decay + total, state[h][2] * decay + cross
        acc[:w, lanes[h]] = plain
        acc[w:, lanes[h]] = tangent
        for r, value in enumerate((most[h], total, cross)):
            stat[r : r + 1, lanes[h]] = value

    for h in range(len(lanes) + 1):
        if h > 0:
            top(h - 1)
        for c in range(len(pieces)):
            if h < len(lanes):
                score(h, c)
            if h > 0:
                soften(h - 1, c)
        if h > 0:
            plain = nn(vt_s[:, at], gather(h - 1, 0))
            moving = nn(vt_s[w:, at], gather(h - 1, 1))
            finish(h - 1, plain, moving)


def by_count(sh, low, count, run, masked):
    head = jnp.where(count <= 6, count, 3 + lax.rem(jnp.maximum(count - 7, 0), 4))
    fours = (count - head) // 4
    for blocks in range(1, min(6, sh.blocks) + 1):

        @pl.when(head == blocks)
        def _(blocks=blocks):
            if masked:
                run(low + count - blocks, blocks, True)
            else:
                run(low, blocks, False)

    def step(i, carry):
        run(low + (0 if masked else head) + 4 * i, 4, False)
        return carry

    if sh.blocks > 6:
        lax.fori_loop(0, fours, step, 0)


def lay_chunk(sh, me_ref, sources, targets):
    for m, (ref, base) in enumerate(sources):
        slot = pl.ds(slot_of(me_ref, m, sh.rows), sh.rows)
        for i, target in enumerate(targets):
            at = base + i * sh.rows
            target[slot, :] = ref[at : at + sh.rows, :]


def lay_queries(sh, me_ref, order, pieces, qq):
    per = sh.rows // sh.block
    for m, ref in zip(order, pieces):
        for i in range(2):
            for g in range(sh.group):
                for r in range(per):
                    block = jnp.bitwise_xor(me_ref[0], m) * per + r
                    at = (i * sh.group + g) * sh.rows + r * sh.block
                    qq[
                        block,
                        g * sh.block : (g + 1) * sh.block,
                        i * sh.width : (i + 1) * sh.width,
                    ] = ref[at : at + sh.block, :]


def lay_span(sh, me_ref, sources, laid):
    w = sh.width
    k_s, v_s, kt_s, tk_s, vt_s, tv_s = laid
    lay_chunk(sh, me_ref, sources, (k_s, v_s, tk_s, tv_s))
    kt_s[...] = transposed(k_s[...])
    vt_s[:w, :] = transposed(tv_s[...])
    vt_s[w : 2 * w, :] = transposed(v_s[...])
    vt_s[2 * w :, :] = jnp.ones((ONES_ROWS, sh.tokens), BF16)


def transposed(x):
    return x.astype(F32).T.astype(BF16)


def located(sh, refs):
    length = refs[0].shape[0]
    return [(ref, at) for ref in refs for at in range(0, ref.shape[0], length)]


def back_of(sh, me_ref, back_ref, qb):
    per = sh.rows // sh.block
    return back_ref[jnp.bitwise_xor(me_ref[0], qb // per) * per + qb % per]


def each_block(count, run):
    def step(i, carry):
        run(i)
        return carry

    lax.fori_loop(0, count, step, 0)


def block_in_turn(sh, me_ref, order, i):
    per = sh.rows // sh.block
    if order == list(range(sh.parts)):
        return i
    partner = order[0]
    for j in range(1, len(order)):
        partner = jnp.where(i // per == j, order[j], partner)
    return jnp.bitwise_xor(me_ref[0], partner) * per + i % per


def kept_shapes(sh):
    return [
        jax.ShapeDtypeStruct((sh.blocks, sh.tokens, sh.lanes), BF16),
        jax.ShapeDtypeStruct((sh.blocks, sh.blocks, 1, sh.lanes), F32),
    ]


def forward_own(sh, me, back, order, queries, chunk, before):
    w = sh.width
    first = before is None
    turns = len(order) * (sh.rows // sh.block)

    def kernel(me_ref, back_ref, *refs):
        refs = list(refs)

        def take(count):
            taken = refs[:count]
            del refs[:count]
            return taken

        q_in = take(len(order))
        if first:
            kv_in = take(len(chunk))
            accs, stats, qq_s, es, ms = take(5)
            laid = refs
            lay_span(sh, me_ref, located(sh, kv_in), laid)
        else:
            laid = take(len(chunk))
            take(5)
            accs, stats, qq_s, es, ms = refs
        k_s, _, _, tk_s, vt_s = laid[:5]
        lay_queries(sh, me_ref, order, q_in, qq_s)

        def query_block(i):
            qb = block_in_turn(sh, me_ref, order, i)
            low = jnp.clip(qb - back_of(sh, me_ref, back_ref, qb), 0, qb)
            run = functools.partial(
                forward_tile,
                sh,
                (k_s, tk_s),
                vt_s,
                accs.at[qb],
                stats.at[qb],
                (es.at[qb], ms.at[qb]),
                qq_s[qb],
            )
            by_count(sh, low, qb + 1 - low, run, True)

        each_block(turns, query_block)

    def array(*shape, dtype=F32):
        return jax.ShapeDtypeStruct(shape, dtype)

    span = array(sh.tokens, w, dtype=BF16)
    out_shape = [
        array(sh.blocks, 2 * w, sh.lanes),
        array(sh.blocks, 8, sh.lanes),
        array(sh.blocks, sh.lanes, 2 * w, dtype=BF16),
        *kept_shapes(sh),
    ]
    operands = [*queries, *chunk]
    aliases = {}
    if first:
        out_shape += [span, span, array(w, sh.tokens, dtype=BF16), span]
        out_shape.append(array(2 * w + ONES_ROWS, sh.tokens, dtype=BF16))
    else:
        aliases = {2 + len(operands) + i: i for i in range(5)}
        operands += before
    work = sh.group * sh.tokens * sh.block * turns // 2
    return pl.pallas_call(
        kernel,
        in_specs=[SMEM, SMEM] + [VMEM] * len(operands),
        out_specs=[VMEM] * len(out_shape),
        out_shape=out_shape,
        input_output_aliases=aliases,
        scratch_shapes=[pltpu.VMEM((sh.tokens, w), BF16)] * first,
        compiler_params=params(),
        cost_estimate=cost(12 * work * w, 4 * sh.tokens * sh.lanes, work),
        name="forward_own",
    )(me, back, *operands)


def forward_chunk(sh, me, back, qq, chunk, distance, state, gain_square=None):
    w = sh.width
    closing = gain_square is not None

    def kernel(me_ref, back_ref, qq_s, *refs):
        refs = list(refs)

        def take(count):
            taken = refs[:count]
            del refs[:count]
            return taken

        kv_in = take(len(chunk))
        take(2)
        if closing:
            (gain_ref,) = take(1)
        k_s, v_s, kt_s, accs, stats = take(5)
        last = take(2)
        if closing:
            lse, sums = last
        tk_s, tv_s, vt_s = refs
        lay_span(sh, me_ref, located(sh, kv_in), (k_s, v_s, kt_s, tk_s, vt_s, tv_s))

        def query_block(qb):
            acc, stat = accs.at[qb], stats.at[qb]
            first = qb - back_of(sh, me_ref, back_ref, qb) + distance * sh.blocks
            first = jnp.clip(first, 0, sh.blocks)
            count = sh.blocks - first

            @pl.when(count > 0)
            def _():
                kept = None if closing else [ref.at[qb] for ref in last]
                run = functools.partial(
                    forward_tile, sh, (k_s, tk_s), vt_s, acc, stat, kept, qq_s[qb]
                )
                by_count(sh, first, count, run, False)

            if closing:
                most, total, cross = load_state(stat, slice(None))
                inverse = 1.0 / total
                plain = acc[:w, :] * inverse
                moved = acc[w:, :] * inverse - (cross * inverse * sh.scale) * plain
                acc[:w, :] = plain
                acc[w:, :] = moved
                lse[qb] = most + jnp.log(total)
                square = plain * plain
                product = plain * moved
                gain = gain_ref[...]
                for r, value in enumerate((square, product, gain * square, gain * product)):
                    line = jnp.sum(value, axis=0, keepdims=True)
                    pieces = [line[:, g * sh.block : (g + 1) * sh.block] for g in range(sh.group)]
                    sums[qb, r : r + 1, :] = functools.reduce(jnp.add, pieces)

        each_block(sh.blocks, query_block)

    def array(*shape, dtype=F32):
        return jax.ShapeDtypeStruct(shape, dtype)

    out_shape = [
        array(sh.tokens, w, dtype=BF16),
        array(sh.tokens, w, dtype=BF16),
        array(w, sh.tokens, dtype=BF16),
        array(sh.blocks, 2 * w, sh.lanes),
        array(sh.blocks, 8, sh.lanes),
    ]
    if closing:
        out_shape += [array(sh.blocks, 1, sh.lanes), array(sh.blocks, 4, sh.block)]
    else:
        out_shape += kept_shapes(sh)
    operands = [qq, *chunk]
    aliases = {2 + len(operands): 3, 3 + len(operands): 4}
    operands += state
    if closing:
        operands.append(gain_square)
    work = sh.group * sh.tokens * sh.tokens // 2
    return pl.pallas_call(
        kernel,
        in_specs=[SMEM, SMEM] + [VMEM] * len(operands),
        out_specs=[VMEM] * len(out_shape),
        out_shape=out_shape,
        input_output_aliases=aliases,
        scratch_shapes=[
            pltpu.VMEM((sh.tokens, w), BF16),
            pltpu.VMEM((sh.tokens, w), BF16),
            pltpu.VMEM((2 * w + ONES_ROWS, sh.tokens), BF16),
        ],
        compiler_params=params(),
        cost_estimate=cost(24 * work * w, 12 * sh.tokens * sh.lanes * 2, work),
        name="forward_far" if closing else "forward_chunk",
    )(me, back, *operands)


def backward_tile(sh, keys, kt_s, dkv_s, dq_s, qg, lse, dot, block, blocks, _):
    start, size = block_rows(sh, block), blocks * sh.block
    rows = pl.ds(start, size)
    k_s, v_s = keys
    k, v = k_s[rows, :], v_s[rows, :]
    empty = jnp.zeros_like(k)
    left = jnp.concatenate([k, empty], axis=0)
    right = jnp.concatenate([empty, v], axis=0)
    stacked = jnp.concatenate([left, right], axis=1)
    scores = [nt(stacked, qg[lanes, :]) for lanes in halves(sh)]
    for lanes, both in zip(halves(sh), scores):
        p = jnp.exp(both[:size] * sh.scale - lse[:, lanes])
        ds = (p * (both[size:] - dot[:, lanes])).astype(BF16)
        dkv_s[0, rows, :] += nn(ds, qg[lanes, : sh.width])
        dkv_s[1, rows, :] += nn(p.astype(BF16), qg[lanes, sh.width :])
        dq_s[:, lanes] += nn(kt_s[:, rows], ds)


def backward_kept(sh, keys, kt_s, dkv_s, dq_s, qg, lse, dot, kept, block, blocks, _):
    start, size = block_rows(sh, block), blocks * sh.block
    rows = pl.ds(start, size)
    v = keys[1][rows, :]
    slopes = [nt(v, qg[lanes, sh.width :]) for lanes in halves(sh)]
    for lanes, slope in zip(halves(sh), slopes):
        parts = []
        for j in range(blocks):
            factor = jnp.exp(kept[1][block + j, :, lanes] - lse[:, lanes])
            at = pl.ds(block_rows(sh, block + j), sh.block)
            parts.append(kept[0][at, lanes].astype(F32) * factor)
        p = jnp.concatenate(parts, axis=0)
        ds = (p * (slope - dot[:, lanes])).astype(BF16)
        dkv_s[0, rows, :] += nn(ds, qg[lanes, : sh.width])
        dkv_s[1, rows, :] += nn(p.astype(BF16), qg[lanes, sh.width :])
        dq_s[:, lanes] += nn(kt_s[:, rows], ds)


def backward_chunk(sh, me, back, qq, keys, distance, grads, lse, dots, dq, norm, order, held):
    w = sh.width
    opening, closing = norm is not None, distance == 0
    per = sh.rows // sh.block

    def kernel(me_ref, back_ref, *refs):
        refs = list(refs)

        def take(count):
            taken = refs[:count]
            del refs[:count]
            return taken

        qq_s, k_s, v_s, kt_s = take(4)
        kept = take(len(keys) - 3)
        (lse_s,) = take(1)
        if opening:
            out_s, gain_ref, *sum_refs = take(2 + len(norm[0]))
        else:
            grad_s, dot_s, dq_in = take(3)
        (held_ref,) = take(1) if held is not None else (None,)
        (dkv_out,) = take(1)
        dq_out = take(len(order) if closing else 1)
        if opening:
            grad_s, dot_s = take(2)
        dkv_s, dq_own = (dkv_out, *refs) if closing else refs
        if held_ref is None:
            dkv_s[...] = jnp.zeros_like(dkv_s)

        def query_block(i):
            qb = block_in_turn(sh, me_ref, order, i)
            dq_s = dq_own if closing else dq_out[0].at[qb]
            if opening:
                features = norm[2]
                token = functools.reduce(jnp.add, [ref[qb] for ref in sum_refs])
                sums = jnp.concatenate([token] * sh.group, axis=1)
                square = sums[0:1] / features + EPSILON
                inverse = lax.rsqrt(square)
                ratio = sums[1:2] / (features * square)
                again = (sums[3:4] - ratio * sums[2:3]) * inverse
                again = again / (features * square)
                plain = out_s[qb, :w, :]
                moved = out_s[qb, w:, :]
                first_grad = gain_ref[...] * (moved - plain * ratio) * inverse
                cot = ((first_grad - plain * again) * inverse).astype(BF16).astype(F32)
                dot_s[qb] = jnp.sum(cot * plain, axis=0, keepdims=True)
                grad_s[qb] = cot.T.astype(BF16)
                dq_s[...] = jnp.zeros((w, sh.lanes), F32)
            elif closing:
                dq_s[...] = dq_in[qb]

            top = sh.blocks if distance else qb + 1
            first = jnp.clip(qb - back_of(sh, me_ref, back_ref, qb) + distance * sh.blocks, 0, top)
            count = top - first

            @pl.when(count > 0)
            def _():
                qg = jnp.concatenate([qq_s[qb, :, :w], grad_s[qb]], axis=1)
                common = (sh, (k_s, v_s), kt_s, dkv_s, dq_s, qg, lse_s[qb], dot_s[qb])
                if kept:
                    run = functools.partial(backward_kept, *common, [ref.at[qb] for ref in kept])
                else:
                    run = functools.partial(backward_tile, *common)
                by_count(sh, first, count, run, False)

            if closing:
                done = (dq_s[...] * sh.scale).T.reshape(sh.group, sh.block, w).astype(BF16)
                at = pl.ds(pl.multiple_of(i % per * sh.block, sh.block), sh.block)
                for j, out in enumerate(dq_out):

                    @pl.when(i // per == j)
                    def _(out=out):
                        out[:, at, :] = done

        each_block(len(order) * per, query_block)
        if not closing:
            dkv_out[0] = (dkv_s[0] * sh.scale).astype(BF16)
            dkv_out[1] = dkv_s[1].astype(BF16)

    def array(*shape, dtype=F32):
        return jax.ShapeDtypeStruct(shape, dtype)

    operands = [qq, *keys, lse]
    if opening:
        operands += [grads, norm[1], *norm[0]]
    else:
        operands += [grads, dots, dq]
    aliases = {}
    if not opening and not closing:
        aliases = {1 + len(operands): 1}
    if held is not None:
        aliases = {2 + len(operands): 0}
        operands.append(held)
    out_shape = [array(2, sh.tokens, w, dtype=F32 if closing else BF16)]
    if closing:
        out_shape += [array(sh.group, sh.rows, w, dtype=BF16)] * len(order)
    else:
        out_shape.append(array(sh.blocks, w, sh.lanes))
    if opening:
        out_shape += [
            array(sh.blocks, sh.lanes, w, dtype=BF16),
            array(sh.blocks, 1, sh.lanes),
        ]
    work = sh.group * sh.tokens * len(order) * sh.rows // 2
    return pl.pallas_call(
        kernel,
        in_specs=[SMEM, SMEM] + [VMEM] * len(operands),
        out_specs=[VMEM] * len(out_shape),
        out_shape=out_shape,
        input_output_aliases=aliases,
        scratch_shapes=[pltpu.VMEM((2, sh.tokens, w), F32)] * (not closing)
        + [pltpu.VMEM((w, sh.lanes), F32)],
        compiler_params=params(),
        cost_estimate=cost(20 * work * w, 12 * len(order) * sh.rows * sh.lanes * 4, work),
        name="backward_chunk",
    )(me, back, *operands)


def combine(sh, me, arrived, held):
    count = len(arrived)

    def kernel(me_ref, held_ref, *refs):
        for m, out in enumerate(refs[count:]):
            slot = pl.ds(slot_of(me_ref, m, sh.rows), sh.rows)
            for a, factor in ((0, sh.scale), (1, 1.0)):
                part = held_ref[a, slot, :] * factor
                for ref in refs[:count]:
                    part += ref[a, slot, :].astype(F32)
                out[a] = part.astype(BF16)

    return pl.pallas_call(
        kernel,
        in_specs=[SMEM] + [VMEM] * (1 + count),
        out_specs=[VMEM] * sh.parts,
        out_shape=[jax.ShapeDtypeStruct((2, sh.rows, sh.width), BF16)] * sh.parts,
        compiler_params=params(),
        cost_estimate=cost(0, 1),
        name="combine",
    )(me, held, *arrived)


def exchanged_with(piece, parts, m):
    return lax.ppermute(piece, "part", [(i, i ^ m) for i in range(parts)]) if m else piece


def exchanged(pieces, parts):
    return [exchanged_with(piece, parts, m) for m, piece in enumerate(pieces)]


def moved_on(value, steps):
    count = lax.axis_size("span")
    pairs = [(i, i + steps) for i in range(count) if 0 <= i + steps < count]
    return lax.ppermute(value, "span", pairs)


def summed_over_head(value):
    count = lax.axis_size("head")
    if count & (count - 1):
        return lax.psum(value, "head")
    step = 1
    while step < count:
        value = value + lax.ppermute(value, "head", [(i, i ^ step) for i in range(count)])
        step *= 2
    return value


def body(queries, keys, values, tangent_queries, tangent_keys, tangent_values, doc_start, out_gain):
    rows, query_heads, width = queries.shape
    key_heads = keys.shape[1]
    group = query_heads // key_heads
    parts = lax.axis_size("part")
    per = doc_start.shape[0]
    block = rows // per
    features = query_heads * width * lax.axis_size("head")
    hops = -(-DOC_DEVS // parts)
    sh = Shape(parts, group, rows, width, block)
    place = lax.axis_index("part")
    me = place.astype(jnp.int32).reshape(1)

    def flat(array):
        return array.reshape(-1, width)

    pieces = split_heads(
        [flat(a) for a in (keys, values, tangent_keys, tangent_values)], parts, 1, doc_start
    )
    q_rows, _ = lax.optimization_barrier(((flat(queries), flat(tangent_queries)), pieces[0]))
    q_pieces = split_heads(q_rows, parts, group)
    own = moved_on(pieces[0], 1)
    pieces = exchanged(pieces, parts)
    chunks = [pieces]
    if parts > 1:
        own, q_pieces = lax.optimization_barrier((own, q_pieces))
        owns = [own]
        for _ in range(hops - 1):
            owns.append(moved_on(owns[-1], 1))
        late, owns = lax.optimization_barrier((pieces[1:], owns))
        rest = jnp.concatenate([moved_on(piece, 1) for piece in late], axis=0)
        chunks.append([owns[0], rest])
        for own in owns[1:]:
            rest = moved_on(rest, 1)
            chunks.append([own, rest])
    else:
        for _ in range(hops):
            chunks.append([own])
            own = moved_on(own, 1)
    q_parts = exchanged(q_pieces[:-1], parts)
    if parts > 1:
        last, _ = lax.optimization_barrier((q_pieces[-1], q_parts[min(1, parts - 2)]))
        q_parts.append(exchanged_with(last, parts, parts - 1))
    else:
        q_parts = q_pieces
    back = jnp.concatenate([p[4 * rows : 4 * rows + per, 0] for p in pieces]).astype(jnp.int32)
    gain = lax.dynamic_index_in_dim(out_gain.reshape(key_heads, group, width), place, 0, False)
    gain_square = jnp.repeat((gain * gain).T, block, axis=1)

    everyone = list(range(parts))
    before, laid = None, chunks[0]
    for order in [everyone[:1], everyone[1:-1], everyone[-1:]] if parts > 1 else [everyone]:
        if order:
            turn = forward_own(sh, me, back, order, [q_parts[m] for m in order], laid, before)
            laid = turn[5:] or laid
            before = list(turn[:5])
    state, qq = before[:2], before[2]
    spans = [(*laid[:3], *before[3:])]
    for distance in range(1, hops):
        k, v, kt, acc, stat, *kept = forward_chunk(
            sh, me, back, qq, chunks[distance], distance, state
        )
        state = [acc, stat]
        spans.append((k, v, kt, *kept))
    k, v, kt, out, _, lse, sums = forward_chunk(
        sh, me, back, qq, chunks[hops], hops, state, gain_square
    )
    spans.append((k, v, kt))
    norm = (exchanged([summed_over_head(sums)] * parts, parts), gain_square, features)

    part, dq, grads, dots = backward_chunk(
        sh, me, back, qq, spans[hops], hops, out, lse, None, None, norm, everyone, None
    )
    arrived = [moved_on(part, -hops)]
    for distance in range(hops - 1, 0, -1):
        part, dq = backward_chunk(
            sh, me, back, qq, spans[distance], distance, grads, lse, dots, dq, None,
            everyone, None,
        )
        arrived.append(moved_on(part, -distance))
    turns = [turn[::-1] for turn in (everyone[-1:], everyone[:-1]) if turn]
    held, dq_pieces = None, [None] * parts
    for order in turns:
        held, *done = backward_chunk(
            sh, me, back, qq, spans[0], 0, grads, lse, dots, dq, None, order, held
        )
        for m, piece in zip(order, done):
            dq_pieces[m] = piece.reshape(1, group, rows, width)
    dq_pieces = exchanged(dq_pieces, parts)
    dq_pieces[-1], held = lax.optimization_barrier((dq_pieces[-1], held))
    dkv_pieces = exchanged(combine(sh, me, arrived, held), parts)
    (product_queries,) = join_heads(dq_pieces, 1, group)
    dkv_pieces = [p.reshape(2, 1, rows, width) for p in dkv_pieces]
    product_keys, product_values = join_heads(dkv_pieces, 2, 1)
    return (
        product_queries.reshape(queries.shape),
        product_keys.reshape(keys.shape),
        product_values.reshape(keys.shape),
    )


def solution(mesh):
    def run(*arguments):
        count, heads = mesh.shape["ctx"], mesh.shape["head"]
        parts = arguments[1].shape[1] // heads
        split = Mesh(
            mesh.devices.reshape(count // parts, parts, heads), ("span", "part", "head")
        )
        ctx = ("span", "part")
        array = P(ctx, "head", None)
        return jax.shard_map(
            body,
            mesh=split,
            in_specs=(array,) * 6 + (P(ctx), P("head")),
            out_specs=(array,) * 3,
            check_vma=False,
        )(*arguments)

    return run
```

```python
import functools

import jax
import jax.numpy as jnp
from jax import lax
from jax.experimental import pallas as pl
from jax.experimental.pallas import tpu as pltpu
from jax.sharding import Mesh, PartitionSpec as P

DOC_DEVS = 8
EPSILON = 1e-06
VMEM_BYTES = 18 * 1024 * 1024
NOTE_ROWS = 16
ONES_ROWS = 16
WIDE_VMEM_BYTES = 60 * 1024 * 1024
MASKED = -1e30
F32 = jnp.float32
BF16 = jnp.bfloat16
SMEM = pl.BlockSpec(memory_space=pltpu.SMEM)
VMEM = pl.BlockSpec(memory_space=pltpu.VMEM)


def params(size=VMEM_BYTES):
    return pltpu.CompilerParams(vmem_limit_bytes=size)


def cost(flops, moved, powers=0):
    return pl.CostEstimate(flops=int(flops), bytes_accessed=int(moved), transcendentals=int(powers))


def nn(a, b):
    return lax.dot_general(a, b, (((1,), (0,)), ((), ())), preferred_element_type=F32)


def nt(a, b):
    return lax.dot_general(a, b, (((1,), (1,)), ((), ())), preferred_element_type=F32)


def split_heads(arrays, parts, per_part, notes=None):
    count = len(arrays)
    total, width = arrays[0].shape
    heads = parts * per_part
    rows = total // heads
    length = count * per_part * rows
    extra = 0 if notes is None else NOTE_ROWS
    scalars = [] if notes is None else [notes]

    def kernel(*refs):
        ins = list(refs[: len(scalars) + count])
        outs, (held, wide, sems) = refs[len(scalars) + count : -3], refs[-3:]
        mine = lax.axis_index("part")
        if extra:
            note_ref = ins.pop(0)
        copies = [pltpu.make_async_copy(ins[a], held.at[a], sems.at[a]) for a in range(count)]
        for copy in copies:
            copy.start()
        if extra:
            first = (lax.axis_index("span") * parts + mine) * notes.shape[0]
            line = lax.broadcasted_iota(jnp.int32, (extra, width), 0)
            lines = jnp.zeros((extra, width), jnp.int32)
            for i in range(notes.shape[0]):
                lines = jnp.where(line == i, first + i - note_ref[i], lines)
            for out in outs:
                out[length:, :] = lines.astype(F32).astype(BF16)
        for a in range(count):
            copies[a].wait()
            wide[...] = held[a].astype(F32)
            for m in range(parts):
                for r in range(per_part):
                    head = jnp.bitwise_xor(mine, m) * per_part + r
                    at = (a * per_part + r) * rows
                    outs[m][at : at + rows, :] = wide[pl.ds(head, rows, stride=heads), :].astype(BF16)

    return pl.pallas_call(
        kernel,
        in_specs=[SMEM] * len(scalars) + [pl.BlockSpec(memory_space=pltpu.HBM)] * count,
        out_specs=[pl.BlockSpec(memory_space=pltpu.VMEM)] * parts,
        out_shape=[jax.ShapeDtypeStruct((length + extra, width), BF16)] * parts,
        scratch_shapes=[
            pltpu.VMEM((count, total, width), BF16),
            pltpu.VMEM((total, width), F32),
            pltpu.SemaphoreType.DMA((count,)),
        ],
        compiler_params=params(VMEM_BYTES if notes is None else WIDE_VMEM_BYTES),
        cost_estimate=cost(0, 4 * count * total * width),
        name="split_heads",
    )(*scalars, *arrays)


def join_heads(pieces, count, per_part):
    parts = len(pieces)
    rows, width = pieces[0].shape[-2:]
    heads = parts * per_part

    steps = 4
    cut = rows // steps

    def kernel(*refs):
        ins, outs = refs[:parts], refs[parts:]
        mine = lax.axis_index("part")
        for a in range(count):
            for m in range(parts):
                for r in range(per_part):
                    head = jnp.bitwise_xor(mine, m) * per_part + r
                    outs[a][pl.ds(head, cut, stride=heads), :] = ins[m][a, r].astype(F32)

    return pl.pallas_call(
        kernel,
        grid=(steps,),
        in_specs=[pl.BlockSpec((count, per_part, cut, width), lambda i: (0, 0, i, 0))] * parts,
        out_specs=[pl.BlockSpec((cut * heads, width), lambda i: (i, 0))] * count,
        out_shape=[jax.ShapeDtypeStruct((rows * heads, width), F32)] * count,
        compiler_params=params(),
        cost_estimate=cost(0, 6 * count * rows * heads * width),
        name="join_heads",
    )(*pieces)


def slot_of(me_ref, m, rows):
    return pl.multiple_of(jnp.bitwise_xor(me_ref[0], m) * rows, rows)


class Shape:
    def __init__(self, parts, group, rows, width, block):
        self.parts, self.group, self.rows, self.width, self.block = parts, group, rows, width, block
        self.tokens = parts * rows
        self.blocks = self.tokens // block
        self.lanes = group * block
        self.scale = width**-0.5


def diagonal(sh):
    shape = (sh.block, sh.block)
    key = lax.broadcasted_iota(jnp.int32, shape, 0)
    query = lax.broadcasted_iota(jnp.int32, shape, 1)
    return key <= query


def below_diagonal(sh, value, other):
    allowed = diagonal(sh)
    cut = [value[:, at : at + sh.block] for at in range(0, value.shape[1], sh.block)]
    return jnp.concatenate([jnp.where(allowed, part, other) for part in cut], axis=1)


def halves(sh):
    if sh.group % 2:
        return [slice(0, sh.lanes)]
    return [slice(0, sh.lanes // 2), slice(sh.lanes // 2, sh.lanes)]


def stacked_keys(keys, start, size):
    k_s, tk_s = keys
    k = k_s[pl.ds(start, size), :]
    tk = tk_s[pl.ds(start, size), :]
    left = jnp.concatenate([k, tk], axis=0)
    right = jnp.concatenate([jnp.zeros_like(k), k], axis=0)
    return jnp.concatenate([left, right], axis=1)


def pieces_of(sh, start, blocks):
    sizes = [2] * (blocks // 2) + [1] * (blocks % 2)
    firsts = [sum(sizes[:i]) for i in range(len(sizes))]
    return [
        (pl.multiple_of(start + first * sh.block, sh.block), size * sh.block, i == len(sizes) - 1)
        for i, (first, size) in enumerate(zip(firsts, sizes))
    ]


def cut_diagonal(sh, value, other):
    low = below_diagonal(sh, value[value.shape[0] - sh.block :], other)
    if value.shape[0] == sh.block:
        return low
    return jnp.concatenate([value[: value.shape[0] - sh.block], low], axis=0)


def block_rows(sh, block):
    return pl.multiple_of(block * sh.block, sh.block)


def load_state(stat, lanes):
    return tuple(stat[r : r + 1, lanes] for r in range(3))


def forward_tile(sh, keys, vt_s, acc, stat, kept, qq, block, blocks, masked):
    w = sh.width
    start = block_rows(sh, block)
    pieces = pieces_of(sh, start, blocks)
    stacked = [stacked_keys(keys, at, size) for at, size, _ in pieces]
    at = pl.ds(start, blocks * sh.block)
    lanes = halves(sh)
    scores = [[] for _ in lanes]
    mixed = [[] for _ in lanes]
    most = [None for _ in lanes]
    state = [None if masked else load_state(stat, part) for part in lanes]

    def score(h, c):
        both = nt(stacked[c], qq[lanes[h], :])
        s, d = both[: pieces[c][1]], both[pieces[c][1] :]
        if masked and pieces[c][2]:
            s = cut_diagonal(sh, s, MASKED)
        scores[h].append((s, d))

    def top(h):
        peaks = [jnp.max(s, axis=0, keepdims=True) for s, _ in scores[h]]
        most[h] = functools.reduce(jnp.maximum, peaks) * sh.scale
        if not masked:
            most[h] = jnp.maximum(most[h], state[h][0])
        if kept is not None:
            for j in range(blocks):
                kept[1][block + j, :, lanes[h]] = most[h]

    def soften(h, c):
        s, d = scores[h][c]
        e = jnp.exp(s * sh.scale - most[h])
        mixed[h].append((e.astype(BF16), (e * d).astype(BF16)))
        if kept is not None:
            kept[0][pl.ds(pieces[c][0], pieces[c][1]), lanes[h]] = mixed[h][-1][0]

    def gather(h, i):
        return jnp.concatenate([pair[i] for pair in mixed[h]], axis=0)

    def finish(h, plain, moving):
        total, cross = plain[2 * w : 2 * w + 1], moving[w : w + 1]
        tangent = plain[:w] + moving[:w] * sh.scale
        plain = plain[w : 2 * w]
        if not masked:
            decay = jnp.exp(state[h][0] - most[h])
            plain = acc[:w, lanes[h]] * decay + plain
            tangent = acc[w:, lanes[h]] * decay + tangent
            total, cross = state[h][1] * decay + total, state[h][2] * decay + cross
        acc[:w, lanes[h]] = plain
        acc[w:, lanes[h]] = tangent
        for r, value in enumerate((most[h], total, cross)):
            stat[r : r + 1, lanes[h]] = value

    for h in range(len(lanes) + 1):
        if h > 0:
            top(h - 1)
        for c in range(len(pieces)):
            if h < len(lanes):
                score(h, c)
            if h > 0:
                soften(h - 1, c)
        if h > 0:
            plain = nn(vt_s[:, at], gather(h - 1, 0))
            moving = nn(vt_s[w:, at], gather(h - 1, 1))
            finish(h - 1, plain, moving)


def by_count(sh, low, count, run, masked):
    head = jnp.where(count <= 6, count, 3 + lax.rem(jnp.maximum(count - 7, 0), 4))
    fours = (count - head) // 4
    for blocks in range(1, min(6, sh.blocks) + 1):

        @pl.when(head == blocks)
        def _(blocks=blocks):
            if masked:
                run(low + count - blocks, blocks, True)
            else:
                run(low, blocks, False)

    def step(i, carry):
        run(low + (0 if masked else head) + 4 * i, 4, False)
        return carry

    if sh.blocks > 6:
        lax.fori_loop(0, fours, step, 0)


def lay_chunk(sh, me_ref, sources, targets):
    for m, (ref, base) in enumerate(sources):
        slot = pl.ds(slot_of(me_ref, m, sh.rows), sh.rows)
        for i, target in enumerate(targets):
            at = base + i * sh.rows
            target[slot, :] = ref[at : at + sh.rows, :]


def lay_queries(sh, me_ref, order, pieces, qq):
    per = sh.rows // sh.block
    for m, ref in zip(order, pieces):
        for i in range(2):
            for g in range(sh.group):
                for r in range(per):
                    block = jnp.bitwise_xor(me_ref[0], m) * per + r
                    at = (i * sh.group + g) * sh.rows + r * sh.block
                    qq[
                        block,
                        g * sh.block : (g + 1) * sh.block,
                        i * sh.width : (i + 1) * sh.width,
                    ] = ref[at : at + sh.block, :]


def lay_span(sh, me_ref, sources, laid):
    w = sh.width
    k_s, v_s, kt_s, tk_s, vt_s, tv_s = laid
    lay_chunk(sh, me_ref, sources, (k_s, v_s, tk_s, tv_s))
    kt_s[...] = transposed(k_s[...])
    vt_s[:w, :] = transposed(tv_s[...])
    vt_s[w : 2 * w, :] = transposed(v_s[...])
    vt_s[2 * w :, :] = jnp.ones((ONES_ROWS, sh.tokens), BF16)


def transposed(x):
    return x.astype(F32).T.astype(BF16)


def located(sh, refs):
    length = refs[0].shape[0]
    return [(ref, at) for ref in refs for at in range(0, ref.shape[0], length)]


def back_of(sh, me_ref, back_ref, qb):
    per = sh.rows // sh.block
    return back_ref[jnp.bitwise_xor(me_ref[0], qb // per) * per + qb % per]


def each_block(count, run):
    def step(i, carry):
        run(i)
        return carry

    lax.fori_loop(0, count, step, 0)


def block_in_turn(sh, me_ref, order, i):
    per = sh.rows // sh.block
    if order == list(range(sh.parts)):
        return i
    partner = order[0]
    for j in range(1, len(order)):
        partner = jnp.where(i // per == j, order[j], partner)
    return jnp.bitwise_xor(me_ref[0], partner) * per + i % per


def kept_shapes(sh):
    return [
        jax.ShapeDtypeStruct((sh.blocks, sh.tokens, sh.lanes), BF16),
        jax.ShapeDtypeStruct((sh.blocks, sh.blocks, 1, sh.lanes), F32),
    ]


def forward_own(sh, me, back, order, queries, chunk, before):
    w = sh.width
    first = before is None
    turns = len(order) * (sh.rows // sh.block)

    def kernel(me_ref, back_ref, *refs):
        refs = list(refs)

        def take(count):
            taken = refs[:count]
            del refs[:count]
            return taken

        q_in = take(len(order))
        if first:
            kv_in = take(len(chunk))
            accs, stats, qq_s, es, ms = take(5)
            laid = refs
            lay_span(sh, me_ref, located(sh, kv_in), laid)
        else:
            laid = take(len(chunk))
            take(5)
            accs, stats, qq_s, es, ms = refs
        k_s, _, _, tk_s, vt_s = laid[:5]
        lay_queries(sh, me_ref, order, q_in, qq_s)

        def query_block(i):
            qb = block_in_turn(sh, me_ref, order, i)
            low = jnp.clip(qb - back_of(sh, me_ref, back_ref, qb), 0, qb)
            run = functools.partial(
                forward_tile,
                sh,
                (k_s, tk_s),
                vt_s,
                accs.at[qb],
                stats.at[qb],
                (es.at[qb], ms.at[qb]),
                qq_s[qb],
            )
            by_count(sh, low, qb + 1 - low, run, True)

        each_block(turns, query_block)

    def array(*shape, dtype=F32):
        return jax.ShapeDtypeStruct(shape, dtype)

    span = array(sh.tokens, w, dtype=BF16)
    out_shape = [
        array(sh.blocks, 2 * w, sh.lanes),
        array(sh.blocks, 8, sh.lanes),
        array(sh.blocks, sh.lanes, 2 * w, dtype=BF16),
        *kept_shapes(sh),
    ]
    operands = [*queries, *chunk]
    aliases = {}
    if first:
        out_shape += [span, span, array(w, sh.tokens, dtype=BF16), span]
        out_shape.append(array(2 * w + ONES_ROWS, sh.tokens, dtype=BF16))
    else:
        aliases = {2 + len(operands) + i: i for i in range(5)}
        operands += before
    work = sh.group * sh.tokens * sh.block * turns // 2
    return pl.pallas_call(
        kernel,
        in_specs=[SMEM, SMEM] + [VMEM] * len(operands),
        out_specs=[VMEM] * len(out_shape),
        out_shape=out_shape,
        input_output_aliases=aliases,
        scratch_shapes=[pltpu.VMEM((sh.tokens, w), BF16)] * first,
        compiler_params=params(),
        cost_estimate=cost(12 * work * w, 4 * sh.tokens * sh.lanes, work),
        name="forward_own",
    )(me, back, *operands)


def forward_chunk(sh, me, back, qq, chunk, distance, state, gain_square=None):
    w = sh.width
    closing = gain_square is not None

    def kernel(me_ref, back_ref, qq_s, *refs):
        refs = list(refs)

        def take(count):
            taken = refs[:count]
            del refs[:count]
            return taken

        kv_in = take(len(chunk))
        take(2)
        if closing:
            (gain_ref,) = take(1)
        k_s, v_s, kt_s, accs, stats = take(5)
        last = take(2)
        if closing:
            lse, sums = last
        tk_s, tv_s, vt_s = refs
        lay_span(sh, me_ref, located(sh, kv_in), (k_s, v_s, kt_s, tk_s, vt_s, tv_s))

        def query_block(qb):
            acc, stat = accs.at[qb], stats.at[qb]
            first = qb - back_of(sh, me_ref, back_ref, qb) + distance * sh.blocks
            first = jnp.clip(first, 0, sh.blocks)
            count = sh.blocks - first

            @pl.when(count > 0)
            def _():
                kept = None if closing else [ref.at[qb] for ref in last]
                run = functools.partial(
                    forward_tile, sh, (k_s, tk_s), vt_s, acc, stat, kept, qq_s[qb]
                )
                by_count(sh, first, count, run, False)

            if closing:
                most, total, cross = load_state(stat, slice(None))
                inverse = 1.0 / total
                plain = acc[:w, :] * inverse
                moved = acc[w:, :] * inverse - (cross * inverse * sh.scale) * plain
                acc[:w, :] = plain
                acc[w:, :] = moved
                lse[qb] = most + jnp.log(total)
                square = plain * plain
                product = plain * moved
                gain = gain_ref[...]
                for r, value in enumerate((square, product, gain * square, gain * product)):
                    line = jnp.sum(value, axis=0, keepdims=True)
                    pieces = [line[:, g * sh.block : (g + 1) * sh.block] for g in range(sh.group)]
                    sums[qb, r : r + 1, :] = functools.reduce(jnp.add, pieces)

        each_block(sh.blocks, query_block)

    def array(*shape, dtype=F32):
        return jax.ShapeDtypeStruct(shape, dtype)

    out_shape = [
        array(sh.tokens, w, dtype=BF16),
        array(sh.tokens, w, dtype=BF16),
        array(w, sh.tokens, dtype=BF16),
        array(sh.blocks, 2 * w, sh.lanes),
        array(sh.blocks, 8, sh.lanes),
    ]
    if closing:
        out_shape += [array(sh.blocks, 1, sh.lanes), array(sh.blocks, 4, sh.block)]
    else:
        out_shape += kept_shapes(sh)
    operands = [qq, *chunk]
    aliases = {2 + len(operands): 3, 3 + len(operands): 4}
    operands += state
    if closing:
        operands.append(gain_square)
    work = sh.group * sh.tokens * sh.tokens // 2
    return pl.pallas_call(
        kernel,
        in_specs=[SMEM, SMEM] + [VMEM] * len(operands),
        out_specs=[VMEM] * len(out_shape),
        out_shape=out_shape,
        input_output_aliases=aliases,
        scratch_shapes=[
            pltpu.VMEM((sh.tokens, w), BF16),
            pltpu.VMEM((sh.tokens, w), BF16),
            pltpu.VMEM((2 * w + ONES_ROWS, sh.tokens), BF16),
        ],
        compiler_params=params(),
        cost_estimate=cost(24 * work * w, 12 * sh.tokens * sh.lanes * 2, work),
        name="forward_far" if closing else "forward_chunk",
    )(me, back, *operands)


def backward_tile(sh, keys, kt_s, dkv_s, dq_s, qg, lse, dot, block, blocks, _):
    start, size = block_rows(sh, block), blocks * sh.block
    rows = pl.ds(start, size)
    k_s, v_s = keys
    k, v = k_s[rows, :], v_s[rows, :]
    empty = jnp.zeros_like(k)
    left = jnp.concatenate([k, empty], axis=0)
    right = jnp.concatenate([empty, v], axis=0)
    stacked = jnp.concatenate([left, right], axis=1)
    scores = [nt(stacked, qg[lanes, :]) for lanes in halves(sh)]
    for lanes, both in zip(halves(sh), scores):
        p = jnp.exp(both[:size] * sh.scale - lse[:, lanes])
        ds = (p * (both[size:] - dot[:, lanes])).astype(BF16)
        dkv_s[0, rows, :] += nn(ds, qg[lanes, : sh.width])
        dkv_s[1, rows, :] += nn(p.astype(BF16), qg[lanes, sh.width :])
        dq_s[:, lanes] += nn(kt_s[:, rows], ds)


def backward_kept(sh, keys, kt_s, dkv_s, dq_s, qg, lse, dot, kept, block, blocks, _):
    start, size = block_rows(sh, block), blocks * sh.block
    rows = pl.ds(start, size)
    v = keys[1][rows, :]
    slopes = [nt(v, qg[lanes, sh.width :]) for lanes in halves(sh)]
    for lanes, slope in zip(halves(sh), slopes):
        parts = []
        for j in range(blocks):
            factor = jnp.exp(kept[1][block + j, :, lanes] - lse[:, lanes])
            at = pl.ds(block_rows(sh, block + j), sh.block)
            parts.append(kept[0][at, lanes].astype(F32) * factor)
        p = jnp.concatenate(parts, axis=0)
        ds = (p * (slope - dot[:, lanes])).astype(BF16)
        dkv_s[0, rows, :] += nn(ds, qg[lanes, : sh.width])
        dkv_s[1, rows, :] += nn(p.astype(BF16), qg[lanes, sh.width :])
        dq_s[:, lanes] += nn(kt_s[:, rows], ds)


def backward_chunk(sh, me, back, qq, keys, distance, grads, lse, dots, dq, norm, order, held):
    w = sh.width
    opening, closing = norm is not None, distance == 0
    per = sh.rows // sh.block

    def kernel(me_ref, back_ref, *refs):
        refs = list(refs)

        def take(count):
            taken = refs[:count]
            del refs[:count]
            return taken

        qq_s, k_s, v_s, kt_s = take(4)
        kept = take(len(keys) - 3)
        (lse_s,) = take(1)
        if opening:
            out_s, gain_ref, *sum_refs = take(2 + len(norm[0]))
        else:
            grad_s, dot_s, dq_in = take(3)
        (held_ref,) = take(1) if held is not None else (None,)
        (dkv_out,) = take(1)
        dq_out = take(len(order) if closing else 1)
        if opening:
            grad_s, dot_s = take(2)
        dkv_s, dq_own = (dkv_out, *refs) if closing else refs
        if held_ref is None:
            dkv_s[...] = jnp.zeros_like(dkv_s)

        def query_block(i):
            qb = block_in_turn(sh, me_ref, order, i)
            dq_s = dq_own if closing else dq_out[0].at[qb]
            if opening:
                features = norm[2]
                token = functools.reduce(jnp.add, [ref[qb] for ref in sum_refs])
                sums = jnp.concatenate([token] * sh.group, axis=1)
                square = sums[0:1] / features + EPSILON
                inverse = lax.rsqrt(square)
                ratio = sums[1:2] / (features * square)
                again = (sums[3:4] - ratio * sums[2:3]) * inverse
                again = again / (features * square)
                plain = out_s[qb, :w, :]
                moved = out_s[qb, w:, :]
                first_grad = gain_ref[...] * (moved - plain * ratio) * inverse
                cot = ((first_grad - plain * again) * inverse).astype(BF16).astype(F32)
                dot_s[qb] = jnp.sum(cot * plain, axis=0, keepdims=True)
                grad_s[qb] = cot.T.astype(BF16)
                dq_s[...] = jnp.zeros((w, sh.lanes), F32)
            elif closing:
                dq_s[...] = dq_in[qb]

            top = sh.blocks if distance else qb + 1
            first = jnp.clip(qb - back_of(sh, me_ref, back_ref, qb) + distance * sh.blocks, 0, top)
            count = top - first

            @pl.when(count > 0)
            def _():
                qg = jnp.concatenate([qq_s[qb, :, :w], grad_s[qb]], axis=1)
                common = (sh, (k_s, v_s), kt_s, dkv_s, dq_s, qg, lse_s[qb], dot_s[qb])
                if kept:
                    run = functools.partial(backward_kept, *common, [ref.at[qb] for ref in kept])
                else:
                    run = functools.partial(backward_tile, *common)
                by_count(sh, first, count, run, False)

            if closing:
                done = (dq_s[...] * sh.scale).T.reshape(sh.group, sh.block, w).astype(BF16)
                at = pl.ds(pl.multiple_of(i % per * sh.block, sh.block), sh.block)
                for j, out in enumerate(dq_out):

                    @pl.when(i // per == j)
                    def _(out=out):
                        out[:, at, :] = done

        each_block(len(order) * per, query_block)
        if not closing:
            dkv_out[0] = (dkv_s[0] * sh.scale).astype(BF16)
            dkv_out[1] = dkv_s[1].astype(BF16)

    def array(*shape, dtype=F32):
        return jax.ShapeDtypeStruct(shape, dtype)

    operands = [qq, *keys, lse]
    if opening:
        operands += [grads, norm[1], *norm[0]]
    else:
        operands += [grads, dots, dq]
    aliases = {}
    if not opening and not closing:
        aliases = {1 + len(operands): 1}
    if held is not None:
        aliases = {2 + len(operands): 0}
        operands.append(held)
    out_shape = [array(2, sh.tokens, w, dtype=F32 if closing else BF16)]
    if closing:
        out_shape += [array(sh.group, sh.rows, w, dtype=BF16)] * len(order)
    else:
        out_shape.append(array(sh.blocks, w, sh.lanes))
    if opening:
        out_shape += [
            array(sh.blocks, sh.lanes, w, dtype=BF16),
            array(sh.blocks, 1, sh.lanes),
        ]
    work = sh.group * sh.tokens * len(order) * sh.rows // 2
    return pl.pallas_call(
        kernel,
        in_specs=[SMEM, SMEM] + [VMEM] * len(operands),
        out_specs=[VMEM] * len(out_shape),
        out_shape=out_shape,
        input_output_aliases=aliases,
        scratch_shapes=[pltpu.VMEM((2, sh.tokens, w), F32)] * (not closing)
        + [pltpu.VMEM((w, sh.lanes), F32)],
        compiler_params=params(),
        cost_estimate=cost(1, 1) if closing else cost(20 * work * w, 16 * work, work),
        name="backward_chunk",
    )(me, back, *operands)


def combine(sh, me, arrived, held):
    count = len(arrived)

    def kernel(me_ref, held_ref, *refs):
        for m, out in enumerate(refs[count:]):
            slot = pl.ds(slot_of(me_ref, m, sh.rows), sh.rows)
            for a, factor in ((0, sh.scale), (1, 1.0)):
                part = held_ref[a, slot, :] * factor
                for ref in refs[:count]:
                    part += ref[a, slot, :].astype(F32)
                out[a] = part.astype(BF16)

    return pl.pallas_call(
        kernel,
        in_specs=[SMEM] + [VMEM] * (1 + count),
        out_specs=[VMEM] * sh.parts,
        out_shape=[jax.ShapeDtypeStruct((2, sh.rows, sh.width), BF16)] * sh.parts,
        compiler_params=params(),
        cost_estimate=cost(0, 1),
        name="combine",
    )(me, held, *arrived)


def exchanged_with(piece, parts, m):
    return lax.ppermute(piece, "part", [(i, i ^ m) for i in range(parts)]) if m else piece


def exchanged(pieces, parts):
    return [exchanged_with(piece, parts, m) for m, piece in enumerate(pieces)]


def moved_on(value, steps):
    count = lax.axis_size("span")
    pairs = [(i, i + steps) for i in range(count) if 0 <= i + steps < count]
    return lax.ppermute(value, "span", pairs)


def summed_over_head(value):
    count = lax.axis_size("head")
    if count & (count - 1):
        return lax.psum(value, "head")
    step = 1
    while step < count:
        value = value + lax.ppermute(value, "head", [(i, i ^ step) for i in range(count)])
        step *= 2
    return value


def body(queries, keys, values, tangent_queries, tangent_keys, tangent_values, doc_start, out_gain):
    rows, query_heads, width = queries.shape
    key_heads = keys.shape[1]
    group = query_heads // key_heads
    parts = lax.axis_size("part")
    per = doc_start.shape[0]
    block = rows // per
    features = query_heads * width * lax.axis_size("head")
    hops = -(-DOC_DEVS // parts)
    sh = Shape(parts, group, rows, width, block)
    place = lax.axis_index("part")
    me = place.astype(jnp.int32).reshape(1)

    def flat(array):
        return array.reshape(-1, width)

    pieces = split_heads(
        [flat(a) for a in (keys, values, tangent_keys, tangent_values)], parts, 1, doc_start
    )
    q_rows, _ = lax.optimization_barrier(((flat(queries), flat(tangent_queries)), pieces[0]))
    q_pieces = split_heads(q_rows, parts, group)
    own = moved_on(pieces[0], 1)
    pieces = exchanged(pieces, parts)
    chunks = [pieces]
    if parts > 1:
        own, q_pieces = lax.optimization_barrier((own, q_pieces))
        owns = [own]
        for _ in range(hops - 1):
            owns.append(moved_on(owns[-1], 1))
        late, owns = lax.optimization_barrier((pieces[1:], owns))
        rest = jnp.concatenate([moved_on(piece, 1) for piece in late], axis=0)
        chunks.append([owns[0], rest])
        for own in owns[1:]:
            rest = moved_on(rest, 1)
            chunks.append([own, rest])
    else:
        for _ in range(hops):
            chunks.append([own])
            own = moved_on(own, 1)
    q_parts = exchanged(q_pieces[:-1], parts)
    if parts > 1:
        last, _ = lax.optimization_barrier((q_pieces[-1], q_parts[min(1, parts - 2)]))
        q_parts.append(exchanged_with(last, parts, parts - 1))
    else:
        q_parts = q_pieces
    back = jnp.concatenate([p[4 * rows : 4 * rows + per, 0] for p in pieces]).astype(jnp.int32)
    gain = lax.dynamic_index_in_dim(out_gain.reshape(key_heads, group, width), place, 0, False)
    gain_square = jnp.repeat((gain * gain).T, block, axis=1)

    everyone = list(range(parts))
    before, laid = None, chunks[0]
    for order in [everyone[:1], everyone[1:-1], everyone[-1:]] if parts > 1 else [everyone]:
        if order:
            turn = forward_own(sh, me, back, order, [q_parts[m] for m in order], laid, before)
            laid = turn[5:] or laid
            before = list(turn[:5])
    state, qq = before[:2], before[2]
    spans = [(*laid[:3], *before[3:])]
    for distance in range(1, hops):
        k, v, kt, acc, stat, *kept = forward_chunk(
            sh, me, back, qq, chunks[distance], distance, state
        )
        state = [acc, stat]
        spans.append((k, v, kt, *kept))
    k, v, kt, out, _, lse, sums = forward_chunk(
        sh, me, back, qq, chunks[hops], hops, state, gain_square
    )
    spans.append((k, v, kt))
    norm = (exchanged([summed_over_head(sums)] * parts, parts), gain_square, features)

    part, dq, grads, dots = backward_chunk(
        sh, me, back, qq, spans[hops], hops, out, lse, None, None, norm, everyone, None
    )
    arrived = [moved_on(part, -hops)]
    for distance in range(hops - 1, 0, -1):
        part, dq = backward_chunk(
            sh, me, back, qq, spans[distance], distance, grads, lse, dots, dq, None,
            everyone, None,
        )
        arrived.append(moved_on(part, -distance))
    turns = [turn[::-1] for turn in (everyone[-1:], everyone[:-1]) if turn]
    held, dq_pieces = None, [None] * parts
    for order in turns:
        if held is not None:
            arrived[0], held = lax.optimization_barrier((arrived[0], held))
        held, *done = backward_chunk(
            sh, me, back, qq, spans[0], 0, grads, lse, dots, dq, None, order, held
        )
        for m, piece in zip(order, done):
            dq_pieces[m] = piece.reshape(1, group, rows, width)
    dq_pieces = exchanged(dq_pieces, parts)
    dq_pieces[-1], held = lax.optimization_barrier((dq_pieces[-1], held))
    dkv_pieces = exchanged(combine(sh, me, arrived, held), parts)
    (product_queries,) = join_heads(dq_pieces, 1, group)
    dkv_pieces = [p.reshape(2, 1, rows, width) for p in dkv_pieces]
    product_keys, product_values = join_heads(dkv_pieces, 2, 1)
    return (
        product_queries.reshape(queries.shape),
        product_keys.reshape(keys.shape),
        product_values.reshape(keys.shape),
    )


def solution(mesh):
    def run(*arguments):
        count, heads = mesh.shape["ctx"], mesh.shape["head"]
        parts = arguments[1].shape[1] // heads
        split = Mesh(
            mesh.devices.reshape(count // parts, parts, heads), ("span", "part", "head")
        )
        ctx = ("span", "part")
        array = P(ctx, "head", None)
        return jax.shard_map(
            body,
            mesh=split,
            in_specs=(array,) * 6 + (P(ctx), P("head")),
            out_specs=(array,) * 3,
            check_vma=False,
        )(*arguments)

    return run
```

```python
import functools

import jax
import jax.numpy as jnp
from jax import lax
from jax.experimental import pallas as pl
from jax.experimental.pallas import tpu as pltpu
from jax.sharding import Mesh, PartitionSpec as P

DOC_DEVS = 8
EPSILON = 1e-06
VMEM_BYTES = 18 * 1024 * 1024
NOTE_ROWS = 16
ONES_ROWS = 16
WIDE_VMEM_BYTES = 60 * 1024 * 1024
MASKED = -1e30
F32 = jnp.float32
BF16 = jnp.bfloat16
SMEM = pl.BlockSpec(memory_space=pltpu.SMEM)
VMEM = pl.BlockSpec(memory_space=pltpu.VMEM)


def params(size=VMEM_BYTES):
    return pltpu.CompilerParams(vmem_limit_bytes=size)


def cost(flops, moved, powers=0):
    return pl.CostEstimate(flops=int(flops), bytes_accessed=int(moved), transcendentals=int(powers))


def nn(a, b):
    return lax.dot_general(a, b, (((1,), (0,)), ((), ())), preferred_element_type=F32)


def nt(a, b):
    return lax.dot_general(a, b, (((1,), (1,)), ((), ())), preferred_element_type=F32)


def split_heads(arrays, parts, per_part, notes=None):
    count = len(arrays)
    total, width = arrays[0].shape
    heads = parts * per_part
    rows = total // heads
    length = count * per_part * rows
    extra = 0 if notes is None else NOTE_ROWS
    scalars = [] if notes is None else [notes]

    def kernel(*refs):
        ins = list(refs[: len(scalars) + count])
        outs, (held, wide, sems) = refs[len(scalars) + count : -3], refs[-3:]
        mine = lax.axis_index("part")
        if extra:
            note_ref = ins.pop(0)
        copies = [pltpu.make_async_copy(ins[a], held.at[a], sems.at[a]) for a in range(count)]
        for copy in copies:
            copy.start()
        if extra:
            first = (lax.axis_index("span") * parts + mine) * notes.shape[0]
            line = lax.broadcasted_iota(jnp.int32, (extra, width), 0)
            lines = jnp.zeros((extra, width), jnp.int32)
            for i in range(notes.shape[0]):
                lines = jnp.where(line == i, first + i - note_ref[i], lines)
            for out in outs:
                out[length:, :] = lines.astype(F32).astype(BF16)
        for a in range(count):
            copies[a].wait()
            wide[...] = held[a].astype(F32)
            for m in range(parts):
                for r in range(per_part):
                    head = jnp.bitwise_xor(mine, m) * per_part + r
                    at = (a * per_part + r) * rows
                    outs[m][at : at + rows, :] = wide[pl.ds(head, rows, stride=heads), :].astype(BF16)

    return pl.pallas_call(
        kernel,
        in_specs=[SMEM] * len(scalars) + [pl.BlockSpec(memory_space=pltpu.HBM)] * count,
        out_specs=[pl.BlockSpec(memory_space=pltpu.VMEM)] * parts,
        out_shape=[jax.ShapeDtypeStruct((length + extra, width), BF16)] * parts,
        scratch_shapes=[
            pltpu.VMEM((count, total, width), BF16),
            pltpu.VMEM((total, width), F32),
            pltpu.SemaphoreType.DMA((count,)),
        ],
        compiler_params=params(VMEM_BYTES if notes is None else WIDE_VMEM_BYTES),
        cost_estimate=cost(0, 4 * count * total * width),
        name="split_heads",
    )(*scalars, *arrays)


def join_heads(pieces, count, per_part):
    parts = len(pieces)
    rows, width = pieces[0].shape[-2:]
    heads = parts * per_part

    steps = 4
    cut = rows // steps

    def kernel(*refs):
        ins, outs = refs[:parts], refs[parts:]
        mine = lax.axis_index("part")
        for a in range(count):
            for m in range(parts):
                for r in range(per_part):
                    head = jnp.bitwise_xor(mine, m) * per_part + r
                    outs[a][pl.ds(head, cut, stride=heads), :] = ins[m][a, r].astype(F32)

    return pl.pallas_call(
        kernel,
        grid=(steps,),
        in_specs=[pl.BlockSpec((count, per_part, cut, width), lambda i: (0, 0, i, 0))] * parts,
        out_specs=[pl.BlockSpec((cut * heads, width), lambda i: (i, 0))] * count,
        out_shape=[jax.ShapeDtypeStruct((rows * heads, width), F32)] * count,
        compiler_params=params(),
        cost_estimate=cost(0, 6 * count * rows * heads * width),
        name="join_heads",
    )(*pieces)


def slot_of(me_ref, m, rows):
    return pl.multiple_of(jnp.bitwise_xor(me_ref[0], m) * rows, rows)


class Shape:
    def __init__(self, parts, group, rows, width, block):
        self.parts, self.group, self.rows, self.width, self.block = parts, group, rows, width, block
        self.tokens = parts * rows
        self.blocks = self.tokens // block
        self.lanes = group * block
        self.scale = width**-0.5


def diagonal(sh):
    shape = (sh.block, sh.block)
    key = lax.broadcasted_iota(jnp.int32, shape, 0)
    query = lax.broadcasted_iota(jnp.int32, shape, 1)
    return key <= query


def below_diagonal(sh, value, other):
    allowed = diagonal(sh)
    cut = [value[:, at : at + sh.block] for at in range(0, value.shape[1], sh.block)]
    return jnp.concatenate([jnp.where(allowed, part, other) for part in cut], axis=1)


def halves(sh):
    if sh.group % 2:
        return [slice(0, sh.lanes)]
    return [slice(0, sh.lanes // 2), slice(sh.lanes // 2, sh.lanes)]


def stacked_keys(keys, start, size):
    k_s, tk_s = keys
    k = k_s[pl.ds(start, size), :]
    tk = tk_s[pl.ds(start, size), :]
    left = jnp.concatenate([k, tk], axis=0)
    right = jnp.concatenate([jnp.zeros_like(k), k], axis=0)
    return jnp.concatenate([left, right], axis=1)


def pieces_of(sh, start, blocks):
    sizes = [2] * (blocks // 2) + [1] * (blocks % 2)
    firsts = [sum(sizes[:i]) for i in range(len(sizes))]
    return [
        (pl.multiple_of(start + first * sh.block, sh.block), size * sh.block, i == len(sizes) - 1)
        for i, (first, size) in enumerate(zip(firsts, sizes))
    ]


def cut_diagonal(sh, value, other):
    low = below_diagonal(sh, value[value.shape[0] - sh.block :], other)
    if value.shape[0] == sh.block:
        return low
    return jnp.concatenate([value[: value.shape[0] - sh.block], low], axis=0)


def block_rows(sh, block):
    return pl.multiple_of(block * sh.block, sh.block)


def load_state(stat, lanes):
    return tuple(stat[r : r + 1, lanes] for r in range(3))


def forward_tile(sh, keys, vt_s, acc, stat, kept, qq, block, blocks, masked):
    w = sh.width
    start = block_rows(sh, block)
    pieces = pieces_of(sh, start, blocks)
    stacked = [stacked_keys(keys, at, size) for at, size, _ in pieces]
    at = pl.ds(start, blocks * sh.block)
    lanes = halves(sh)
    scores = [[] for _ in lanes]
    mixed = [[] for _ in lanes]
    most = [None for _ in lanes]
    state = [None if masked else load_state(stat, part) for part in lanes]

    def score(h, c):
        both = nt(stacked[c], qq[lanes[h], :])
        s, d = both[: pieces[c][1]], both[pieces[c][1] :]
        if masked and pieces[c][2]:
            s = cut_diagonal(sh, s, MASKED)
        scores[h].append((s, d))

    def top(h):
        peaks = [jnp.max(s, axis=0, keepdims=True) for s, _ in scores[h]]
        most[h] = functools.reduce(jnp.maximum, peaks) * sh.scale
        if not masked:
            most[h] = jnp.maximum(most[h], state[h][0])
        if kept is not None:
            for j in range(blocks):
                kept[1][block + j, :, lanes[h]] = most[h]

    def soften(h, c):
        s, d = scores[h][c]
        e = jnp.exp(s * sh.scale - most[h])
        mixed[h].append((e.astype(BF16), (e * d).astype(BF16)))
        if kept is not None:
            kept[0][pl.ds(pieces[c][0], pieces[c][1]), lanes[h]] = mixed[h][-1][0]

    def gather(h, i):
        return jnp.concatenate([pair[i] for pair in mixed[h]], axis=0)

    def finish(h, plain, moving):
        total, cross = plain[2 * w : 2 * w + 1], moving[w : w + 1]
        tangent = plain[:w] + moving[:w] * sh.scale
        plain = plain[w : 2 * w]
        if not masked:
            decay = jnp.exp(state[h][0] - most[h])
            plain = acc[:w, lanes[h]] * decay + plain
            tangent = acc[w:, lanes[h]] * decay + tangent
            total, cross = state[h][1] * decay + total, state[h][2] * decay + cross
        acc[:w, lanes[h]] = plain
        acc[w:, lanes[h]] = tangent
        for r, value in enumerate((most[h], total, cross)):
            stat[r : r + 1, lanes[h]] = value

    for h in range(len(lanes) + 1):
        if h > 0:
            top(h - 1)
        for c in range(len(pieces)):
            if h < len(lanes):
                score(h, c)
            if h > 0:
                soften(h - 1, c)
        if h > 0:
            plain = nn(vt_s[:, at], gather(h - 1, 0))
            moving = nn(vt_s[w:, at], gather(h - 1, 1))
            finish(h - 1, plain, moving)


def by_count(sh, low, count, run, masked):
    head = jnp.where(count <= 6, count, 3 + lax.rem(jnp.maximum(count - 7, 0), 4))
    fours = (count - head) // 4
    for blocks in range(1, min(6, sh.blocks) + 1):

        @pl.when(head == blocks)
        def _(blocks=blocks):
            if masked:
                run(low + count - blocks, blocks, True)
            else:
                run(low, blocks, False)

    def step(i, carry):
        run(low + (0 if masked else head) + 4 * i, 4, False)
        return carry

    if sh.blocks > 6:
        lax.fori_loop(0, fours, step, 0)


def lay_chunk(sh, me_ref, sources, targets):
    for m, (ref, base) in enumerate(sources):
        slot = pl.ds(slot_of(me_ref, m, sh.rows), sh.rows)
        for i, target in enumerate(targets):
            at = base + i * sh.rows
            target[slot, :] = ref[at : at + sh.rows, :]


def lay_queries(sh, me_ref, order, pieces, qq):
    per = sh.rows // sh.block
    for m, ref in zip(order, pieces):
        for i in range(2):
            for g in range(sh.group):
                for r in range(per):
                    block = jnp.bitwise_xor(me_ref[0], m) * per + r
                    at = (i * sh.group + g) * sh.rows + r * sh.block
                    qq[
                        block,
                        g * sh.block : (g + 1) * sh.block,
                        i * sh.width : (i + 1) * sh.width,
                    ] = ref[at : at + sh.block, :]


def lay_span(sh, me_ref, sources, laid):
    w = sh.width
    k_s, v_s, kt_s, tk_s, vt_s, tv_s = laid
    lay_chunk(sh, me_ref, sources, (k_s, v_s, tk_s, tv_s))
    kt_s[...] = transposed(k_s[...])
    vt_s[:w, :] = transposed(tv_s[...])
    vt_s[w : 2 * w, :] = transposed(v_s[...])
    vt_s[2 * w :, :] = jnp.ones((ONES_ROWS, sh.tokens), BF16)


def transposed(x):
    return x.astype(F32).T.astype(BF16)


def located(sh, refs):
    if len(refs) == sh.parts:
        return [(ref, 0) for ref in refs]
    length = refs[0].shape[0] // sh.parts
    return [(refs[0], m * length) for m in range(sh.parts)]


def back_of(sh, me_ref, back_ref, qb):
    per = sh.rows // sh.block
    return back_ref[jnp.bitwise_xor(me_ref[0], qb // per) * per + qb % per]


def each_block(count, run):
    def step(i, carry):
        run(i)
        return carry

    lax.fori_loop(0, count, step, 0)


def block_in_turn(sh, me_ref, order, i):
    per = sh.rows // sh.block
    if order == list(range(sh.parts)):
        return i
    partner = order[0]
    for j in range(1, len(order)):
        partner = jnp.where(i // per == j, order[j], partner)
    return jnp.bitwise_xor(me_ref[0], partner) * per + i % per


def kept_shapes(sh):
    return [
        jax.ShapeDtypeStruct((sh.blocks, sh.tokens, sh.lanes), BF16),
        jax.ShapeDtypeStruct((sh.blocks, sh.blocks, 1, sh.lanes), F32),
    ]


def forward_own(sh, me, back, order, queries, chunk, before):
    w = sh.width
    first = before is None
    turns = len(order) * (sh.rows // sh.block)

    def kernel(me_ref, back_ref, *refs):
        refs = list(refs)

        def take(count):
            taken = refs[:count]
            del refs[:count]
            return taken

        q_in = take(len(order))
        if first:
            kv_in = take(len(chunk))
            accs, stats, qq_s, es, ms = take(5)
            laid = refs
            lay_span(sh, me_ref, located(sh, kv_in), laid)
        else:
            laid = take(len(chunk))
            take(5)
            accs, stats, qq_s, es, ms = refs
        k_s, _, _, tk_s, vt_s = laid[:5]
        lay_queries(sh, me_ref, order, q_in, qq_s)

        def query_block(i):
            qb = block_in_turn(sh, me_ref, order, i)
            low = jnp.clip(qb - back_of(sh, me_ref, back_ref, qb), 0, qb)
            run = functools.partial(
                forward_tile,
                sh,
                (k_s, tk_s),
                vt_s,
                accs.at[qb],
                stats.at[qb],
                (es.at[qb], ms.at[qb]),
                qq_s[qb],
            )
            by_count(sh, low, qb + 1 - low, run, True)

        each_block(turns, query_block)

    def array(*shape, dtype=F32):
        return jax.ShapeDtypeStruct(shape, dtype)

    span = array(sh.tokens, w, dtype=BF16)
    out_shape = [
        array(sh.blocks, 2 * w, sh.lanes),
        array(sh.blocks, 8, sh.lanes),
        array(sh.blocks, sh.lanes, 2 * w, dtype=BF16),
        *kept_shapes(sh),
    ]
    operands = [*queries, *chunk]
    aliases = {}
    if first:
        out_shape += [span, span, array(w, sh.tokens, dtype=BF16), span]
        out_shape.append(array(2 * w + ONES_ROWS, sh.tokens, dtype=BF16))
    else:
        aliases = {2 + len(operands) + i: i for i in range(5)}
        operands += before
    work = sh.group * sh.tokens * sh.block * turns // 2
    return pl.pallas_call(
        kernel,
        in_specs=[SMEM, SMEM] + [VMEM] * len(operands),
        out_specs=[VMEM] * len(out_shape),
        out_shape=out_shape,
        input_output_aliases=aliases,
        scratch_shapes=[pltpu.VMEM((sh.tokens, w), BF16)] * first,
        compiler_params=params(),
        cost_estimate=cost(12 * work * w, 4 * sh.tokens * sh.lanes, work),
        name="forward_own",
    )(me, back, *operands)


def forward_chunk(sh, me, back, qq, chunk, distance, state, gain_square=None):
    w = sh.width
    closing = gain_square is not None

    def kernel(me_ref, back_ref, qq_s, *refs):
        refs = list(refs)

        def take(count):
            taken = refs[:count]
            del refs[:count]
            return taken

        kv_in = take(len(chunk))
        take(2)
        if closing:
            (gain_ref,) = take(1)
        k_s, v_s, kt_s, accs, stats = take(5)
        last = take(2)
        if closing:
            lse, sums = last
        tk_s, tv_s, vt_s = refs
        lay_span(sh, me_ref, located(sh, kv_in), (k_s, v_s, kt_s, tk_s, vt_s, tv_s))

        def query_block(qb):
            acc, stat = accs.at[qb], stats.at[qb]
            first = qb - back_of(sh, me_ref, back_ref, qb) + distance * sh.blocks
            first = jnp.clip(first, 0, sh.blocks)
            count = sh.blocks - first

            @pl.when(count > 0)
            def _():
                kept = None if closing else [ref.at[qb] for ref in last]
                run = functools.partial(
                    forward_tile, sh, (k_s, tk_s), vt_s, acc, stat, kept, qq_s[qb]
                )
                by_count(sh, first, count, run, False)

            if closing:
                most, total, cross = load_state(stat, slice(None))
                inverse = 1.0 / total
                plain = acc[:w, :] * inverse
                moved = acc[w:, :] * inverse - (cross * inverse * sh.scale) * plain
                acc[:w, :] = plain
                acc[w:, :] = moved
                lse[qb] = most + jnp.log(total)
                square = plain * plain
                product = plain * moved
                gain = gain_ref[...]
                for r, value in enumerate((square, product, gain * square, gain * product)):
                    line = jnp.sum(value, axis=0, keepdims=True)
                    pieces = [line[:, g * sh.block : (g + 1) * sh.block] for g in range(sh.group)]
                    sums[qb, r : r + 1, :] = functools.reduce(jnp.add, pieces)

        each_block(sh.blocks, query_block)

    def array(*shape, dtype=F32):
        return jax.ShapeDtypeStruct(shape, dtype)

    out_shape = [
        array(sh.tokens, w, dtype=BF16),
        array(sh.tokens, w, dtype=BF16),
        array(w, sh.tokens, dtype=BF16),
        array(sh.blocks, 2 * w, sh.lanes),
        array(sh.blocks, 8, sh.lanes),
    ]
    if closing:
        out_shape += [array(sh.blocks, 1, sh.lanes), array(sh.blocks, 4, sh.block)]
    else:
        out_shape += kept_shapes(sh)
    operands = [qq, *chunk]
    aliases = {2 + len(operands): 3, 3 + len(operands): 4}
    operands += state
    if closing:
        operands.append(gain_square)
    work = sh.group * sh.tokens * sh.tokens // 2
    return pl.pallas_call(
        kernel,
        in_specs=[SMEM, SMEM] + [VMEM] * len(operands),
        out_specs=[VMEM] * len(out_shape),
        out_shape=out_shape,
        input_output_aliases=aliases,
        scratch_shapes=[
            pltpu.VMEM((sh.tokens, w), BF16),
            pltpu.VMEM((sh.tokens, w), BF16),
            pltpu.VMEM((2 * w + ONES_ROWS, sh.tokens), BF16),
        ],
        compiler_params=params(),
        cost_estimate=cost(24 * work * w, 12 * sh.tokens * sh.lanes * 2, work),
        name="forward_far" if closing else "forward_chunk",
    )(me, back, *operands)


def backward_tile(sh, keys, kt_s, dkv_s, dq_s, qg, lse, dot, block, blocks, _):
    start, size = block_rows(sh, block), blocks * sh.block
    rows = pl.ds(start, size)
    k_s, v_s = keys
    k, v = k_s[rows, :], v_s[rows, :]
    empty = jnp.zeros_like(k)
    left = jnp.concatenate([k, empty], axis=0)
    right = jnp.concatenate([empty, v], axis=0)
    stacked = jnp.concatenate([left, right], axis=1)
    scores = [nt(stacked, qg[lanes, :]) for lanes in halves(sh)]
    for lanes, both in zip(halves(sh), scores):
        p = jnp.exp(both[:size] * sh.scale - lse[:, lanes])
        ds = (p * (both[size:] - dot[:, lanes])).astype(BF16)
        dkv_s[0, rows, :] += nn(ds, qg[lanes, : sh.width])
        dkv_s[1, rows, :] += nn(p.astype(BF16), qg[lanes, sh.width :])
        dq_s[:, lanes] += nn(kt_s[:, rows], ds)


def backward_kept(sh, keys, kt_s, dkv_s, dq_s, qg, lse, dot, kept, block, blocks, _):
    start, size = block_rows(sh, block), blocks * sh.block
    rows = pl.ds(start, size)
    v = keys[1][rows, :]
    slopes = [nt(v, qg[lanes, sh.width :]) for lanes in halves(sh)]
    for lanes, slope in zip(halves(sh), slopes):
        parts = []
        for j in range(blocks):
            factor = jnp.exp(kept[1][block + j, :, lanes] - lse[:, lanes])
            at = pl.ds(block_rows(sh, block + j), sh.block)
            parts.append(kept[0][at, lanes].astype(F32) * factor)
        p = jnp.concatenate(parts, axis=0)
        ds = (p * (slope - dot[:, lanes])).astype(BF16)
        dkv_s[0, rows, :] += nn(ds, qg[lanes, : sh.width])
        dkv_s[1, rows, :] += nn(p.astype(BF16), qg[lanes, sh.width :])
        dq_s[:, lanes] += nn(kt_s[:, rows], ds)


def backward_chunk(sh, me, back, qq, keys, distance, grads, lse, dots, dq, norm, order, held):
    w = sh.width
    opening, closing = norm is not None, distance == 0
    per = sh.rows // sh.block

    def kernel(me_ref, back_ref, *refs):
        refs = list(refs)

        def take(count):
            taken = refs[:count]
            del refs[:count]
            return taken

        qq_s, k_s, v_s, kt_s = take(4)
        kept = take(len(keys) - 3)
        (lse_s,) = take(1)
        if opening:
            out_s, gain_ref, *sum_refs = take(2 + len(norm[0]))
        else:
            grad_s, dot_s, dq_in = take(3)
        (held_ref,) = take(1) if held is not None else (None,)
        (dkv_out,) = take(1)
        dq_out = take(len(order) if closing else 1)
        if opening:
            grad_s, dot_s = take(2)
        dkv_s, dq_own = (dkv_out, *refs) if closing else refs
        if held_ref is None:
            dkv_s[...] = jnp.zeros_like(dkv_s)

        def query_block(i):
            qb = block_in_turn(sh, me_ref, order, i)
            dq_s = dq_own if closing else dq_out[0].at[qb]
            if opening:
                features = norm[2]
                token = functools.reduce(jnp.add, [ref[qb] for ref in sum_refs])
                sums = jnp.concatenate([token] * sh.group, axis=1)
                square = sums[0:1] / features + EPSILON
                inverse = lax.rsqrt(square)
                ratio = sums[1:2] / (features * square)
                again = (sums[3:4] - ratio * sums[2:3]) * inverse
                again = again / (features * square)
                plain = out_s[qb, :w, :]
                moved = out_s[qb, w:, :]
                first_grad = gain_ref[...] * (moved - plain * ratio) * inverse
                cot = ((first_grad - plain * again) * inverse).astype(BF16).astype(F32)
                dot_s[qb] = jnp.sum(cot * plain, axis=0, keepdims=True)
                grad_s[qb] = cot.T.astype(BF16)
                dq_s[...] = jnp.zeros((w, sh.lanes), F32)
            elif closing:
                dq_s[...] = dq_in[qb]

            top = sh.blocks if distance else qb + 1
            first = jnp.clip(qb - back_of(sh, me_ref, back_ref, qb) + distance * sh.blocks, 0, top)
            count = top - first

            @pl.when(count > 0)
            def _():
                qg = jnp.concatenate([qq_s[qb, :, :w], grad_s[qb]], axis=1)
                common = (sh, (k_s, v_s), kt_s, dkv_s, dq_s, qg, lse_s[qb], dot_s[qb])
                if kept:
                    run = functools.partial(backward_kept, *common, [ref.at[qb] for ref in kept])
                else:
                    run = functools.partial(backward_tile, *common)
                by_count(sh, first, count, run, False)

            if closing:
                done = (dq_s[...] * sh.scale).T.reshape(sh.group, sh.block, w).astype(BF16)
                at = pl.ds(pl.multiple_of(i % per * sh.block, sh.block), sh.block)
                for j, out in enumerate(dq_out):

                    @pl.when(i // per == j)
                    def _(out=out):
                        out[:, at, :] = done

        each_block(len(order) * per, query_block)
        if not closing:
            dkv_out[0] = (dkv_s[0] * sh.scale).astype(BF16)
            dkv_out[1] = dkv_s[1].astype(BF16)

    def array(*shape, dtype=F32):
        return jax.ShapeDtypeStruct(shape, dtype)

    operands = [qq, *keys, lse]
    if opening:
        operands += [grads, norm[1], *norm[0]]
    else:
        operands += [grads, dots, dq]
    aliases = {}
    if not opening and not closing:
        aliases = {1 + len(operands): 1}
    if held is not None:
        aliases = {2 + len(operands): 0}
        operands.append(held)
    out_shape = [array(2, sh.tokens, w, dtype=F32 if closing else BF16)]
    if closing:
        out_shape += [array(sh.group, sh.rows, w, dtype=BF16)] * len(order)
    else:
        out_shape.append(array(sh.blocks, w, sh.lanes))
    if opening:
        out_shape += [
            array(sh.blocks, sh.lanes, w, dtype=BF16),
            array(sh.blocks, 1, sh.lanes),
        ]
    work = sh.group * sh.tokens * len(order) * sh.rows // 2
    return pl.pallas_call(
        kernel,
        in_specs=[SMEM, SMEM] + [VMEM] * len(operands),
        out_specs=[VMEM] * len(out_shape),
        out_shape=out_shape,
        input_output_aliases=aliases,
        scratch_shapes=[pltpu.VMEM((2, sh.tokens, w), F32)] * (not closing)
        + [pltpu.VMEM((w, sh.lanes), F32)],
        compiler_params=params(),
        cost_estimate=cost(1, 1) if closing else cost(20 * work * w, 16 * work, work),
        name="backward_chunk",
    )(me, back, *operands)


def combine(sh, me, arrived, held):
    count = len(arrived)

    def kernel(me_ref, held_ref, *refs):
        for m, out in enumerate(refs[count:]):
            slot = pl.ds(slot_of(me_ref, m, sh.rows), sh.rows)
            for a, factor in ((0, sh.scale), (1, 1.0)):
                part = held_ref[a, slot, :] * factor
                for ref in refs[:count]:
                    part += ref[a, slot, :].astype(F32)
                out[a] = part.astype(BF16)

    return pl.pallas_call(
        kernel,
        in_specs=[SMEM] + [VMEM] * (1 + count),
        out_specs=[VMEM] * sh.parts,
        out_shape=[jax.ShapeDtypeStruct((2, sh.rows, sh.width), BF16)] * sh.parts,
        compiler_params=params(),
        cost_estimate=cost(0, 1),
        name="combine",
    )(me, held, *arrived)


def exchanged_with(piece, parts, m):
    return lax.ppermute(piece, "part", [(i, i ^ m) for i in range(parts)]) if m else piece


def exchanged(pieces, parts):
    return [exchanged_with(piece, parts, m) for m, piece in enumerate(pieces)]


def moved_on(value, steps):
    count = lax.axis_size("span")
    pairs = [(i, i + steps) for i in range(count) if 0 <= i + steps < count]
    return lax.ppermute(value, "span", pairs)


def summed_over_head(value):
    count = lax.axis_size("head")
    if count & (count - 1):
        return lax.psum(value, "head")
    step = 1
    while step < count:
        value = value + lax.ppermute(value, "head", [(i, i ^ step) for i in range(count)])
        step *= 2
    return value


def body(queries, keys, values, tangent_queries, tangent_keys, tangent_values, doc_start, out_gain):
    rows, query_heads, width = queries.shape
    key_heads = keys.shape[1]
    group = query_heads // key_heads
    parts = lax.axis_size("part")
    per = doc_start.shape[0]
    block = rows // per
    features = query_heads * width * lax.axis_size("head")
    hops = -(-DOC_DEVS // parts)
    sh = Shape(parts, group, rows, width, block)
    place = lax.axis_index("part")
    me = place.astype(jnp.int32).reshape(1)

    def flat(array):
        return array.reshape(-1, width)

    pieces = split_heads(
        [flat(a) for a in (keys, values, tangent_keys, tangent_values)], parts, 1, doc_start
    )
    q_rows, _ = lax.optimization_barrier(((flat(queries), flat(tangent_queries)), pieces[0]))
    q_pieces = split_heads(q_rows, parts, group)
    own, q_pieces = lax.optimization_barrier((pieces[0], q_pieces))
    pieces = exchanged(pieces, parts)
    late, q_pieces = lax.optimization_barrier((pieces[1:], q_pieces))
    chunks = [pieces, [moved_on(piece, 1) for piece in [own, *late]]]
    q_parts = exchanged(q_pieces[:-1], parts)
    if parts > 1:
        last, _ = lax.optimization_barrier((q_pieces[-1], q_parts[min(1, parts - 2)]))
        q_parts.append(exchanged_with(last, parts, parts - 1))
    else:
        q_parts = q_pieces
    back = jnp.concatenate([p[4 * rows : 4 * rows + per, 0] for p in pieces]).astype(jnp.int32)
    gain = lax.dynamic_index_in_dim(out_gain.reshape(key_heads, group, width), place, 0, False)
    gain_square = jnp.repeat((gain * gain).T, block, axis=1)

    everyone = list(range(parts))
    before, laid, ahead = None, chunks[0], chunks[1]
    for order in [everyone[:1], everyone[1:-1], everyone[-1:]] if parts > 1 else [everyone]:
        if order:
            turn = forward_own(sh, me, back, order, [q_parts[m] for m in order], laid, before)
            laid = turn[5:] or laid
            before = list(turn[:5])
        if parts > 1 and order == everyone[:1]:
            ahead, before[0] = lax.optimization_barrier((chunks[1], before[0]))
    for _ in range(hops - 1):
        ahead = [moved_on(jnp.concatenate(ahead, axis=0) if ahead[1:] else ahead[0], 1)]
        chunks.append(ahead)
    state, qq = before[:2], before[2]
    spans = [(*laid[:3], *before[3:])]
    for distance in range(1, hops):
        k, v, kt, acc, stat, *kept = forward_chunk(
            sh, me, back, qq, chunks[distance], distance, state
        )
        state = [acc, stat]
        spans.append((k, v, kt, *kept))
    k, v, kt, out, _, lse, sums = forward_chunk(
        sh, me, back, qq, chunks[hops], hops, state, gain_square
    )
    spans.append((k, v, kt))
    norm = (exchanged([summed_over_head(sums)] * parts, parts), gain_square, features)

    part, dq, grads, dots = backward_chunk(
        sh, me, back, qq, spans[hops], hops, out, lse, None, None, norm, everyone, None
    )
    arrived = [moved_on(part, -hops)]
    for distance in range(hops - 1, 0, -1):
        part, dq = backward_chunk(
            sh, me, back, qq, spans[distance], distance, grads, lse, dots, dq, None,
            everyone, None,
        )
        arrived.append(moved_on(part, -distance))
    turns = [turn[::-1] for turn in (everyone[-1:], everyone[:-1]) if turn]
    held, dq_pieces = None, [None] * parts
    for order in turns:
        if held is not None:
            arrived[0], held = lax.optimization_barrier((arrived[0], held))
        held, *done = backward_chunk(
            sh, me, back, qq, spans[0], 0, grads, lse, dots, dq, None, order, held
        )
        for m, piece in zip(order, done):
            dq_pieces[m] = piece.reshape(1, group, rows, width)
    dq_pieces = exchanged(dq_pieces, parts)
    dq_pieces[-1], held = lax.optimization_barrier((dq_pieces[-1], held))
    dkv_pieces = exchanged(combine(sh, me, arrived, held), parts)
    (product_queries,) = join_heads(dq_pieces, 1, group)
    dkv_pieces, _ = lax.optimization_barrier((dkv_pieces, product_queries))
    dkv_pieces = [p.reshape(2, 1, rows, width) for p in dkv_pieces]
    product_keys, product_values = join_heads(dkv_pieces, 2, 1)
    return (
        product_queries.reshape(queries.shape),
        product_keys.reshape(keys.shape),
        product_values.reshape(keys.shape),
    )


def solution(mesh):
    def run(*arguments):
        count, heads = mesh.shape["ctx"], mesh.shape["head"]
        parts = arguments[1].shape[1] // heads
        split = Mesh(
            mesh.devices.reshape(count // parts, parts, heads), ("span", "part", "head")
        )
        ctx = ("span", "part")
        array = P(ctx, "head", None)
        return jax.shard_map(
            body,
            mesh=split,
            in_specs=(array,) * 6 + (P(ctx), P("head")),
            out_specs=(array,) * 3,
            check_vma=False,
        )(*arguments)

    return run
```

```python
import functools

import jax
import jax.numpy as jnp
from jax import lax
from jax.experimental import pallas as pl
from jax.experimental.pallas import tpu as pltpu
from jax.sharding import Mesh, PartitionSpec as P

DOC_DEVS = 8
EPSILON = 1e-06
VMEM_BYTES = 10 * 1024 * 1024
NOTE_ROWS = 16
ONES_ROWS = 16
WIDE_VMEM_BYTES = 60 * 1024 * 1024
MASKED = -1e30
F32 = jnp.float32
BF16 = jnp.bfloat16
SMEM = pl.BlockSpec(memory_space=pltpu.SMEM)
VMEM = pl.BlockSpec(memory_space=pltpu.VMEM)


def params(size=VMEM_BYTES):
    return pltpu.CompilerParams(vmem_limit_bytes=size)


def cost(flops, moved, powers=0):
    return pl.CostEstimate(flops=int(flops), bytes_accessed=int(moved), transcendentals=int(powers))


def nn(a, b):
    return lax.dot_general(a, b, (((1,), (0,)), ((), ())), preferred_element_type=F32)


def nt(a, b):
    return lax.dot_general(a, b, (((1,), (1,)), ((), ())), preferred_element_type=F32)


def split_heads(arrays, parts, per_part, notes=None):
    count = len(arrays)
    total, width = arrays[0].shape
    heads = parts * per_part
    rows = total // heads
    length = count * per_part * rows
    extra = 0 if notes is None else NOTE_ROWS
    scalars = [] if notes is None else [notes]

    def kernel(*refs):
        ins = list(refs[: len(scalars) + count])
        outs, (held, wide, sems) = refs[len(scalars) + count : -3], refs[-3:]
        mine = lax.axis_index("part")
        if extra:
            note_ref = ins.pop(0)
        copies = [pltpu.make_async_copy(ins[a], held.at[a], sems.at[a]) for a in range(count)]
        for copy in copies:
            copy.start()
        if extra:
            first = (lax.axis_index("span") * parts + mine) * notes.shape[0]
            line = lax.broadcasted_iota(jnp.int32, (extra, width), 0)
            lines = jnp.zeros((extra, width), jnp.int32)
            for i in range(notes.shape[0]):
                lines = jnp.where(line == i, first + i - note_ref[i], lines)
            for out in outs:
                out[length:, :] = lines.astype(F32).astype(BF16)
        for a in range(count):
            copies[a].wait()
            wide[...] = held[a].astype(F32)
            for m in range(parts):
                for r in range(per_part):
                    head = jnp.bitwise_xor(mine, m) * per_part + r
                    at = (a * per_part + r) * rows
                    outs[m][at : at + rows, :] = wide[pl.ds(head, rows, stride=heads), :].astype(BF16)

    return pl.pallas_call(
        kernel,
        in_specs=[SMEM] * len(scalars) + [pl.BlockSpec(memory_space=pltpu.HBM)] * count,
        out_specs=[pl.BlockSpec(memory_space=pltpu.VMEM)] * parts,
        out_shape=[jax.ShapeDtypeStruct((length + extra, width), BF16)] * parts,
        scratch_shapes=[
            pltpu.VMEM((count, total, width), BF16),
            pltpu.VMEM((total, width), F32),
            pltpu.SemaphoreType.DMA((count,)),
        ],
        compiler_params=params(VMEM_BYTES if notes is None else WIDE_VMEM_BYTES),
        cost_estimate=cost(0, 4 * count * total * width),
        name="split_heads",
    )(*scalars, *arrays)


def join_heads(pieces, count, per_part, after=None):
    parts = len(pieces)
    rows, width = pieces[0].shape[-2:]
    heads = parts * per_part
    steps = 4
    cut = rows // steps
    marks = [] if after is None else [after]

    def kernel(*refs):
        ins, outs = refs[:parts], refs[parts + len(marks) :]
        mine = lax.axis_index("part")
        outs[-1][0] = mine
        for a in range(count):
            for m in range(parts):
                for r in range(per_part):
                    head = jnp.bitwise_xor(mine, m) * per_part + r
                    outs[a][pl.ds(head, cut, stride=heads), :] = ins[m][a, r].astype(F32)

    return pl.pallas_call(
        kernel,
        grid=(steps,),
        in_specs=[pl.BlockSpec((count, per_part, cut, width), lambda i: (0, 0, i, 0))] * parts
        + [SMEM] * len(marks),
        out_specs=[pl.BlockSpec((cut * heads, width), lambda i: (i, 0))] * count + [SMEM],
        out_shape=[jax.ShapeDtypeStruct((rows * heads, width), F32)] * count
        + [jax.ShapeDtypeStruct((1,), jnp.int32)],
        compiler_params=params(),
        cost_estimate=cost(0, 6 * count * rows * heads * width),
        name="join_heads",
    )(*pieces, *marks)


def slot_of(me_ref, m, rows):
    return pl.multiple_of(jnp.bitwise_xor(me_ref[0], m) * rows, rows)


class Shape:
    def __init__(self, parts, group, rows, width, block):
        self.parts, self.group, self.rows, self.width, self.block = parts, group, rows, width, block
        self.tokens = parts * rows
        self.blocks = self.tokens // block
        self.lanes = group * block
        self.scale = width**-0.5


def diagonal(sh):
    shape = (sh.block, sh.block)
    key = lax.broadcasted_iota(jnp.int32, shape, 0)
    query = lax.broadcasted_iota(jnp.int32, shape, 1)
    return key <= query


def below_diagonal(sh, value, other):
    allowed = diagonal(sh)
    cut = [value[:, at : at + sh.block] for at in range(0, value.shape[1], sh.block)]
    return jnp.concatenate([jnp.where(allowed, part, other) for part in cut], axis=1)


def halves(sh):
    if sh.group % 2:
        return [slice(0, sh.lanes)]
    return [slice(0, sh.lanes // 2), slice(sh.lanes // 2, sh.lanes)]


def stacked_keys(keys, start, size):
    k_s, tk_s = keys
    k = k_s[pl.ds(start, size), :]
    tk = tk_s[pl.ds(start, size), :]
    left = jnp.concatenate([k, tk], axis=0)
    right = jnp.concatenate([jnp.zeros_like(k), k], axis=0)
    return jnp.concatenate([left, right], axis=1)


def pieces_of(sh, start, blocks):
    sizes = [2] * (blocks // 2) + [1] * (blocks % 2)
    firsts = [sum(sizes[:i]) for i in range(len(sizes))]
    return [
        (pl.multiple_of(start + first * sh.block, sh.block), size * sh.block, i == len(sizes) - 1)
        for i, (first, size) in enumerate(zip(firsts, sizes))
    ]


def cut_diagonal(sh, value, other):
    low = below_diagonal(sh, value[value.shape[0] - sh.block :], other)
    if value.shape[0] == sh.block:
        return low
    return jnp.concatenate([value[: value.shape[0] - sh.block], low], axis=0)


def block_rows(sh, block):
    return pl.multiple_of(block * sh.block, sh.block)


def load_state(stat, lanes):
    return tuple(stat[r : r + 1, lanes] for r in range(3))


def forward_tile(sh, keys, vt_s, acc, stat, kept, qq, block, blocks, masked):
    w = sh.width
    start = block_rows(sh, block)
    pieces = pieces_of(sh, start, blocks)
    stacked = [stacked_keys(keys, at, size) for at, size, _ in pieces]
    at = pl.ds(start, blocks * sh.block)
    lanes = halves(sh)
    scores = [[] for _ in lanes]
    mixed = [[] for _ in lanes]
    most = [None for _ in lanes]
    state = [None if masked else load_state(stat, part) for part in lanes]

    def score(h, c):
        both = nt(stacked[c], qq[lanes[h], :])
        s, d = both[: pieces[c][1]], both[pieces[c][1] :]
        if masked and pieces[c][2]:
            s = cut_diagonal(sh, s, MASKED)
        scores[h].append((s, d))

    def top(h):
        peaks = [jnp.max(s, axis=0, keepdims=True) for s, _ in scores[h]]
        most[h] = functools.reduce(jnp.maximum, peaks) * sh.scale
        if not masked:
            most[h] = jnp.maximum(most[h], state[h][0])
        if kept is not None:
            for j in range(blocks):
                kept[1][block + j, :, lanes[h]] = most[h]

    def soften(h, c):
        s, d = scores[h][c]
        e = jnp.exp(s * sh.scale - most[h])
        mixed[h].append((e.astype(BF16), (e * d).astype(BF16)))
        if kept is not None:
            kept[0][pl.ds(pieces[c][0], pieces[c][1]), lanes[h]] = mixed[h][-1][0]

    def gather(h, i):
        return jnp.concatenate([pair[i] for pair in mixed[h]], axis=0)

    def finish(h, plain, moving):
        total, cross = plain[2 * w : 2 * w + 1], moving[w : w + 1]
        tangent = plain[:w] + moving[:w] * sh.scale
        plain = plain[w : 2 * w]
        if not masked:
            decay = jnp.exp(state[h][0] - most[h])
            plain = acc[:w, lanes[h]] * decay + plain
            tangent = acc[w:, lanes[h]] * decay + tangent
            total, cross = state[h][1] * decay + total, state[h][2] * decay + cross
        acc[:w, lanes[h]] = plain
        acc[w:, lanes[h]] = tangent
        for r, value in enumerate((most[h], total, cross)):
            stat[r : r + 1, lanes[h]] = value

    for h in range(len(lanes) + 1):
        if h > 0:
            top(h - 1)
        for c in range(len(pieces)):
            if h < len(lanes):
                score(h, c)
            if h > 0:
                soften(h - 1, c)
        if h > 0:
            plain = nn(vt_s[:, at], gather(h - 1, 0))
            moving = nn(vt_s[w:, at], gather(h - 1, 1))
            finish(h - 1, plain, moving)


def by_count(sh, low, count, run, masked):
    head = jnp.where(count <= 6, count, 3 + lax.rem(jnp.maximum(count - 7, 0), 4))
    fours = (count - head) // 4
    for blocks in range(1, min(6, sh.blocks) + 1):

        @pl.when(head == blocks)
        def _(blocks=blocks):
            if masked:
                run(low + count - blocks, blocks, True)
            else:
                run(low, blocks, False)

    def step(i, carry):
        run(low + (0 if masked else head) + 4 * i, 4, False)
        return carry

    if sh.blocks > 6:
        lax.fori_loop(0, fours, step, 0)


def lay_chunk(sh, me_ref, sources, targets):
    for m, (ref, base) in enumerate(sources):
        slot = pl.ds(slot_of(me_ref, m, sh.rows), sh.rows)
        for i, target in enumerate(targets):
            at = base + i * sh.rows
            target[slot, :] = ref[at : at + sh.rows, :]


def lay_queries(sh, me_ref, order, pieces, qq):
    per = sh.rows // sh.block
    for m, ref in zip(order, pieces):
        for i in range(2):
            for g in range(sh.group):
                for r in range(per):
                    block = jnp.bitwise_xor(me_ref[0], m) * per + r
                    at = (i * sh.group + g) * sh.rows + r * sh.block
                    qq[
                        block,
                        g * sh.block : (g + 1) * sh.block,
                        i * sh.width : (i + 1) * sh.width,
                    ] = ref[at : at + sh.block, :]


def lay_span(sh, me_ref, sources, laid):
    w = sh.width
    k_s, v_s, kt_s, tk_s, vt_s, tv_s = laid
    lay_chunk(sh, me_ref, sources, (k_s, v_s, tk_s, tv_s))
    kt_s[...] = transposed(k_s[...])
    vt_s[:w, :] = transposed(tv_s[...])
    vt_s[w : 2 * w, :] = transposed(v_s[...])
    vt_s[2 * w :, :] = jnp.ones((ONES_ROWS, sh.tokens), BF16)


def transposed(x):
    return x.astype(F32).T.astype(BF16)


def located(sh, refs):
    if len(refs) == sh.parts:
        return [(ref, 0) for ref in refs]
    length = refs[0].shape[0] // sh.parts
    return [(refs[0], m * length) for m in range(sh.parts)]


def back_of(sh, me_ref, back_ref, qb):
    per = sh.rows // sh.block
    return back_ref[jnp.bitwise_xor(me_ref[0], qb // per) * per + qb % per]


def each_block(count, run):
    def step(i, carry):
        run(i)
        return carry

    lax.fori_loop(0, count, step, 0)


def block_in_turn(sh, me_ref, order, i):
    per = sh.rows // sh.block
    if order == list(range(sh.parts)):
        return i
    partner = order[0]
    for j in range(1, len(order)):
        partner = jnp.where(i // per == j, order[j], partner)
    return jnp.bitwise_xor(me_ref[0], partner) * per + i % per


def kept_shapes(sh):
    return [
        jax.ShapeDtypeStruct((sh.blocks, sh.tokens, sh.lanes), BF16),
        jax.ShapeDtypeStruct((sh.blocks, sh.blocks, 1, sh.lanes), F32),
    ]


def forward_own(sh, me, back, order, queries, chunk, before):
    w = sh.width
    first = before is None
    turns = len(order) * (sh.rows // sh.block)

    def kernel(me_ref, back_ref, *refs):
        refs = list(refs)

        def take(count):
            taken = refs[:count]
            del refs[:count]
            return taken

        q_in = take(len(order))
        if first:
            kv_in = take(len(chunk))
            accs, stats, qq_s, es, ms = take(5)
            back_out = refs.pop(5)
            for i in range(sh.blocks):
                back_out[i] = back_ref[i]
            laid = refs
            lay_span(sh, me_ref, located(sh, kv_in), laid)
        else:
            laid = take(len(chunk))
            take(5)
            accs, stats, qq_s, es, ms = refs
        k_s, _, _, tk_s, vt_s = laid[:5]
        lay_queries(sh, me_ref, order, q_in, qq_s)

        def query_block(i):
            qb = block_in_turn(sh, me_ref, order, i)
            low = jnp.clip(qb - back_of(sh, me_ref, back_ref, qb), 0, qb)
            run = functools.partial(
                forward_tile,
                sh,
                (k_s, tk_s),
                vt_s,
                accs.at[qb],
                stats.at[qb],
                (es.at[qb], ms.at[qb]),
                qq_s[qb],
            )
            by_count(sh, low, qb + 1 - low, run, True)

        each_block(turns, query_block)

    def array(*shape, dtype=F32):
        return jax.ShapeDtypeStruct(shape, dtype)

    span = array(sh.tokens, w, dtype=BF16)
    out_shape = [
        array(sh.blocks, 2 * w, sh.lanes),
        array(sh.blocks, 8, sh.lanes),
        array(sh.blocks, sh.lanes, 2 * w, dtype=BF16),
        *kept_shapes(sh),
    ]
    operands = [*queries, *chunk]
    aliases = {}
    if first:
        out_shape += [span, span, array(w, sh.tokens, dtype=BF16), span]
        out_shape.append(array(2 * w + ONES_ROWS, sh.tokens, dtype=BF16))
        out_shape.append(array(sh.blocks, dtype=jnp.int32))
    else:
        aliases = {2 + len(operands) + i: i for i in range(5)}
        operands += before
    work = sh.group * sh.tokens * sh.block * turns // 2
    return pl.pallas_call(
        kernel,
        in_specs=[SMEM, SMEM] + [VMEM] * len(operands),
        out_specs=[VMEM if len(shape.shape) > 1 else SMEM for shape in out_shape],
        out_shape=out_shape,
        input_output_aliases=aliases,
        scratch_shapes=[pltpu.VMEM((sh.tokens, w), BF16)] * first,
        compiler_params=params(),
        cost_estimate=cost(12 * work * w, 4 * sh.tokens * sh.lanes, work),
        name="forward_own",
    )(me, back, *operands)


def forward_chunk(sh, me, back, qq, chunk, distance, state, gain_square=None):
    w = sh.width
    closing = gain_square is not None

    def kernel(me_ref, back_ref, qq_s, *refs):
        refs = list(refs)

        def take(count):
            taken = refs[:count]
            del refs[:count]
            return taken

        kv_in = take(len(chunk))
        take(2)
        if closing:
            (gain_ref,) = take(1)
        k_s, v_s, kt_s, accs, stats = take(5)
        last = take(2)
        if closing:
            lse, sums = last
        tk_s, tv_s, vt_s = refs
        lay_span(sh, me_ref, located(sh, kv_in), (k_s, v_s, kt_s, tk_s, vt_s, tv_s))

        def query_block(qb):
            acc, stat = accs.at[qb], stats.at[qb]
            first = qb - back_of(sh, me_ref, back_ref, qb) + distance * sh.blocks
            first = jnp.clip(first, 0, sh.blocks)
            count = sh.blocks - first

            @pl.when(count > 0)
            def _():
                kept = None if closing else [ref.at[qb] for ref in last]
                run = functools.partial(
                    forward_tile, sh, (k_s, tk_s), vt_s, acc, stat, kept, qq_s[qb]
                )
                by_count(sh, first, count, run, False)

            if closing:
                most, total, cross = load_state(stat, slice(None))
                inverse = 1.0 / total
                plain = acc[:w, :] * inverse
                moved = acc[w:, :] * inverse - (cross * inverse * sh.scale) * plain
                acc[:w, :] = plain
                acc[w:, :] = moved
                lse[qb] = most + jnp.log(total)
                square = plain * plain
                product = plain * moved
                gain = gain_ref[...]
                for r, value in enumerate((square, product, gain * square, gain * product)):
                    line = jnp.sum(value, axis=0, keepdims=True)
                    pieces = [line[:, g * sh.block : (g + 1) * sh.block] for g in range(sh.group)]
                    sums[qb, r : r + 1, :] = functools.reduce(jnp.add, pieces)

        each_block(sh.blocks, query_block)

    def array(*shape, dtype=F32):
        return jax.ShapeDtypeStruct(shape, dtype)

    out_shape = [
        array(sh.tokens, w, dtype=BF16),
        array(sh.tokens, w, dtype=BF16),
        array(w, sh.tokens, dtype=BF16),
        array(sh.blocks, 2 * w, sh.lanes),
        array(sh.blocks, 8, sh.lanes),
    ]
    if closing:
        out_shape += [array(sh.blocks, 1, sh.lanes), array(sh.blocks, 4, sh.block)]
    else:
        out_shape += kept_shapes(sh)
    operands = [qq, *chunk]
    aliases = {2 + len(operands): 3, 3 + len(operands): 4}
    operands += state
    if closing:
        operands.append(gain_square)
    work = sh.group * sh.tokens * sh.tokens // 2
    return pl.pallas_call(
        kernel,
        in_specs=[SMEM, SMEM] + [VMEM] * len(operands),
        out_specs=[VMEM] * len(out_shape),
        out_shape=out_shape,
        input_output_aliases=aliases,
        scratch_shapes=[
            pltpu.VMEM((sh.tokens, w), BF16),
            pltpu.VMEM((sh.tokens, w), BF16),
            pltpu.VMEM((2 * w + ONES_ROWS, sh.tokens), BF16),
        ],
        compiler_params=params(),
        cost_estimate=cost(24 * work * w, 12 * sh.tokens * sh.lanes * 2, work),
        name="forward_far" if closing else "forward_chunk",
    )(me, back, *operands)


def backward_tile(sh, keys, kt_s, dkv_s, dq_s, qg, lse, dot, block, blocks, _):
    start, size = block_rows(sh, block), blocks * sh.block
    rows = pl.ds(start, size)
    k_s, v_s = keys
    k, v = k_s[rows, :], v_s[rows, :]
    empty = jnp.zeros_like(k)
    left = jnp.concatenate([k, empty], axis=0)
    right = jnp.concatenate([empty, v], axis=0)
    stacked = jnp.concatenate([left, right], axis=1)
    scores = [nt(stacked, qg[lanes, :]) for lanes in halves(sh)]
    for lanes, both in zip(halves(sh), scores):
        p = jnp.exp(both[:size] * sh.scale - lse[:, lanes])
        ds = (p * (both[size:] - dot[:, lanes])).astype(BF16)
        dkv_s[0, rows, :] += nn(ds, qg[lanes, : sh.width])
        dkv_s[1, rows, :] += nn(p.astype(BF16), qg[lanes, sh.width :])
        dq_s[:, lanes] += nn(kt_s[:, rows], ds)


def backward_kept(sh, keys, kt_s, dkv_s, dq_s, qg, lse, dot, kept, block, blocks, _):
    start, size = block_rows(sh, block), blocks * sh.block
    rows = pl.ds(start, size)
    v = keys[1][rows, :]
    slopes = [nt(v, qg[lanes, sh.width :]) for lanes in halves(sh)]
    for lanes, slope in zip(halves(sh), slopes):
        parts = []
        for j in range(blocks):
            factor = jnp.exp(kept[1][block + j, :, lanes] - lse[:, lanes])
            at = pl.ds(block_rows(sh, block + j), sh.block)
            parts.append(kept[0][at, lanes].astype(F32) * factor)
        p = jnp.concatenate(parts, axis=0)
        ds = (p * (slope - dot[:, lanes])).astype(BF16)
        dkv_s[0, rows, :] += nn(ds, qg[lanes, : sh.width])
        dkv_s[1, rows, :] += nn(p.astype(BF16), qg[lanes, sh.width :])
        dq_s[:, lanes] += nn(kt_s[:, rows], ds)


def backward_chunk(sh, me, back, qq, keys, distance, grads, lse, dots, dq, norm, order, held):
    w = sh.width
    opening, closing = norm is not None, distance == 0
    per = sh.rows // sh.block

    def kernel(me_ref, back_ref, *refs):
        refs = list(refs)

        def take(count):
            taken = refs[:count]
            del refs[:count]
            return taken

        qq_s, k_s, v_s, kt_s = take(4)
        kept = take(len(keys) - 3)
        (lse_s,) = take(1)
        if opening:
            out_s, gain_ref, *sum_refs = take(2 + len(norm[0]))
        else:
            grad_s, dot_s, dq_in = take(3)
        (held_ref,) = take(1) if held is not None else (None,)
        (dkv_out,) = take(1)
        dq_out = take(len(order) if closing else 1)
        if opening:
            grad_s, dot_s = take(2)
        dkv_s, dq_own = (dkv_out, *refs) if closing else refs
        if held_ref is None:
            dkv_s[...] = jnp.zeros_like(dkv_s)

        def query_block(i):
            qb = block_in_turn(sh, me_ref, order, i)
            dq_s = dq_own if closing else dq_out[0].at[qb]
            if opening:
                features = norm[2]
                token = functools.reduce(jnp.add, [ref[qb] for ref in sum_refs])
                sums = jnp.concatenate([token] * sh.group, axis=1)
                square = sums[0:1] / features + EPSILON
                inverse = lax.rsqrt(square)
                ratio = sums[1:2] / (features * square)
                again = (sums[3:4] - ratio * sums[2:3]) * inverse
                again = again / (features * square)
                plain = out_s[qb, :w, :]
                moved = out_s[qb, w:, :]
                first_grad = gain_ref[...] * (moved - plain * ratio) * inverse
                cot = ((first_grad - plain * again) * inverse).astype(BF16).astype(F32)
                dot_s[qb] = jnp.sum(cot * plain, axis=0, keepdims=True)
                grad_s[qb] = cot.T.astype(BF16)
                dq_s[...] = jnp.zeros((w, sh.lanes), F32)
            elif closing:
                dq_s[...] = dq_in[qb]

            top = sh.blocks if distance else qb + 1
            first = jnp.clip(qb - back_of(sh, me_ref, back_ref, qb) + distance * sh.blocks, 0, top)
            count = top - first

            @pl.when(count > 0)
            def _():
                qg = jnp.concatenate([qq_s[qb, :, :w], grad_s[qb]], axis=1)
                common = (sh, (k_s, v_s), kt_s, dkv_s, dq_s, qg, lse_s[qb], dot_s[qb])
                if kept:
                    run = functools.partial(backward_kept, *common, [ref.at[qb] for ref in kept])
                else:
                    run = functools.partial(backward_tile, *common)
                by_count(sh, first, count, run, False)

            if closing:
                done = (dq_s[...] * sh.scale).T.reshape(sh.group, sh.block, w).astype(BF16)
                at = pl.ds(pl.multiple_of(i % per * sh.block, sh.block), sh.block)
                for j, out in enumerate(dq_out):

                    @pl.when(i // per == j)
                    def _(out=out):
                        out[:, at, :] = done

        each_block(len(order) * per, query_block)
        if not closing:
            dkv_out[0] = (dkv_s[0] * sh.scale).astype(BF16)
            dkv_out[1] = dkv_s[1].astype(BF16)

    def array(*shape, dtype=F32):
        return jax.ShapeDtypeStruct(shape, dtype)

    operands = [qq, *keys, lse]
    if opening:
        operands += [grads, norm[1], *norm[0]]
    else:
        operands += [grads, dots, dq]
    aliases = {}
    if not opening and not closing:
        aliases = {1 + len(operands): 1}
    if held is not None:
        aliases = {2 + len(operands): 0}
        operands.append(held)
    out_shape = [array(2, sh.tokens, w, dtype=F32 if closing else BF16)]
    if closing:
        out_shape += [array(sh.group, sh.rows, w, dtype=BF16)] * len(order)
    else:
        out_shape.append(array(sh.blocks, w, sh.lanes))
    if opening:
        out_shape += [
            array(sh.blocks, sh.lanes, w, dtype=BF16),
            array(sh.blocks, 1, sh.lanes),
        ]
    work = sh.group * sh.tokens * len(order) * sh.rows // 2
    return pl.pallas_call(
        kernel,
        in_specs=[SMEM, SMEM] + [VMEM] * len(operands),
        out_specs=[VMEM] * len(out_shape),
        out_shape=out_shape,
        input_output_aliases=aliases,
        scratch_shapes=[pltpu.VMEM((2, sh.tokens, w), F32)] * (not closing)
        + [pltpu.VMEM((w, sh.lanes), F32)],
        compiler_params=params(),
        cost_estimate=cost(1, 1) if closing else cost(20 * work * w, 16 * work, work),
        name="backward_chunk",
    )(me, back, *operands)


def combine(sh, me, arrived, held):
    count = len(arrived)

    def kernel(me_ref, held_ref, *refs):
        for m, out in enumerate(refs[count:]):
            slot = pl.ds(slot_of(me_ref, m, sh.rows), sh.rows)
            for a, factor in ((0, sh.scale), (1, 1.0)):
                part = held_ref[a, slot, :] * factor
                for ref in refs[:count]:
                    part += ref[a, slot, :].astype(F32)
                out[a] = part.astype(BF16)

    return pl.pallas_call(
        kernel,
        in_specs=[SMEM] + [VMEM] * (1 + count),
        out_specs=[VMEM] * sh.parts,
        out_shape=[jax.ShapeDtypeStruct((2, sh.rows, sh.width), BF16)] * sh.parts,
        compiler_params=params(),
        cost_estimate=cost(0, 1),
        name="combine",
    )(me, held, *arrived)


def exchanged_with(piece, parts, m):
    return lax.ppermute(piece, "part", [(i, i ^ m) for i in range(parts)]) if m else piece


def exchanged(pieces, parts):
    return [exchanged_with(piece, parts, m) for m, piece in enumerate(pieces)]


def moved_on(value, steps):
    count = lax.axis_size("span")
    pairs = [(i, i + steps) for i in range(count) if 0 <= i + steps < count]
    return lax.ppermute(value, "span", pairs)


def summed_over_head(value):
    count = lax.axis_size("head")
    if count & (count - 1):
        return lax.psum(value, "head")
    step = 1
    while step < count:
        value = value + lax.ppermute(value, "head", [(i, i ^ step) for i in range(count)])
        step *= 2
    return value


def body(queries, keys, values, tangent_queries, tangent_keys, tangent_values, doc_start, out_gain):
    rows, query_heads, width = queries.shape
    key_heads = keys.shape[1]
    group = query_heads // key_heads
    parts = lax.axis_size("part")
    per = doc_start.shape[0]
    block = rows // per
    features = query_heads * width * lax.axis_size("head")
    hops = -(-DOC_DEVS // parts)
    sh = Shape(parts, group, rows, width, block)
    place = lax.axis_index("part")
    me = place.astype(jnp.int32).reshape(1)

    def flat(array):
        return array.reshape(-1, width)

    pieces = list(
        split_heads(
            [flat(a) for a in (keys, values, tangent_keys, tangent_values)], parts, 1, doc_start
        )
    )
    q_rows, pieces[0] = lax.optimization_barrier(((flat(queries), flat(tangent_queries)), pieces[0]))
    q_pieces = split_heads(q_rows, parts, group)
    own, q_pieces = lax.optimization_barrier((pieces[0], q_pieces))
    pieces = exchanged(pieces, parts)
    late, q_pieces = lax.optimization_barrier((pieces[1:], q_pieces))
    chunks = [pieces, [moved_on(piece, 1) for piece in [own, *late]]]
    q_parts = exchanged(q_pieces, parts)
    back = jnp.concatenate([p[4 * rows : 4 * rows + per, 0] for p in pieces]).astype(jnp.int32)
    gain = lax.dynamic_index_in_dim(out_gain.reshape(key_heads, group, width), place, 0, False)
    gain_square = jnp.repeat((gain * gain).T, block, axis=1)

    everyone = list(range(parts))
    before, laid, ahead = None, chunks[0], chunks[1]
    for order in [everyone[:1], everyone[1:-1], everyone[-1:]] if parts > 1 else [everyone]:
        if order:
            turn = forward_own(sh, me, back, order, [q_parts[m] for m in order], laid, before)
            laid = turn[5:10] or laid
            before = list(turn[:5])
        if parts > 1 and order == everyone[:1]:
            ahead, back = lax.optimization_barrier((chunks[1], turn[-1]))
    for _ in range(hops - 1):
        ahead = [moved_on(jnp.concatenate(ahead, axis=0) if ahead[1:] else ahead[0], 1)]
        chunks.append(ahead)
    state, qq = before[:2], before[2]
    spans = [(*laid[:3], *before[3:])]
    for distance in range(1, hops):
        k, v, kt, acc, stat, *kept = forward_chunk(
            sh, me, back, qq, chunks[distance], distance, state
        )
        state = [acc, stat]
        spans.append((k, v, kt, *kept))
    k, v, kt, out, _, lse, sums = forward_chunk(
        sh, me, back, qq, chunks[hops], hops, state, gain_square
    )
    spans.append((k, v, kt))
    norm = (exchanged([summed_over_head(sums)] * parts, parts), gain_square, features)

    part, dq, grads, dots = backward_chunk(
        sh, me, back, qq, spans[hops], hops, out, lse, None, None, norm, everyone, None
    )
    arrived = [moved_on(part, -hops)]
    for distance in range(hops - 1, 0, -1):
        part, dq = backward_chunk(
            sh, me, back, qq, spans[distance], distance, grads, lse, dots, dq, None,
            everyone, None,
        )
        arrived.append(moved_on(part, -distance))
    turns = [turn[::-1] for turn in (everyone[-1:], everyone[:-1]) if turn]
    held, dq_pieces = None, [None] * parts
    for order in turns:
        if held is not None:
            arrived[0], held = lax.optimization_barrier((arrived[0], held))
        held, *done = backward_chunk(
            sh, me, back, qq, spans[0], 0, grads, lse, dots, dq, None, order, held
        )
        for m, piece in zip(order, done):
            dq_pieces[m] = piece.reshape(1, group, rows, width)
    dq_pieces = exchanged(dq_pieces, parts)
    dq_pieces[-1], held = lax.optimization_barrier((dq_pieces[-1], held))
    dkv_pieces = exchanged(combine(sh, me, arrived, held), parts)
    product_queries, mark = join_heads(dq_pieces, 1, group)
    dkv_pieces = [p.reshape(2, 1, rows, width) for p in dkv_pieces]
    product_keys, product_values, _ = join_heads(dkv_pieces, 2, 1, mark)
    return (
        product_queries.reshape(queries.shape),
        product_keys.reshape(keys.shape),
        product_values.reshape(keys.shape),
    )


def solution(mesh):
    def run(*arguments):
        count, heads = mesh.shape["ctx"], mesh.shape["head"]
        parts = arguments[1].shape[1] // heads
        split = Mesh(
            mesh.devices.reshape(count // parts, parts, heads), ("span", "part", "head")
        )
        ctx = ("span", "part")
        array = P(ctx, "head", None)
        return jax.shard_map(
            body,
            mesh=split,
            in_specs=(array,) * 6 + (P(ctx), P("head")),
            out_specs=(array,) * 3,
            check_vma=False,
        )(*arguments)

    return run
```

```python
import functools

import jax
import jax.numpy as jnp
from jax import lax
from jax.experimental import pallas as pl
from jax.experimental.pallas import tpu as pltpu
from jax.sharding import Mesh, PartitionSpec as P

DOC_DEVS = 8
EPSILON = 1e-06
VMEM_BYTES = 18 * 1024 * 1024
NOTE_ROWS = 16
ONES_ROWS = 16
WIDE_VMEM_BYTES = 60 * 1024 * 1024
MASKED = -1e30
F32 = jnp.float32
BF16 = jnp.bfloat16
SMEM = pl.BlockSpec(memory_space=pltpu.SMEM)
VMEM = pl.BlockSpec(memory_space=pltpu.VMEM)


def params(size=VMEM_BYTES):
    return pltpu.CompilerParams(vmem_limit_bytes=size)


def cost(flops, moved, powers=0):
    return pl.CostEstimate(flops=int(flops), bytes_accessed=int(moved), transcendentals=int(powers))


def nn(a, b):
    return lax.dot_general(a, b, (((1,), (0,)), ((), ())), preferred_element_type=F32)


def nt(a, b):
    return lax.dot_general(a, b, (((1,), (1,)), ((), ())), preferred_element_type=F32)


def split_heads(arrays, parts, per_part, notes=None):
    count = len(arrays)
    total, width = arrays[0].shape
    heads = parts * per_part
    rows = total // heads
    length = count * per_part * rows
    span = per_part * rows
    extra = 0 if notes is None else NOTE_ROWS
    scalars = [] if notes is None else [notes]

    def kernel(*refs):
        ins = list(refs[: len(scalars) + count])
        results = refs[len(scalars) + count : len(scalars) + count + parts]
        held, wide, sems, *staged = refs[len(scalars) + count + parts :]
        outs, out_sems = (staged[:-1], staged[-1]) if extra else (results, None)
        mine = lax.axis_index("part")
        if extra:
            note_ref = ins.pop(0)
        copies = [pltpu.make_async_copy(ins[a], held.at[a], sems.at[a]) for a in range(count)]
        for copy in copies:
            copy.start()
        leaving = []

        def leave(m, a, start, size):
            part = pl.ds(start, size)
            sem = out_sems.at[m * (count + 1) + a]
            leaving.append(pltpu.make_async_copy(outs[m].at[part], results[m].at[part], sem))
            leaving[-1].start()

        if extra:
            first = (lax.axis_index("span") * parts + mine) * notes.shape[0]
            line = lax.broadcasted_iota(jnp.int32, (extra, width), 0)
            lines = jnp.zeros((extra, width), jnp.int32)
            for i in range(notes.shape[0]):
                lines = jnp.where(line == i, first + i - note_ref[i], lines)
            for m, out in enumerate(outs):
                out[length:, :] = lines.astype(F32).astype(BF16)
                leave(m, count, length, extra)
        for a in range(count):
            copies[a].wait()
            wide[...] = held[a].astype(F32)
            for m in range(parts):
                for r in range(per_part):
                    head = jnp.bitwise_xor(mine, m) * per_part + r
                    at = (a * per_part + r) * rows
                    outs[m][at : at + rows, :] = wide[pl.ds(head, rows, stride=heads), :].astype(BF16)
                if extra:
                    leave(m, a, a * span, span)
        for copy in leaving:
            copy.wait()

    piece = (length + extra, width)
    scratch = [
        pltpu.VMEM((count, total, width), BF16),
        pltpu.VMEM((total, width), F32),
        pltpu.SemaphoreType.DMA((count,)),
    ]
    if extra:
        scratch += [pltpu.VMEM(piece, BF16)] * parts
        scratch.append(pltpu.SemaphoreType.DMA((parts * (count + 1),)))
    return pl.pallas_call(
        kernel,
        in_specs=[SMEM] * len(scalars) + [pl.BlockSpec(memory_space=pltpu.HBM)] * count,
        out_specs=[pl.BlockSpec(memory_space=pltpu.HBM) if extra else VMEM] * parts,
        out_shape=[jax.ShapeDtypeStruct(piece, BF16)] * parts,
        scratch_shapes=scratch,
        compiler_params=params(VMEM_BYTES if notes is None else WIDE_VMEM_BYTES),
        cost_estimate=cost(0, 4 * count * total * width),
        name="split_heads",
    )(*scalars, *arrays)


def join_heads(pieces, count, per_part, after=None):
    parts = len(pieces)
    rows, width = pieces[0].shape[-2:]
    heads = parts * per_part
    steps = 4
    cut = rows // steps
    marks = [] if after is None else [after]

    def kernel(*refs):
        ins, outs = refs[:parts], refs[parts + len(marks) :]
        mine = lax.axis_index("part")
        outs[-1][0] = mine
        for a in range(count):
            for m in range(parts):
                for r in range(per_part):
                    head = jnp.bitwise_xor(mine, m) * per_part + r
                    outs[a][pl.ds(head, cut, stride=heads), :] = ins[m][a, r].astype(F32)

    return pl.pallas_call(
        kernel,
        grid=(steps,),
        in_specs=[pl.BlockSpec((count, per_part, cut, width), lambda i: (0, 0, i, 0))] * parts
        + [SMEM] * len(marks),
        out_specs=[pl.BlockSpec((cut * heads, width), lambda i: (i, 0))] * count + [SMEM],
        out_shape=[jax.ShapeDtypeStruct((rows * heads, width), F32)] * count
        + [jax.ShapeDtypeStruct((1,), jnp.int32)],
        compiler_params=params(),
        cost_estimate=cost(0, 6 * count * rows * heads * width),
        name="join_heads",
    )(*pieces, *marks)


def slot_of(me_ref, m, rows):
    return pl.multiple_of(jnp.bitwise_xor(me_ref[0], m) * rows, rows)


class Shape:
    def __init__(self, parts, group, rows, width, block):
        self.parts, self.group, self.rows, self.width, self.block = parts, group, rows, width, block
        self.tokens = parts * rows
        self.blocks = self.tokens // block
        self.lanes = group * block
        self.scale = width**-0.5


def diagonal(sh):
    shape = (sh.block, sh.block)
    key = lax.broadcasted_iota(jnp.int32, shape, 0)
    query = lax.broadcasted_iota(jnp.int32, shape, 1)
    return key <= query


def below_diagonal(sh, value, other):
    allowed = diagonal(sh)
    cut = [value[:, at : at + sh.block] for at in range(0, value.shape[1], sh.block)]
    return jnp.concatenate([jnp.where(allowed, part, other) for part in cut], axis=1)


def halves(sh):
    if sh.group % 2:
        return [slice(0, sh.lanes)]
    return [slice(0, sh.lanes // 2), slice(sh.lanes // 2, sh.lanes)]


def stacked_keys(keys, start, size):
    k_s, tk_s = keys
    k = k_s[pl.ds(start, size), :]
    tk = tk_s[pl.ds(start, size), :]
    left = jnp.concatenate([k, tk], axis=0)
    right = jnp.concatenate([jnp.zeros_like(k), k], axis=0)
    return jnp.concatenate([left, right], axis=1)


def pieces_of(sh, start, blocks):
    sizes = [2] * (blocks // 2) + [1] * (blocks % 2)
    firsts = [sum(sizes[:i]) for i in range(len(sizes))]
    return [
        (pl.multiple_of(start + first * sh.block, sh.block), size * sh.block, i == len(sizes) - 1)
        for i, (first, size) in enumerate(zip(firsts, sizes))
    ]


def cut_diagonal(sh, value, other):
    low = below_diagonal(sh, value[value.shape[0] - sh.block :], other)
    if value.shape[0] == sh.block:
        return low
    return jnp.concatenate([value[: value.shape[0] - sh.block], low], axis=0)


def block_rows(sh, block):
    return pl.multiple_of(block * sh.block, sh.block)


def load_state(stat, lanes):
    return tuple(stat[r : r + 1, lanes] for r in range(3))


def forward_tile(sh, keys, vt_s, acc, stat, kept, qq, block, blocks, masked):
    w = sh.width
    start = block_rows(sh, block)
    pieces = pieces_of(sh, start, blocks)
    stacked = [stacked_keys(keys, at, size) for at, size, _ in pieces]
    at = pl.ds(start, blocks * sh.block)
    lanes = halves(sh)
    scores = [[] for _ in lanes]
    mixed = [[] for _ in lanes]
    most = [None for _ in lanes]
    state = [None if masked else load_state(stat, part) for part in lanes]

    def score(h, c):
        both = nt(stacked[c], qq[lanes[h], :])
        s, d = both[: pieces[c][1]], both[pieces[c][1] :]
        if masked and pieces[c][2]:
            s = cut_diagonal(sh, s, MASKED)
        scores[h].append((s, d))

    def top(h):
        peaks = [jnp.max(s, axis=0, keepdims=True) for s, _ in scores[h]]
        most[h] = functools.reduce(jnp.maximum, peaks) * sh.scale
        if not masked:
            most[h] = jnp.maximum(most[h], state[h][0])
        if kept is not None:
            for j in range(blocks):
                kept[1][block + j, :, lanes[h]] = most[h]

    def soften(h, c):
        s, d = scores[h][c]
        e = jnp.exp(s * sh.scale - most[h])
        mixed[h].append((e.astype(BF16), (e * d).astype(BF16)))
        if kept is not None:
            kept[0][pl.ds(pieces[c][0], pieces[c][1]), lanes[h]] = mixed[h][-1][0]

    def gather(h, i):
        return jnp.concatenate([pair[i] for pair in mixed[h]], axis=0)

    def finish(h, plain, moving):
        total, cross = plain[2 * w : 2 * w + 1], moving[w : w + 1]
        tangent = plain[:w] + moving[:w] * sh.scale
        plain = plain[w : 2 * w]
        if not masked:
            decay = jnp.exp(state[h][0] - most[h])
            plain = acc[:w, lanes[h]] * decay + plain
            tangent = acc[w:, lanes[h]] * decay + tangent
            total, cross = state[h][1] * decay + total, state[h][2] * decay + cross
        acc[:w, lanes[h]] = plain
        acc[w:, lanes[h]] = tangent
        for r, value in enumerate((most[h], total, cross)):
            stat[r : r + 1, lanes[h]] = value

    for h in range(len(lanes) + 1):
        if h > 0:
            top(h - 1)
        for c in range(len(pieces)):
            if h < len(lanes):
                score(h, c)
            if h > 0:
                soften(h - 1, c)
        if h > 0:
            plain = nn(vt_s[:, at], gather(h - 1, 0))
            moving = nn(vt_s[w:, at], gather(h - 1, 1))
            finish(h - 1, plain, moving)


def by_count(sh, low, count, run, masked):
    head = jnp.where(count <= 6, count, 3 + lax.rem(jnp.maximum(count - 7, 0), 4))
    fours = (count - head) // 4
    for blocks in range(1, min(6, sh.blocks) + 1):

        @pl.when(head == blocks)
        def _(blocks=blocks):
            if masked:
                run(low + count - blocks, blocks, True)
            else:
                run(low, blocks, False)

    def step(i, carry):
        run(low + (0 if masked else head) + 4 * i, 4, False)
        return carry

    if sh.blocks > 6:
        lax.fori_loop(0, fours, step, 0)


def lay_chunk(sh, me_ref, sources, targets):
    for m, (ref, base) in enumerate(sources):
        slot = pl.ds(slot_of(me_ref, m, sh.rows), sh.rows)
        for i, target in enumerate(targets):
            at = base + i * sh.rows
            target[slot, :] = ref[at : at + sh.rows, :]


def lay_queries(sh, me_ref, order, pieces, qq):
    per = sh.rows // sh.block
    for m, ref in zip(order, pieces):
        for i in range(2):
            for g in range(sh.group):
                for r in range(per):
                    block = jnp.bitwise_xor(me_ref[0], m) * per + r
                    at = (i * sh.group + g) * sh.rows + r * sh.block
                    qq[
                        block,
                        g * sh.block : (g + 1) * sh.block,
                        i * sh.width : (i + 1) * sh.width,
                    ] = ref[at : at + sh.block, :]


def lay_span(sh, me_ref, sources, laid):
    w = sh.width
    k_s, v_s, kt_s, tk_s, vt_s, tv_s = laid
    lay_chunk(sh, me_ref, sources, (k_s, v_s, tk_s, tv_s))
    kt_s[...] = transposed(k_s[...])
    vt_s[:w, :] = transposed(tv_s[...])
    vt_s[w : 2 * w, :] = transposed(v_s[...])
    vt_s[2 * w :, :] = jnp.ones((ONES_ROWS, sh.tokens), BF16)


def transposed(x):
    return x.astype(F32).T.astype(BF16)


def located(sh, refs):
    length = refs[0].shape[0]
    return [(ref, at) for ref in refs for at in range(0, ref.shape[0], length)]


def back_of(sh, me_ref, back_ref, qb):
    per = sh.rows // sh.block
    return back_ref[jnp.bitwise_xor(me_ref[0], qb // per) * per + qb % per]


def each_block(count, run):
    def step(i, carry):
        run(i)
        return carry

    lax.fori_loop(0, count, step, 0)


def block_in_turn(sh, me_ref, order, i):
    per = sh.rows // sh.block
    if order == list(range(sh.parts)):
        return i
    partner = order[0]
    for j in range(1, len(order)):
        partner = jnp.where(i // per == j, order[j], partner)
    return jnp.bitwise_xor(me_ref[0], partner) * per + i % per


def kept_shapes(sh):
    return [
        jax.ShapeDtypeStruct((sh.blocks, sh.tokens, sh.lanes), BF16),
        jax.ShapeDtypeStruct((sh.blocks, sh.blocks, 1, sh.lanes), F32),
    ]


def forward_own(sh, me, back, order, queries, chunk, before):
    w = sh.width
    first = before is None
    turns = len(order) * (sh.rows // sh.block)

    def kernel(me_ref, back_ref, *refs):
        refs = list(refs)

        def take(count):
            taken = refs[:count]
            del refs[:count]
            return taken

        q_in = take(len(order))
        if first:
            kv_in = take(len(chunk))
            accs, stats, qq_s, es, ms = take(5)
            laid = refs
            lay_span(sh, me_ref, located(sh, kv_in), laid)
        else:
            laid = take(len(chunk))
            take(5)
            accs, stats, qq_s, es, ms = refs
        k_s, _, _, tk_s, vt_s = laid[:5]
        lay_queries(sh, me_ref, order, q_in, qq_s)

        def query_block(i):
            qb = block_in_turn(sh, me_ref, order, i)
            low = jnp.clip(qb - back_of(sh, me_ref, back_ref, qb), 0, qb)
            run = functools.partial(
                forward_tile,
                sh,
                (k_s, tk_s),
                vt_s,
                accs.at[qb],
                stats.at[qb],
                (es.at[qb], ms.at[qb]),
                qq_s[qb],
            )
            by_count(sh, low, qb + 1 - low, run, True)

        each_block(turns, query_block)

    def array(*shape, dtype=F32):
        return jax.ShapeDtypeStruct(shape, dtype)

    span = array(sh.tokens, w, dtype=BF16)
    out_shape = [
        array(sh.blocks, 2 * w, sh.lanes),
        array(sh.blocks, 8, sh.lanes),
        array(sh.blocks, sh.lanes, 2 * w, dtype=BF16),
        *kept_shapes(sh),
    ]
    operands = [*queries, *chunk]
    aliases = {}
    if first:
        out_shape += [span, span, array(w, sh.tokens, dtype=BF16), span]
        out_shape.append(array(2 * w + ONES_ROWS, sh.tokens, dtype=BF16))
    else:
        aliases = {2 + len(operands) + i: i for i in range(5)}
        operands += before
    work = sh.group * sh.tokens * sh.block * turns // 2
    return pl.pallas_call(
        kernel,
        in_specs=[SMEM, SMEM] + [VMEM] * len(operands),
        out_specs=[VMEM] * len(out_shape),
        out_shape=out_shape,
        input_output_aliases=aliases,
        scratch_shapes=[pltpu.VMEM((sh.tokens, w), BF16)] * first,
        compiler_params=params(),
        cost_estimate=cost(12 * work * w, 4 * sh.tokens * sh.lanes, work),
        name="forward_own",
    )(me, back, *operands)


def forward_chunk(sh, me, back, qq, chunk, distance, state, gain_square=None):
    w = sh.width
    closing = gain_square is not None

    def kernel(me_ref, back_ref, qq_s, *refs):
        refs = list(refs)

        def take(count):
            taken = refs[:count]
            del refs[:count]
            return taken

        kv_in = take(len(chunk))
        take(2)
        if closing:
            (gain_ref,) = take(1)
        k_s, v_s, kt_s, accs, stats = take(5)
        last = take(2)
        if closing:
            lse, sums = last
        tk_s, tv_s, vt_s = refs
        lay_span(sh, me_ref, located(sh, kv_in), (k_s, v_s, kt_s, tk_s, vt_s, tv_s))

        def query_block(qb):
            acc, stat = accs.at[qb], stats.at[qb]
            first = qb - back_of(sh, me_ref, back_ref, qb) + distance * sh.blocks
            first = jnp.clip(first, 0, sh.blocks)
            count = sh.blocks - first

            @pl.when(count > 0)
            def _():
                kept = None if closing else [ref.at[qb] for ref in last]
                run = functools.partial(
                    forward_tile, sh, (k_s, tk_s), vt_s, acc, stat, kept, qq_s[qb]
                )
                by_count(sh, first, count, run, False)

            if closing:
                most, total, cross = load_state(stat, slice(None))
                inverse = 1.0 / total
                plain = acc[:w, :] * inverse
                moved = acc[w:, :] * inverse - (cross * inverse * sh.scale) * plain
                acc[:w, :] = plain
                acc[w:, :] = moved
                lse[qb] = most + jnp.log(total)
                square = plain * plain
                product = plain * moved
                gain = gain_ref[...]
                for r, value in enumerate((square, product, gain * square, gain * product)):
                    line = jnp.sum(value, axis=0, keepdims=True)
                    pieces = [line[:, g * sh.block : (g + 1) * sh.block] for g in range(sh.group)]
                    sums[qb, r : r + 1, :] = functools.reduce(jnp.add, pieces)

        each_block(sh.blocks, query_block)

    def array(*shape, dtype=F32):
        return jax.ShapeDtypeStruct(shape, dtype)

    out_shape = [
        array(sh.tokens, w, dtype=BF16),
        array(sh.tokens, w, dtype=BF16),
        array(w, sh.tokens, dtype=BF16),
        array(sh.blocks, 2 * w, sh.lanes),
        array(sh.blocks, 8, sh.lanes),
    ]
    if closing:
        out_shape += [array(sh.blocks, 1, sh.lanes), array(sh.blocks, 4, sh.block)]
    else:
        out_shape += kept_shapes(sh)
    operands = [qq, *chunk]
    aliases = {2 + len(operands): 3, 3 + len(operands): 4}
    operands += state
    if closing:
        operands.append(gain_square)
    work = sh.group * sh.tokens * sh.tokens // 2
    return pl.pallas_call(
        kernel,
        in_specs=[SMEM, SMEM] + [VMEM] * len(operands),
        out_specs=[VMEM] * len(out_shape),
        out_shape=out_shape,
        input_output_aliases=aliases,
        scratch_shapes=[
            pltpu.VMEM((sh.tokens, w), BF16),
            pltpu.VMEM((sh.tokens, w), BF16),
            pltpu.VMEM((2 * w + ONES_ROWS, sh.tokens), BF16),
        ],
        compiler_params=params(),
        cost_estimate=cost(24 * work * w, 12 * sh.tokens * sh.lanes * 2, work),
        name="forward_far" if closing else "forward_chunk",
    )(me, back, *operands)


def backward_tile(sh, keys, kt_s, dkv_s, dq_s, qg, lse, dot, block, blocks, _):
    start, size = block_rows(sh, block), blocks * sh.block
    rows = pl.ds(start, size)
    k_s, v_s = keys
    k, v = k_s[rows, :], v_s[rows, :]
    empty = jnp.zeros_like(k)
    left = jnp.concatenate([k, empty], axis=0)
    right = jnp.concatenate([empty, v], axis=0)
    stacked = jnp.concatenate([left, right], axis=1)
    scores = [nt(stacked, qg[lanes, :]) for lanes in halves(sh)]
    for lanes, both in zip(halves(sh), scores):
        p = jnp.exp(both[:size] * sh.scale - lse[:, lanes])
        ds = (p * (both[size:] - dot[:, lanes])).astype(BF16)
        dkv_s[0, rows, :] += nn(ds, qg[lanes, : sh.width])
        dkv_s[1, rows, :] += nn(p.astype(BF16), qg[lanes, sh.width :])
        dq_s[:, lanes] += nn(kt_s[:, rows], ds)


def backward_kept(sh, keys, kt_s, dkv_s, dq_s, qg, lse, dot, kept, block, blocks, _):
    start, size = block_rows(sh, block), blocks * sh.block
    rows = pl.ds(start, size)
    v = keys[1][rows, :]
    slopes = [nt(v, qg[lanes, sh.width :]) for lanes in halves(sh)]
    for lanes, slope in zip(halves(sh), slopes):
        parts = []
        for j in range(blocks):
            factor = jnp.exp(kept[1][block + j, :, lanes] - lse[:, lanes])
            at = pl.ds(block_rows(sh, block + j), sh.block)
            parts.append(kept[0][at, lanes].astype(F32) * factor)
        p = jnp.concatenate(parts, axis=0)
        ds = (p * (slope - dot[:, lanes])).astype(BF16)
        dkv_s[0, rows, :] += nn(ds, qg[lanes, : sh.width])
        dkv_s[1, rows, :] += nn(p.astype(BF16), qg[lanes, sh.width :])
        dq_s[:, lanes] += nn(kt_s[:, rows], ds)


def backward_chunk(sh, me, back, qq, keys, distance, grads, lse, dots, dq, norm, order, held):
    w = sh.width
    opening, closing = norm is not None, distance == 0
    per = sh.rows // sh.block

    def kernel(me_ref, back_ref, *refs):
        refs = list(refs)

        def take(count):
            taken = refs[:count]
            del refs[:count]
            return taken

        qq_s, k_s, v_s, kt_s = take(4)
        kept = take(len(keys) - 3)
        (lse_s,) = take(1)
        if opening:
            out_s, gain_ref, *sum_refs = take(2 + len(norm[0]))
        else:
            grad_s, dot_s, dq_in = take(3)
        (held_ref,) = take(1) if held is not None else (None,)
        (dkv_out,) = take(1)
        dq_out = take(len(order) if closing else 1)
        if opening:
            grad_s, dot_s = take(2)
        dkv_s, dq_own = (dkv_out, *refs) if closing else refs
        if held_ref is None:
            dkv_s[...] = jnp.zeros_like(dkv_s)

        def query_block(i):
            qb = block_in_turn(sh, me_ref, order, i)
            dq_s = dq_own if closing else dq_out[0].at[qb]
            if opening:
                features = norm[2]
                token = functools.reduce(jnp.add, [ref[qb] for ref in sum_refs])
                sums = jnp.concatenate([token] * sh.group, axis=1)
                square = sums[0:1] / features + EPSILON
                inverse = lax.rsqrt(square)
                ratio = sums[1:2] / (features * square)
                again = (sums[3:4] - ratio * sums[2:3]) * inverse
                again = again / (features * square)
                plain = out_s[qb, :w, :]
                moved = out_s[qb, w:, :]
                first_grad = gain_ref[...] * (moved - plain * ratio) * inverse
                cot = ((first_grad - plain * again) * inverse).astype(BF16).astype(F32)
                dot_s[qb] = jnp.sum(cot * plain, axis=0, keepdims=True)
                grad_s[qb] = cot.T.astype(BF16)
                dq_s[...] = jnp.zeros((w, sh.lanes), F32)
            elif closing:
                dq_s[...] = dq_in[qb]

            top = sh.blocks if distance else qb + 1
            first = jnp.clip(qb - back_of(sh, me_ref, back_ref, qb) + distance * sh.blocks, 0, top)
            count = top - first

            @pl.when(count > 0)
            def _():
                qg = jnp.concatenate([qq_s[qb, :, :w], grad_s[qb]], axis=1)
                common = (sh, (k_s, v_s), kt_s, dkv_s, dq_s, qg, lse_s[qb], dot_s[qb])
                if kept:
                    run = functools.partial(backward_kept, *common, [ref.at[qb] for ref in kept])
                else:
                    run = functools.partial(backward_tile, *common)
                by_count(sh, first, count, run, False)

            if closing:
                done = (dq_s[...] * sh.scale).T.reshape(sh.group, sh.block, w).astype(BF16)
                at = pl.ds(pl.multiple_of(i % per * sh.block, sh.block), sh.block)
                for j, out in enumerate(dq_out):

                    @pl.when(i // per == j)
                    def _(out=out):
                        out[:, at, :] = done

        each_block(len(order) * per, query_block)
        if not closing:
            dkv_out[0] = (dkv_s[0] * sh.scale).astype(BF16)
            dkv_out[1] = dkv_s[1].astype(BF16)

    def array(*shape, dtype=F32):
        return jax.ShapeDtypeStruct(shape, dtype)

    operands = [qq, *keys, lse]
    if opening:
        operands += [grads, norm[1], *norm[0]]
    else:
        operands += [grads, dots, dq]
    aliases = {}
    if not opening and not closing:
        aliases = {1 + len(operands): 1}
    if held is not None:
        aliases = {2 + len(operands): 0}
        operands.append(held)
    out_shape = [array(2, sh.tokens, w, dtype=F32 if closing else BF16)]
    if closing:
        out_shape += [array(sh.group, sh.rows, w, dtype=BF16)] * len(order)
    else:
        out_shape.append(array(sh.blocks, w, sh.lanes))
    if opening:
        out_shape += [
            array(sh.blocks, sh.lanes, w, dtype=BF16),
            array(sh.blocks, 1, sh.lanes),
        ]
    work = sh.group * sh.tokens * len(order) * sh.rows // 2
    return pl.pallas_call(
        kernel,
        in_specs=[SMEM, SMEM] + [VMEM] * len(operands),
        out_specs=[VMEM] * len(out_shape),
        out_shape=out_shape,
        input_output_aliases=aliases,
        scratch_shapes=[pltpu.VMEM((2, sh.tokens, w), F32)] * (not closing)
        + [pltpu.VMEM((w, sh.lanes), F32)],
        compiler_params=params(),
        cost_estimate=cost(1, 1) if closing else cost(20 * work * w, 16 * work, work),
        name="backward_chunk",
    )(me, back, *operands)


def combine(sh, me, arrived, held):
    count = len(arrived)

    def kernel(me_ref, held_ref, *refs):
        for m, out in enumerate(refs[count:]):
            slot = pl.ds(slot_of(me_ref, m, sh.rows), sh.rows)
            for a, factor in ((0, sh.scale), (1, 1.0)):
                part = held_ref[a, slot, :] * factor
                for ref in refs[:count]:
                    part += ref[a, slot, :].astype(F32)
                out[a] = part.astype(BF16)

    return pl.pallas_call(
        kernel,
        in_specs=[SMEM] + [VMEM] * (1 + count),
        out_specs=[VMEM] * sh.parts,
        out_shape=[jax.ShapeDtypeStruct((2, sh.rows, sh.width), BF16)] * sh.parts,
        compiler_params=params(),
        cost_estimate=cost(0, 1),
        name="combine",
    )(me, held, *arrived)


def exchanged_with(piece, parts, m):
    return lax.ppermute(piece, "part", [(i, i ^ m) for i in range(parts)]) if m else piece


def exchanged(pieces, parts):
    return [exchanged_with(piece, parts, m) for m, piece in enumerate(pieces)]


def moved_on(value, steps):
    count = lax.axis_size("span")
    pairs = [(i, i + steps) for i in range(count) if 0 <= i + steps < count]
    return lax.ppermute(value, "span", pairs)


def summed_over_head(value):
    count = lax.axis_size("head")
    if count & (count - 1):
        return lax.psum(value, "head")
    step = 1
    while step < count:
        value = value + lax.ppermute(value, "head", [(i, i ^ step) for i in range(count)])
        step *= 2
    return value


def body(queries, keys, values, tangent_queries, tangent_keys, tangent_values, doc_start, out_gain):
    rows, query_heads, width = queries.shape
    key_heads = keys.shape[1]
    group = query_heads // key_heads
    parts = lax.axis_size("part")
    per = doc_start.shape[0]
    block = rows // per
    features = query_heads * width * lax.axis_size("head")
    hops = -(-DOC_DEVS // parts)
    sh = Shape(parts, group, rows, width, block)
    place = lax.axis_index("part")
    me = place.astype(jnp.int32).reshape(1)

    def flat(array):
        return array.reshape(-1, width)

    pieces = split_heads(
        [flat(a) for a in (keys, values, tangent_keys, tangent_values)], parts, 1, doc_start
    )
    q_rows, _ = lax.optimization_barrier(((flat(queries), flat(tangent_queries)), pieces[0]))
    q_pieces = split_heads(q_rows, parts, group)
    own = moved_on(pieces[0], 1)
    pieces = exchanged(pieces, parts)
    chunks = [pieces]
    if parts > 1:
        own, q_pieces = lax.optimization_barrier((own, q_pieces))
        owns = [own]
        for _ in range(hops - 1):
            owns.append(moved_on(owns[-1], 1))
        late, owns = lax.optimization_barrier((pieces[1:], owns))
        rest = jnp.concatenate([moved_on(piece, 1) for piece in late], axis=0)
        chunks.append([owns[0], rest])
        for own in owns[1:]:
            rest = moved_on(rest, 1)
            chunks.append([own, rest])
    else:
        for _ in range(hops):
            chunks.append([own])
            own = moved_on(own, 1)
    q_parts = exchanged(q_pieces[:-1], parts)
    if parts > 1:
        last, _ = lax.optimization_barrier((q_pieces[-1], q_parts[min(1, parts - 2)]))
        q_parts.append(exchanged_with(last, parts, parts - 1))
    else:
        q_parts = q_pieces
    back = jnp.concatenate([p[4 * rows : 4 * rows + per, 0] for p in pieces]).astype(jnp.int32)
    gain = lax.dynamic_index_in_dim(out_gain.reshape(key_heads, group, width), place, 0, False)
    gain_square = jnp.repeat((gain * gain).T, block, axis=1)

    everyone = list(range(parts))
    before, laid = None, chunks[0]
    for order in [everyone[:1], everyone[1:-1], everyone[-1:]] if parts > 1 else [everyone]:
        if order:
            turn = forward_own(sh, me, back, order, [q_parts[m] for m in order], laid, before)
            laid = turn[5:] or laid
            before = list(turn[:5])
    state, qq = before[:2], before[2]
    spans = [(*laid[:3], *before[3:])]
    for distance in range(1, hops):
        k, v, kt, acc, stat, *kept = forward_chunk(
            sh, me, back, qq, chunks[distance], distance, state
        )
        state = [acc, stat]
        spans.append((k, v, kt, *kept))
    k, v, kt, out, _, lse, sums = forward_chunk(
        sh, me, back, qq, chunks[hops], hops, state, gain_square
    )
    spans.append((k, v, kt))
    norm = (exchanged([summed_over_head(sums)] * parts, parts), gain_square, features)

    part, dq, grads, dots = backward_chunk(
        sh, me, back, qq, spans[hops], hops, out, lse, None, None, norm, everyone, None
    )
    arrived = [moved_on(part, -hops)]
    for distance in range(hops - 1, 0, -1):
        part, dq = backward_chunk(
            sh, me, back, qq, spans[distance], distance, grads, lse, dots, dq, None,
            everyone, None,
        )
        arrived.append(moved_on(part, -distance))
    turns = [turn[::-1] for turn in (everyone[-1:], everyone[:-1]) if turn]
    held, dq_pieces = None, [None] * parts
    for order in turns:
        if held is not None:
            arrived[0], held = lax.optimization_barrier((arrived[0], held))
        held, *done = backward_chunk(
            sh, me, back, qq, spans[0], 0, grads, lse, dots, dq, None, order, held
        )
        for m, piece in zip(order, done):
            dq_pieces[m] = piece.reshape(1, group, rows, width)
    dq_pieces = exchanged(dq_pieces, parts)
    dq_pieces[-1], held = lax.optimization_barrier((dq_pieces[-1], held))
    dkv_pieces = exchanged(combine(sh, me, arrived, held), parts)
    product_queries, mark = join_heads(dq_pieces, 1, group)
    dkv_pieces = [p.reshape(2, 1, rows, width) for p in dkv_pieces]
    product_keys, product_values, _ = join_heads(dkv_pieces, 2, 1, mark)
    return (
        product_queries.reshape(queries.shape),
        product_keys.reshape(keys.shape),
        product_values.reshape(keys.shape),
    )


def solution(mesh):
    def run(*arguments):
        count, heads = mesh.shape["ctx"], mesh.shape["head"]
        parts = arguments[1].shape[1] // heads
        split = Mesh(
            mesh.devices.reshape(count // parts, parts, heads), ("span", "part", "head")
        )
        ctx = ("span", "part")
        array = P(ctx, "head", None)
        return jax.shard_map(
            body,
            mesh=split,
            in_specs=(array,) * 6 + (P(ctx), P("head")),
            out_specs=(array,) * 3,
            check_vma=False,
        )(*arguments)

    return run
```

```python
import functools

import jax
import jax.numpy as jnp
from jax import lax
from jax.experimental import pallas as pl
from jax.experimental.pallas import tpu as pltpu
from jax.sharding import Mesh, PartitionSpec as P

DOC_DEVS = 8
EPSILON = 1e-06
VMEM_BYTES = 18 * 1024 * 1024
NOTE_ROWS = 16
ONES_ROWS = 16
WIDE_VMEM_BYTES = 60 * 1024 * 1024
MASKED = -1e30
F32 = jnp.float32
BF16 = jnp.bfloat16
SMEM = pl.BlockSpec(memory_space=pltpu.SMEM)
VMEM = pl.BlockSpec(memory_space=pltpu.VMEM)


def params(size=VMEM_BYTES):
    return pltpu.CompilerParams(vmem_limit_bytes=size)


def cost(flops, moved, powers=0):
    return pl.CostEstimate(flops=int(flops), bytes_accessed=int(moved), transcendentals=int(powers))


def nn(a, b):
    return lax.dot_general(a, b, (((1,), (0,)), ((), ())), preferred_element_type=F32)


def nt(a, b):
    return lax.dot_general(a, b, (((1,), (1,)), ((), ())), preferred_element_type=F32)


def split_heads(arrays, parts, per_part, notes=None):
    count = len(arrays)
    total, width = arrays[0].shape
    heads = parts * per_part
    rows = total // heads
    length = count * per_part * rows
    span = per_part * rows
    extra = 0 if notes is None else NOTE_ROWS
    scalars = [] if notes is None else [notes]

    def kernel(*refs):
        ins = list(refs[: len(scalars) + count])
        results = refs[len(scalars) + count : len(scalars) + count + parts]
        held, wide, sems, *staged = refs[len(scalars) + count + parts :]
        outs, out_sems = (staged[:-1], staged[-1]) if extra else (results, None)
        mine = lax.axis_index("part")
        if extra:
            note_ref = ins.pop(0)
        copies = [pltpu.make_async_copy(ins[a], held.at[a], sems.at[a]) for a in range(count)]
        for copy in copies:
            copy.start()
        leaving = []

        def leave(m, a, start, size):
            part = pl.ds(start, size)
            sem = out_sems.at[m * (count + 1) + a]
            leaving.append(pltpu.make_async_copy(outs[m].at[part], results[m].at[part], sem))
            leaving[-1].start()

        if extra:
            first = (lax.axis_index("span") * parts + mine) * notes.shape[0]
            line = lax.broadcasted_iota(jnp.int32, (extra, width), 0)
            lines = jnp.zeros((extra, width), jnp.int32)
            for i in range(notes.shape[0]):
                lines = jnp.where(line == i, first + i - note_ref[i], lines)
            for m, out in enumerate(outs):
                out[length:, :] = lines.astype(F32).astype(BF16)
                leave(m, count, length, extra)
        for a in range(count):
            copies[a].wait()
            wide[...] = held[a].astype(F32)
            for m in range(parts):
                for r in range(per_part):
                    head = jnp.bitwise_xor(mine, m) * per_part + r
                    at = (a * per_part + r) * rows
                    outs[m][at : at + rows, :] = wide[pl.ds(head, rows, stride=heads), :].astype(BF16)
                if extra:
                    leave(m, a, a * span, span)
        for copy in leaving:
            copy.wait()

    piece = (length + extra, width)
    scratch = [
        pltpu.VMEM((count, total, width), BF16),
        pltpu.VMEM((total, width), F32),
        pltpu.SemaphoreType.DMA((count,)),
    ]
    if extra:
        scratch += [pltpu.VMEM(piece, BF16)] * parts
        scratch.append(pltpu.SemaphoreType.DMA((parts * (count + 1),)))
    return pl.pallas_call(
        kernel,
        in_specs=[SMEM] * len(scalars) + [pl.BlockSpec(memory_space=pltpu.HBM)] * count,
        out_specs=[pl.BlockSpec(memory_space=pltpu.HBM) if extra else VMEM] * parts,
        out_shape=[jax.ShapeDtypeStruct(piece, BF16)] * parts,
        scratch_shapes=scratch,
        compiler_params=params(VMEM_BYTES if notes is None else WIDE_VMEM_BYTES),
        cost_estimate=cost(0, 4 * count * total * width),
        name="split_heads",
    )(*scalars, *arrays)


def join_heads(pieces, count, per_part):
    parts = len(pieces)
    rows, width = pieces[0].shape[-2:]
    heads = parts * per_part

    steps = 4
    cut = rows // steps

    def kernel(*refs):
        ins, outs = refs[:parts], refs[parts:]
        mine = lax.axis_index("part")
        for a in range(count):
            for m in range(parts):
                for r in range(per_part):
                    head = jnp.bitwise_xor(mine, m) * per_part + r
                    outs[a][pl.ds(head, cut, stride=heads), :] = ins[m][a, r].astype(F32)

    return pl.pallas_call(
        kernel,
        grid=(steps,),
        in_specs=[pl.BlockSpec((count, per_part, cut, width), lambda i: (0, 0, i, 0))] * parts,
        out_specs=[pl.BlockSpec((cut * heads, width), lambda i: (i, 0))] * count,
        out_shape=[jax.ShapeDtypeStruct((rows * heads, width), F32)] * count,
        compiler_params=params(),
        cost_estimate=cost(0, 6 * count * rows * heads * width),
        name="join_heads",
    )(*pieces)


def slot_of(me_ref, m, rows):
    return pl.multiple_of(jnp.bitwise_xor(me_ref[0], m) * rows, rows)


class Shape:
    def __init__(self, parts, group, rows, width, block):
        self.parts, self.group, self.rows, self.width, self.block = parts, group, rows, width, block
        self.tokens = parts * rows
        self.blocks = self.tokens // block
        self.lanes = group * block
        self.scale = width**-0.5


def diagonal(sh):
    shape = (sh.block, sh.block)
    key = lax.broadcasted_iota(jnp.int32, shape, 0)
    query = lax.broadcasted_iota(jnp.int32, shape, 1)
    return key <= query


def below_diagonal(sh, value, other):
    allowed = diagonal(sh)
    cut = [value[:, at : at + sh.block] for at in range(0, value.shape[1], sh.block)]
    return jnp.concatenate([jnp.where(allowed, part, other) for part in cut], axis=1)


def halves(sh):
    if sh.group % 2:
        return [slice(0, sh.lanes)]
    return [slice(0, sh.lanes // 2), slice(sh.lanes // 2, sh.lanes)]


def stacked_keys(keys, start, size):
    k_s, tk_s = keys
    k = k_s[pl.ds(start, size), :]
    tk = tk_s[pl.ds(start, size), :]
    left = jnp.concatenate([k, tk], axis=0)
    right = jnp.concatenate([jnp.zeros_like(k), k], axis=0)
    return jnp.concatenate([left, right], axis=1)


def pieces_of(sh, start, blocks):
    sizes = [2] * (blocks // 2) + [1] * (blocks % 2)
    firsts = [sum(sizes[:i]) for i in range(len(sizes))]
    return [
        (pl.multiple_of(start + first * sh.block, sh.block), size * sh.block, i == len(sizes) - 1)
        for i, (first, size) in enumerate(zip(firsts, sizes))
    ]


def cut_diagonal(sh, value, other):
    low = below_diagonal(sh, value[value.shape[0] - sh.block :], other)
    if value.shape[0] == sh.block:
        return low
    return jnp.concatenate([value[: value.shape[0] - sh.block], low], axis=0)


def block_rows(sh, block):
    return pl.multiple_of(block * sh.block, sh.block)


def load_state(stat, lanes):
    return tuple(stat[r : r + 1, lanes] for r in range(3))


def forward_tile(sh, keys, vt_s, acc, stat, kept, qq, block, blocks, masked):
    w = sh.width
    start = block_rows(sh, block)
    pieces = pieces_of(sh, start, blocks)
    stacked = [stacked_keys(keys, at, size) for at, size, _ in pieces]
    at = pl.ds(start, blocks * sh.block)
    lanes = halves(sh)
    scores = [[] for _ in lanes]
    mixed = [[] for _ in lanes]
    most = [None for _ in lanes]
    state = [None if masked else load_state(stat, part) for part in lanes]

    def score(h, c):
        both = nt(stacked[c], qq[lanes[h], :])
        s, d = both[: pieces[c][1]], both[pieces[c][1] :]
        if masked and pieces[c][2]:
            s = cut_diagonal(sh, s, MASKED)
        scores[h].append((s, d))

    def top(h):
        peaks = [jnp.max(s, axis=0, keepdims=True) for s, _ in scores[h]]
        most[h] = functools.reduce(jnp.maximum, peaks) * sh.scale
        if not masked:
            most[h] = jnp.maximum(most[h], state[h][0])
        if kept is not None:
            for j in range(blocks):
                kept[1][block + j, :, lanes[h]] = most[h]

    def soften(h, c):
        s, d = scores[h][c]
        e = jnp.exp(s * sh.scale - most[h])
        mixed[h].append((e.astype(BF16), (e * d).astype(BF16)))
        if kept is not None:
            kept[0][pl.ds(pieces[c][0], pieces[c][1]), lanes[h]] = mixed[h][-1][0]

    def gather(h, i):
        return jnp.concatenate([pair[i] for pair in mixed[h]], axis=0)

    def finish(h, plain, moving):
        total, cross = plain[2 * w : 2 * w + 1], moving[w : w + 1]
        tangent = plain[:w] + moving[:w] * sh.scale
        plain = plain[w : 2 * w]
        if not masked:
            decay = jnp.exp(state[h][0] - most[h])
            plain = acc[:w, lanes[h]] * decay + plain
            tangent = acc[w:, lanes[h]] * decay + tangent
            total, cross = state[h][1] * decay + total, state[h][2] * decay + cross
        acc[:w, lanes[h]] = plain
        acc[w:, lanes[h]] = tangent
        for r, value in enumerate((most[h], total, cross)):
            stat[r : r + 1, lanes[h]] = value

    for h in range(len(lanes) + 1):
        if h > 0:
            top(h - 1)
        for c in range(len(pieces)):
            if h < len(lanes):
                score(h, c)
            if h > 0:
                soften(h - 1, c)
        if h > 0:
            plain = nn(vt_s[:, at], gather(h - 1, 0))
            moving = nn(vt_s[w:, at], gather(h - 1, 1))
            finish(h - 1, plain, moving)


def by_count(sh, low, count, run, masked):
    most = min(4 if masked else 3, sh.blocks)
    head = lax.rem(count - 1, 4) + 1 if masked else lax.rem(count, 4)
    for blocks in range(1, most + 1):

        @pl.when(head == blocks)
        def _(blocks=blocks):
            run(low + count - blocks if masked else low, blocks, masked)

    def step(i, carry):
        run(low + (0 if masked else head) + 4 * i, 4, False)
        return carry

    if sh.blocks >= 4:
        lax.fori_loop(0, (count - head) // 4, step, 0)


def lay_chunk(sh, me_ref, sources, targets):
    for m, (ref, base) in enumerate(sources):
        slot = pl.ds(slot_of(me_ref, m, sh.rows), sh.rows)
        for i, target in enumerate(targets):
            at = base + i * sh.rows
            target[slot, :] = ref[at : at + sh.rows, :]


def lay_queries(sh, me_ref, order, pieces, qq):
    per = sh.rows // sh.block
    for m, ref in zip(order, pieces):
        for i in range(2):
            for g in range(sh.group):
                for r in range(per):
                    block = jnp.bitwise_xor(me_ref[0], m) * per + r
                    at = (i * sh.group + g) * sh.rows + r * sh.block
                    qq[
                        block,
                        g * sh.block : (g + 1) * sh.block,
                        i * sh.width : (i + 1) * sh.width,
                    ] = ref[at : at + sh.block, :]


def lay_span(sh, me_ref, sources, laid):
    w = sh.width
    k_s, v_s, kt_s, tk_s, vt_s, tv_s = laid
    lay_chunk(sh, me_ref, sources, (k_s, v_s, tk_s, tv_s))
    kt_s[...] = transposed(k_s[...])
    vt_s[:w, :] = transposed(tv_s[...])
    vt_s[w : 2 * w, :] = transposed(v_s[...])
    vt_s[2 * w :, :] = jnp.ones((ONES_ROWS, sh.tokens), BF16)


def transposed(x):
    return x.astype(F32).T.astype(BF16)


def located(sh, refs):
    length = refs[0].shape[0]
    return [(ref, at) for ref in refs for at in range(0, ref.shape[0], length)]


def back_of(sh, me_ref, back_ref, qb):
    per = sh.rows // sh.block
    return back_ref[jnp.bitwise_xor(me_ref[0], qb // per) * per + qb % per]


def each_block(count, run):
    def step(i, carry):
        run(i)
        return carry

    lax.fori_loop(0, count, step, 0)


def block_in_turn(sh, me_ref, order, i):
    per = sh.rows // sh.block
    if order == list(range(sh.parts)):
        return i
    partner = order[0]
    for j in range(1, len(order)):
        partner = jnp.where(i // per == j, order[j], partner)
    return jnp.bitwise_xor(me_ref[0], partner) * per + i % per


def kept_shapes(sh):
    return [
        jax.ShapeDtypeStruct((sh.blocks, sh.tokens, sh.lanes), BF16),
        jax.ShapeDtypeStruct((sh.blocks, sh.blocks, 1, sh.lanes), F32),
    ]


def forward_own(sh, me, back, order, queries, chunk, before):
    w = sh.width
    first = before is None
    turns = len(order) * (sh.rows // sh.block)

    def kernel(me_ref, back_ref, *refs):
        refs = list(refs)

        def take(count):
            taken = refs[:count]
            del refs[:count]
            return taken

        q_in = take(len(order))
        if first:
            kv_in = take(len(chunk))
            accs, stats, qq_s, es, ms = take(5)
            laid = refs
            lay_span(sh, me_ref, located(sh, kv_in), laid)
        else:
            laid = take(len(chunk))
            take(5)
            accs, stats, qq_s, es, ms = refs
        k_s, _, _, tk_s, vt_s = laid[:5]
        lay_queries(sh, me_ref, order, q_in, qq_s)

        def query_block(i):
            qb = block_in_turn(sh, me_ref, order, i)
            low = jnp.clip(qb - back_of(sh, me_ref, back_ref, qb), 0, qb)
            run = functools.partial(
                forward_tile,
                sh,
                (k_s, tk_s),
                vt_s,
                accs.at[qb],
                stats.at[qb],
                (es.at[qb], ms.at[qb]),
                qq_s[qb],
            )
            by_count(sh, low, qb + 1 - low, run, True)

        each_block(turns, query_block)

    def array(*shape, dtype=F32):
        return jax.ShapeDtypeStruct(shape, dtype)

    span = array(sh.tokens, w, dtype=BF16)
    out_shape = [
        array(sh.blocks, 2 * w, sh.lanes),
        array(sh.blocks, 8, sh.lanes),
        array(sh.blocks, sh.lanes, 2 * w, dtype=BF16),
        *kept_shapes(sh),
    ]
    operands = [*queries, *chunk]
    aliases = {}
    if first:
        out_shape += [span, span, array(w, sh.tokens, dtype=BF16), span]
        out_shape.append(array(2 * w + ONES_ROWS, sh.tokens, dtype=BF16))
    else:
        aliases = {2 + len(operands) + i: i for i in range(5)}
        operands += before
    work = sh.group * sh.tokens * sh.block * turns // 2
    return pl.pallas_call(
        kernel,
        in_specs=[SMEM, SMEM] + [VMEM] * len(operands),
        out_specs=[VMEM] * len(out_shape),
        out_shape=out_shape,
        input_output_aliases=aliases,
        scratch_shapes=[pltpu.VMEM((sh.tokens, w), BF16)] * first,
        compiler_params=params(),
        cost_estimate=cost(12 * work * w, 4 * sh.tokens * sh.lanes, work),
        name="forward_own",
    )(me, back, *operands)


def forward_chunk(sh, me, back, qq, chunk, distance, state, gain_square=None):
    w = sh.width
    closing = gain_square is not None

    def kernel(me_ref, back_ref, qq_s, *refs):
        refs = list(refs)

        def take(count):
            taken = refs[:count]
            del refs[:count]
            return taken

        kv_in = take(len(chunk))
        take(2)
        if closing:
            (gain_ref,) = take(1)
        k_s, v_s, kt_s, accs, stats = take(5)
        last = take(2)
        if closing:
            lse, sums = last
        tk_s, tv_s, vt_s = refs
        lay_span(sh, me_ref, located(sh, kv_in), (k_s, v_s, kt_s, tk_s, vt_s, tv_s))

        def query_block(qb):
            acc, stat = accs.at[qb], stats.at[qb]
            first = qb - back_of(sh, me_ref, back_ref, qb) + distance * sh.blocks
            first = jnp.clip(first, 0, sh.blocks)
            count = sh.blocks - first

            @pl.when(count > 0)
            def _():
                kept = None if closing else [ref.at[qb] for ref in last]
                run = functools.partial(
                    forward_tile, sh, (k_s, tk_s), vt_s, acc, stat, kept, qq_s[qb]
                )
                by_count(sh, first, count, run, False)

            if closing:
                most, total, cross = load_state(stat, slice(None))
                inverse = 1.0 / total
                plain = acc[:w, :] * inverse
                moved = acc[w:, :] * inverse - (cross * inverse * sh.scale) * plain
                acc[:w, :] = plain
                acc[w:, :] = moved
                lse[qb] = most + jnp.log(total)
                square = plain * plain
                product = plain * moved
                gain = gain_ref[...]
                for r, value in enumerate((square, product, gain * square, gain * product)):
                    line = jnp.sum(value, axis=0, keepdims=True)
                    pieces = [line[:, g * sh.block : (g + 1) * sh.block] for g in range(sh.group)]
                    sums[qb, r : r + 1, :] = functools.reduce(jnp.add, pieces)

        each_block(sh.blocks, query_block)

    def array(*shape, dtype=F32):
        return jax.ShapeDtypeStruct(shape, dtype)

    out_shape = [
        array(sh.tokens, w, dtype=BF16),
        array(sh.tokens, w, dtype=BF16),
        array(w, sh.tokens, dtype=BF16),
        array(sh.blocks, 2 * w, sh.lanes),
        array(sh.blocks, 8, sh.lanes),
    ]
    if closing:
        out_shape += [array(sh.blocks, 1, sh.lanes), array(sh.blocks, 4, sh.block)]
    else:
        out_shape += kept_shapes(sh)
    operands = [qq, *chunk]
    aliases = {2 + len(operands): 3, 3 + len(operands): 4}
    operands += state
    if closing:
        operands.append(gain_square)
    work = sh.group * sh.tokens * sh.tokens // 2
    return pl.pallas_call(
        kernel,
        in_specs=[SMEM, SMEM] + [VMEM] * len(operands),
        out_specs=[VMEM] * len(out_shape),
        out_shape=out_shape,
        input_output_aliases=aliases,
        scratch_shapes=[
            pltpu.VMEM((sh.tokens, w), BF16),
            pltpu.VMEM((sh.tokens, w), BF16),
            pltpu.VMEM((2 * w + ONES_ROWS, sh.tokens), BF16),
        ],
        compiler_params=params(),
        cost_estimate=cost(24 * work * w, 12 * sh.tokens * sh.lanes * 2, work),
        name="forward_far" if closing else "forward_chunk",
    )(me, back, *operands)


def backward_tile(sh, keys, kt_s, dkv_s, dq_s, qg, lse, dot, block, blocks, _):
    start, size = block_rows(sh, block), blocks * sh.block
    rows = pl.ds(start, size)
    k_s, v_s = keys
    k, v = k_s[rows, :], v_s[rows, :]
    empty = jnp.zeros_like(k)
    left = jnp.concatenate([k, empty], axis=0)
    right = jnp.concatenate([empty, v], axis=0)
    stacked = jnp.concatenate([left, right], axis=1)
    scores = [nt(stacked, qg[lanes, :]) for lanes in halves(sh)]
    for lanes, both in zip(halves(sh), scores):
        p = jnp.exp(both[:size] * sh.scale - lse[:, lanes])
        ds = (p * (both[size:] - dot[:, lanes])).astype(BF16)
        dkv_s[0, rows, :] += nn(ds, qg[lanes, : sh.width])
        dkv_s[1, rows, :] += nn(p.astype(BF16), qg[lanes, sh.width :])
        dq_s[:, lanes] += nn(kt_s[:, rows], ds)


def backward_kept(sh, keys, kt_s, dkv_s, dq_s, qg, lse, dot, kept, block, blocks, _):
    start, size = block_rows(sh, block), blocks * sh.block
    rows = pl.ds(start, size)
    v = keys[1][rows, :]
    slopes = [nt(v, qg[lanes, sh.width :]) for lanes in halves(sh)]
    for lanes, slope in zip(halves(sh), slopes):
        parts = []
        for j in range(blocks):
            factor = jnp.exp(kept[1][block + j, :, lanes] - lse[:, lanes])
            at = pl.ds(block_rows(sh, block + j), sh.block)
            parts.append(kept[0][at, lanes].astype(F32) * factor)
        p = jnp.concatenate(parts, axis=0)
        ds = (p * (slope - dot[:, lanes])).astype(BF16)
        dkv_s[0, rows, :] += nn(ds, qg[lanes, : sh.width])
        dkv_s[1, rows, :] += nn(p.astype(BF16), qg[lanes, sh.width :])
        dq_s[:, lanes] += nn(kt_s[:, rows], ds)


def backward_chunk(sh, me, back, qq, keys, distance, grads, lse, dots, dq, norm, order, held):
    w = sh.width
    opening, closing = norm is not None, distance == 0
    per = sh.rows // sh.block

    def kernel(me_ref, back_ref, *refs):
        refs = list(refs)

        def take(count):
            taken = refs[:count]
            del refs[:count]
            return taken

        qq_s, k_s, v_s, kt_s = take(4)
        kept = take(len(keys) - 3)
        (lse_s,) = take(1)
        if opening:
            out_s, gain_ref, *sum_refs = take(2 + len(norm[0]))
        else:
            grad_s, dot_s, dq_in = take(3)
        (held_ref,) = take(1) if held is not None else (None,)
        (dkv_out,) = take(1)
        dq_out = take(len(order) if closing else 1)
        if opening:
            grad_s, dot_s = take(2)
        dkv_s, dq_own = (dkv_out, *refs) if closing else refs
        if held_ref is None:
            dkv_s[...] = jnp.zeros_like(dkv_s)

        def query_block(i):
            qb = block_in_turn(sh, me_ref, order, i)
            dq_s = dq_own if closing else dq_out[0].at[qb]
            if opening:
                features = norm[2]
                token = functools.reduce(jnp.add, [ref[qb] for ref in sum_refs])
                sums = jnp.concatenate([token] * sh.group, axis=1)
                square = sums[0:1] / features + EPSILON
                inverse = lax.rsqrt(square)
                ratio = sums[1:2] / (features * square)
                again = (sums[3:4] - ratio * sums[2:3]) * inverse
                again = again / (features * square)
                plain = out_s[qb, :w, :]
                moved = out_s[qb, w:, :]
                first_grad = gain_ref[...] * (moved - plain * ratio) * inverse
                cot = ((first_grad - plain * again) * inverse).astype(BF16).astype(F32)
                dot_s[qb] = jnp.sum(cot * plain, axis=0, keepdims=True)
                grad_s[qb] = cot.T.astype(BF16)
                dq_s[...] = jnp.zeros((w, sh.lanes), F32)
            elif closing:
                dq_s[...] = dq_in[qb]

            top = sh.blocks if distance else qb + 1
            first = jnp.clip(qb - back_of(sh, me_ref, back_ref, qb) + distance * sh.blocks, 0, top)
            count = top - first

            @pl.when(count > 0)
            def _():
                qg = jnp.concatenate([qq_s[qb, :, :w], grad_s[qb]], axis=1)
                common = (sh, (k_s, v_s), kt_s, dkv_s, dq_s, qg, lse_s[qb], dot_s[qb])
                if kept:
                    run = functools.partial(backward_kept, *common, [ref.at[qb] for ref in kept])
                else:
                    run = functools.partial(backward_tile, *common)
                by_count(sh, first, count, run, False)

            if closing:
                done = (dq_s[...] * sh.scale).T.reshape(sh.group, sh.block, w).astype(BF16)
                at = pl.ds(pl.multiple_of(i % per * sh.block, sh.block), sh.block)
                for j, out in enumerate(dq_out):

                    @pl.when(i // per == j)
                    def _(out=out):
                        out[:, at, :] = done

        each_block(len(order) * per, query_block)
        if not closing:
            dkv_out[0] = (dkv_s[0] * sh.scale).astype(BF16)
            dkv_out[1] = dkv_s[1].astype(BF16)

    def array(*shape, dtype=F32):
        return jax.ShapeDtypeStruct(shape, dtype)

    operands = [qq, *keys, lse]
    if opening:
        operands += [grads, norm[1], *norm[0]]
    else:
        operands += [grads, dots, dq]
    aliases = {}
    if not opening and not closing:
        aliases = {1 + len(operands): 1}
    if held is not None:
        aliases = {2 + len(operands): 0}
        operands.append(held)
    out_shape = [array(2, sh.tokens, w, dtype=F32 if closing else BF16)]
    if closing:
        out_shape += [array(sh.group, sh.rows, w, dtype=BF16)] * len(order)
    else:
        out_shape.append(array(sh.blocks, w, sh.lanes))
    if opening:
        out_shape += [
            array(sh.blocks, sh.lanes, w, dtype=BF16),
            array(sh.blocks, 1, sh.lanes),
        ]
    work = sh.group * sh.tokens * len(order) * sh.rows // 2
    return pl.pallas_call(
        kernel,
        in_specs=[SMEM, SMEM] + [VMEM] * len(operands),
        out_specs=[VMEM] * len(out_shape),
        out_shape=out_shape,
        input_output_aliases=aliases,
        scratch_shapes=[pltpu.VMEM((2, sh.tokens, w), F32)] * (not closing)
        + [pltpu.VMEM((w, sh.lanes), F32)],
        compiler_params=params(),
        cost_estimate=cost(1, 1) if closing else cost(20 * work * w, 16 * work, work),
        name="backward_chunk",
    )(me, back, *operands)


def combine(sh, me, arrived, held):
    count = len(arrived)

    def kernel(me_ref, held_ref, *refs):
        for m, out in enumerate(refs[count:]):
            slot = pl.ds(slot_of(me_ref, m, sh.rows), sh.rows)
            for a, factor in ((0, sh.scale), (1, 1.0)):
                part = held_ref[a, slot, :] * factor
                for ref in refs[:count]:
                    part += ref[a, slot, :].astype(F32)
                out[a] = part.astype(BF16)

    return pl.pallas_call(
        kernel,
        in_specs=[SMEM] + [VMEM] * (1 + count),
        out_specs=[VMEM] * sh.parts,
        out_shape=[jax.ShapeDtypeStruct((2, sh.rows, sh.width), BF16)] * sh.parts,
        compiler_params=params(),
        cost_estimate=cost(0, 1),
        name="combine",
    )(me, held, *arrived)


def exchanged_with(piece, parts, m):
    return lax.ppermute(piece, "part", [(i, i ^ m) for i in range(parts)]) if m else piece


def exchanged(pieces, parts):
    return [exchanged_with(piece, parts, m) for m, piece in enumerate(pieces)]


def moved_on(value, steps):
    count = lax.axis_size("span")
    pairs = [(i, i + steps) for i in range(count) if 0 <= i + steps < count]
    return lax.ppermute(value, "span", pairs)


def summed_over_head(value):
    count = lax.axis_size("head")
    if count & (count - 1):
        return lax.psum(value, "head")
    step = 1
    while step < count:
        value = value + lax.ppermute(value, "head", [(i, i ^ step) for i in range(count)])
        step *= 2
    return value


def body(queries, keys, values, tangent_queries, tangent_keys, tangent_values, doc_start, out_gain):
    rows, query_heads, width = queries.shape
    key_heads = keys.shape[1]
    group = query_heads // key_heads
    parts = lax.axis_size("part")
    per = doc_start.shape[0]
    block = rows // per
    features = query_heads * width * lax.axis_size("head")
    hops = -(-DOC_DEVS // parts)
    sh = Shape(parts, group, rows, width, block)
    place = lax.axis_index("part")
    me = place.astype(jnp.int32).reshape(1)

    def flat(array):
        return array.reshape(-1, width)

    pieces = split_heads(
        [flat(a) for a in (keys, values, tangent_keys, tangent_values)], parts, 1, doc_start
    )
    q_rows, _ = lax.optimization_barrier(((flat(queries), flat(tangent_queries)), pieces[0]))
    q_pieces = split_heads(q_rows, parts, group)
    own = moved_on(pieces[0], 1)
    pieces = exchanged(pieces, parts)
    chunks = [pieces]
    if parts > 1:
        own, q_pieces = lax.optimization_barrier((own, q_pieces))
        owns = [own]
        for _ in range(hops - 1):
            owns.append(moved_on(owns[-1], 1))
        late, owns = lax.optimization_barrier((pieces[1:], owns))
        rest = jnp.concatenate([moved_on(piece, 1) for piece in late], axis=0)
        chunks.append([owns[0], rest])
        for own in owns[1:]:
            rest = moved_on(rest, 1)
            chunks.append([own, rest])
    else:
        for _ in range(hops):
            chunks.append([own])
            own = moved_on(own, 1)
    q_parts = exchanged(q_pieces[:-1], parts)
    if parts > 1:
        last, _ = lax.optimization_barrier((q_pieces[-1], q_parts[min(1, parts - 2)]))
        q_parts.append(exchanged_with(last, parts, parts - 1))
    else:
        q_parts = q_pieces
    back = jnp.concatenate([p[4 * rows : 4 * rows + per, 0] for p in pieces]).astype(jnp.int32)
    gain = lax.dynamic_index_in_dim(out_gain.reshape(key_heads, group, width), place, 0, False)
    gain_square = jnp.repeat((gain * gain).T, block, axis=1)

    everyone = list(range(parts))
    before, laid = None, chunks[0]
    for order in [everyone[:1], everyone[1:-1], everyone[-1:]] if parts > 1 else [everyone]:
        if order:
            turn = forward_own(sh, me, back, order, [q_parts[m] for m in order], laid, before)
            laid = turn[5:] or laid
            before = list(turn[:5])
    state, qq = before[:2], before[2]
    spans = [(*laid[:3], *before[3:])]
    for distance in range(1, hops):
        k, v, kt, acc, stat, *kept = forward_chunk(
            sh, me, back, qq, chunks[distance], distance, state
        )
        state = [acc, stat]
        spans.append((k, v, kt, *kept))
    k, v, kt, out, _, lse, sums = forward_chunk(
        sh, me, back, qq, chunks[hops], hops, state, gain_square
    )
    spans.append((k, v, kt))
    norm = (exchanged([summed_over_head(sums)] * parts, parts), gain_square, features)

    part, dq, grads, dots = backward_chunk(
        sh, me, back, qq, spans[hops], hops, out, lse, None, None, norm, everyone, None
    )
    arrived = [moved_on(part, -hops)]
    for distance in range(hops - 1, 0, -1):
        part, dq = backward_chunk(
            sh, me, back, qq, spans[distance], distance, grads, lse, dots, dq, None,
            everyone, None,
        )
        arrived.append(moved_on(part, -distance))
    turns = [turn[::-1] for turn in (everyone[-1:], everyone[:-1]) if turn]
    held, dq_pieces = None, [None] * parts
    for order in turns:
        if held is not None:
            arrived[0], held = lax.optimization_barrier((arrived[0], held))
        held, *done = backward_chunk(
            sh, me, back, qq, spans[0], 0, grads, lse, dots, dq, None, order, held
        )
        for m, piece in zip(order, done):
            dq_pieces[m] = piece.reshape(1, group, rows, width)
    dq_pieces = exchanged(dq_pieces, parts)
    dq_pieces[-1], held = lax.optimization_barrier((dq_pieces[-1], held))
    dkv_pieces = exchanged(combine(sh, me, arrived, held), parts)
    (product_queries,) = join_heads(dq_pieces, 1, group)
    dkv_pieces = [p.reshape(2, 1, rows, width) for p in dkv_pieces]
    product_keys, product_values = join_heads(dkv_pieces, 2, 1)
    return (
        product_queries.reshape(queries.shape),
        product_keys.reshape(keys.shape),
        product_values.reshape(keys.shape),
    )


def solution(mesh):
    def run(*arguments):
        count, heads = mesh.shape["ctx"], mesh.shape["head"]
        parts = arguments[1].shape[1] // heads
        split = Mesh(
            mesh.devices.reshape(count // parts, parts, heads), ("span", "part", "head")
        )
        ctx = ("span", "part")
        array = P(ctx, "head", None)
        return jax.shard_map(
            body,
            mesh=split,
            in_specs=(array,) * 6 + (P(ctx), P("head")),
            out_specs=(array,) * 3,
            check_vma=False,
        )(*arguments)

    return run
```

```python
import functools

import jax
import jax.numpy as jnp
from jax import lax
from jax.experimental import pallas as pl
from jax.experimental.pallas import tpu as pltpu
from jax.sharding import Mesh, PartitionSpec as P

DOC_DEVS = 8
EPSILON = 1e-06
VMEM_BYTES = 18 * 1024 * 1024
NOTE_ROWS = 16
ONES_ROWS = 16
WIDE_VMEM_BYTES = 60 * 1024 * 1024
MASKED = -1e30
F32 = jnp.float32
BF16 = jnp.bfloat16
SMEM = pl.BlockSpec(memory_space=pltpu.SMEM)
VMEM = pl.BlockSpec(memory_space=pltpu.VMEM)


def params(size=VMEM_BYTES):
    return pltpu.CompilerParams(vmem_limit_bytes=size)


def cost(flops, moved, powers=0):
    return pl.CostEstimate(flops=int(flops), bytes_accessed=int(moved), transcendentals=int(powers))


def nn(a, b):
    return lax.dot_general(a, b, (((1,), (0,)), ((), ())), preferred_element_type=F32)


def nt(a, b):
    return lax.dot_general(a, b, (((1,), (1,)), ((), ())), preferred_element_type=F32)


def split_heads(arrays, parts, per_part, notes=None):
    count = len(arrays)
    total, width = arrays[0].shape
    heads = parts * per_part
    rows = total // heads
    length = count * per_part * rows
    span = per_part * rows
    extra = 0 if notes is None else NOTE_ROWS
    scalars = [] if notes is None else [notes]

    def kernel(*refs):
        ins = list(refs[: len(scalars) + count])
        results = refs[len(scalars) + count : len(scalars) + count + parts]
        held, wide, sems, *staged = refs[len(scalars) + count + parts :]
        outs, out_sems = (staged[:-1], staged[-1]) if extra else (results, None)
        mine = lax.axis_index("part")
        if extra:
            note_ref = ins.pop(0)
        copies = [pltpu.make_async_copy(ins[a], held.at[a], sems.at[a]) for a in range(count)]
        for copy in copies:
            copy.start()
        leaving = []

        def leave(m, a, start, size):
            part = pl.ds(start, size)
            sem = out_sems.at[m * (count + 1) + a]
            leaving.append(pltpu.make_async_copy(outs[m].at[part], results[m].at[part], sem))
            leaving[-1].start()

        if extra:
            first = (lax.axis_index("span") * parts + mine) * notes.shape[0]
            line = lax.broadcasted_iota(jnp.int32, (extra, width), 0)
            lines = jnp.zeros((extra, width), jnp.int32)
            for i in range(notes.shape[0]):
                lines = jnp.where(line == i, first + i - note_ref[i], lines)
            for m, out in enumerate(outs):
                out[length:, :] = lines.astype(F32).astype(BF16)
                leave(m, count, length, extra)
        for a in range(count):
            copies[a].wait()
            wide[...] = held[a].astype(F32)
            for m in range(parts):
                for r in range(per_part):
                    head = jnp.bitwise_xor(mine, m) * per_part + r
                    at = (a * per_part + r) * rows
                    outs[m][at : at + rows, :] = wide[pl.ds(head, rows, stride=heads), :].astype(BF16)
                if extra:
                    leave(m, a, a * span, span)
        for copy in leaving:
            copy.wait()

    piece = (length + extra, width)
    scratch = [
        pltpu.VMEM((count, total, width), BF16),
        pltpu.VMEM((total, width), F32),
        pltpu.SemaphoreType.DMA((count,)),
    ]
    if extra:
        scratch += [pltpu.VMEM(piece, BF16)] * parts
        scratch.append(pltpu.SemaphoreType.DMA((parts * (count + 1),)))
    return pl.pallas_call(
        kernel,
        in_specs=[SMEM] * len(scalars) + [pl.BlockSpec(memory_space=pltpu.HBM)] * count,
        out_specs=[pl.BlockSpec(memory_space=pltpu.HBM) if extra else VMEM] * parts,
        out_shape=[jax.ShapeDtypeStruct(piece, BF16)] * parts,
        scratch_shapes=scratch,
        compiler_params=params(VMEM_BYTES if notes is None else WIDE_VMEM_BYTES),
        cost_estimate=cost(0, 4 * count * total * width),
        name="split_heads",
    )(*scalars, *arrays)


def join_heads(pieces, count, per_part):
    parts = len(pieces)
    rows, width = pieces[0].shape[-2:]
    heads = parts * per_part

    steps = 4
    cut = rows // steps

    def kernel(*refs):
        ins, outs = refs[:parts], refs[parts:]
        mine = lax.axis_index("part")
        for a in range(count):
            for m in range(parts):
                for r in range(per_part):
                    head = jnp.bitwise_xor(mine, m) * per_part + r
                    outs[a][pl.ds(head, cut, stride=heads), :] = ins[m][a, r].astype(F32)

    return pl.pallas_call(
        kernel,
        grid=(steps,),
        in_specs=[pl.BlockSpec((count, per_part, cut, width), lambda i: (0, 0, i, 0))] * parts,
        out_specs=[pl.BlockSpec((cut * heads, width), lambda i: (i, 0))] * count,
        out_shape=[jax.ShapeDtypeStruct((rows * heads, width), F32)] * count,
        compiler_params=params(),
        cost_estimate=cost(0, 6 * count * rows * heads * width),
        name="join_heads",
    )(*pieces)


def slot_of(me_ref, m, rows):
    return pl.multiple_of(jnp.bitwise_xor(me_ref[0], m) * rows, rows)


class Shape:
    def __init__(self, parts, group, rows, width, block):
        self.parts, self.group, self.rows, self.width, self.block = parts, group, rows, width, block
        self.tokens = parts * rows
        self.blocks = self.tokens // block
        self.lanes = group * block
        self.scale = width**-0.5


def diagonal(sh):
    shape = (sh.block, sh.block)
    key = lax.broadcasted_iota(jnp.int32, shape, 0)
    query = lax.broadcasted_iota(jnp.int32, shape, 1)
    return key <= query


def below_diagonal(sh, value, other):
    allowed = diagonal(sh)
    cut = [value[:, at : at + sh.block] for at in range(0, value.shape[1], sh.block)]
    return jnp.concatenate([jnp.where(allowed, part, other) for part in cut], axis=1)


def halves(sh):
    if sh.group % 2:
        return [slice(0, sh.lanes)]
    return [slice(0, sh.lanes // 2), slice(sh.lanes // 2, sh.lanes)]


def stacked_keys(keys, start, size):
    k_s, tk_s = keys
    k = k_s[pl.ds(start, size), :]
    tk = tk_s[pl.ds(start, size), :]
    left = jnp.concatenate([k, tk], axis=0)
    right = jnp.concatenate([jnp.zeros_like(k), k], axis=0)
    return jnp.concatenate([left, right], axis=1)


def pieces_of(sh, start, blocks):
    sizes = [2] * (blocks // 2) + [1] * (blocks % 2)
    firsts = [sum(sizes[:i]) for i in range(len(sizes))]
    return [
        (pl.multiple_of(start + first * sh.block, sh.block), size * sh.block, i == len(sizes) - 1)
        for i, (first, size) in enumerate(zip(firsts, sizes))
    ]


def cut_diagonal(sh, value, other):
    low = below_diagonal(sh, value[value.shape[0] - sh.block :], other)
    if value.shape[0] == sh.block:
        return low
    return jnp.concatenate([value[: value.shape[0] - sh.block], low], axis=0)


def block_rows(sh, block):
    return pl.multiple_of(block * sh.block, sh.block)


def load_state(stat, lanes):
    return tuple(stat[r : r + 1, lanes] for r in range(3))


def forward_tile(sh, keys, vt_s, acc, stat, kept, qq, block, blocks, masked):
    w = sh.width
    start = block_rows(sh, block)
    pieces = pieces_of(sh, start, blocks)
    stacked = [stacked_keys(keys, at, size) for at, size, _ in pieces]
    at = pl.ds(start, blocks * sh.block)
    lanes = halves(sh)
    scores = [[] for _ in lanes]
    mixed = [[] for _ in lanes]
    most = [None for _ in lanes]
    state = [None if masked else load_state(stat, part) for part in lanes]

    def score(h, c):
        both = nt(stacked[c], qq[lanes[h], :])
        s, d = both[: pieces[c][1]], both[pieces[c][1] :]
        if masked and pieces[c][2]:
            s = cut_diagonal(sh, s, MASKED)
        scores[h].append((s, d))

    def top(h):
        peaks = [jnp.max(s, axis=0, keepdims=True) for s, _ in scores[h]]
        most[h] = functools.reduce(jnp.maximum, peaks) * sh.scale
        if not masked:
            most[h] = jnp.maximum(most[h], state[h][0])
        if kept is not None:
            for j in range(blocks):
                kept[1][block + j, :, lanes[h]] = most[h]

    def soften(h, c):
        s, d = scores[h][c]
        e = jnp.exp(s * sh.scale - most[h])
        mixed[h].append((e.astype(BF16), (e * d).astype(BF16)))
        if kept is not None:
            kept[0][pl.ds(pieces[c][0], pieces[c][1]), lanes[h]] = mixed[h][-1][0]

    def gather(h, i):
        return jnp.concatenate([pair[i] for pair in mixed[h]], axis=0)

    def finish(h, plain, moving):
        total, cross = plain[2 * w : 2 * w + 1], moving[w : w + 1]
        tangent = plain[:w] + moving[:w] * sh.scale
        plain = plain[w : 2 * w]
        if not masked:
            decay = jnp.exp(state[h][0] - most[h])
            plain = acc[:w, lanes[h]] * decay + plain
            tangent = acc[w:, lanes[h]] * decay + tangent
            total, cross = state[h][1] * decay + total, state[h][2] * decay + cross
        acc[:w, lanes[h]] = plain
        acc[w:, lanes[h]] = tangent
        for r, value in enumerate((most[h], total, cross)):
            stat[r : r + 1, lanes[h]] = value

    for h in range(len(lanes) + 1):
        if h > 0:
            top(h - 1)
        for c in range(len(pieces)):
            if h < len(lanes):
                score(h, c)
            if h > 0:
                soften(h - 1, c)
        if h > 0:
            plain = nn(vt_s[:, at], gather(h - 1, 0))
            moving = nn(vt_s[w:, at], gather(h - 1, 1))
            finish(h - 1, plain, moving)


def by_count(sh, low, count, run, masked):
    most = min(4 if masked else 3, sh.blocks)
    head = lax.rem(count - 1, 4) + 1 if masked else lax.rem(count, 4)
    for blocks in range(1, most + 1):

        @pl.when(head == blocks)
        def _(blocks=blocks):
            run(low + count - blocks if masked else low, blocks, masked)

    def step(i, carry):
        run(low + (0 if masked else head) + 4 * i, 4, False)
        return carry

    if sh.blocks >= 4:
        lax.fori_loop(0, (count - head) // 4, step, 0)


def lay_chunk(sh, me_ref, sources, targets):
    for m, (ref, base) in enumerate(sources):
        slot = pl.ds(slot_of(me_ref, m, sh.rows), sh.rows)
        for i, target in enumerate(targets):
            at = base + i * sh.rows
            target[slot, :] = ref[at : at + sh.rows, :]


def lay_queries(sh, me_ref, order, pieces, qq):
    per = sh.rows // sh.block
    for m, ref in zip(order, pieces):
        for i in range(2):
            for g in range(sh.group):
                for r in range(per):
                    block = jnp.bitwise_xor(me_ref[0], m) * per + r
                    at = (i * sh.group + g) * sh.rows + r * sh.block
                    qq[
                        block,
                        g * sh.block : (g + 1) * sh.block,
                        i * sh.width : (i + 1) * sh.width,
                    ] = ref[at : at + sh.block, :]


def lay_span(sh, me_ref, sources, laid):
    w = sh.width
    k_s, v_s, kt_s, tk_s, vt_s, tv_s = laid
    lay_chunk(sh, me_ref, sources, (k_s, v_s, tk_s, tv_s))
    kt_s[...] = transposed(k_s[...])
    vt_s[:w, :] = transposed(tv_s[...])
    vt_s[w : 2 * w, :] = transposed(v_s[...])
    vt_s[2 * w :, :] = jnp.ones((ONES_ROWS, sh.tokens), BF16)


def transposed(x):
    return x.astype(F32).T.astype(BF16)


def located(sh, refs):
    length = refs[0].shape[0]
    return [(ref, at) for ref in refs for at in range(0, ref.shape[0], length)]


def back_of(sh, me_ref, back_ref, qb):
    per = sh.rows // sh.block
    return back_ref[jnp.bitwise_xor(me_ref[0], qb // per) * per + qb % per]


def each_block(count, run):
    def step(i, carry):
        run(i)
        return carry

    lax.fori_loop(0, count, step, 0)


def block_in_turn(sh, me_ref, order, i):
    per = sh.rows // sh.block
    if order == list(range(sh.parts)):
        return i
    partner = order[0]
    for j in range(1, len(order)):
        partner = jnp.where(i // per == j, order[j], partner)
    return jnp.bitwise_xor(me_ref[0], partner) * per + i % per


def kept_shapes(sh):
    return [
        jax.ShapeDtypeStruct((sh.blocks, sh.tokens, sh.lanes), BF16),
        jax.ShapeDtypeStruct((sh.blocks, sh.blocks, 1, sh.lanes), F32),
    ]


def forward_own(sh, me, back, order, queries, chunk, before):
    w = sh.width
    first = before is None
    turns = len(order) * (sh.rows // sh.block)

    def kernel(me_ref, back_ref, *refs):
        refs = list(refs)

        def take(count):
            taken = refs[:count]
            del refs[:count]
            return taken

        q_in = take(len(order))
        if first:
            kv_in = take(len(chunk))
            accs, stats, qq_s, es, ms = take(5)
            laid = refs
            lay_span(sh, me_ref, located(sh, kv_in), laid)
        else:
            laid = take(len(chunk))
            take(5)
            accs, stats, qq_s, es, ms = refs
        k_s, _, _, tk_s, vt_s = laid[:5]
        lay_queries(sh, me_ref, order, q_in, qq_s)

        def query_block(i):
            qb = block_in_turn(sh, me_ref, order, i)
            low = jnp.clip(qb - back_of(sh, me_ref, back_ref, qb), 0, qb)
            run = functools.partial(
                forward_tile,
                sh,
                (k_s, tk_s),
                vt_s,
                accs.at[qb],
                stats.at[qb],
                (es.at[qb], ms.at[qb]),
                qq_s[qb],
            )
            by_count(sh, low, qb + 1 - low, run, True)

        each_block(turns, query_block)

    def array(*shape, dtype=F32):
        return jax.ShapeDtypeStruct(shape, dtype)

    span = array(sh.tokens, w, dtype=BF16)
    out_shape = [
        array(sh.blocks, 2 * w, sh.lanes),
        array(sh.blocks, 8, sh.lanes),
        array(sh.blocks, sh.lanes, 2 * w, dtype=BF16),
        *kept_shapes(sh),
    ]
    operands = [*queries, *chunk]
    aliases = {}
    if first:
        out_shape += [span, span, array(w, sh.tokens, dtype=BF16), span]
        out_shape.append(array(2 * w + ONES_ROWS, sh.tokens, dtype=BF16))
    else:
        aliases = {2 + len(operands) + i: i for i in range(5)}
        operands += before
    work = sh.group * sh.tokens * sh.block * turns // 2
    return pl.pallas_call(
        kernel,
        in_specs=[SMEM, SMEM] + [VMEM] * len(operands),
        out_specs=[VMEM] * len(out_shape),
        out_shape=out_shape,
        input_output_aliases=aliases,
        scratch_shapes=[pltpu.VMEM((sh.tokens, w), BF16)] * first,
        compiler_params=params(),
        cost_estimate=cost(12 * work * w, 4 * sh.tokens * sh.lanes, work),
        name="forward_own",
    )(me, back, *operands)


def forward_chunk(sh, me, back, qq, chunk, distance, state, gain_square=None):
    w = sh.width
    closing = gain_square is not None

    def kernel(me_ref, back_ref, qq_s, *refs):
        refs = list(refs)

        def take(count):
            taken = refs[:count]
            del refs[:count]
            return taken

        kv_in = take(len(chunk))
        take(2)
        if closing:
            (gain_ref,) = take(1)
        k_s, v_s, kt_s, accs, stats = take(5)
        last = take(2)
        if closing:
            lse, sums = last
        tk_s, tv_s, vt_s = refs
        lay_span(sh, me_ref, located(sh, kv_in), (k_s, v_s, kt_s, tk_s, vt_s, tv_s))

        def query_block(qb):
            acc, stat = accs.at[qb], stats.at[qb]
            first = qb - back_of(sh, me_ref, back_ref, qb) + distance * sh.blocks
            first = jnp.clip(first, 0, sh.blocks)
            count = sh.blocks - first

            @pl.when(count > 0)
            def _():
                kept = None if closing else [ref.at[qb] for ref in last]
                run = functools.partial(
                    forward_tile, sh, (k_s, tk_s), vt_s, acc, stat, kept, qq_s[qb]
                )
                by_count(sh, first, count, run, False)

            if closing:
                most, total, cross = load_state(stat, slice(None))
                inverse = 1.0 / total
                plain = acc[:w, :] * inverse
                moved = acc[w:, :] * inverse - (cross * inverse * sh.scale) * plain
                acc[:w, :] = plain
                acc[w:, :] = moved
                lse[qb] = most + jnp.log(total)
                square = plain * plain
                product = plain * moved
                gain = gain_ref[...]
                for r, value in enumerate((square, product, gain * square, gain * product)):
                    line = jnp.sum(value, axis=0, keepdims=True)
                    pieces = [line[:, g * sh.block : (g + 1) * sh.block] for g in range(sh.group)]
                    sums[qb, r : r + 1, :] = functools.reduce(jnp.add, pieces)

        each_block(sh.blocks, query_block)

    def array(*shape, dtype=F32):
        return jax.ShapeDtypeStruct(shape, dtype)

    out_shape = [
        array(sh.tokens, w, dtype=BF16),
        array(sh.tokens, w, dtype=BF16),
        array(w, sh.tokens, dtype=BF16),
        array(sh.blocks, 2 * w, sh.lanes),
        array(sh.blocks, 8, sh.lanes),
    ]
    if closing:
        out_shape += [array(sh.blocks, 1, sh.lanes), array(sh.blocks, 4, sh.block)]
    else:
        out_shape += kept_shapes(sh)
    operands = [qq, *chunk]
    aliases = {2 + len(operands): 3, 3 + len(operands): 4}
    operands += state
    if closing:
        operands.append(gain_square)
    work = sh.group * sh.tokens * sh.tokens // 2
    return pl.pallas_call(
        kernel,
        in_specs=[SMEM, SMEM] + [VMEM] * len(operands),
        out_specs=[VMEM] * len(out_shape),
        out_shape=out_shape,
        input_output_aliases=aliases,
        scratch_shapes=[
            pltpu.VMEM((sh.tokens, w), BF16),
            pltpu.VMEM((sh.tokens, w), BF16),
            pltpu.VMEM((2 * w + ONES_ROWS, sh.tokens), BF16),
        ],
        compiler_params=params(),
        cost_estimate=cost(24 * work * w, 12 * sh.tokens * sh.lanes * 2, work),
        name="forward_far" if closing else "forward_chunk",
    )(me, back, *operands)


def backward_tile(sh, keys, kt_s, dkv_s, dq_s, qg, lse, dot, block, blocks, _):
    start, size = block_rows(sh, block), blocks * sh.block
    rows = pl.ds(start, size)
    k_s, v_s = keys
    k, v = k_s[rows, :], v_s[rows, :]
    empty = jnp.zeros_like(k)
    left = jnp.concatenate([k, empty], axis=0)
    right = jnp.concatenate([empty, v], axis=0)
    stacked = jnp.concatenate([left, right], axis=1)
    scores = [nt(stacked, qg[lanes, :]) for lanes in halves(sh)]
    for lanes, both in zip(halves(sh), scores):
        p = jnp.exp(both[:size] * sh.scale - lse[:, lanes])
        ds = (p * (both[size:] - dot[:, lanes])).astype(BF16)
        dkv_s[0, rows, :] += nn(ds, qg[lanes, : sh.width])
        dkv_s[1, rows, :] += nn(p.astype(BF16), qg[lanes, sh.width :])
        dq_s[:, lanes] += nn(kt_s[:, rows], ds)


def backward_kept(sh, keys, kt_s, dkv_s, dq_s, qg, lse, dot, kept, block, blocks, _):
    start, size = block_rows(sh, block), blocks * sh.block
    rows = pl.ds(start, size)
    v = keys[1][rows, :]
    slopes = [nt(v, qg[lanes, sh.width :]) for lanes in halves(sh)]
    for lanes, slope in zip(halves(sh), slopes):
        parts = []
        for j in range(blocks):
            factor = jnp.exp(kept[1][block + j, :, lanes] - lse[:, lanes])
            at = pl.ds(block_rows(sh, block + j), sh.block)
            parts.append(kept[0][at, lanes].astype(F32) * factor)
        p = jnp.concatenate(parts, axis=0)
        ds = (p * (slope - dot[:, lanes])).astype(BF16)
        dkv_s[0, rows, :] += nn(ds, qg[lanes, : sh.width])
        dkv_s[1, rows, :] += nn(p.astype(BF16), qg[lanes, sh.width :])
        dq_s[:, lanes] += nn(kt_s[:, rows], ds)


def backward_chunk(sh, me, back, qq, keys, distance, grads, lse, dots, dq, norm, order, held):
    w = sh.width
    opening, closing = norm is not None, distance == 0
    per = sh.rows // sh.block

    def kernel(me_ref, back_ref, *refs):
        refs = list(refs)

        def take(count):
            taken = refs[:count]
            del refs[:count]
            return taken

        qq_s, k_s, v_s, kt_s = take(4)
        kept = take(len(keys) - 3)
        (lse_s,) = take(1)
        if opening:
            out_s, gain_ref, *sum_refs = take(2 + len(norm[0]))
        else:
            grad_s, dot_s, dq_in = take(3)
        (held_ref,) = take(1) if held is not None else (None,)
        (dkv_out,) = take(1)
        dq_out = take(len(order) if closing else 1)
        if opening:
            grad_s, dot_s = take(2)
        dkv_s, dq_own = (dkv_out, *refs) if closing else refs
        if held_ref is None:
            dkv_s[...] = jnp.zeros_like(dkv_s)

        def query_block(i):
            qb = block_in_turn(sh, me_ref, order, i)
            dq_s = dq_own if closing else dq_out[0].at[qb]
            if opening:
                features = norm[2]
                token = functools.reduce(jnp.add, [ref[qb] for ref in sum_refs])
                sums = jnp.concatenate([token] * sh.group, axis=1)
                square = sums[0:1] / features + EPSILON
                inverse = lax.rsqrt(square)
                ratio = sums[1:2] / (features * square)
                again = (sums[3:4] - ratio * sums[2:3]) * inverse
                again = again / (features * square)
                plain = out_s[qb, :w, :]
                moved = out_s[qb, w:, :]
                first_grad = gain_ref[...] * (moved - plain * ratio) * inverse
                cot = ((first_grad - plain * again) * inverse).astype(BF16).astype(F32)
                dot_s[qb] = jnp.sum(cot * plain, axis=0, keepdims=True)
                grad_s[qb] = cot.T.astype(BF16)
                dq_s[...] = jnp.zeros((w, sh.lanes), F32)
            elif closing:
                dq_s[...] = dq_in[qb]

            top = sh.blocks if distance else qb + 1
            first = jnp.clip(qb - back_of(sh, me_ref, back_ref, qb) + distance * sh.blocks, 0, top)
            count = top - first

            @pl.when(count > 0)
            def _():
                qg = jnp.concatenate([qq_s[qb, :, :w], grad_s[qb]], axis=1)
                common = (sh, (k_s, v_s), kt_s, dkv_s, dq_s, qg, lse_s[qb], dot_s[qb])
                if kept:
                    run = functools.partial(backward_kept, *common, [ref.at[qb] for ref in kept])
                else:
                    run = functools.partial(backward_tile, *common)
                by_count(sh, first, count, run, False)

            if closing:
                done = (dq_s[...] * sh.scale).T.reshape(sh.group, sh.block, w).astype(BF16)
                at = pl.ds(pl.multiple_of(i % per * sh.block, sh.block), sh.block)
                for j, out in enumerate(dq_out):

                    @pl.when(i // per == j)
                    def _(out=out):
                        out[:, at, :] = done

        each_block(len(order) * per, query_block)
        if not closing:
            dkv_out[...] = dkv_s[...].astype(BF16)

    def array(*shape, dtype=F32):
        return jax.ShapeDtypeStruct(shape, dtype)

    operands = [qq, *keys, lse]
    if opening:
        operands += [grads, norm[1], *norm[0]]
    else:
        operands += [grads, dots, dq]
    aliases = {}
    if not opening and not closing:
        aliases = {1 + len(operands): 1}
    if held is not None:
        aliases = {2 + len(operands): 0}
        operands.append(held)
    out_shape = [array(2, sh.tokens, w, dtype=F32 if closing else BF16)]
    if closing:
        out_shape += [array(sh.group, sh.rows, w, dtype=BF16)] * len(order)
    else:
        out_shape.append(array(sh.blocks, w, sh.lanes))
    if opening:
        out_shape += [
            array(sh.blocks, sh.lanes, w, dtype=BF16),
            array(sh.blocks, 1, sh.lanes),
        ]
    work = sh.group * sh.tokens * len(order) * sh.rows // 2
    return pl.pallas_call(
        kernel,
        in_specs=[SMEM, SMEM] + [VMEM] * len(operands),
        out_specs=[VMEM] * len(out_shape),
        out_shape=out_shape,
        input_output_aliases=aliases,
        scratch_shapes=[pltpu.VMEM((2, sh.tokens, w), F32)] * (not closing)
        + [pltpu.VMEM((w, sh.lanes), F32)],
        compiler_params=params(),
        cost_estimate=cost(1, 1) if closing else cost(20 * work * w, 16 * work, work),
        name="backward_chunk",
    )(me, back, *operands)


def add_arrived(held, arrived):
    def kernel(held_ref, *refs):
        total = held_ref[...]
        for ref in refs[:-1]:
            total += ref[...].astype(F32)
        refs[-1][...] = total

    return pl.pallas_call(
        kernel,
        in_specs=[VMEM] * (1 + len(arrived)),
        out_specs=VMEM,
        out_shape=jax.ShapeDtypeStruct(held.shape, F32),
        input_output_aliases={0: 0},
        compiler_params=params(),
        cost_estimate=cost(0, 10 * held.size),
        name="add_arrived",
    )(held, *arrived)


def combine(sh, me, arrived, held):
    def kernel(me_ref, held_ref, arrived_ref, *outs):
        for m, out in enumerate(outs):
            slot = pl.ds(slot_of(me_ref, m, sh.rows), sh.rows)
            for a, factor in ((0, sh.scale), (1, 1.0)):
                total = held_ref[a, slot, :] + arrived_ref[a, slot, :].astype(F32)
                out[a] = (total * factor).astype(BF16)

    return pl.pallas_call(
        kernel,
        in_specs=[SMEM, VMEM, VMEM],
        out_specs=[VMEM] * sh.parts,
        out_shape=[jax.ShapeDtypeStruct((2, sh.rows, sh.width), BF16)] * sh.parts,
        compiler_params=params(),
        cost_estimate=cost(0, 1),
        name="combine",
    )(me, held, arrived)


def exchanged_with(piece, parts, m):
    return lax.ppermute(piece, "part", [(i, i ^ m) for i in range(parts)]) if m else piece


def exchanged(pieces, parts):
    return [exchanged_with(piece, parts, m) for m, piece in enumerate(pieces)]


def moved_on(value, steps):
    count = lax.axis_size("span")
    pairs = [(i, i + steps) for i in range(count) if 0 <= i + steps < count]
    return lax.ppermute(value, "span", pairs)


def summed_over_head(value):
    count = lax.axis_size("head")
    if count & (count - 1):
        return lax.psum(value, "head")
    step = 1
    while step < count:
        value = value + lax.ppermute(value, "head", [(i, i ^ step) for i in range(count)])
        step *= 2
    return value


def body(queries, keys, values, tangent_queries, tangent_keys, tangent_values, doc_start, out_gain):
    rows, query_heads, width = queries.shape
    key_heads = keys.shape[1]
    group = query_heads // key_heads
    parts = lax.axis_size("part")
    per = doc_start.shape[0]
    block = rows // per
    features = query_heads * width * lax.axis_size("head")
    hops = -(-DOC_DEVS // parts)
    sh = Shape(parts, group, rows, width, block)
    place = lax.axis_index("part")
    me = place.astype(jnp.int32).reshape(1)

    def flat(array):
        return array.reshape(-1, width)

    pieces = split_heads(
        [flat(a) for a in (keys, values, tangent_keys, tangent_values)], parts, 1, doc_start
    )
    q_rows, _ = lax.optimization_barrier(((flat(queries), flat(tangent_queries)), pieces[0]))
    q_pieces = split_heads(q_rows, parts, group)
    own = moved_on(pieces[0], 1)
    pieces = exchanged(pieces, parts)
    chunks = [pieces]
    if parts > 1:
        own, q_pieces = lax.optimization_barrier((own, q_pieces))
        owns = [own]
        for _ in range(hops - 1):
            owns.append(moved_on(owns[-1], 1))
        late, owns = lax.optimization_barrier((pieces[1:], owns))
        rest = jnp.concatenate([moved_on(piece, 1) for piece in late], axis=0)
        chunks.append([owns[0], rest])
        for own in owns[1:]:
            rest = moved_on(rest, 1)
            chunks.append([own, rest])
    else:
        for _ in range(hops):
            chunks.append([own])
            own = moved_on(own, 1)
    q_parts = exchanged(q_pieces[:-1], parts)
    if parts > 1:
        last, _ = lax.optimization_barrier((q_pieces[-1], q_parts[min(1, parts - 2)]))
        q_parts.append(exchanged_with(last, parts, parts - 1))
    else:
        q_parts = q_pieces
    back = jnp.concatenate([p[4 * rows : 4 * rows + per, 0] for p in pieces]).astype(jnp.int32)
    gain = lax.dynamic_index_in_dim(out_gain.reshape(key_heads, group, width), place, 0, False)
    gain_square = jnp.repeat((gain * gain).T, block, axis=1)

    everyone = list(range(parts))
    before, laid = None, chunks[0]
    for order in [everyone[:1], everyone[1:-1], everyone[-1:]] if parts > 1 else [everyone]:
        if order:
            turn = forward_own(sh, me, back, order, [q_parts[m] for m in order], laid, before)
            laid = turn[5:] or laid
            before = list(turn[:5])
    state, qq = before[:2], before[2]
    spans = [(*laid[:3], *before[3:])]
    for distance in range(1, hops):
        k, v, kt, acc, stat, *kept = forward_chunk(
            sh, me, back, qq, chunks[distance], distance, state
        )
        state = [acc, stat]
        spans.append((k, v, kt, *kept))
    k, v, kt, out, _, lse, sums = forward_chunk(
        sh, me, back, qq, chunks[hops], hops, state, gain_square
    )
    spans.append((k, v, kt))
    norm = (exchanged([summed_over_head(sums)] * parts, parts), gain_square, features)

    part, dq, grads, dots = backward_chunk(
        sh, me, back, qq, spans[hops], hops, out, lse, None, None, norm, everyone, None
    )
    arrived = [moved_on(part, -hops)]
    for distance in range(hops - 1, 0, -1):
        part, dq = backward_chunk(
            sh, me, back, qq, spans[distance], distance, grads, lse, dots, dq, None,
            everyone, None,
        )
        arrived.append(moved_on(part, -distance))
    turns = [turn[::-1] for turn in (everyone[-1:], everyone[:-1]) if turn]
    held, dq_pieces = None, [None] * parts
    for order in turns:
        held, *done = backward_chunk(
            sh, me, back, qq, spans[0], 0, grads, lse, dots, dq, None, order, held
        )
        for m, piece in zip(order, done):
            dq_pieces[m] = piece.reshape(1, group, rows, width)
    dq_pieces = exchanged(dq_pieces, parts)
    dq_pieces[-1], held = lax.optimization_barrier((dq_pieces[-1], held))
    if arrived[1:]:
        held = add_arrived(held, arrived[:-1])
    dkv_pieces = exchanged(combine(sh, me, arrived[-1], held), parts)
    (product_queries,) = join_heads(dq_pieces, 1, group)
    dkv_pieces = [p.reshape(2, 1, rows, width) for p in dkv_pieces]
    product_keys, product_values = join_heads(dkv_pieces, 2, 1)
    return (
        product_queries.reshape(queries.shape),
        product_keys.reshape(keys.shape),
        product_values.reshape(keys.shape),
    )


def solution(mesh):
    def run(*arguments):
        count, heads = mesh.shape["ctx"], mesh.shape["head"]
        parts = arguments[1].shape[1] // heads
        split = Mesh(
            mesh.devices.reshape(count // parts, parts, heads), ("span", "part", "head")
        )
        ctx = ("span", "part")
        array = P(ctx, "head", None)
        return jax.shard_map(
            body,
            mesh=split,
            in_specs=(array,) * 6 + (P(ctx), P("head")),
            out_specs=(array,) * 3,
            check_vma=False,
        )(*arguments)

    return run
```

```python
import functools

import jax
import jax.numpy as jnp
from jax import lax
from jax.experimental import pallas as pl
from jax.experimental.pallas import tpu as pltpu
from jax.sharding import Mesh, PartitionSpec as P

DOC_DEVS = 8
EPSILON = 1e-06
VMEM_BYTES = 18 * 1024 * 1024
NOTE_ROWS = 16
ONES_ROWS = 16
WIDE_VMEM_BYTES = 60 * 1024 * 1024
MASKED = -1e30
F32 = jnp.float32
BF16 = jnp.bfloat16
SMEM = pl.BlockSpec(memory_space=pltpu.SMEM)
VMEM = pl.BlockSpec(memory_space=pltpu.VMEM)


def params(size=VMEM_BYTES):
    return pltpu.CompilerParams(vmem_limit_bytes=size)


def cost(flops, moved, powers=0):
    return pl.CostEstimate(flops=int(flops), bytes_accessed=int(moved), transcendentals=int(powers))


def nn(a, b):
    return lax.dot_general(a, b, (((1,), (0,)), ((), ())), preferred_element_type=F32)


def nt(a, b):
    return lax.dot_general(a, b, (((1,), (1,)), ((), ())), preferred_element_type=F32)


def split_heads(arrays, parts, per_part, notes=None):
    count = len(arrays)
    total, width = arrays[0].shape
    heads = parts * per_part
    rows = total // heads
    length = count * per_part * rows
    span = per_part * rows
    extra = 0 if notes is None else NOTE_ROWS
    scalars = [] if notes is None else [notes]

    def kernel(*refs):
        ins = list(refs[: len(scalars) + count])
        results = refs[len(scalars) + count : len(scalars) + count + parts]
        held, wide, sems, *staged = refs[len(scalars) + count + parts :]
        outs, out_sems = (staged[:-1], staged[-1]) if extra else (results, None)
        mine = lax.axis_index("part")
        if extra:
            note_ref = ins.pop(0)
        copies = [pltpu.make_async_copy(ins[a], held.at[a], sems.at[a]) for a in range(count)]
        for copy in copies:
            copy.start()
        leaving = []

        def leave(m, a, start, size):
            part = pl.ds(start, size)
            sem = out_sems.at[m * (count + 1) + a]
            leaving.append(pltpu.make_async_copy(outs[m].at[part], results[m].at[part], sem))
            leaving[-1].start()

        if extra:
            first = (lax.axis_index("span") * parts + mine) * notes.shape[0]
            line = lax.broadcasted_iota(jnp.int32, (extra, width), 0)
            lines = jnp.zeros((extra, width), jnp.int32)
            for i in range(notes.shape[0]):
                lines = jnp.where(line == i, first + i - note_ref[i], lines)
            for m, out in enumerate(outs):
                out[length:, :] = lines.astype(F32).astype(BF16)
                leave(m, count, length, extra)
        for a in range(count):
            copies[a].wait()
            wide[...] = held[a].astype(F32)
            for m in range(parts):
                for r in range(per_part):
                    head = jnp.bitwise_xor(mine, m) * per_part + r
                    at = (a * per_part + r) * rows
                    outs[m][at : at + rows, :] = wide[pl.ds(head, rows, stride=heads), :].astype(BF16)
                if extra:
                    leave(m, a, a * span, span)
        for copy in leaving:
            copy.wait()

    piece = (length + extra, width)
    scratch = [
        pltpu.VMEM((count, total, width), BF16),
        pltpu.VMEM((total, width), F32),
        pltpu.SemaphoreType.DMA((count,)),
    ]
    if extra:
        scratch += [pltpu.VMEM(piece, BF16)] * parts
        scratch.append(pltpu.SemaphoreType.DMA((parts * (count + 1),)))
    return pl.pallas_call(
        kernel,
        in_specs=[SMEM] * len(scalars) + [pl.BlockSpec(memory_space=pltpu.HBM)] * count,
        out_specs=[pl.BlockSpec(memory_space=pltpu.HBM) if extra else VMEM] * parts,
        out_shape=[jax.ShapeDtypeStruct(piece, BF16)] * parts,
        scratch_shapes=scratch,
        compiler_params=params(VMEM_BYTES if notes is None else WIDE_VMEM_BYTES),
        cost_estimate=cost(0, 4 * count * total * width),
        name="split_heads",
    )(*scalars, *arrays)


def join_heads(groups):
    parts = len(groups[0][0])
    rows, width = groups[0][0][0].shape[-2:]
    steps = 4
    cut = rows // steps

    def kernel(*refs):
        ins, outs = list(refs[: parts * len(groups)]), list(refs[parts * len(groups) :])
        mine = lax.axis_index("part")
        for _, count, per_part in groups:
            for a in range(count):
                for m in range(parts):
                    for r in range(per_part):
                        head = jnp.bitwise_xor(mine, m) * per_part + r
                        rows_of_head = pl.ds(head, cut, stride=parts * per_part)
                        outs[a][rows_of_head, :] = ins[m][a, r].astype(F32)
            del ins[:parts], outs[:count]

    in_specs, out_specs, out_shape = [], [], []
    for _, count, per_part in groups:
        heads = parts * per_part
        block = (count, per_part, cut, width)
        in_specs += [pl.BlockSpec(block, lambda i: (0, 0, i, 0))] * parts
        out_specs += [pl.BlockSpec((cut * heads, width), lambda i: (i, 0))] * count
        out_shape += [jax.ShapeDtypeStruct((rows * heads, width), F32)] * count
    return pl.pallas_call(
        kernel,
        grid=(steps,),
        in_specs=in_specs,
        out_specs=out_specs,
        out_shape=out_shape,
        compiler_params=params(),
        cost_estimate=cost(0, sum(6 * shape.size for shape in out_shape)),
        name="join_heads",
    )(*[piece for pieces, _, _ in groups for piece in pieces])


def slot_of(me_ref, m, rows):
    return pl.multiple_of(jnp.bitwise_xor(me_ref[0], m) * rows, rows)


class Shape:
    def __init__(self, parts, group, rows, width, block):
        self.parts, self.group, self.rows, self.width, self.block = parts, group, rows, width, block
        self.tokens = parts * rows
        self.blocks = self.tokens // block
        self.lanes = group * block
        self.scale = width**-0.5


def diagonal(sh):
    shape = (sh.block, sh.block)
    key = lax.broadcasted_iota(jnp.int32, shape, 0)
    query = lax.broadcasted_iota(jnp.int32, shape, 1)
    return key <= query


def below_diagonal(sh, value, other):
    allowed = diagonal(sh)
    cut = [value[:, at : at + sh.block] for at in range(0, value.shape[1], sh.block)]
    return jnp.concatenate([jnp.where(allowed, part, other) for part in cut], axis=1)


def halves(sh):
    if sh.group % 2:
        return [slice(0, sh.lanes)]
    return [slice(0, sh.lanes // 2), slice(sh.lanes // 2, sh.lanes)]


def stacked_keys(keys, start, size):
    k_s, tk_s = keys
    k = k_s[pl.ds(start, size), :]
    tk = tk_s[pl.ds(start, size), :]
    left = jnp.concatenate([k, tk], axis=0)
    right = jnp.concatenate([jnp.zeros_like(k), k], axis=0)
    return jnp.concatenate([left, right], axis=1)


def pieces_of(sh, start, blocks):
    sizes = [2] * (blocks // 2) + [1] * (blocks % 2)
    firsts = [sum(sizes[:i]) for i in range(len(sizes))]
    return [
        (pl.multiple_of(start + first * sh.block, sh.block), size * sh.block, i == len(sizes) - 1)
        for i, (first, size) in enumerate(zip(firsts, sizes))
    ]


def cut_diagonal(sh, value, other):
    low = below_diagonal(sh, value[value.shape[0] - sh.block :], other)
    if value.shape[0] == sh.block:
        return low
    return jnp.concatenate([value[: value.shape[0] - sh.block], low], axis=0)


def block_rows(sh, block):
    return pl.multiple_of(block * sh.block, sh.block)


def load_state(stat, lanes):
    return tuple(stat[r : r + 1, lanes] for r in range(3))


def forward_tile(sh, keys, vt_s, acc, stat, kept, qq, block, blocks, masked):
    w = sh.width
    start = block_rows(sh, block)
    pieces = pieces_of(sh, start, blocks)
    stacked = [stacked_keys(keys, at, size) for at, size, _ in pieces]
    at = pl.ds(start, blocks * sh.block)
    lanes = halves(sh)
    scores = [[] for _ in lanes]
    mixed = [[] for _ in lanes]
    most = [None for _ in lanes]
    state = [None if masked else load_state(stat, part) for part in lanes]

    def score(h, c):
        both = nt(stacked[c], qq[lanes[h], :])
        s, d = both[: pieces[c][1]], both[pieces[c][1] :]
        if masked and pieces[c][2]:
            s = cut_diagonal(sh, s, MASKED)
        scores[h].append((s, d))

    def top(h):
        peaks = [jnp.max(s, axis=0, keepdims=True) for s, _ in scores[h]]
        most[h] = functools.reduce(jnp.maximum, peaks) * sh.scale
        if not masked:
            most[h] = jnp.maximum(most[h], state[h][0])
        if kept is not None:
            for j in range(blocks):
                kept[1][block + j, :, lanes[h]] = most[h]

    def soften(h, c):
        s, d = scores[h][c]
        e = jnp.exp(s * sh.scale - most[h])
        mixed[h].append((e.astype(BF16), (e * d).astype(BF16)))
        if kept is not None:
            kept[0][pl.ds(pieces[c][0], pieces[c][1]), lanes[h]] = mixed[h][-1][0]

    def gather(h, i):
        return jnp.concatenate([pair[i] for pair in mixed[h]], axis=0)

    def finish(h, plain, moving):
        total, cross = plain[2 * w : 2 * w + 1], moving[w : w + 1]
        tangent = plain[:w] + moving[:w] * sh.scale
        plain = plain[w : 2 * w]
        if not masked:
            decay = jnp.exp(state[h][0] - most[h])
            plain = acc[:w, lanes[h]] * decay + plain
            tangent = acc[w:, lanes[h]] * decay + tangent
            total, cross = state[h][1] * decay + total, state[h][2] * decay + cross
        acc[:w, lanes[h]] = plain
        acc[w:, lanes[h]] = tangent
        for r, value in enumerate((most[h], total, cross)):
            stat[r : r + 1, lanes[h]] = value

    for h in range(len(lanes) + 1):
        if h > 0:
            top(h - 1)
        for c in range(len(pieces)):
            if h < len(lanes):
                score(h, c)
            if h > 0:
                soften(h - 1, c)
        if h > 0:
            plain = nn(vt_s[:, at], gather(h - 1, 0))
            moving = nn(vt_s[w:, at], gather(h - 1, 1))
            finish(h - 1, plain, moving)


def by_count(sh, low, count, run, masked):
    most = min(4 if masked else 3, sh.blocks)
    head = lax.rem(count - 1, 4) + 1 if masked else lax.rem(count, 4)
    for blocks in range(1, most + 1):

        @pl.when(head == blocks)
        def _(blocks=blocks):
            run(low + count - blocks if masked else low, blocks, masked)

    def step(i, carry):
        run(low + (0 if masked else head) + 4 * i, 4, False)
        return carry

    if sh.blocks >= 4:
        lax.fori_loop(0, (count - head) // 4, step, 0)


def lay_chunk(sh, me_ref, sources, targets):
    for m, (ref, base) in enumerate(sources):
        slot = pl.ds(slot_of(me_ref, m, sh.rows), sh.rows)
        for i, target in enumerate(targets):
            at = base + i * sh.rows
            target[slot, :] = ref[at : at + sh.rows, :]


def lay_queries(sh, me_ref, order, pieces, qq):
    per = sh.rows // sh.block
    for m, ref in zip(order, pieces):
        for i in range(2):
            for g in range(sh.group):
                for r in range(per):
                    block = jnp.bitwise_xor(me_ref[0], m) * per + r
                    at = (i * sh.group + g) * sh.rows + r * sh.block
                    qq[
                        block,
                        g * sh.block : (g + 1) * sh.block,
                        i * sh.width : (i + 1) * sh.width,
                    ] = ref[at : at + sh.block, :]


def lay_span(sh, me_ref, sources, laid):
    w = sh.width
    k_s, v_s, kt_s, tk_s, vt_s, tv_s = laid
    lay_chunk(sh, me_ref, sources, (k_s, v_s, tk_s, tv_s))
    kt_s[...] = transposed(k_s[...])
    vt_s[:w, :] = transposed(tv_s[...])
    vt_s[w : 2 * w, :] = transposed(v_s[...])
    vt_s[2 * w :, :] = jnp.ones((ONES_ROWS, sh.tokens), BF16)


def transposed(x):
    return x.astype(F32).T.astype(BF16)


def located(sh, refs):
    length = refs[0].shape[0]
    return [(ref, at) for ref in refs for at in range(0, ref.shape[0], length)]


def back_of(sh, me_ref, back_ref, qb):
    per = sh.rows // sh.block
    return back_ref[jnp.bitwise_xor(me_ref[0], qb // per) * per + qb % per]


def each_block(count, run):
    def step(i, carry):
        run(i)
        return carry

    lax.fori_loop(0, count, step, 0)


def block_in_turn(sh, me_ref, order, i):
    per = sh.rows // sh.block
    if order == list(range(sh.parts)):
        return i
    partner = order[0]
    for j in range(1, len(order)):
        partner = jnp.where(i // per == j, order[j], partner)
    return jnp.bitwise_xor(me_ref[0], partner) * per + i % per


def kept_shapes(sh):
    return [
        jax.ShapeDtypeStruct((sh.blocks, sh.tokens, sh.lanes), BF16),
        jax.ShapeDtypeStruct((sh.blocks, sh.blocks, 1, sh.lanes), F32),
    ]


def forward_own(sh, me, back, order, queries, chunk, before):
    w = sh.width
    first = before is None
    turns = len(order) * (sh.rows // sh.block)

    def kernel(me_ref, back_ref, *refs):
        refs = list(refs)

        def take(count):
            taken = refs[:count]
            del refs[:count]
            return taken

        q_in = take(len(order))
        if first:
            kv_in = take(len(chunk))
            accs, stats, qq_s, es, ms = take(5)
            laid = refs
            lay_span(sh, me_ref, located(sh, kv_in), laid)
        else:
            laid = take(len(chunk))
            take(5)
            accs, stats, qq_s, es, ms = refs
        k_s, _, _, tk_s, vt_s = laid[:5]
        lay_queries(sh, me_ref, order, q_in, qq_s)

        def query_block(i):
            qb = block_in_turn(sh, me_ref, order, i)
            low = jnp.clip(qb - back_of(sh, me_ref, back_ref, qb), 0, qb)
            run = functools.partial(
                forward_tile,
                sh,
                (k_s, tk_s),
                vt_s,
                accs.at[qb],
                stats.at[qb],
                (es.at[qb], ms.at[qb]),
                qq_s[qb],
            )
            by_count(sh, low, qb + 1 - low, run, True)

        each_block(turns, query_block)

    def array(*shape, dtype=F32):
        return jax.ShapeDtypeStruct(shape, dtype)

    span = array(sh.tokens, w, dtype=BF16)
    out_shape = [
        array(sh.blocks, 2 * w, sh.lanes),
        array(sh.blocks, 8, sh.lanes),
        array(sh.blocks, sh.lanes, 2 * w, dtype=BF16),
        *kept_shapes(sh),
    ]
    operands = [*queries, *chunk]
    aliases = {}
    if first:
        out_shape += [span, span, array(w, sh.tokens, dtype=BF16), span]
        out_shape.append(array(2 * w + ONES_ROWS, sh.tokens, dtype=BF16))
    else:
        aliases = {2 + len(operands) + i: i for i in range(5)}
        operands += before
    work = sh.group * sh.tokens * sh.block * turns // 2
    return pl.pallas_call(
        kernel,
        in_specs=[SMEM, SMEM] + [VMEM] * len(operands),
        out_specs=[VMEM] * len(out_shape),
        out_shape=out_shape,
        input_output_aliases=aliases,
        scratch_shapes=[pltpu.VMEM((sh.tokens, w), BF16)] * first,
        compiler_params=params(),
        cost_estimate=cost(12 * work * w, 4 * sh.tokens * sh.lanes, work),
        name="forward_own",
    )(me, back, *operands)


def forward_chunk(sh, me, back, qq, chunk, distance, state, gain_square=None):
    w = sh.width
    closing = gain_square is not None

    def kernel(me_ref, back_ref, qq_s, *refs):
        refs = list(refs)

        def take(count):
            taken = refs[:count]
            del refs[:count]
            return taken

        kv_in = take(len(chunk))
        take(2)
        if closing:
            (gain_ref,) = take(1)
        k_s, v_s, kt_s, accs, stats = take(5)
        last = take(2)
        if closing:
            lse, sums = last
        tk_s, tv_s, vt_s = refs
        lay_span(sh, me_ref, located(sh, kv_in), (k_s, v_s, kt_s, tk_s, vt_s, tv_s))

        def query_block(qb):
            acc, stat = accs.at[qb], stats.at[qb]
            first = qb - back_of(sh, me_ref, back_ref, qb) + distance * sh.blocks
            first = jnp.clip(first, 0, sh.blocks)
            count = sh.blocks - first

            @pl.when(count > 0)
            def _():
                kept = None if closing else [ref.at[qb] for ref in last]
                run = functools.partial(
                    forward_tile, sh, (k_s, tk_s), vt_s, acc, stat, kept, qq_s[qb]
                )
                by_count(sh, first, count, run, False)

            if closing:
                most, total, cross = load_state(stat, slice(None))
                inverse = 1.0 / total
                plain = acc[:w, :] * inverse
                moved = acc[w:, :] * inverse - (cross * inverse * sh.scale) * plain
                acc[:w, :] = plain
                acc[w:, :] = moved
                lse[qb] = most + jnp.log(total)
                square = plain * plain
                product = plain * moved
                gain = gain_ref[...]
                for r, value in enumerate((square, product, gain * square, gain * product)):
                    line = jnp.sum(value, axis=0, keepdims=True)
                    pieces = [line[:, g * sh.block : (g + 1) * sh.block] for g in range(sh.group)]
                    sums[qb, r : r + 1, :] = functools.reduce(jnp.add, pieces)

        each_block(sh.blocks, query_block)

    def array(*shape, dtype=F32):
        return jax.ShapeDtypeStruct(shape, dtype)

    out_shape = [
        array(sh.tokens, w, dtype=BF16),
        array(sh.tokens, w, dtype=BF16),
        array(w, sh.tokens, dtype=BF16),
        array(sh.blocks, 2 * w, sh.lanes),
        array(sh.blocks, 8, sh.lanes),
    ]
    if closing:
        out_shape += [array(sh.blocks, 1, sh.lanes), array(sh.blocks, 4, sh.block)]
    else:
        out_shape += kept_shapes(sh)
    operands = [qq, *chunk]
    aliases = {2 + len(operands): 3, 3 + len(operands): 4}
    operands += state
    if closing:
        operands.append(gain_square)
    work = sh.group * sh.tokens * sh.tokens // 2
    return pl.pallas_call(
        kernel,
        in_specs=[SMEM, SMEM] + [VMEM] * len(operands),
        out_specs=[VMEM] * len(out_shape),
        out_shape=out_shape,
        input_output_aliases=aliases,
        scratch_shapes=[
            pltpu.VMEM((sh.tokens, w), BF16),
            pltpu.VMEM((sh.tokens, w), BF16),
            pltpu.VMEM((2 * w + ONES_ROWS, sh.tokens), BF16),
        ],
        compiler_params=params(),
        cost_estimate=cost(24 * work * w, 12 * sh.tokens * sh.lanes * 2, work),
        name="forward_far" if closing else "forward_chunk",
    )(me, back, *operands)


def backward_tile(sh, keys, kt_s, dkv_s, dq_s, qg, lse, dot, block, blocks, _):
    start, size = block_rows(sh, block), blocks * sh.block
    rows = pl.ds(start, size)
    k_s, v_s = keys
    k, v = k_s[rows, :], v_s[rows, :]
    empty = jnp.zeros_like(k)
    left = jnp.concatenate([k, empty], axis=0)
    right = jnp.concatenate([empty, v], axis=0)
    stacked = jnp.concatenate([left, right], axis=1)
    scores = [nt(stacked, qg[lanes, :]) for lanes in halves(sh)]
    for lanes, both in zip(halves(sh), scores):
        p = jnp.exp(both[:size] * sh.scale - lse[:, lanes])
        ds = (p * (both[size:] - dot[:, lanes])).astype(BF16)
        dkv_s[0, rows, :] += nn(ds, qg[lanes, : sh.width])
        dkv_s[1, rows, :] += nn(p.astype(BF16), qg[lanes, sh.width :])
        dq_s[:, lanes] += nn(kt_s[:, rows], ds)


def backward_kept(sh, keys, kt_s, dkv_s, dq_s, qg, lse, dot, kept, block, blocks, _):
    start, size = block_rows(sh, block), blocks * sh.block
    rows = pl.ds(start, size)
    v = keys[1][rows, :]
    slopes = [nt(v, qg[lanes, sh.width :]) for lanes in halves(sh)]
    for lanes, slope in zip(halves(sh), slopes):
        parts = []
        for j in range(blocks):
            factor = jnp.exp(kept[1][block + j, :, lanes] - lse[:, lanes])
            at = pl.ds(block_rows(sh, block + j), sh.block)
            parts.append(kept[0][at, lanes].astype(F32) * factor)
        p = jnp.concatenate(parts, axis=0)
        ds = (p * (slope - dot[:, lanes])).astype(BF16)
        dkv_s[0, rows, :] += nn(ds, qg[lanes, : sh.width])
        dkv_s[1, rows, :] += nn(p.astype(BF16), qg[lanes, sh.width :])
        dq_s[:, lanes] += nn(kt_s[:, rows], ds)


def backward_chunk(sh, me, back, qq, keys, distance, grads, lse, dots, dq, norm, order, held):
    w = sh.width
    opening, closing = norm is not None, distance == 0
    per = sh.rows // sh.block

    def kernel(me_ref, back_ref, *refs):
        refs = list(refs)

        def take(count):
            taken = refs[:count]
            del refs[:count]
            return taken

        qq_s, k_s, v_s, kt_s = take(4)
        kept = take(len(keys) - 3)
        (lse_s,) = take(1)
        if opening:
            out_s, gain_ref, *sum_refs = take(2 + len(norm[0]))
        else:
            grad_s, dot_s, dq_in = take(3)
        (held_ref,) = take(1) if held is not None else (None,)
        (dkv_out,) = take(1)
        dq_out = take(len(order) if closing else 1)
        if opening:
            grad_s, dot_s = take(2)
        dkv_s, dq_own = (dkv_out, *refs) if closing else refs
        if held_ref is None:
            dkv_s[...] = jnp.zeros_like(dkv_s)

        def query_block(i):
            qb = block_in_turn(sh, me_ref, order, i)
            dq_s = dq_own if closing else dq_out[0].at[qb]
            if opening:
                features = norm[2]
                token = functools.reduce(jnp.add, [ref[qb] for ref in sum_refs])
                sums = jnp.concatenate([token] * sh.group, axis=1)
                square = sums[0:1] / features + EPSILON
                inverse = lax.rsqrt(square)
                ratio = sums[1:2] / (features * square)
                again = (sums[3:4] - ratio * sums[2:3]) * inverse
                again = again / (features * square)
                plain = out_s[qb, :w, :]
                moved = out_s[qb, w:, :]
                first_grad = gain_ref[...] * (moved - plain * ratio) * inverse
                cot = ((first_grad - plain * again) * inverse).astype(BF16).astype(F32)
                dot_s[qb] = jnp.sum(cot * plain, axis=0, keepdims=True)
                grad_s[qb] = cot.T.astype(BF16)
                dq_s[...] = jnp.zeros((w, sh.lanes), F32)
            elif closing:
                dq_s[...] = dq_in[qb]

            top = sh.blocks if distance else qb + 1
            first = jnp.clip(qb - back_of(sh, me_ref, back_ref, qb) + distance * sh.blocks, 0, top)
            count = top - first

            @pl.when(count > 0)
            def _():
                qg = jnp.concatenate([qq_s[qb, :, :w], grad_s[qb]], axis=1)
                common = (sh, (k_s, v_s), kt_s, dkv_s, dq_s, qg, lse_s[qb], dot_s[qb])
                if kept:
                    run = functools.partial(backward_kept, *common, [ref.at[qb] for ref in kept])
                else:
                    run = functools.partial(backward_tile, *common)
                by_count(sh, first, count, run, False)

            if closing:
                done = (dq_s[...] * sh.scale).T.reshape(sh.group, sh.block, w).astype(BF16)
                at = pl.ds(pl.multiple_of(i % per * sh.block, sh.block), sh.block)
                for j, out in enumerate(dq_out):

                    @pl.when(i // per == j)
                    def _(out=out):
                        out[:, at, :] = done

        each_block(len(order) * per, query_block)
        if not closing:
            dkv_out[...] = dkv_s[...].astype(BF16)

    def array(*shape, dtype=F32):
        return jax.ShapeDtypeStruct(shape, dtype)

    operands = [qq, *keys, lse]
    if opening:
        operands += [grads, norm[1], *norm[0]]
    else:
        operands += [grads, dots, dq]
    aliases = {}
    if not opening and not closing:
        aliases = {1 + len(operands): 1}
    if held is not None:
        aliases = {2 + len(operands): 0}
        operands.append(held)
    out_shape = [array(2, sh.tokens, w, dtype=F32 if closing else BF16)]
    if closing:
        out_shape += [array(sh.group, sh.rows, w, dtype=BF16)] * len(order)
    else:
        out_shape.append(array(sh.blocks, w, sh.lanes))
    if opening:
        out_shape += [
            array(sh.blocks, sh.lanes, w, dtype=BF16),
            array(sh.blocks, 1, sh.lanes),
        ]
    work = sh.group * sh.tokens * len(order) * sh.rows // 2
    return pl.pallas_call(
        kernel,
        in_specs=[SMEM, SMEM] + [VMEM] * len(operands),
        out_specs=[VMEM] * len(out_shape),
        out_shape=out_shape,
        input_output_aliases=aliases,
        scratch_shapes=[pltpu.VMEM((2, sh.tokens, w), F32)] * (not closing)
        + [pltpu.VMEM((w, sh.lanes), F32)],
        compiler_params=params(),
        cost_estimate=cost(1, 1) if closing else cost(20 * work * w, 16 * work, work),
        name="backward_chunk",
    )(me, back, *operands)


def add_arrived(held, arrived):
    def kernel(held_ref, *refs):
        total = held_ref[...]
        for ref in refs[:-1]:
            total += ref[...].astype(F32)
        refs[-1][...] = total

    return pl.pallas_call(
        kernel,
        in_specs=[VMEM] * (1 + len(arrived)),
        out_specs=VMEM,
        out_shape=jax.ShapeDtypeStruct(held.shape, F32),
        input_output_aliases={0: 0},
        compiler_params=params(),
        cost_estimate=cost(0, 10 * held.size),
        name="add_arrived",
    )(held, *arrived)


def combine(sh, me, arrived, held):
    def kernel(me_ref, held_ref, arrived_ref, *outs):
        for m, out in enumerate(outs):
            slot = pl.ds(slot_of(me_ref, m, sh.rows), sh.rows)
            for a, factor in ((0, sh.scale), (1, 1.0)):
                total = held_ref[a, slot, :] + arrived_ref[a, slot, :].astype(F32)
                out[a] = (total * factor).astype(BF16)

    return pl.pallas_call(
        kernel,
        in_specs=[SMEM, VMEM, VMEM],
        out_specs=[VMEM] * sh.parts,
        out_shape=[jax.ShapeDtypeStruct((2, sh.rows, sh.width), BF16)] * sh.parts,
        compiler_params=params(),
        cost_estimate=cost(0, 1),
        name="combine",
    )(me, held, arrived)


def exchanged_with(piece, parts, m):
    return lax.ppermute(piece, "part", [(i, i ^ m) for i in range(parts)]) if m else piece


def exchanged(pieces, parts):
    return [exchanged_with(piece, parts, m) for m, piece in enumerate(pieces)]


def moved_on(value, steps):
    count = lax.axis_size("span")
    pairs = [(i, i + steps) for i in range(count) if 0 <= i + steps < count]
    return lax.ppermute(value, "span", pairs)


def summed_over_head(value):
    count = lax.axis_size("head")
    if count & (count - 1):
        return lax.psum(value, "head")
    step = 1
    while step < count:
        value = value + lax.ppermute(value, "head", [(i, i ^ step) for i in range(count)])
        step *= 2
    return value


def body(queries, keys, values, tangent_queries, tangent_keys, tangent_values, doc_start, out_gain):
    rows, query_heads, width = queries.shape
    key_heads = keys.shape[1]
    group = query_heads // key_heads
    parts = lax.axis_size("part")
    per = doc_start.shape[0]
    block = rows // per
    features = query_heads * width * lax.axis_size("head")
    hops = -(-DOC_DEVS // parts)
    sh = Shape(parts, group, rows, width, block)
    place = lax.axis_index("part")
    me = place.astype(jnp.int32).reshape(1)

    def flat(array):
        return array.reshape(-1, width)

    pieces = split_heads(
        [flat(a) for a in (keys, values, tangent_keys, tangent_values)], parts, 1, doc_start
    )
    q_rows, _ = lax.optimization_barrier(((flat(queries), flat(tangent_queries)), pieces[0]))
    q_pieces = split_heads(q_rows, parts, group)
    own = moved_on(pieces[0], 1)
    pieces = exchanged(pieces, parts)
    chunks = [pieces]
    if parts > 1:
        own, q_pieces = lax.optimization_barrier((own, q_pieces))
        owns = [own]
        for _ in range(hops - 1):
            owns.append(moved_on(owns[-1], 1))
        late, owns = lax.optimization_barrier((pieces[1:], owns))
        rest = jnp.concatenate([moved_on(piece, 1) for piece in late], axis=0)
        chunks.append([owns[0], rest])
        for own in owns[1:]:
            rest = moved_on(rest, 1)
            chunks.append([own, rest])
    else:
        for _ in range(hops):
            chunks.append([own])
            own = moved_on(own, 1)
    q_parts = exchanged(q_pieces[:-1], parts)
    if parts > 1:
        last, _ = lax.optimization_barrier((q_pieces[-1], q_parts[min(1, parts - 2)]))
        q_parts.append(exchanged_with(last, parts, parts - 1))
    else:
        q_parts = q_pieces
    back = jnp.concatenate([p[4 * rows : 4 * rows + per, 0] for p in pieces]).astype(jnp.int32)
    gain = lax.dynamic_index_in_dim(out_gain.reshape(key_heads, group, width), place, 0, False)
    gain_square = jnp.repeat((gain * gain).T, block, axis=1)

    everyone = list(range(parts))
    before, laid = None, chunks[0]
    for order in [everyone[:1], everyone[1:-1], everyone[-1:]] if parts > 1 else [everyone]:
        if order:
            turn = forward_own(sh, me, back, order, [q_parts[m] for m in order], laid, before)
            laid = turn[5:] or laid
            before = list(turn[:5])
    state, qq = before[:2], before[2]
    spans = [(*laid[:3], *before[3:])]
    for distance in range(1, hops):
        k, v, kt, acc, stat, *kept = forward_chunk(
            sh, me, back, qq, chunks[distance], distance, state
        )
        state = [acc, stat]
        spans.append((k, v, kt, *kept))
    k, v, kt, out, _, lse, sums = forward_chunk(
        sh, me, back, qq, chunks[hops], hops, state, gain_square
    )
    spans.append((k, v, kt))
    norm = (exchanged([summed_over_head(sums)] * parts, parts), gain_square, features)

    part, dq, grads, dots = backward_chunk(
        sh, me, back, qq, spans[hops], hops, out, lse, None, None, norm, everyone, None
    )
    arrived = [moved_on(part, -hops)]
    for distance in range(hops - 1, 0, -1):
        part, dq = backward_chunk(
            sh, me, back, qq, spans[distance], distance, grads, lse, dots, dq, None,
            everyone, None,
        )
        arrived.append(moved_on(part, -distance))
    turns = [everyone[-1:], everyone[1:-1], everyone[:1]] if parts > 1 else [everyone]
    held, dq_pieces = None, [None] * parts
    for order in filter(None, turns):
        held, *done = backward_chunk(
            sh, me, back, qq, spans[0], 0, grads, lse, dots, dq, None, order, held
        )
        for m, piece in zip(order, done):
            dq_pieces[m] = piece.reshape(1, group, rows, width)
    dq_pieces = exchanged(dq_pieces, parts)
    dq_pieces[-1], held = lax.optimization_barrier((dq_pieces[-1], held))
    if arrived[1:]:
        held = add_arrived(held, arrived[:-1])
    dkv_pieces = exchanged(combine(sh, me, arrived[-1], held), parts)
    dkv_pieces = [p.reshape(2, 1, rows, width) for p in dkv_pieces]
    product_queries, product_keys, product_values = join_heads(
        [(dq_pieces, 1, group), (dkv_pieces, 2, 1)]
    )
    return (
        product_queries.reshape(queries.shape),
        product_keys.reshape(keys.shape),
        product_values.reshape(keys.shape),
    )


def solution(mesh):
    def run(*arguments):
        count, heads = mesh.shape["ctx"], mesh.shape["head"]
        parts = arguments[1].shape[1] // heads
        split = Mesh(
            mesh.devices.reshape(count // parts, parts, heads), ("span", "part", "head")
        )
        ctx = ("span", "part")
        array = P(ctx, "head", None)
        return jax.shard_map(
            body,
            mesh=split,
            in_specs=(array,) * 6 + (P(ctx), P("head")),
            out_specs=(array,) * 3,
            check_vma=False,
        )(*arguments)

    return run
```

```python
import functools

import jax
import jax.numpy as jnp
from jax import lax
from jax.experimental import pallas as pl
from jax.experimental.pallas import tpu as pltpu
from jax.sharding import Mesh, PartitionSpec as P

DOC_DEVS = 8
EPSILON = 1e-06
VMEM_BYTES = 18 * 1024 * 1024
NOTE_ROWS = 16
ONES_ROWS = 16
WIDE_VMEM_BYTES = 60 * 1024 * 1024
MASKED = -1e30
F32 = jnp.float32
BF16 = jnp.bfloat16
SMEM = pl.BlockSpec(memory_space=pltpu.SMEM)
VMEM = pl.BlockSpec(memory_space=pltpu.VMEM)


def params(size=VMEM_BYTES):
    return pltpu.CompilerParams(vmem_limit_bytes=size)


def cost(flops, moved, powers=0):
    return pl.CostEstimate(flops=int(flops), bytes_accessed=int(moved), transcendentals=int(powers))


def nn(a, b):
    return lax.dot_general(a, b, (((1,), (0,)), ((), ())), preferred_element_type=F32)


def nt(a, b):
    return lax.dot_general(a, b, (((1,), (1,)), ((), ())), preferred_element_type=F32)


def split_heads(arrays, parts, per_part, notes=None):
    count = len(arrays)
    total, width = arrays[0].shape
    heads = parts * per_part
    rows = total // heads
    length = count * per_part * rows
    span = per_part * rows
    extra = 0 if notes is None else NOTE_ROWS
    scalars = [] if notes is None else [notes]

    def kernel(*refs):
        ins = list(refs[: len(scalars) + count])
        results = refs[len(scalars) + count : len(scalars) + count + parts]
        held, wide, sems, *staged = refs[len(scalars) + count + parts :]
        outs, out_sems = (staged[:-1], staged[-1]) if extra else (results, None)
        mine = lax.axis_index("part")
        if extra:
            note_ref = ins.pop(0)
        copies = [pltpu.make_async_copy(ins[a], held.at[a], sems.at[a]) for a in range(count)]
        for copy in copies:
            copy.start()
        leaving = []

        def leave(m, a, start, size):
            part = pl.ds(start, size)
            sem = out_sems.at[m * (count + 1) + a]
            leaving.append(pltpu.make_async_copy(outs[m].at[part], results[m].at[part], sem))
            leaving[-1].start()

        if extra:
            first = (lax.axis_index("span") * parts + mine) * notes.shape[0]
            line = lax.broadcasted_iota(jnp.int32, (extra, width), 0)
            lines = jnp.zeros((extra, width), jnp.int32)
            for i in range(notes.shape[0]):
                lines = jnp.where(line == i, first + i - note_ref[i], lines)
            for m, out in enumerate(outs):
                out[length:, :] = lines.astype(F32).astype(BF16)
                leave(m, count, length, extra)
        for a in range(count):
            copies[a].wait()
            wide[...] = held[a].astype(F32)
            for m in range(parts):
                for r in range(per_part):
                    head = jnp.bitwise_xor(mine, m) * per_part + r
                    at = (a * per_part + r) * rows
                    outs[m][at : at + rows, :] = wide[pl.ds(head, rows, stride=heads), :].astype(BF16)
                if extra:
                    leave(m, a, a * span, span)
        for copy in leaving:
            copy.wait()

    piece = (length + extra, width)
    scratch = [
        pltpu.VMEM((count, total, width), BF16),
        pltpu.VMEM((total, width), F32),
        pltpu.SemaphoreType.DMA((count,)),
    ]
    if extra:
        scratch += [pltpu.VMEM(piece, BF16)] * parts
        scratch.append(pltpu.SemaphoreType.DMA((parts * (count + 1),)))
    return pl.pallas_call(
        kernel,
        in_specs=[SMEM] * len(scalars) + [pl.BlockSpec(memory_space=pltpu.HBM)] * count,
        out_specs=[pl.BlockSpec(memory_space=pltpu.HBM) if extra else VMEM] * parts,
        out_shape=[jax.ShapeDtypeStruct(piece, BF16)] * parts,
        scratch_shapes=scratch,
        compiler_params=params(VMEM_BYTES if notes is None else WIDE_VMEM_BYTES),
        cost_estimate=cost(0, 4 * count * total * width),
        name="split_heads",
    )(*scalars, *arrays)


def join_heads(groups):
    parts = len(groups[0][0])
    rows, width = groups[0][0][0].shape[-2:]
    steps = 4
    cut = rows // steps

    def kernel(*refs):
        ins, outs = list(refs[: parts * len(groups)]), list(refs[parts * len(groups) :])
        mine = lax.axis_index("part")
        for _, count, per_part in groups:
            for a in range(count):
                for m in range(parts):
                    for r in range(per_part):
                        head = jnp.bitwise_xor(mine, m) * per_part + r
                        rows_of_head = pl.ds(head, cut, stride=parts * per_part)
                        outs[a][rows_of_head, :] = ins[m][a, r].astype(F32)
            del ins[:parts], outs[:count]

    in_specs, out_specs, out_shape = [], [], []
    for _, count, per_part in groups:
        heads = parts * per_part
        block = (count, per_part, cut, width)
        in_specs += [pl.BlockSpec(block, lambda i: (0, 0, i, 0))] * parts
        out_specs += [pl.BlockSpec((cut * heads, width), lambda i: (i, 0))] * count
        out_shape += [jax.ShapeDtypeStruct((rows * heads, width), F32)] * count
    return pl.pallas_call(
        kernel,
        grid=(steps,),
        in_specs=in_specs,
        out_specs=out_specs,
        out_shape=out_shape,
        compiler_params=params(),
        cost_estimate=cost(0, sum(6 * shape.size for shape in out_shape)),
        name="join_heads",
    )(*[piece for pieces, _, _ in groups for piece in pieces])


def slot_of(me_ref, m, rows):
    return pl.multiple_of(jnp.bitwise_xor(me_ref[0], m) * rows, rows)


class Shape:
    def __init__(self, parts, group, rows, width, block):
        self.parts, self.group, self.rows, self.width, self.block = parts, group, rows, width, block
        self.tokens = parts * rows
        self.blocks = self.tokens // block
        self.lanes = group * block
        self.scale = width**-0.5


def diagonal(sh):
    shape = (sh.block, sh.block)
    key = lax.broadcasted_iota(jnp.int32, shape, 0)
    query = lax.broadcasted_iota(jnp.int32, shape, 1)
    return key <= query


def below_diagonal(sh, value, other):
    allowed = diagonal(sh)
    cut = [value[:, at : at + sh.block] for at in range(0, value.shape[1], sh.block)]
    return jnp.concatenate([jnp.where(allowed, part, other) for part in cut], axis=1)


def halves(sh):
    if sh.group % 2:
        return [slice(0, sh.lanes)]
    return [slice(0, sh.lanes // 2), slice(sh.lanes // 2, sh.lanes)]


def stacked_keys(keys, start, size):
    k_s, tk_s = keys
    k = k_s[pl.ds(start, size), :]
    tk = tk_s[pl.ds(start, size), :]
    left = jnp.concatenate([k, tk], axis=0)
    right = jnp.concatenate([jnp.zeros_like(k), k], axis=0)
    return jnp.concatenate([left, right], axis=1)


def pieces_of(sh, start, blocks):
    sizes = [2] * (blocks // 2) + [1] * (blocks % 2)
    firsts = [sum(sizes[:i]) for i in range(len(sizes))]
    return [
        (pl.multiple_of(start + first * sh.block, sh.block), size * sh.block, i == len(sizes) - 1)
        for i, (first, size) in enumerate(zip(firsts, sizes))
    ]


def cut_diagonal(sh, value, other):
    low = below_diagonal(sh, value[value.shape[0] - sh.block :], other)
    if value.shape[0] == sh.block:
        return low
    return jnp.concatenate([value[: value.shape[0] - sh.block], low], axis=0)


def block_rows(sh, block):
    return pl.multiple_of(block * sh.block, sh.block)


def load_state(stat, lanes):
    return tuple(stat[r : r + 1, lanes] for r in range(3))


def forward_tile(sh, keys, vt_s, acc, stat, kept, qq, block, blocks, masked):
    w = sh.width
    start = block_rows(sh, block)
    pieces = pieces_of(sh, start, blocks)
    stacked = [stacked_keys(keys, at, size) for at, size, _ in pieces]
    at = pl.ds(start, blocks * sh.block)
    lanes = halves(sh)
    scores = [[] for _ in lanes]
    mixed = [[] for _ in lanes]
    most = [None for _ in lanes]
    state = [None if masked else load_state(stat, part) for part in lanes]

    def score(h, c):
        both = nt(stacked[c], qq[lanes[h], :])
        s, d = both[: pieces[c][1]], both[pieces[c][1] :]
        if masked and pieces[c][2]:
            s = cut_diagonal(sh, s, MASKED)
        scores[h].append((s, d))

    def top(h):
        peaks = [jnp.max(s, axis=0, keepdims=True) for s, _ in scores[h]]
        most[h] = functools.reduce(jnp.maximum, peaks) * sh.scale
        if not masked:
            most[h] = jnp.maximum(most[h], state[h][0])
        if kept is not None:
            for j in range(blocks):
                kept[1][block + j, :, lanes[h]] = most[h]

    def soften(h, c):
        s, d = scores[h][c]
        e = jnp.exp(s * sh.scale - most[h])
        mixed[h].append((e.astype(BF16), (e * d).astype(BF16)))
        if kept is not None:
            kept[0][pl.ds(pieces[c][0], pieces[c][1]), lanes[h]] = mixed[h][-1][0]

    def gather(h, i):
        return jnp.concatenate([pair[i] for pair in mixed[h]], axis=0)

    def finish(h, plain, moving):
        total, cross = plain[2 * w : 2 * w + 1], moving[w : w + 1]
        tangent = plain[:w] + moving[:w] * sh.scale
        plain = plain[w : 2 * w]
        if not masked:
            decay = jnp.exp(state[h][0] - most[h])
            plain = acc[:w, lanes[h]] * decay + plain
            tangent = acc[w:, lanes[h]] * decay + tangent
            total, cross = state[h][1] * decay + total, state[h][2] * decay + cross
        acc[:w, lanes[h]] = plain
        acc[w:, lanes[h]] = tangent
        for r, value in enumerate((most[h], total, cross)):
            stat[r : r + 1, lanes[h]] = value

    for h in range(len(lanes) + 1):
        if h > 0:
            top(h - 1)
        for c in range(len(pieces)):
            if h < len(lanes):
                score(h, c)
            if h > 0:
                soften(h - 1, c)
        if h > 0:
            plain = nn(vt_s[:, at], gather(h - 1, 0))
            moving = nn(vt_s[w:, at], gather(h - 1, 1))
            finish(h - 1, plain, moving)


def by_count(sh, low, count, run, masked):
    most = min(4 if masked else 3, sh.blocks)
    head = lax.rem(count - 1, 4) + 1 if masked else lax.rem(count, 4)
    for blocks in range(1, most + 1):

        @pl.when(head == blocks)
        def _(blocks=blocks):
            run(low + count - blocks if masked else low, blocks, masked)

    def step(i, carry):
        run(low + (0 if masked else head) + 4 * i, 4, False)
        return carry

    if sh.blocks >= 4:
        lax.fori_loop(0, (count - head) // 4, step, 0)


def lay_chunk(sh, me_ref, sources, targets):
    for m, (ref, base) in enumerate(sources):
        slot = pl.ds(slot_of(me_ref, m, sh.rows), sh.rows)
        for i, target in enumerate(targets):
            at = base + i * sh.rows
            target[slot, :] = ref[at : at + sh.rows, :]


def lay_queries(sh, me_ref, order, pieces, qq):
    per = sh.rows // sh.block
    for m, ref in zip(order, pieces):
        for i in range(2):
            for g in range(sh.group):
                for r in range(per):
                    block = jnp.bitwise_xor(me_ref[0], m) * per + r
                    at = (i * sh.group + g) * sh.rows + r * sh.block
                    qq[
                        block,
                        g * sh.block : (g + 1) * sh.block,
                        i * sh.width : (i + 1) * sh.width,
                    ] = ref[at : at + sh.block, :]


def lay_span(sh, me_ref, sources, laid):
    w = sh.width
    k_s, v_s, kt_s, tk_s, vt_s, tv_s = laid
    lay_chunk(sh, me_ref, sources, (k_s, v_s, tk_s, tv_s))
    kt_s[...] = transposed(k_s[...])
    vt_s[:w, :] = transposed(tv_s[...])
    vt_s[w : 2 * w, :] = transposed(v_s[...])
    vt_s[2 * w :, :] = jnp.ones((ONES_ROWS, sh.tokens), BF16)


def transposed(x):
    return x.astype(F32).T.astype(BF16)


def located(sh, refs):
    length = refs[0].shape[0]
    return [(ref, at) for ref in refs for at in range(0, ref.shape[0], length)]


def back_of(sh, me_ref, back_ref, qb):
    per = sh.rows // sh.block
    return back_ref[jnp.bitwise_xor(me_ref[0], qb // per) * per + qb % per]


def each_block(count, run):
    def step(i, carry):
        run(i)
        return carry

    lax.fori_loop(0, count, step, 0)


def block_in_turn(sh, me_ref, order, i):
    per = sh.rows // sh.block
    if order == list(range(sh.parts)):
        return i
    partner = order[0]
    for j in range(1, len(order)):
        partner = jnp.where(i // per == j, order[j], partner)
    return jnp.bitwise_xor(me_ref[0], partner) * per + i % per


def kept_shapes(sh):
    return [
        jax.ShapeDtypeStruct((sh.blocks, sh.tokens, sh.lanes), BF16),
        jax.ShapeDtypeStruct((sh.blocks, sh.blocks, 1, sh.lanes), F32),
    ]


def forward_own(sh, me, back, order, queries, chunk, before):
    w = sh.width
    first = before is None
    turns = len(order) * (sh.rows // sh.block)

    def kernel(me_ref, back_ref, *refs):
        refs = list(refs)

        def take(count):
            taken = refs[:count]
            del refs[:count]
            return taken

        q_in = take(len(order))
        if first:
            kv_in = take(len(chunk))
            accs, stats, qq_s, es, ms = take(5)
            laid = refs
            lay_span(sh, me_ref, located(sh, kv_in), laid)
        else:
            laid = take(len(chunk))
            take(5)
            accs, stats, qq_s, es, ms = refs
        k_s, _, _, tk_s, vt_s = laid[:5]
        lay_queries(sh, me_ref, order, q_in, qq_s)

        def query_block(i):
            qb = block_in_turn(sh, me_ref, order, i)
            low = jnp.clip(qb - back_of(sh, me_ref, back_ref, qb), 0, qb)
            run = functools.partial(
                forward_tile,
                sh,
                (k_s, tk_s),
                vt_s,
                accs.at[qb],
                stats.at[qb],
                (es.at[qb], ms.at[qb]),
                qq_s[qb],
            )
            by_count(sh, low, qb + 1 - low, run, True)

        each_block(turns, query_block)

    def array(*shape, dtype=F32):
        return jax.ShapeDtypeStruct(shape, dtype)

    span = array(sh.tokens, w, dtype=BF16)
    out_shape = [
        array(sh.blocks, 2 * w, sh.lanes),
        array(sh.blocks, 8, sh.lanes),
        array(sh.blocks, sh.lanes, 2 * w, dtype=BF16),
        *kept_shapes(sh),
    ]
    operands = [*queries, *chunk]
    aliases = {}
    if first:
        out_shape += [span, span, array(w, sh.tokens, dtype=BF16), span]
        out_shape.append(array(2 * w + ONES_ROWS, sh.tokens, dtype=BF16))
    else:
        aliases = {2 + len(operands) + i: i for i in range(5)}
        operands += before
    work = sh.group * sh.tokens * sh.block * turns // 2
    return pl.pallas_call(
        kernel,
        in_specs=[SMEM, SMEM] + [VMEM] * len(operands),
        out_specs=[VMEM] * len(out_shape),
        out_shape=out_shape,
        input_output_aliases=aliases,
        scratch_shapes=[pltpu.VMEM((sh.tokens, w), BF16)] * first,
        compiler_params=params(),
        cost_estimate=cost(12 * work * w, 4 * sh.tokens * sh.lanes, work),
        name="forward_own",
    )(me, back, *operands)


def forward_chunk(sh, me, back, qq, chunk, distance, state, gain_square=None):
    w = sh.width
    closing = gain_square is not None

    def kernel(me_ref, back_ref, qq_s, *refs):
        refs = list(refs)

        def take(count):
            taken = refs[:count]
            del refs[:count]
            return taken

        kv_in = take(len(chunk))
        take(2)
        if closing:
            (gain_ref,) = take(1)
        k_s, v_s, kt_s, accs, stats = take(5)
        last = take(2)
        if closing:
            lse, sums = last
        tk_s, tv_s, vt_s = refs
        lay_span(sh, me_ref, located(sh, kv_in), (k_s, v_s, kt_s, tk_s, vt_s, tv_s))

        def query_block(qb):
            acc, stat = accs.at[qb], stats.at[qb]
            first = qb - back_of(sh, me_ref, back_ref, qb) + distance * sh.blocks
            first = jnp.clip(first, 0, sh.blocks)
            count = sh.blocks - first

            @pl.when(count > 0)
            def _():
                kept = None if closing else [ref.at[qb] for ref in last]
                run = functools.partial(
                    forward_tile, sh, (k_s, tk_s), vt_s, acc, stat, kept, qq_s[qb]
                )
                by_count(sh, first, count, run, False)

            if closing:
                most, total, cross = load_state(stat, slice(None))
                inverse = 1.0 / total
                plain = acc[:w, :] * inverse
                moved = acc[w:, :] * inverse - (cross * inverse * sh.scale) * plain
                acc[:w, :] = plain
                acc[w:, :] = moved
                lse[qb] = most + jnp.log(total)
                square = plain * plain
                product = plain * moved
                gain = gain_ref[...]
                for r, value in enumerate((square, product, gain * square, gain * product)):
                    line = jnp.sum(value, axis=0, keepdims=True)
                    pieces = [line[:, g * sh.block : (g + 1) * sh.block] for g in range(sh.group)]
                    sums[qb, r : r + 1, :] = functools.reduce(jnp.add, pieces)

        each_block(sh.blocks, query_block)

    def array(*shape, dtype=F32):
        return jax.ShapeDtypeStruct(shape, dtype)

    out_shape = [
        array(sh.tokens, w, dtype=BF16),
        array(sh.tokens, w, dtype=BF16),
        array(w, sh.tokens, dtype=BF16),
        array(sh.blocks, 2 * w, sh.lanes),
        array(sh.blocks, 8, sh.lanes),
    ]
    if closing:
        out_shape += [array(sh.blocks, 1, sh.lanes), array(sh.blocks, 4, sh.block)]
    else:
        out_shape += kept_shapes(sh)
    operands = [qq, *chunk]
    aliases = {2 + len(operands): 3, 3 + len(operands): 4}
    operands += state
    if closing:
        operands.append(gain_square)
    work = sh.group * sh.tokens * sh.tokens // 2
    return pl.pallas_call(
        kernel,
        in_specs=[SMEM, SMEM] + [VMEM] * len(operands),
        out_specs=[VMEM] * len(out_shape),
        out_shape=out_shape,
        input_output_aliases=aliases,
        scratch_shapes=[
            pltpu.VMEM((sh.tokens, w), BF16),
            pltpu.VMEM((sh.tokens, w), BF16),
            pltpu.VMEM((2 * w + ONES_ROWS, sh.tokens), BF16),
        ],
        compiler_params=params(),
        cost_estimate=cost(24 * work * w, 12 * sh.tokens * sh.lanes * 2, work),
        name="forward_far" if closing else "forward_chunk",
    )(me, back, *operands)


def backward_tile(sh, keys, kt_s, dkv_s, dq_s, qg, lse, dot, block, blocks, _):
    start, size = block_rows(sh, block), blocks * sh.block
    rows = pl.ds(start, size)
    k_s, v_s = keys
    k, v = k_s[rows, :], v_s[rows, :]
    empty = jnp.zeros_like(k)
    left = jnp.concatenate([k, empty], axis=0)
    right = jnp.concatenate([empty, v], axis=0)
    stacked = jnp.concatenate([left, right], axis=1)
    scores = [nt(stacked, qg[lanes, :]) for lanes in halves(sh)]
    for lanes, both in zip(halves(sh), scores):
        p = jnp.exp(both[:size] * sh.scale - lse[:, lanes])
        ds = (p * (both[size:] - dot[:, lanes])).astype(BF16)
        dkv_s[0, rows, :] += nn(ds, qg[lanes, : sh.width])
        dkv_s[1, rows, :] += nn(p.astype(BF16), qg[lanes, sh.width :])
        dq_s[:, lanes] += nn(kt_s[:, rows], ds)


def backward_kept(sh, keys, kt_s, dkv_s, dq_s, qg, lse, dot, kept, block, blocks, _):
    start, size = block_rows(sh, block), blocks * sh.block
    rows = pl.ds(start, size)
    v = keys[1][rows, :]
    slopes = [nt(v, qg[lanes, sh.width :]) for lanes in halves(sh)]
    for lanes, slope in zip(halves(sh), slopes):
        parts = []
        for j in range(blocks):
            factor = jnp.exp(kept[1][block + j, :, lanes] - lse[:, lanes])
            at = pl.ds(block_rows(sh, block + j), sh.block)
            parts.append(kept[0][at, lanes].astype(F32) * factor)
        p = jnp.concatenate(parts, axis=0)
        ds = (p * (slope - dot[:, lanes])).astype(BF16)
        dkv_s[0, rows, :] += nn(ds, qg[lanes, : sh.width])
        dkv_s[1, rows, :] += nn(p.astype(BF16), qg[lanes, sh.width :])
        dq_s[:, lanes] += nn(kt_s[:, rows], ds)


def backward_chunk(sh, me, back, qq, keys, distance, grads, lse, dots, dq, norm, order, held):
    w = sh.width
    opening, closing = norm is not None, distance == 0
    per = sh.rows // sh.block

    def kernel(me_ref, back_ref, *refs):
        refs = list(refs)

        def take(count):
            taken = refs[:count]
            del refs[:count]
            return taken

        qq_s, k_s, v_s, kt_s = take(4)
        kept = take(len(keys) - 3)
        (lse_s,) = take(1)
        if opening:
            out_s, gain_ref, *sum_refs = take(2 + len(norm[0]))
        else:
            grad_s, dot_s, dq_in = take(3)
        (held_ref,) = take(1) if held is not None else (None,)
        (dkv_out,) = take(1)
        dq_out = take(len(order) if closing else 1)
        if opening:
            grad_s, dot_s = take(2)
        dkv_s, dq_own = (dkv_out, *refs) if closing else refs
        if held_ref is None:
            dkv_s[...] = jnp.zeros_like(dkv_s)

        def query_block(i):
            qb = block_in_turn(sh, me_ref, order, i)
            dq_s = dq_own if closing else dq_out[0].at[qb]
            if opening:
                features = norm[2]
                token = functools.reduce(jnp.add, [ref[qb] for ref in sum_refs])
                sums = jnp.concatenate([token] * sh.group, axis=1)
                square = sums[0:1] / features + EPSILON
                inverse = lax.rsqrt(square)
                ratio = sums[1:2] / (features * square)
                again = (sums[3:4] - ratio * sums[2:3]) * inverse
                again = again / (features * square)
                plain = out_s[qb, :w, :]
                moved = out_s[qb, w:, :]
                first_grad = gain_ref[...] * (moved - plain * ratio) * inverse
                cot = ((first_grad - plain * again) * inverse).astype(BF16).astype(F32)
                dot_s[qb] = jnp.sum(cot * plain, axis=0, keepdims=True)
                grad_s[qb] = cot.T.astype(BF16)
                dq_s[...] = jnp.zeros((w, sh.lanes), F32)
            elif closing:
                dq_s[...] = dq_in[qb]

            top = sh.blocks if distance else qb + 1
            first = jnp.clip(qb - back_of(sh, me_ref, back_ref, qb) + distance * sh.blocks, 0, top)
            count = top - first

            @pl.when(count > 0)
            def _():
                qg = jnp.concatenate([qq_s[qb, :, :w], grad_s[qb]], axis=1)
                common = (sh, (k_s, v_s), kt_s, dkv_s, dq_s, qg, lse_s[qb], dot_s[qb])
                if kept:
                    run = functools.partial(backward_kept, *common, [ref.at[qb] for ref in kept])
                else:
                    run = functools.partial(backward_tile, *common)
                by_count(sh, first, count, run, False)

            if closing:
                done = (dq_s[...] * sh.scale).T.reshape(sh.group, sh.block, w).astype(BF16)
                at = pl.ds(pl.multiple_of(i % per * sh.block, sh.block), sh.block)
                for j, out in enumerate(dq_out):

                    @pl.when(i // per == j)
                    def _(out=out):
                        out[:, at, :] = done

        each_block(len(order) * per, query_block)
        if not closing:
            dkv_out[...] = dkv_s[...].astype(BF16)

    def array(*shape, dtype=F32):
        return jax.ShapeDtypeStruct(shape, dtype)

    operands = [qq, *keys, lse]
    if opening:
        operands += [grads, norm[1], *norm[0]]
    else:
        operands += [grads, dots, dq]
    aliases = {}
    if not opening and not closing:
        aliases = {1 + len(operands): 1}
    if held is not None:
        aliases = {2 + len(operands): 0}
        operands.append(held)
    out_shape = [array(2, sh.tokens, w, dtype=F32 if closing else BF16)]
    if closing:
        out_shape += [array(sh.group, sh.rows, w, dtype=BF16)] * len(order)
    else:
        out_shape.append(array(sh.blocks, w, sh.lanes))
    if opening:
        out_shape += [
            array(sh.blocks, sh.lanes, w, dtype=BF16),
            array(sh.blocks, 1, sh.lanes),
        ]
    work = sh.group * sh.tokens * len(order) * sh.rows // 2
    return pl.pallas_call(
        kernel,
        in_specs=[SMEM, SMEM] + [VMEM] * len(operands),
        out_specs=[VMEM] * len(out_shape),
        out_shape=out_shape,
        input_output_aliases=aliases,
        scratch_shapes=[pltpu.VMEM((2, sh.tokens, w), F32)] * (not closing)
        + [pltpu.VMEM((w, sh.lanes), F32)],
        compiler_params=params(),
        cost_estimate=cost(1, 1) if closing else cost(20 * work * w, 16 * work, work),
        name="backward_chunk",
    )(me, back, *operands)


def add_arrived(held, arrived):
    def kernel(held_ref, *refs):
        total = held_ref[...]
        for ref in refs[:-1]:
            total += ref[...].astype(F32)
        refs[-1][...] = total

    return pl.pallas_call(
        kernel,
        in_specs=[VMEM] * (1 + len(arrived)),
        out_specs=VMEM,
        out_shape=jax.ShapeDtypeStruct(held.shape, F32),
        input_output_aliases={0: 0},
        compiler_params=params(),
        cost_estimate=cost(0, 10 * held.size),
        name="add_arrived",
    )(held, *arrived)


def combine(sh, me, arrived, held):
    def kernel(me_ref, held_ref, arrived_ref, *outs):
        for m, out in enumerate(outs):
            slot = pl.ds(slot_of(me_ref, m, sh.rows), sh.rows)
            for a, factor in ((0, sh.scale), (1, 1.0)):
                total = held_ref[a, slot, :] + arrived_ref[a, slot, :].astype(F32)
                out[a] = (total * factor).astype(BF16)

    return pl.pallas_call(
        kernel,
        in_specs=[SMEM, VMEM, VMEM],
        out_specs=[VMEM] * sh.parts,
        out_shape=[jax.ShapeDtypeStruct((2, sh.rows, sh.width), BF16)] * sh.parts,
        compiler_params=params(),
        cost_estimate=cost(0, 1),
        name="combine",
    )(me, held, arrived)


def exchanged_with(piece, parts, m):
    return lax.ppermute(piece, "part", [(i, i ^ m) for i in range(parts)]) if m else piece


def exchanged(pieces, parts):
    return [exchanged_with(piece, parts, m) for m, piece in enumerate(pieces)]


def moved_on(value, steps):
    count = lax.axis_size("span")
    pairs = [(i, i + steps) for i in range(count) if 0 <= i + steps < count]
    return lax.ppermute(value, "span", pairs)


def summed_over_head(value):
    count = lax.axis_size("head")
    if count & (count - 1):
        return lax.psum(value, "head")
    step = 1
    while step < count:
        value = value + lax.ppermute(value, "head", [(i, i ^ step) for i in range(count)])
        step *= 2
    return value


def body(queries, keys, values, tangent_queries, tangent_keys, tangent_values, doc_start, out_gain):
    rows, query_heads, width = queries.shape
    key_heads = keys.shape[1]
    group = query_heads // key_heads
    parts = lax.axis_size("part")
    per = doc_start.shape[0]
    block = rows // per
    features = query_heads * width * lax.axis_size("head")
    hops = -(-DOC_DEVS // parts)
    sh = Shape(parts, group, rows, width, block)
    place = lax.axis_index("part")
    me = place.astype(jnp.int32).reshape(1)

    def flat(array):
        return array.reshape(-1, width)

    pieces = split_heads(
        [flat(a) for a in (keys, values, tangent_keys, tangent_values)], parts, 1, doc_start
    )
    q_rows, _ = lax.optimization_barrier(((flat(queries), flat(tangent_queries)), pieces[0]))
    q_pieces = split_heads(q_rows, parts, group)
    own = moved_on(pieces[0], 1)
    pieces = exchanged(pieces, parts)
    chunks = [pieces]
    if parts > 1:
        own, q_pieces = lax.optimization_barrier((own, q_pieces))
        owns = [own]
        for _ in range(hops - 1):
            owns.append(moved_on(owns[-1], 1))
        late, owns = lax.optimization_barrier((pieces[1:], owns))
        rest = jnp.concatenate([moved_on(piece, 1) for piece in late], axis=0)
        chunks.append([owns[0], rest])
        for own in owns[1:]:
            rest = moved_on(rest, 1)
            chunks.append([own, rest])
    else:
        for _ in range(hops):
            chunks.append([own])
            own = moved_on(own, 1)
    q_parts = exchanged(q_pieces[:-1], parts)
    if parts > 1:
        last, _ = lax.optimization_barrier((q_pieces[-1], q_parts[min(1, parts - 2)]))
        q_parts.append(exchanged_with(last, parts, parts - 1))
    else:
        q_parts = q_pieces
    back = jnp.concatenate([p[4 * rows : 4 * rows + per, 0] for p in pieces]).astype(jnp.int32)
    gain = lax.dynamic_index_in_dim(out_gain.reshape(key_heads, group, width), place, 0, False)
    gain_square = jnp.repeat((gain * gain).T, block, axis=1)

    everyone = list(range(parts))
    before, laid = None, chunks[0]
    for order in [everyone[:1], everyone[1:-1], everyone[-1:]] if parts > 1 else [everyone]:
        if order:
            turn = forward_own(sh, me, back, order, [q_parts[m] for m in order], laid, before)
            laid = turn[5:] or laid
            before = list(turn[:5])
    state, qq = before[:2], before[2]
    spans = [(*laid[:3], *before[3:])]
    for distance in range(1, hops):
        k, v, kt, acc, stat, *kept = forward_chunk(
            sh, me, back, qq, chunks[distance], distance, state
        )
        state = [acc, stat]
        spans.append((k, v, kt, *kept))
    k, v, kt, out, _, lse, sums = forward_chunk(
        sh, me, back, qq, chunks[hops], hops, state, gain_square
    )
    spans.append((k, v, kt))
    norm = (exchanged([summed_over_head(sums)] * parts, parts), gain_square, features)

    part, dq, grads, dots = backward_chunk(
        sh, me, back, qq, spans[hops], hops, out, lse, None, None, norm, everyone, None
    )
    arrived = [moved_on(part, -hops)]
    for distance in range(hops - 1, 0, -1):
        part, dq = backward_chunk(
            sh, me, back, qq, spans[distance], distance, grads, lse, dots, dq, None,
            everyone, None,
        )
        arrived.append(moved_on(part, -distance))
    turns = [everyone[-1:], everyone[1:-1], everyone[:1]] if parts > 1 else [everyone]
    held, dq_pieces = None, [None] * parts
    for order in filter(None, turns):
        held, *done = backward_chunk(
            sh, me, back, qq, spans[0], 0, grads, lse, dots, dq, None, order, held
        )
        for m, piece in zip(order, done):
            dq_pieces[m] = piece.reshape(1, group, rows, width)
    dq_pieces = exchanged(dq_pieces, parts)
    dq_pieces[-1], held = lax.optimization_barrier((dq_pieces[-1], held))
    if arrived[1:]:
        held = add_arrived(held, arrived[:-1])
    dkv_pieces = exchanged(combine(sh, me, arrived[-1], held), parts)
    dkv_pieces = [p.reshape(2, 1, rows, width) for p in dkv_pieces]
    (product_queries,) = join_heads([(dq_pieces, 1, group)])
    product_keys, product_values = join_heads([(dkv_pieces, 2, 1)])
    return (
        product_queries.reshape(queries.shape),
        product_keys.reshape(keys.shape),
        product_values.reshape(keys.shape),
    )


def solution(mesh):
    def run(*arguments):
        count, heads = mesh.shape["ctx"], mesh.shape["head"]
        parts = arguments[1].shape[1] // heads
        split = Mesh(
            mesh.devices.reshape(count // parts, parts, heads), ("span", "part", "head")
        )
        ctx = ("span", "part")
        array = P(ctx, "head", None)
        return jax.shard_map(
            body,
            mesh=split,
            in_specs=(array,) * 6 + (P(ctx), P("head")),
            out_specs=(array,) * 3,
            check_vma=False,
        )(*arguments)

    return run
```

```python
import functools

import jax
import jax.numpy as jnp
from jax import lax
from jax.experimental import pallas as pl
from jax.experimental.pallas import tpu as pltpu
from jax.sharding import Mesh, PartitionSpec as P

DOC_DEVS = 8
EPSILON = 1e-06
VMEM_BYTES = 18 * 1024 * 1024
NOTE_ROWS = 16
ONES_ROWS = 16
WIDE_VMEM_BYTES = 60 * 1024 * 1024
MASKED = -1e30
F32 = jnp.float32
BF16 = jnp.bfloat16
SMEM = pl.BlockSpec(memory_space=pltpu.SMEM)
VMEM = pl.BlockSpec(memory_space=pltpu.VMEM)


def params(size=VMEM_BYTES):
    return pltpu.CompilerParams(vmem_limit_bytes=size)


def cost(flops, moved, powers=0):
    return pl.CostEstimate(flops=int(flops), bytes_accessed=int(moved), transcendentals=int(powers))


def nn(a, b):
    return lax.dot_general(a, b, (((1,), (0,)), ((), ())), preferred_element_type=F32)


def nt(a, b):
    return lax.dot_general(a, b, (((1,), (1,)), ((), ())), preferred_element_type=F32)


def split_heads(arrays, parts, per_part, notes=None):
    count = len(arrays)
    total, width = arrays[0].shape
    heads = parts * per_part
    rows = total // heads
    length = count * per_part * rows
    span = per_part * rows
    extra = 0 if notes is None else NOTE_ROWS
    scalars = [] if notes is None else [notes]

    def kernel(*refs):
        ins = list(refs[: len(scalars) + count])
        results = refs[len(scalars) + count : len(scalars) + count + parts]
        held, wide, sems, *staged = refs[len(scalars) + count + parts :]
        outs, out_sems = (staged[:-1], staged[-1]) if extra else (results, None)
        mine = lax.axis_index("part")
        if extra:
            note_ref = ins.pop(0)
        copies = [pltpu.make_async_copy(ins[a], held.at[a], sems.at[a]) for a in range(count)]
        for copy in copies:
            copy.start()
        leaving = []

        def leave(m, a, start, size):
            part = pl.ds(start, size)
            sem = out_sems.at[m * (count + 1) + a]
            leaving.append(pltpu.make_async_copy(outs[m].at[part], results[m].at[part], sem))
            leaving[-1].start()

        if extra:
            first = (lax.axis_index("span") * parts + mine) * notes.shape[0]
            line = lax.broadcasted_iota(jnp.int32, (extra, width), 0)
            lines = jnp.zeros((extra, width), jnp.int32)
            for i in range(notes.shape[0]):
                lines = jnp.where(line == i, first + i - note_ref[i], lines)
            for m, out in enumerate(outs):
                out[length:, :] = lines.astype(F32).astype(BF16)
                leave(m, count, length, extra)
        for a in range(count):
            copies[a].wait()
            wide[...] = held[a].astype(F32)
            for m in range(parts):
                for r in range(per_part):
                    head = jnp.bitwise_xor(mine, m) * per_part + r
                    at = (a * per_part + r) * rows
                    outs[m][at : at + rows, :] = wide[pl.ds(head, rows, stride=heads), :].astype(BF16)
                if extra:
                    leave(m, a, a * span, span)
        for copy in leaving:
            copy.wait()

    piece = (length + extra, width)
    scratch = [
        pltpu.VMEM((count, total, width), BF16),
        pltpu.VMEM((total, width), F32),
        pltpu.SemaphoreType.DMA((count,)),
    ]
    if extra:
        scratch += [pltpu.VMEM(piece, BF16)] * parts
        scratch.append(pltpu.SemaphoreType.DMA((parts * (count + 1),)))
    return pl.pallas_call(
        kernel,
        in_specs=[SMEM] * len(scalars) + [pl.BlockSpec(memory_space=pltpu.HBM)] * count,
        out_specs=[pl.BlockSpec(memory_space=pltpu.HBM) if extra else VMEM] * parts,
        out_shape=[jax.ShapeDtypeStruct(piece, BF16)] * parts,
        scratch_shapes=scratch,
        compiler_params=params(VMEM_BYTES if notes is None else WIDE_VMEM_BYTES),
        cost_estimate=cost(0, 4 * count * total * width),
        name="split_heads",
    )(*scalars, *arrays)


def join_heads(groups):
    parts = len(groups[0][0])
    rows, width = groups[0][0][0].shape[-2:]
    steps = 4
    cut = rows // steps

    def kernel(*refs):
        ins, outs = list(refs[: parts * len(groups)]), list(refs[parts * len(groups) :])
        mine = lax.axis_index("part")
        for _, count, per_part in groups:
            for a in range(count):
                for m in range(parts):
                    for r in range(per_part):
                        head = jnp.bitwise_xor(mine, m) * per_part + r
                        rows_of_head = pl.ds(head, cut, stride=parts * per_part)
                        outs[a][rows_of_head, :] = ins[m][a, r].astype(F32)
            del ins[:parts], outs[:count]

    in_specs, out_specs, out_shape = [], [], []
    for _, count, per_part in groups:
        heads = parts * per_part
        block = (count, per_part, cut, width)
        in_specs += [pl.BlockSpec(block, lambda i: (0, 0, i, 0))] * parts
        out_specs += [pl.BlockSpec((cut * heads, width), lambda i: (i, 0))] * count
        out_shape += [jax.ShapeDtypeStruct((rows * heads, width), F32)] * count
    return pl.pallas_call(
        kernel,
        grid=(steps,),
        in_specs=in_specs,
        out_specs=out_specs,
        out_shape=out_shape,
        compiler_params=params(),
        cost_estimate=cost(0, sum(6 * shape.size for shape in out_shape)),
        name="join_heads",
    )(*[piece for pieces, _, _ in groups for piece in pieces])


def slot_of(me_ref, m, rows):
    return pl.multiple_of(jnp.bitwise_xor(me_ref[0], m) * rows, rows)


class Shape:
    def __init__(self, parts, group, rows, width, block):
        self.parts, self.group, self.rows, self.width, self.block = parts, group, rows, width, block
        self.tokens = parts * rows
        self.blocks = self.tokens // block
        self.lanes = group * block
        self.scale = width**-0.5


def diagonal(sh):
    shape = (sh.block, sh.block)
    key = lax.broadcasted_iota(jnp.int32, shape, 0)
    query = lax.broadcasted_iota(jnp.int32, shape, 1)
    return key <= query


def below_diagonal(sh, value, other):
    allowed = diagonal(sh)
    cut = [value[:, at : at + sh.block] for at in range(0, value.shape[1], sh.block)]
    return jnp.concatenate([jnp.where(allowed, part, other) for part in cut], axis=1)


def halves(sh):
    if sh.group % 2:
        return [slice(0, sh.lanes)]
    return [slice(0, sh.lanes // 2), slice(sh.lanes // 2, sh.lanes)]


def stacked_keys(keys, start, size):
    k_s, tk_s = keys
    k = k_s[pl.ds(start, size), :]
    tk = tk_s[pl.ds(start, size), :]
    left = jnp.concatenate([k, tk], axis=0)
    right = jnp.concatenate([jnp.zeros_like(k), k], axis=0)
    return jnp.concatenate([left, right], axis=1)


def pieces_of(sh, start, blocks):
    sizes = [2] * (blocks // 2) + [1] * (blocks % 2)
    firsts = [sum(sizes[:i]) for i in range(len(sizes))]
    return [
        (pl.multiple_of(start + first * sh.block, sh.block), size * sh.block, i == len(sizes) - 1)
        for i, (first, size) in enumerate(zip(firsts, sizes))
    ]


def cut_diagonal(sh, value, other):
    low = below_diagonal(sh, value[value.shape[0] - sh.block :], other)
    if value.shape[0] == sh.block:
        return low
    return jnp.concatenate([value[: value.shape[0] - sh.block], low], axis=0)


def block_rows(sh, block):
    return pl.multiple_of(block * sh.block, sh.block)


def load_state(stat, lanes):
    return tuple(stat[r : r + 1, lanes] for r in range(3))


def forward_tile(sh, keys, vt_s, acc, stat, kept, qq, block, blocks, masked):
    w = sh.width
    start = block_rows(sh, block)
    pieces = pieces_of(sh, start, blocks)
    stacked = [stacked_keys(keys, at, size) for at, size, _ in pieces]
    at = pl.ds(start, blocks * sh.block)
    lanes = halves(sh)
    scores = [[] for _ in lanes]
    mixed = [[] for _ in lanes]
    most = [None for _ in lanes]
    state = [None if masked else load_state(stat, part) for part in lanes]

    def score(h, c):
        both = nt(stacked[c], qq[lanes[h], :])
        s, d = both[: pieces[c][1]], both[pieces[c][1] :]
        if masked and pieces[c][2]:
            s = cut_diagonal(sh, s, MASKED)
        scores[h].append((s, d))

    def top(h):
        peaks = [jnp.max(s, axis=0, keepdims=True) for s, _ in scores[h]]
        most[h] = functools.reduce(jnp.maximum, peaks) * sh.scale
        if not masked:
            most[h] = jnp.maximum(most[h], state[h][0])
        if kept is not None:
            for j in range(blocks):
                kept[1][block + j, :, lanes[h]] = most[h]

    def soften(h, c):
        s, d = scores[h][c]
        e = jnp.exp(s * sh.scale - most[h])
        mixed[h].append((e.astype(BF16), (e * d).astype(BF16)))
        if kept is not None:
            kept[0][pl.ds(pieces[c][0], pieces[c][1]), lanes[h]] = mixed[h][-1][0]

    def gather(h, i):
        return jnp.concatenate([pair[i] for pair in mixed[h]], axis=0)

    def finish(h, plain, moving):
        total, cross = plain[2 * w : 2 * w + 1], moving[w : w + 1]
        tangent = plain[:w] + moving[:w] * sh.scale
        plain = plain[w : 2 * w]
        if not masked:
            decay = jnp.exp(state[h][0] - most[h])
            plain = acc[:w, lanes[h]] * decay + plain
            tangent = acc[w:, lanes[h]] * decay + tangent
            total, cross = state[h][1] * decay + total, state[h][2] * decay + cross
        acc[:w, lanes[h]] = plain
        acc[w:, lanes[h]] = tangent
        for r, value in enumerate((most[h], total, cross)):
            stat[r : r + 1, lanes[h]] = value

    for h in range(len(lanes) + 1):
        if h > 0:
            top(h - 1)
        for c in range(len(pieces)):
            if h < len(lanes):
                score(h, c)
            if h > 0:
                soften(h - 1, c)
        if h > 0:
            plain = nn(vt_s[:, at], gather(h - 1, 0))
            moving = nn(vt_s[w:, at], gather(h - 1, 1))
            finish(h - 1, plain, moving)


def by_count(sh, low, count, run, masked):
    most = min(4 if masked else 3, sh.blocks)
    head = lax.rem(count - 1, 4) + 1 if masked else lax.rem(count, 4)
    for blocks in range(1, most + 1):

        @pl.when(head == blocks)
        def _(blocks=blocks):
            run(low + count - blocks if masked else low, blocks, masked)

    def step(i, carry):
        run(low + (0 if masked else head) + 4 * i, 4, False)
        return carry

    if sh.blocks >= 4:
        lax.fori_loop(0, (count - head) // 4, step, 0)


def lay_chunk(sh, me_ref, sources, targets):
    for m, (ref, base) in enumerate(sources):
        slot = pl.ds(slot_of(me_ref, m, sh.rows), sh.rows)
        for i, target in enumerate(targets):
            at = base + i * sh.rows
            target[slot, :] = ref[at : at + sh.rows, :]


def lay_queries(sh, me_ref, order, pieces, qq):
    per = sh.rows // sh.block
    for m, ref in zip(order, pieces):
        for i in range(2):
            for g in range(sh.group):
                for r in range(per):
                    block = jnp.bitwise_xor(me_ref[0], m) * per + r
                    at = (i * sh.group + g) * sh.rows + r * sh.block
                    qq[
                        block,
                        g * sh.block : (g + 1) * sh.block,
                        i * sh.width : (i + 1) * sh.width,
                    ] = ref[at : at + sh.block, :]


def lay_span(sh, me_ref, sources, laid):
    w = sh.width
    k_s, v_s, kt_s, tk_s, vt_s, tv_s = laid
    lay_chunk(sh, me_ref, sources, (k_s, v_s, tk_s, tv_s))
    kt_s[...] = transposed(k_s[...])
    vt_s[:w, :] = transposed(tv_s[...])
    vt_s[w : 2 * w, :] = transposed(v_s[...])
    vt_s[2 * w :, :] = jnp.ones((ONES_ROWS, sh.tokens), BF16)


def transposed(x):
    return x.astype(F32).T.astype(BF16)


def located(sh, refs):
    length = refs[0].shape[0]
    return [(ref, at) for ref in refs for at in range(0, ref.shape[0], length)]


def back_of(sh, me_ref, back_ref, qb):
    per = sh.rows // sh.block
    return back_ref[jnp.bitwise_xor(me_ref[0], qb // per) * per + qb % per]


def each_block(count, run):
    def step(i, carry):
        run(i)
        return carry

    lax.fori_loop(0, count, step, 0)


def block_in_turn(sh, me_ref, order, i):
    per = sh.rows // sh.block
    if order == list(range(sh.parts)):
        return i
    partner = order[0]
    for j in range(1, len(order)):
        partner = jnp.where(i // per == j, order[j], partner)
    return jnp.bitwise_xor(me_ref[0], partner) * per + i % per


def kept_shapes(sh):
    return [
        jax.ShapeDtypeStruct((sh.blocks, sh.tokens, sh.lanes), BF16),
        jax.ShapeDtypeStruct((sh.blocks, sh.blocks, 1, sh.lanes), F32),
    ]


def forward_own(sh, me, back, order, queries, chunk, before):
    w = sh.width
    first = before is None
    turns = len(order) * (sh.rows // sh.block)

    def kernel(me_ref, back_ref, *refs):
        refs = list(refs)

        def take(count):
            taken = refs[:count]
            del refs[:count]
            return taken

        q_in = take(len(order))
        if first:
            kv_in = take(len(chunk))
            accs, stats, qq_s, es, ms = take(5)
            laid = refs
            lay_span(sh, me_ref, located(sh, kv_in), laid)
        else:
            laid = take(len(chunk))
            take(5)
            accs, stats, qq_s, es, ms = refs
        k_s, _, _, tk_s, vt_s = laid[:5]
        lay_queries(sh, me_ref, order, q_in, qq_s)

        def query_block(i):
            qb = block_in_turn(sh, me_ref, order, i)
            low = jnp.clip(qb - back_of(sh, me_ref, back_ref, qb), 0, qb)
            run = functools.partial(
                forward_tile,
                sh,
                (k_s, tk_s),
                vt_s,
                accs.at[qb],
                stats.at[qb],
                (es.at[qb], ms.at[qb]),
                qq_s[qb],
            )
            by_count(sh, low, qb + 1 - low, run, True)

        each_block(turns, query_block)

    def array(*shape, dtype=F32):
        return jax.ShapeDtypeStruct(shape, dtype)

    span = array(sh.tokens, w, dtype=BF16)
    out_shape = [
        array(sh.blocks, 2 * w, sh.lanes),
        array(sh.blocks, 8, sh.lanes),
        array(sh.blocks, sh.lanes, 2 * w, dtype=BF16),
        *kept_shapes(sh),
    ]
    operands = [*queries, *chunk]
    aliases = {}
    if first:
        out_shape += [span, span, array(w, sh.tokens, dtype=BF16), span]
        out_shape.append(array(2 * w + ONES_ROWS, sh.tokens, dtype=BF16))
    else:
        aliases = {2 + len(operands) + i: i for i in range(5)}
        operands += before
    work = sh.group * sh.tokens * sh.block * turns // 2
    return pl.pallas_call(
        kernel,
        in_specs=[SMEM, SMEM] + [VMEM] * len(operands),
        out_specs=[VMEM] * len(out_shape),
        out_shape=out_shape,
        input_output_aliases=aliases,
        scratch_shapes=[pltpu.VMEM((sh.tokens, w), BF16)] * first,
        compiler_params=params(),
        cost_estimate=cost(12 * work * w, 4 * sh.tokens * sh.lanes, work),
        name="forward_own",
    )(me, back, *operands)


def forward_chunk(sh, me, back, qq, chunk, distance, state, gain_square=None):
    w = sh.width
    closing = gain_square is not None

    def kernel(me_ref, back_ref, qq_s, *refs):
        refs = list(refs)

        def take(count):
            taken = refs[:count]
            del refs[:count]
            return taken

        kv_in = take(len(chunk))
        take(2)
        if closing:
            (gain_ref,) = take(1)
        k_s, v_s, kt_s, accs, stats = take(5)
        last = take(2)
        if closing:
            lse, sums = last
        tk_s, tv_s, vt_s = refs
        lay_span(sh, me_ref, located(sh, kv_in), (k_s, v_s, kt_s, tk_s, vt_s, tv_s))

        def query_block(qb):
            acc, stat = accs.at[qb], stats.at[qb]
            first = qb - back_of(sh, me_ref, back_ref, qb) + distance * sh.blocks
            first = jnp.clip(first, 0, sh.blocks)
            count = sh.blocks - first

            @pl.when(count > 0)
            def _():
                kept = None if closing else [ref.at[qb] for ref in last]
                run = functools.partial(
                    forward_tile, sh, (k_s, tk_s), vt_s, acc, stat, kept, qq_s[qb]
                )
                by_count(sh, first, count, run, False)

            if closing:
                most, total, cross = load_state(stat, slice(None))
                inverse = 1.0 / total
                plain = acc[:w, :] * inverse
                moved = acc[w:, :] * inverse - (cross * inverse * sh.scale) * plain
                acc[:w, :] = plain
                acc[w:, :] = moved
                lse[qb] = most + jnp.log(total)
                square = plain * plain
                product = plain * moved
                gain = gain_ref[...]
                for r, value in enumerate((square, product, gain * square, gain * product)):
                    line = jnp.sum(value, axis=0, keepdims=True)
                    pieces = [line[:, g * sh.block : (g + 1) * sh.block] for g in range(sh.group)]
                    sums[qb, r : r + 1, :] = functools.reduce(jnp.add, pieces)

        each_block(sh.blocks, query_block)

    def array(*shape, dtype=F32):
        return jax.ShapeDtypeStruct(shape, dtype)

    out_shape = [
        array(sh.tokens, w, dtype=BF16),
        array(sh.tokens, w, dtype=BF16),
        array(w, sh.tokens, dtype=BF16),
        array(sh.blocks, 2 * w, sh.lanes),
        array(sh.blocks, 8, sh.lanes),
    ]
    if closing:
        out_shape += [array(sh.blocks, 1, sh.lanes), array(sh.blocks, 4, sh.block)]
    else:
        out_shape += kept_shapes(sh)
    operands = [qq, *chunk]
    aliases = {2 + len(operands): 3, 3 + len(operands): 4}
    operands += state
    if closing:
        operands.append(gain_square)
    work = sh.group * sh.tokens * sh.tokens // 2
    return pl.pallas_call(
        kernel,
        in_specs=[SMEM, SMEM] + [VMEM] * len(operands),
        out_specs=[VMEM] * len(out_shape),
        out_shape=out_shape,
        input_output_aliases=aliases,
        scratch_shapes=[
            pltpu.VMEM((sh.tokens, w), BF16),
            pltpu.VMEM((sh.tokens, w), BF16),
            pltpu.VMEM((2 * w + ONES_ROWS, sh.tokens), BF16),
        ],
        compiler_params=params(),
        cost_estimate=cost(24 * work * w, 12 * sh.tokens * sh.lanes * 2, work),
        name="forward_far" if closing else "forward_chunk",
    )(me, back, *operands)


def backward_tile(sh, keys, kt_s, dkv_s, dq_s, qg, lse, dot, block, blocks, _):
    start, size = block_rows(sh, block), blocks * sh.block
    rows = pl.ds(start, size)
    k_s, v_s = keys
    k, v = k_s[rows, :], v_s[rows, :]
    empty = jnp.zeros_like(k)
    left = jnp.concatenate([k, empty], axis=0)
    right = jnp.concatenate([empty, v], axis=0)
    stacked = jnp.concatenate([left, right], axis=1)
    scores = [nt(stacked, qg[lanes, :]) for lanes in halves(sh)]
    for lanes, both in zip(halves(sh), scores):
        p = jnp.exp(both[:size] * sh.scale - lse[:, lanes])
        ds = (p * (both[size:] - dot[:, lanes])).astype(BF16)
        dkv_s[0, rows, :] += nn(ds, qg[lanes, : sh.width])
        dkv_s[1, rows, :] += nn(p.astype(BF16), qg[lanes, sh.width :])
        dq_s[:, lanes] += nn(kt_s[:, rows], ds)


def backward_kept(sh, keys, kt_s, dkv_s, dq_s, qg, lse, dot, kept, block, blocks, _):
    start, size = block_rows(sh, block), blocks * sh.block
    rows = pl.ds(start, size)
    v = keys[1][rows, :]
    slopes = [nt(v, qg[lanes, sh.width :]) for lanes in halves(sh)]
    for lanes, slope in zip(halves(sh), slopes):
        parts = []
        for j in range(blocks):
            factor = jnp.exp(kept[1][block + j, :, lanes] - lse[:, lanes])
            at = pl.ds(block_rows(sh, block + j), sh.block)
            parts.append(kept[0][at, lanes].astype(F32) * factor)
        p = jnp.concatenate(parts, axis=0)
        ds = (p * (slope - dot[:, lanes])).astype(BF16)
        dkv_s[0, rows, :] += nn(ds, qg[lanes, : sh.width])
        dkv_s[1, rows, :] += nn(p.astype(BF16), qg[lanes, sh.width :])
        dq_s[:, lanes] += nn(kt_s[:, rows], ds)


def backward_chunk(sh, me, back, qq, keys, distance, grads, lse, dots, dq, norm, order, held):
    w = sh.width
    opening, closing = norm is not None, distance == 0
    skip = sh.unreached if opening else 0
    per = sh.rows // sh.block

    def kernel(me_ref, back_ref, *refs):
        refs = list(refs)

        def take(count):
            taken = refs[:count]
            del refs[:count]
            return taken

        qq_s, k_s, v_s, kt_s = take(4)
        kept = take(len(keys) - 3)
        (lse_s,) = take(1)
        if opening:
            out_s, gain_ref, *sum_refs = take(2 + len(norm[0]))
        else:
            grad_s, dot_s, dq_in = take(3)
        (held_ref,) = take(1) if held is not None else (None,)
        (dkv_out,) = take(1)
        dq_out = take(len(order) if closing else 1)
        if opening:
            grad_s, dot_s = take(2)
        dkv_s, dq_own = (dkv_out, *refs) if closing else refs
        if held_ref is None:
            dkv_s[...] = jnp.zeros_like(dkv_s)

        def query_block(i):
            qb = block_in_turn(sh, me_ref, order, i)
            dq_s = dq_own if closing else dq_out[0].at[qb]
            if opening:
                features = norm[2]
                token = functools.reduce(jnp.add, [ref[qb] for ref in sum_refs])
                sums = jnp.concatenate([token] * sh.group, axis=1)
                square = sums[0:1] / features + EPSILON
                inverse = lax.rsqrt(square)
                ratio = sums[1:2] / (features * square)
                again = (sums[3:4] - ratio * sums[2:3]) * inverse
                again = again / (features * square)
                plain = out_s[qb, :w, :]
                moved = out_s[qb, w:, :]
                first_grad = gain_ref[...] * (moved - plain * ratio) * inverse
                cot = ((first_grad - plain * again) * inverse).astype(BF16).astype(F32)
                dot_s[qb] = jnp.sum(cot * plain, axis=0, keepdims=True)
                grad_s[qb] = cot.T.astype(BF16)
                dq_s[...] = jnp.zeros((w, sh.lanes), F32)
            elif closing:
                dq_s[...] = dq_in[qb]

            top = sh.blocks if distance else qb + 1
            first = jnp.clip(qb - back_of(sh, me_ref, back_ref, qb) + distance * sh.blocks, 0, top)
            count = top - first

            @pl.when(count > 0)
            def _():
                qg = jnp.concatenate([qq_s[qb, :, :w], grad_s[qb]], axis=1)
                common = (sh, (k_s, v_s), kt_s, dkv_s, dq_s, qg, lse_s[qb], dot_s[qb])
                if kept:
                    run = functools.partial(backward_kept, *common, [ref.at[qb] for ref in kept])
                else:
                    run = functools.partial(backward_tile, *common)
                by_count(sh, first, count, run, False)

            if closing:
                done = (dq_s[...] * sh.scale).T.reshape(sh.group, sh.block, w).astype(BF16)
                at = pl.ds(pl.multiple_of(i % per * sh.block, sh.block), sh.block)
                for j, out in enumerate(dq_out):

                    @pl.when(i // per == j)
                    def _(out=out):
                        out[:, at, :] = done

        each_block(len(order) * per, query_block)
        if not closing:
            dkv_out[...] = dkv_s[:, skip:, :].astype(BF16)

    def array(*shape, dtype=F32):
        return jax.ShapeDtypeStruct(shape, dtype)

    operands = [qq, *keys, lse]
    if opening:
        operands += [grads, norm[1], *norm[0]]
    else:
        operands += [grads, dots, dq]
    aliases = {}
    if not opening and not closing:
        aliases = {1 + len(operands): 1}
    if held is not None:
        aliases = {2 + len(operands): 0}
        operands.append(held)
    out_shape = [array(2, sh.tokens - skip, w, dtype=F32 if closing else BF16)]
    if closing:
        out_shape += [array(sh.group, sh.rows, w, dtype=BF16)] * len(order)
    else:
        out_shape.append(array(sh.blocks, w, sh.lanes))
    if opening:
        out_shape += [
            array(sh.blocks, sh.lanes, w, dtype=BF16),
            array(sh.blocks, 1, sh.lanes),
        ]
    work = sh.group * sh.tokens * len(order) * sh.rows // 2
    return pl.pallas_call(
        kernel,
        in_specs=[SMEM, SMEM] + [VMEM] * len(operands),
        out_specs=[VMEM] * len(out_shape),
        out_shape=out_shape,
        input_output_aliases=aliases,
        scratch_shapes=[pltpu.VMEM((2, sh.tokens, w), F32)] * (not closing)
        + [pltpu.VMEM((w, sh.lanes), F32)],
        compiler_params=params(),
        cost_estimate=cost(1, 1) if closing else cost(20 * work * w, 16 * work, work),
        name="backward_chunk",
    )(me, back, *operands)


def add_arrived(held, arrived):
    def kernel(held_ref, *refs):
        total = refs[-1]
        total[...] = held_ref[...]
        for ref in refs[:-1]:
            start = total.shape[1] - ref.shape[1]
            total[:, start:, :] += ref[...].astype(F32)

    return pl.pallas_call(
        kernel,
        in_specs=[VMEM] * (1 + len(arrived)),
        out_specs=VMEM,
        out_shape=jax.ShapeDtypeStruct(held.shape, F32),
        input_output_aliases={0: 0},
        compiler_params=params(),
        cost_estimate=cost(0, 10 * held.size),
        name="add_arrived",
    )(held, *arrived)


def combine(sh, me, arrived, held):
    def kernel(me_ref, held_ref, arrived_ref, *outs):
        for m, out in enumerate(outs):
            slot = pl.ds(slot_of(me_ref, m, sh.rows), sh.rows)
            for a, factor in ((0, sh.scale), (1, 1.0)):
                total = held_ref[a, slot, :] + arrived_ref[a, slot, :].astype(F32)
                out[a] = (total * factor).astype(BF16)

    return pl.pallas_call(
        kernel,
        in_specs=[SMEM, VMEM, VMEM],
        out_specs=[VMEM] * sh.parts,
        out_shape=[jax.ShapeDtypeStruct((2, sh.rows, sh.width), BF16)] * sh.parts,
        compiler_params=params(),
        cost_estimate=cost(0, 1),
        name="combine",
    )(me, held, arrived)


def exchanged_with(piece, parts, m):
    return lax.ppermute(piece, "part", [(i, i ^ m) for i in range(parts)]) if m else piece


def exchanged(pieces, parts):
    return [exchanged_with(piece, parts, m) for m, piece in enumerate(pieces)]


def moved_on(value, steps):
    count = lax.axis_size("span")
    pairs = [(i, i + steps) for i in range(count) if 0 <= i + steps < count]
    return lax.ppermute(value, "span", pairs)


def summed_over_head(value):
    count = lax.axis_size("head")
    if count & (count - 1):
        return lax.psum(value, "head")
    step = 1
    while step < count:
        value = value + lax.ppermute(value, "head", [(i, i ^ step) for i in range(count)])
        step *= 2
    return value


def body(queries, keys, values, tangent_queries, tangent_keys, tangent_values, doc_start, out_gain):
    rows, query_heads, width = queries.shape
    key_heads = keys.shape[1]
    group = query_heads // key_heads
    parts = lax.axis_size("part")
    per = doc_start.shape[0]
    block = rows // per
    features = query_heads * width * lax.axis_size("head")
    hops = -(-DOC_DEVS // parts)
    sh = Shape(parts, group, rows, width, block)
    sh.unreached = max(0, hops * sh.blocks - DOC_DEVS * per + 1) * block if hops > 1 else 0
    place = lax.axis_index("part")
    me = place.astype(jnp.int32).reshape(1)

    def flat(array):
        return array.reshape(-1, width)

    pieces = split_heads(
        [flat(a) for a in (keys, values, tangent_keys, tangent_values)], parts, 1, doc_start
    )
    q_rows, _ = lax.optimization_barrier(((flat(queries), flat(tangent_queries)), pieces[0]))
    q_pieces = split_heads(q_rows, parts, group)
    own = moved_on(pieces[0], 1)
    pieces = exchanged(pieces, parts)
    chunks = [pieces]
    if parts > 1:
        own, q_pieces = lax.optimization_barrier((own, q_pieces))
        owns = [own]
        for _ in range(hops - 1):
            owns.append(moved_on(owns[-1], 1))
        late, owns = lax.optimization_barrier((pieces[1:], owns))
        rest = jnp.concatenate([moved_on(piece, 1) for piece in late], axis=0)
        chunks.append([owns[0], rest])
        for own in owns[1:]:
            rest = moved_on(rest, 1)
            chunks.append([own, rest])
    else:
        for _ in range(hops):
            chunks.append([own])
            own = moved_on(own, 1)
    q_parts = exchanged(q_pieces[:-1], parts)
    if parts > 1:
        last, _ = lax.optimization_barrier((q_pieces[-1], q_parts[min(1, parts - 2)]))
        q_parts.append(exchanged_with(last, parts, parts - 1))
    else:
        q_parts = q_pieces
    back = jnp.concatenate([p[4 * rows : 4 * rows + per, 0] for p in pieces]).astype(jnp.int32)
    gain = lax.dynamic_index_in_dim(out_gain.reshape(key_heads, group, width), place, 0, False)
    gain_square = jnp.repeat((gain * gain).T, block, axis=1)

    everyone = list(range(parts))
    before, laid = None, chunks[0]
    for order in [everyone[:1], everyone[1:-1], everyone[-1:]] if parts > 1 else [everyone]:
        if order:
            turn = forward_own(sh, me, back, order, [q_parts[m] for m in order], laid, before)
            laid = turn[5:] or laid
            before = list(turn[:5])
    state, qq = before[:2], before[2]
    spans = [(*laid[:3], *before[3:])]
    for distance in range(1, hops):
        k, v, kt, acc, stat, *kept = forward_chunk(
            sh, me, back, qq, chunks[distance], distance, state
        )
        state = [acc, stat]
        spans.append((k, v, kt, *kept))
    k, v, kt, out, _, lse, sums = forward_chunk(
        sh, me, back, qq, chunks[hops], hops, state, gain_square
    )
    spans.append((k, v, kt))
    norm = (exchanged([summed_over_head(sums)] * parts, parts), gain_square, features)

    part, dq, grads, dots = backward_chunk(
        sh, me, back, qq, spans[hops], hops, out, lse, None, None, norm, everyone, None
    )
    arrived = [moved_on(part, -hops)]
    for distance in range(hops - 1, 0, -1):
        part, dq = backward_chunk(
            sh, me, back, qq, spans[distance], distance, grads, lse, dots, dq, None,
            everyone, None,
        )
        arrived.append(moved_on(part, -distance))
    turns = [everyone[-1:], everyone[1:-1], everyone[:1]] if parts > 1 else [everyone]
    held, dq_pieces = None, [None] * parts
    for order in filter(None, turns):
        held, *done = backward_chunk(
            sh, me, back, qq, spans[0], 0, grads, lse, dots, dq, None, order, held
        )
        for m, piece in zip(order, done):
            dq_pieces[m] = piece.reshape(1, group, rows, width)
    dq_pieces = exchanged(dq_pieces, parts)
    dq_pieces[-1], held = lax.optimization_barrier((dq_pieces[-1], held))
    if arrived[1:]:
        held = add_arrived(held, arrived[:-1])
    dkv_pieces = exchanged(combine(sh, me, arrived[-1], held), parts)
    dkv_pieces = [p.reshape(2, 1, rows, width) for p in dkv_pieces]
    (product_queries,) = join_heads([(dq_pieces, 1, group)])
    product_keys, product_values = join_heads([(dkv_pieces, 2, 1)])
    return (
        product_queries.reshape(queries.shape),
        product_keys.reshape(keys.shape),
        product_values.reshape(keys.shape),
    )


def solution(mesh):
    def run(*arguments):
        count, heads = mesh.shape["ctx"], mesh.shape["head"]
        parts = arguments[1].shape[1] // heads
        split = Mesh(
            mesh.devices.reshape(count // parts, parts, heads), ("span", "part", "head")
        )
        ctx = ("span", "part")
        array = P(ctx, "head", None)
        return jax.shard_map(
            body,
            mesh=split,
            in_specs=(array,) * 6 + (P(ctx), P("head")),
            out_specs=(array,) * 3,
            check_vma=False,
        )(*arguments)

    return run
```
